32 devices in a mesh: seq: 8 (over z, x), head: 4 (over y, core).
Axes of the slice: x: 2, y: 2, z: 4, core: 2. Of those that a mesh axis runs over, the one named last changes fastest.
Arguments:
- tokens: bfloat16 [2048, 1536], P('seq'), may hold values from -6 to 6
- attn_gain: float32 [1536], replicated, may hold values from 0.5 to 1.5
- query_weight: bfloat16 [1536, 1536], P('seq', 'head'), may hold values from -0.15625 to 0.15625
- key_weight: bfloat16 [1536, 1536], P('seq', 'head'), may hold values from -0.15625 to 0.15625
- value_weight: bfloat16 [1536, 1536], P('seq', 'head'), may hold values from -0.15625 to 0.15625
- forget_weight: bfloat16 [1536, 24], P('seq', 'head'), may hold values from -0.15625 to 0.15625
- forget_bias: float32 [24], P('head'), may hold values from 3 to 10
- out_weight: bfloat16 [1536, 1536], P('head', 'seq'), may hold values from -1.5 to 1.5
- ffn_gain: float32 [1536], replicated, may hold values from 0.5 to 1.5
- gate_weight: bfloat16 [1536, 4096], P('seq', 'head'), may hold values from -0.15625 to 0.15625
- up_weight: bfloat16 [1536, 4096], P('seq', 'head'), may hold values from -0.15625 to 0.15625
- down_weight: bfloat16 [4096, 1536], P('head', 'seq'), may hold values from -0.09375 to 0.09375
- doc_lengths: int32 [4], replicated, may hold values from 1 to 1024, 2048 in all
- out_grad: bfloat16 [2048, 1536], P('seq'), may hold values from -6 to 6
Outputs:
- layer_out: bfloat16 [2048, 1536], P('seq')
- tokens_grad: bfloat16 [2048, 1536], P('seq')
- attn_gain_grad: float32 [1536], replicated
- query_weight_grad: float32 [1536, 1536], P('seq', 'head')
- key_weight_grad: float32 [1536, 1536], P('seq', 'head')
- value_weight_grad: float32 [1536, 1536], P('seq', 'head')
- forget_weight_grad: float32 [1536, 24], P('seq', 'head')
- forget_bias_grad: float32 [24], P('head')
- out_weight_grad: float32 [1536, 1536], P('head', 'seq')
- ffn_gain_grad: float32 [1536], replicated
- gate_weight_grad: float32 [1536, 4096], P('seq', 'head')
- up_weight_grad: float32 [1536, 4096], P('seq', 'head')
- down_weight_grad: float32 [4096, 1536], P('head', 'seq')
The draws below stay inside these ranges and needn't reach their ends.
Inputs may be any that keep to these rules, and one draw needn't show every extreme that they name: `doc_lengths`: document lengths in position order summing to 2048; the longest is exactly 1024.
All inputs are finite; a program needn't handle non-finite values.
Results may differ from the reference program's by a relative error of at most 0.02.
Values may be sent and summed in bfloat16 or wider, within the bound.
A program may use at most 256 MiB of HBM per device.

```python
import math
from functools import partial
import jax
import jax.numpy as jnp
import numpy as np
from jax import lax

D = 1536
HEADS = 24
HEAD_DIM = 64
FF = 4096
TOKENS = 2048
HD = 1536
DOCS = 4
LONGEST = 1024
N_SEQ = 8


def spiked(array, key, source, target, parts, factor):
    def block_of(axis_at):
        return (jnp.arange(array.shape[axis_at]) // (array.shape[axis_at] // parts)).reshape((-1,) + (1,) * (array.ndim - 1 - axis_at))

    near = jax.random.permutation(key, parts)[block_of(target)]
    second = (block_of(target) + parts // 2) % parts
    return jnp.where((block_of(source) == near) | (block_of(source) == second), factor * array, array)


def block_scale(stream_key, extent, pieces, low, high):
    def one(position, blocks):
        draws = jax.random.uniform(jax.random.fold_in(jax.random.fold_in(stream_key, 6), position), (blocks,), jnp.float32, low / len(pieces), high / len(pieces))
        return jnp.repeat(jnp.exp(draws), extent[position] // blocks).reshape((-1,) + (1,) * (len(extent) - position - 1))

    level = one(*pieces[0])
    for cut in pieces[1:]:
        level = level * one(*cut)
    return level


def length_profile(number_of, total, bound, slope):
    loads = [(1 << 20) // math.isqrt(grade ** slope) + 1 for grade in range(2, number_of + 1)]
    spare, given = total - bound - (number_of - 1), [1] * (number_of - 1)
    while spare > 0:
        candidates = [i for i in range(number_of - 1) if given[i] < bound]
        mass, left = sum([loads[i] for i in candidates]), spare
        for i in candidates:
            extra = min(bound - given[i], max(1, left * loads[i] // mass), spare)
            given[i] = given[i] + extra
            spare = spare - extra
    return np.array([bound] + given)


def ragged(own_key, amount, total, bound, lean):
    if amount == 2:
        one = jax.random.randint(own_key, (), max(1, total - bound), min(bound, total - 1) + 1)
        return jnp.stack([one, total - one])
    sizes = jnp.asarray(length_profile(amount, total, bound, lean), jnp.int32)
    twos = (amount - 1) // 2
    giver, taker = sizes[1:1 + 2 * twos:2], sizes[2:2 + 2 * twos:2]
    margin = jnp.minimum(giver - 1, bound - taker)
    shifted = jax.random.randint(jax.random.fold_in(own_key, 1), (twos,), 0, 1 << 20) % (margin + 1)
    sizes = sizes.at[1:1 + 2 * twos:2].set(giver - shifted).at[2:2 + 2 * twos:2].set(taker + shifted)
    return sizes[jax.random.permutation(jax.random.fold_in(own_key, 2), amount)]


def noise(stream_key, extent, width, bound, pieces=(), held_as=jnp.bfloat16):
    loudness = block_scale(stream_key, extent, pieces, -0.22, 0.18) if pieces else 1.0
    result = jax.random.normal(stream_key, extent, jnp.float32) * width * loudness
    return jnp.minimum(jnp.maximum(result, -bound), bound).astype(held_as)


def bell_draw_with(key, extent, width, most, shards, heavy, kind=jnp.bfloat16):
    entries = width * jax.random.normal(key, extent, jnp.float32)
    if shards:
        entries = entries * block_scale(key, extent, shards, -0.22, 0.18)
    return jnp.clip(spiked(entries, jax.random.fold_in(key, 3), *heavy), -most, most).astype(kind)


def setup_inputs(seed: int = 0) -> dict:
    keys = jax.random.split(jax.random.key(seed), 15)
    return {
        "tokens": noise(keys[0], (TOKENS, D), 1.0, 6.0, ((0, 8),)),
        "attn_gain": jnp.clip(1.0 + 0.1 * jax.random.normal(keys[1], (D,), jnp.float32), 0.5, 1.5),
        "query_weight": noise(keys[2], (D, HD), D ** -0.5, 0.15625, ((0, 8), (1, 4))),
        "key_weight": noise(keys[3], (D, HD), D ** -0.5, 0.15625, ((0, 8), (1, 4))),
        "value_weight": noise(keys[4], (D, HD), D ** -0.5, 0.15625, ((0, 8), (1, 4))),
        "forget_weight": noise(keys[5], (D, HEADS), D ** -0.5, 0.15625, ((0, 8), (1, 4))),
        "forget_bias": jnp.clip(3.0 + 7.0 * jax.random.uniform(keys[6], (HEADS,), jnp.float32) ** block_scale(keys[6], (HEADS,), ((0, 4),), -0.2, 0.2), 3.0, 10.0),
        "out_weight": noise(keys[7], (HD, D), 16 ** -0.5, 1.5, ((0, 4), (1, 8))),
        "ffn_gain": jnp.clip(1.0 + 0.1 * jax.random.normal(keys[8], (D,), jnp.float32), 0.5, 1.5),
        "gate_weight": noise(keys[9], (D, FF), D ** -0.5, 0.15625, ((0, 8), (1, 4))),
        "up_weight": noise(keys[10], (D, FF), D ** -0.5, 0.15625, ((0, 8), (1, 4))),
        "down_weight": noise(keys[11], (FF, D), FF ** -0.5, 0.09375, ((0, 4), (1, 8))),
        "doc_lengths": ragged(keys[12], DOCS, TOKENS, LONGEST, 2).astype(jnp.int32),
        "out_grad": bell_draw_with(keys[13], (TOKENS, D), 1.0, 6.0, ((0, 8),), (0, 1, 8, 2.0)),
    }


@jax.custom_vjp
def low(v):
    return lax.optimization_barrier(v.astype(jnp.bfloat16)).astype(jnp.float32)

@jax.custom_vjp
def low_back(v):
    return v

def low_keep(v):
    return (low(v), None)

def low_pass(kept, grad):
    return (grad,)

def back_keep(v):
    return (v, None)

def back_low(kept, grad):
    return (low(grad),)
low.defvjp(low_keep, low_pass)
low_back.defvjp(back_keep, back_low)
EPSILON = 1e-06
HIGHEST = lax.Precision.HIGHEST
MASKED = -1e+30

def matmul(left, right):
    return jnp.dot(left, right, precision=HIGHEST)

def rms_scaled(values_in, gain):
    inverse = lax.rsqrt(lax.optimization_barrier(jnp.mean(values_in * values_in, axis=-1, keepdims=True)) + EPSILON)
    return values_in * inverse * gain

def head_attention(head_inputs, doc_ids):
    query_head, key_head, value_head, offset_head = head_inputs
    total_rows = query_head.shape[0]
    block_rows = min(512, total_rows)
    positions = jnp.arange(total_rows, dtype=jnp.int32)

    @jax.checkpoint
    def one_block(block_index):
        start_row = (block_index * block_rows).astype(jnp.int32)
        query_rows = lax.dynamic_slice_in_dim(query_head, start_row, block_rows, 0)
        offset_rows = lax.dynamic_slice_in_dim(offset_head, start_row, block_rows, 0)
        doc_rows = lax.dynamic_slice_in_dim(doc_ids, start_row, block_rows, 0)
        row_positions = start_row + jnp.arange(block_rows, dtype=jnp.int32)
        scores = matmul(query_rows, key_head.T) * HEAD_DIM ** (-0.5) + offset_rows[:, None] - offset_head[None, :]
        scores = low_back(scores)
        allowed = (doc_rows[:, None] == doc_ids[None, :]) & (positions[None, :] <= row_positions[:, None])
        weights = low(jax.nn.softmax(jnp.where(allowed, scores, MASKED), axis=-1))
        return matmul(weights, value_head)
    outputs = lax.map(one_block, jnp.arange(total_rows // block_rows, dtype=jnp.int32))
    return outputs.reshape(total_rows, -1)

def layer(inputs, attn_gain, query_weight, key_weight, value_weight, forget_weight, forget_bias, out_weight, ffn_gain, gate_weight, up_weight, down_weight, doc_ids):
    total_rows = inputs.shape[0]
    normed_one = low(rms_scaled(inputs, attn_gain))
    query_all = low_back(low(matmul(normed_one, query_weight)))
    key_all = low_back(low(matmul(normed_one, key_weight)))
    value_all = low_back(low(matmul(normed_one, value_weight)))
    forget_logit = matmul(normed_one, forget_weight) + forget_bias
    offsets = jnp.cumsum(jax.nn.log_sigmoid(forget_logit), axis=0)

    def by_head(matrix):
        return matrix.reshape(total_rows, HEADS, HEAD_DIM).transpose(1, 0, 2)

    def one_head(head_inputs):
        return head_attention(head_inputs, doc_ids)
    attended = lax.map(one_head, (by_head(query_all), by_head(key_all), by_head(value_all), offsets.T))
    mixed = low_back(low(attended.transpose(1, 0, 2).reshape(total_rows, HEADS * HEAD_DIM)))
    middle = inputs + low_back(matmul(mixed, out_weight))
    normed_two = low(rms_scaled(middle, ffn_gain))
    gate_value = low_back(matmul(normed_two, gate_weight))
    up_value = low_back(matmul(normed_two, up_weight))
    activation = low(jax.nn.silu(gate_value) * up_value)
    return middle + low_back(matmul(activation, down_weight))

def reference(tokens, attn_gain, query_weight, key_weight, value_weight, forget_weight, forget_bias, out_weight, ffn_gain, gate_weight, up_weight, down_weight, doc_lengths, out_grad):
    total_rows = tokens.shape[0]
    local_rows = total_rows // N_SEQ
    half_rows = local_rows // 2
    rows = jnp.arange(total_rows, dtype=jnp.int32)
    device_of = rows // local_rows
    within = rows % local_rows
    group_of = jnp.where(within < half_rows, device_of, 2 * N_SEQ - 1 - device_of).astype(jnp.int32)
    pos_of_row = (group_of * half_rows + within % half_rows).astype(jnp.int32)
    pos_group = rows // half_rows
    pos_device = jnp.where(pos_group < N_SEQ, pos_group, 2 * N_SEQ - 1 - pos_group)
    pos_side = jnp.where(pos_group < N_SEQ, 0, 1)
    row_of_pos = (pos_device * local_rows + pos_side * half_rows + rows % half_rows).astype(jnp.int32)
    positions = rows
    doc_ends = jnp.cumsum(doc_lengths).astype(jnp.int32)
    doc_ids = lax.optimization_barrier(jnp.sum((positions[:, None] >= doc_ends[None, :]).astype(jnp.int32), axis=1)).astype(jnp.int32)
    ordered_tokens = jnp.take(tokens, row_of_pos, axis=0)
    ordered_grad = jnp.take(out_grad, row_of_pos, axis=0)
    floats = jax.tree.map(lambda tensor: tensor.astype(jnp.float32), (ordered_tokens, attn_gain, query_weight, key_weight, value_weight, forget_weight, forget_bias, out_weight, ffn_gain, gate_weight, up_weight, down_weight))
    layer_out, pullback = jax.vjp(partial(layer, doc_ids=doc_ids), *floats)
    grads = pullback(ordered_grad.astype(jnp.float32))
    stored_out = jnp.take(layer_out, pos_of_row, axis=0)
    stored_grad = jnp.take(grads[0], pos_of_row, axis=0)
    return (stored_out.astype(jnp.bfloat16), stored_grad.astype(jnp.bfloat16), grads[1], grads[2], grads[3], grads[4], grads[5], grads[6], grads[7], grads[8], grads[9], grads[10], grads[11])
```

```python
import jax
import jax.numpy as jnp
from jax import lax
from jax.sharding import PartitionSpec as P

HEAD_DIM = 64


EPSILON = 1e-06
HIGHEST = lax.Precision.HIGHEST
MASKED = -1e30


def unchanged(carried):
    return carried


def contract_rows(left, right):
    return lax.dot_general(
        left, right, (((0,), (0,)), ((), ())), preferred_element_type=jnp.float32
    )


def contract_cols(left, right):
    return lax.dot_general(
        left, right, (((1,), (1,)), ((), ())), preferred_element_type=jnp.float32
    )


def norm_rows(values_in, gain):
    inverse = lax.rsqrt(jnp.mean(values_in * values_in, axis=-1, keepdims=True) + EPSILON)
    normed = values_in * inverse
    return (normed, inverse, normed * gain)


def norm_back(grad_in, normed, inverse, gain):
    scaled = grad_in * gain
    inner = jnp.mean(scaled * normed, axis=-1, keepdims=True)
    return (inverse * (scaled - normed * inner), jnp.sum(grad_in * normed, axis=0))


def doc_index(positions, doc_ends):
    return jnp.sum((positions[:, None] >= doc_ends[None, :]).astype(jnp.int32), axis=1)


def stored_positions(rows, n_seq, local_rows):
    half_rows = local_rows // 2
    device_of = rows // local_rows
    within = rows % local_rows
    group_of = jnp.where(within < half_rows, device_of, 2 * n_seq - 1 - device_of)
    return group_of * half_rows + within % half_rows


def block_scores(
    query_heads, key_heads, query_offsets, key_offsets, query_pos, key_pos, query_docs, key_docs
):
    raw_scores = jnp.einsum(
        "qhd,khd->hqk", query_heads, key_heads, preferred_element_type=jnp.float32
    )
    scores = (
        raw_scores * HEAD_DIM ** (-0.5) + query_offsets.T[:, :, None] - key_offsets.T[:, None, :]
    )
    allowed = (query_docs[:, None] == key_docs[None, :]) & (key_pos[None, :] <= query_pos[:, None])
    return (jnp.where(allowed[None], scores, MASKED), allowed)


def piece_grads(
    query_heads,
    grad_heads,
    log_mass,
    row_delta,
    query_offsets,
    key_heads,
    value_heads,
    key_offsets,
    query_pos,
    key_pos,
    query_docs,
    key_docs,
):
    scores, allowed = block_scores(
        query_heads, key_heads, query_offsets, key_offsets, query_pos, key_pos, query_docs, key_docs
    )
    probs = jnp.where(allowed[None], jnp.exp(scores - log_mass[:, :, None]), 0.0)
    grad_probs = jnp.einsum(
        "qhd,khd->hqk", grad_heads, value_heads, preferred_element_type=jnp.float32
    )
    grad_scores = (probs * (grad_probs - row_delta[:, :, None])).astype(jnp.bfloat16)
    score_sums = grad_scores.astype(jnp.float32)
    query_rows = query_heads.shape[0]
    key_rows = key_heads.shape[0]
    grad_query = jnp.einsum(
        "hqk,khd->qhd", grad_scores, key_heads, preferred_element_type=jnp.float32
    ).reshape(query_rows, -1)
    grad_key = (
        jnp.einsum("hqk,qhd->khd", grad_scores, query_heads, preferred_element_type=jnp.float32)
        * HEAD_DIM ** (-0.5)
    ).reshape(key_rows, -1)
    grad_value = jnp.einsum(
        "hqk,qhd->khd", probs.astype(jnp.bfloat16), grad_heads, preferred_element_type=jnp.float32
    ).reshape(key_rows, -1)
    return (
        grad_query,
        jnp.sum(score_sums, axis=2).T,
        grad_key,
        grad_value,
        -jnp.sum(score_sums, axis=1).T,
    )


def body(
    tokens,
    attn_gain,
    query_weight,
    key_weight,
    value_weight,
    forget_weight,
    forget_bias,
    out_weight,
    ffn_gain,
    gate_weight,
    up_weight,
    down_weight,
    doc_lengths,
    out_grad,
):
    local_rows = tokens.shape[0]
    local_heads = forget_bias.shape[0]
    head_cols = local_heads * HEAD_DIM
    n_seq = lax.axis_size("seq")
    my_index = lax.axis_index("seq")
    first_row = my_index * local_rows
    docs = doc_lengths.shape[0]
    doc_ends = jnp.sum(jnp.where(jnp.tri(docs, dtype=jnp.bool_), doc_lengths[None, :], 0), axis=1)
    local_pos = stored_positions(
        first_row + jnp.arange(local_rows, dtype=jnp.int32), n_seq, local_rows
    )
    local_docs = doc_index(local_pos, doc_ends)
    pos_low = jnp.min(local_pos)
    pos_high = jnp.max(local_pos)
    doc_low = jnp.min(local_docs)
    doc_high = jnp.max(local_docs)
    hidden = gate_weight.shape[1]
    forget_pad = jnp.pad(forget_weight, ((0, 0), (0, 128 - local_heads)))
    w_attn = lax.all_gather(
        jnp.concatenate([query_weight, key_weight, value_weight, forget_pad], axis=1),
        "seq",
        axis=0,
        tiled=True,
    )
    w_rest = lax.all_gather(
        jnp.concatenate([out_weight.T, gate_weight, up_weight, down_weight.T], axis=1),
        "seq",
        axis=0,
        tiled=True,
    )
    w_query = w_attn[:, :head_cols]
    w_key = w_attn[:, head_cols : 2 * head_cols]
    w_value = w_attn[:, 2 * head_cols : 3 * head_cols]
    w_forget = w_attn[:, 3 * head_cols : 3 * head_cols + local_heads]
    w_out_t = w_rest[:, :head_cols]
    w_gate = w_rest[:, head_cols : head_cols + hidden]
    w_up = w_rest[:, head_cols + hidden : head_cols + 2 * hidden]
    w_down_t = w_rest[:, head_cols + 2 * hidden :]
    inputs = tokens.astype(jnp.float32)
    normed_one, inverse_one, scaled_one = norm_rows(inputs, attn_gain)
    h_one = scaled_one.astype(jnp.bfloat16)
    query_flat = jnp.dot(h_one, w_query, preferred_element_type=jnp.float32).astype(jnp.bfloat16)
    key_flat = jnp.dot(h_one, w_key, preferred_element_type=jnp.float32).astype(jnp.bfloat16)
    value_flat = jnp.dot(h_one, w_value, preferred_element_type=jnp.float32).astype(jnp.bfloat16)
    forget_logit = jnp.dot(h_one, w_forget, preferred_element_type=jnp.float32) + forget_bias
    log_forget_all = lax.all_gather(jax.nn.log_sigmoid(forget_logit), "seq", axis=0, tiled=True)
    all_pos = stored_positions(
        jnp.arange(n_seq * local_rows, dtype=jnp.int32), n_seq, local_rows
    )
    earlier = (all_pos[None, :] <= all_pos[:, None]).astype(jnp.float32)
    offsets_all = jnp.dot(earlier, log_forget_all, precision=HIGHEST)
    offsets = lax.dynamic_slice_in_dim(offsets_all, first_row, local_rows, 0)
    query_heads = query_flat.reshape(local_rows, local_heads, HEAD_DIM)
    key_heads = key_flat.reshape(local_rows, local_heads, HEAD_DIM)
    value_heads = value_flat.reshape(local_rows, local_heads, HEAD_DIM)

    def key_range(piece_rows):
        key_pos = stored_positions(jnp.arange(piece_rows, dtype=jnp.int32), n_seq, local_rows)
        key_docs = doc_index(key_pos, doc_ends)
        is_live = (
            (jnp.min(key_pos) <= pos_high)
            & (jnp.max(key_docs) >= doc_low)
            & (jnp.min(key_docs) <= doc_high)
        )
        return (key_pos, key_docs, offsets_all, is_live)

    mass_state = (
        jnp.full((local_heads, local_rows), MASKED, jnp.float32),
        jnp.zeros((local_heads, local_rows), jnp.float32),
    )
    gathered = lax.all_gather(
        jnp.concatenate([key_flat, value_flat, query_flat], axis=1), "seq", axis=0, tiled=True
    )
    key_block = gathered[:, :head_cols]
    piece_rows = key_block.shape[0]
    key_pos, key_docs, key_offsets, is_live = key_range(piece_rows)

    def mass_update(carried_in):
        running_max, running_sum = carried_in
        scores, allowed = block_scores(
            query_heads,
            key_block.reshape(piece_rows, local_heads, HEAD_DIM),
            offsets,
            key_offsets,
            local_pos,
            key_pos,
            local_docs,
            key_docs,
        )
        new_max = jnp.maximum(running_max, jnp.max(scores, axis=2))
        weights = jnp.where(allowed[None], jnp.exp(scores - new_max[:, :, None]), 0.0)
        return (new_max, jnp.sum(weights, axis=2))

    running_max, running_sum = lax.cond(is_live, mass_update, unchanged, mass_state)
    log_mass = running_max + jnp.log(running_sum)
    start_state = (
        jnp.zeros((local_heads, local_rows, HEAD_DIM), jnp.float32),
        jnp.zeros((local_heads, local_rows, HEAD_DIM), jnp.float32),
    )
    attend_key_block = key_block
    value_block = gathered[:, head_cols : 2 * head_cols]
    attend_piece_rows = attend_key_block.shape[0]
    attend_key_pos, attend_key_docs, attend_key_offsets, is_live = key_range(attend_piece_rows)

    def attend_update(carried_in):
        scores, allowed = block_scores(
            query_heads,
            attend_key_block.reshape(attend_piece_rows, local_heads, HEAD_DIM),
            offsets,
            attend_key_offsets,
            local_pos,
            attend_key_pos,
            local_docs,
            attend_key_docs,
        )
        probs = jnp.where(allowed[None], jnp.exp(scores - log_mass[:, :, None]), 0.0)
        probs_low = probs.astype(jnp.bfloat16)
        remainder = (probs - probs_low.astype(jnp.float32)).astype(jnp.bfloat16)
        value_piece = value_block.reshape(attend_piece_rows, local_heads, HEAD_DIM)
        rounded_acc = jnp.einsum(
            "hqk,khd->hqd", probs_low, value_piece, preferred_element_type=jnp.float32
        )
        remainder_acc = jnp.einsum(
            "hqk,khd->hqd", remainder, value_piece, preferred_element_type=jnp.float32
        )
        return (rounded_acc, remainder_acc)

    rounded_acc, remainder_acc = lax.cond(is_live, attend_update, unchanged, start_state)
    attended_rows = rounded_acc.transpose(1, 0, 2)
    exact_rows = (rounded_acc + remainder_acc).transpose(1, 0, 2)
    mixed = attended_rows.reshape(local_rows, head_cols).astype(jnp.bfloat16)
    attn_part = contract_cols(mixed, w_out_t)
    middle = inputs + lax.psum(attn_part, "head")
    normed_two, inverse_two, scaled_two = norm_rows(middle, ffn_gain)
    h_two = scaled_two.astype(jnp.bfloat16)
    gate_value = jnp.dot(h_two, w_gate, preferred_element_type=jnp.float32)
    up_value = jnp.dot(h_two, w_up, preferred_element_type=jnp.float32)
    gate_sigmoid = jax.nn.sigmoid(gate_value)
    gate_silu = gate_value * gate_sigmoid
    activation = (gate_silu * up_value).astype(jnp.bfloat16)
    ffn_part = contract_cols(activation, w_down_t)
    layer_out = (
        middle + lax.psum(ffn_part.astype(jnp.bfloat16), "head").astype(jnp.float32)
    ).astype(jnp.bfloat16)
    grad_act = jnp.dot(out_grad, w_down_t, preferred_element_type=jnp.float32)
    grad_gate = (
        grad_act * up_value * gate_sigmoid * (1.0 + gate_value * (1.0 - gate_sigmoid))
    ).astype(jnp.bfloat16)
    grad_up = (grad_act * gate_silu).astype(jnp.bfloat16)
    part_two = contract_cols(grad_gate, w_gate) + contract_cols(grad_up, w_up)
    grad_two = lax.psum(part_two, "head")
    back_two, gain_two = norm_back(grad_two, normed_two, inverse_two, ffn_gain)
    grad_middle = out_grad.astype(jnp.float32) + back_two
    grad_attn = grad_middle.astype(jnp.bfloat16)
    grad_mixed = jnp.dot(grad_attn, w_out_t, preferred_element_type=jnp.float32).astype(
        jnp.bfloat16
    )
    grad_heads = grad_mixed.reshape(local_rows, local_heads, HEAD_DIM)
    row_delta = jnp.sum(grad_heads.astype(jnp.float32) * exact_rows, axis=2).T
    back_state = (
        jnp.zeros((local_rows, head_cols), jnp.float32),
        jnp.zeros((local_rows, local_heads), jnp.float32),
    )
    back_key_block = key_block
    back_value_block = value_block
    back_piece_rows = back_key_block.shape[0]
    back_key_pos, back_key_docs, back_key_offsets, is_live = key_range(back_piece_rows)

    def back_update(carried_in):
        terms = piece_grads(
            query_heads,
            grad_heads,
            log_mass,
            row_delta,
            offsets,
            back_key_block.reshape(back_piece_rows, local_heads, HEAD_DIM),
            back_value_block.reshape(back_piece_rows, local_heads, HEAD_DIM),
            back_key_offsets,
            local_pos,
            back_key_pos,
            local_docs,
            back_key_docs,
        )
        return (terms[0], terms[1])

    grad_query, grad_query_off = lax.cond(is_live, back_update, unchanged, back_state)
    stats = lax.all_gather(
        jnp.concatenate([log_mass.T, row_delta.T], axis=1), "seq", axis=0, tiled=True
    )
    stats_mass, stats_delta = stats[:, :local_heads], stats[:, local_heads:]
    key_state = (
        jnp.zeros((local_rows, head_cols), jnp.float32),
        jnp.zeros((local_rows, head_cols), jnp.float32),
        jnp.zeros((local_rows, local_heads), jnp.float32),
    )
    piece_query = gathered[:, 2 * head_cols :]
    piece_grad = lax.all_gather(grad_mixed, "seq", axis=0, tiled=True)
    key_piece_rows = piece_query.shape[0]
    piece_pos = stored_positions(jnp.arange(key_piece_rows, dtype=jnp.int32), n_seq, local_rows)
    piece_docs = doc_index(piece_pos, doc_ends)
    is_live = (
        (pos_low <= jnp.max(piece_pos))
        & (jnp.max(piece_docs) >= doc_low)
        & (jnp.min(piece_docs) <= doc_high)
    )

    def key_update(carried_in):
        piece_mass = stats_mass.T
        piece_delta = stats_delta.T
        terms = piece_grads(
            piece_query.reshape(key_piece_rows, local_heads, HEAD_DIM),
            piece_grad.reshape(key_piece_rows, local_heads, HEAD_DIM),
            piece_mass,
            piece_delta,
            offsets_all,
            key_heads,
            value_heads,
            offsets,
            piece_pos,
            local_pos,
            piece_docs,
            local_docs,
        )
        return (terms[2], terms[3], terms[4])

    grad_key, grad_value, grad_key_off = lax.cond(is_live, key_update, unchanged, key_state)
    grad_query_low = (grad_query * HEAD_DIM ** (-0.5)).astype(jnp.bfloat16)
    grad_key_low = grad_key.astype(jnp.bfloat16)
    grad_value_low = grad_value.astype(jnp.bfloat16)
    grad_offsets = grad_query_off + grad_key_off
    grad_off_all = lax.all_gather(grad_offsets, "seq", axis=0, tiled=True)
    later = (all_pos[None, :] >= local_pos[:, None]).astype(jnp.float32)
    grad_log = jnp.dot(later, grad_off_all, precision=HIGHEST)
    grad_logit = grad_log * jax.nn.sigmoid(-forget_logit)
    forget_table = w_forget.astype(jnp.float32)
    part_one = (
        contract_cols(grad_query_low, w_query)
        + contract_cols(grad_key_low, w_key)
        + contract_cols(grad_value_low, w_value)
        + lax.dot_general(grad_logit, forget_table, (((1,), (1,)), ((), ())), precision=HIGHEST)
    )
    grad_one = lax.psum(part_one.astype(jnp.bfloat16), "head").astype(jnp.float32)
    back_one, gain_one = norm_back(grad_one, normed_one, inverse_one, attn_gain)
    tokens_grad = (grad_middle + back_one).astype(jnp.bfloat16)
    forget_term = lax.dot_general(
        h_one.astype(jnp.float32), grad_logit, (((0,), (0,)), ((), ())), precision=HIGHEST
    )
    scatter_cols = [
        contract_rows(grad_attn, mixed),
        contract_rows(h_two, grad_gate),
        contract_rows(h_two, grad_up),
        contract_rows(out_grad, activation),
        contract_rows(h_one, grad_query_low),
        contract_rows(h_one, grad_key_low),
        contract_rows(h_one, grad_value_low),
        jnp.pad(forget_term, ((0, 0), (0, 128 - local_heads))),
    ]
    first_sum = lax.psum_scatter(
        jnp.concatenate([t.astype(jnp.bfloat16) for t in scatter_cols[:4]], axis=1),
        "seq",
        scatter_dimension=0,
        tiled=True,
    ).astype(jnp.float32)
    second_sum = lax.psum_scatter(
        jnp.concatenate([t.astype(jnp.bfloat16) for t in scatter_cols[4:]], axis=1),
        "seq",
        scatter_dimension=0,
        tiled=True,
    ).astype(jnp.float32)
    out_weight_grad = first_sum[:, :head_cols].T
    gate_weight_grad = first_sum[:, head_cols : head_cols + hidden]
    up_weight_grad = first_sum[:, head_cols + hidden : head_cols + 2 * hidden]
    down_weight_grad = first_sum[:, head_cols + 2 * hidden :].T
    query_weight_grad = second_sum[:, :head_cols]
    key_weight_grad = second_sum[:, head_cols : 2 * head_cols]
    value_weight_grad = second_sum[:, 2 * head_cols : 3 * head_cols]
    forget_weight_grad = second_sum[:, 3 * head_cols : 3 * head_cols + local_heads]
    attn_gain_grad, ffn_gain_grad, forget_bias_grad = lax.psum(
        (gain_one, gain_two, jnp.sum(grad_logit, axis=0)), "seq"
    )
    return (
        layer_out,
        tokens_grad,
        attn_gain_grad,
        query_weight_grad,
        key_weight_grad,
        value_weight_grad,
        forget_weight_grad,
        forget_bias_grad,
        out_weight_grad,
        ffn_gain_grad,
        gate_weight_grad,
        up_weight_grad,
        down_weight_grad,
    )


def solution(mesh):
    return jax.shard_map(
        body,
        mesh=mesh,
        in_specs=(
            P("seq", None),
            P(),
            P("seq", "head"),
            P("seq", "head"),
            P("seq", "head"),
            P("seq", "head"),
            P("head"),
            P("head", "seq"),
            P(),
            P("seq", "head"),
            P("seq", "head"),
            P("head", "seq"),
            P(),
            P("seq", None),
        ),
        out_specs=(
            P("seq", None),
            P("seq", None),
            P(),
            P("seq", "head"),
            P("seq", "head"),
            P("seq", "head"),
            P("seq", "head"),
            P("head"),
            P("head", "seq"),
            P(),
            P("seq", "head"),
            P("seq", "head"),
            P("head", "seq"),
        ),
        check_vma=False,
    )
```

```python
import functools
import math

import jax
import jax.numpy as jnp
from jax import lax
from jax.experimental import pallas as pl
from jax.experimental.pallas import tpu as pltpu
from jax.sharding import PartitionSpec as P

HEAD_DIM = 64
EPSILON = 1e-06
HIGHEST = lax.Precision.HIGHEST
MASKED = -1e30
MESH_ID = pl.DeviceIdType.MESH
F32 = jnp.float32
BF16 = jnp.bfloat16
LANES = 128


def dot_nn(left, right):
    return jnp.dot(left, right, preferred_element_type=F32)


def dot_nt(left, right):
    return lax.dot_general(left, right, (((1,), (1,)), ((), ())), preferred_element_type=F32)


class Net:
    def __init__(self, n_seq, sems):
        self.n_seq = n_seq
        self.line = n_seq // 2
        self.s = lax.axis_index("seq")
        self.h = lax.axis_index("head")
        self.z = self.s // 2
        self.x = self.s % 2
        self.y = self.h // 2
        self.c = self.h % 2
        self.sems = sems
        self.used = 0
        self.pending = []

    def alloc(self, count):
        first = self.used
        self.used += count
        return first

    def at_line(self, z):
        return (z * 2 + self.x, self.h)

    def side(self):
        return (self.z * 2 + 1 - self.x, self.h)

    def lower(self):
        return (self.s, self.y * 2 + 1 - self.c)

    def upper(self):
        return (self.s, (1 - self.y) * 2 + self.c)

    def barrier(self):
        sem = pltpu.get_barrier_semaphore()
        for step in range(1, self.n_seq):
            peer = (self.s + step) % self.n_seq
            pl.semaphore_signal(sem, 1, device_id=(peer, self.h), device_id_type=MESH_ID)
        for peer in (self.lower(), self.upper()):
            pl.semaphore_signal(sem, 1, device_id=peer, device_id_type=MESH_ID)
        pl.semaphore_wait(sem, self.n_seq + 1)

    def copy(self, src, dst, send, recv, device):
        return pltpu.make_async_remote_copy(
            src_ref=src,
            dst_ref=dst,
            send_sem=self.sems.at[send],
            recv_sem=self.sems.at[recv],
            device_id=device,
            device_id_type=MESH_ID,
        )

    def send(self, src, dst, device):
        first = self.alloc(2)
        made = self.copy(src, dst, first, first + 1, device)
        made.start()
        self.pending.append(made.wait_send)
        return made

    def drain(self):
        for wait in self.pending:
            wait()
        self.pending = []


class Line:
    def __init__(self, net, slot):
        self.net = net
        self.slot = slot
        self.recv = net.alloc(net.line)
        self.direct = net.alloc(4)
        self.passed = net.alloc(net.line)
        self.deltas = [d for d in (1, -1, 2, -2) if abs(d) < net.line]

    def own(self, index):
        net = self.net
        mine = self.slot(net.z)
        return net.copy(
            mine,
            mine,
            self.direct + index,
            self.recv + net.z,
            net.at_line((net.z + self.deltas[index] + net.line) % net.line),
        )

    def here(self, index):
        to = self.net.z + self.deltas[index]
        return (to >= 0) & (to < self.net.line)

    def start(self):
        for index in range(len(self.deltas)):
            pl.when(self.here(index))(lambda index=index: self.own(index).start())

    def handed(self, src, sign):
        net = self.net
        block = self.slot(src)
        return net.copy(
            block,
            block,
            self.passed + src,
            self.recv + src,
            net.at_line((net.z - sign + net.line) % net.line),
        )

    def each(self, act):
        net = self.net
        for k in range(1, net.line):
            for sign in (-1, 1):
                src = net.z + sign * k
                there = (src >= 0) & (src < net.line)
                onward = (net.z - sign >= 0) & (net.z - sign < net.line)
                act(k, sign, (src + net.line) % net.line, there, onward)

    def arrive(self, then=None):
        def act(k, sign, src, there, onward):
            @pl.when(there)
            def _():
                self.handed(src, sign).wait_recv()
                if then is not None:
                    then(src)
                if k >= 2:
                    pl.when(onward)(lambda: self.handed(src, sign).start())

        self.each(act)

    def drain(self):
        for index in range(len(self.deltas)):
            pl.when(self.here(index))(lambda index=index: self.own(index).wait_send())

        def act(k, sign, src, there, onward):
            if k >= 2:
                pl.when(there & onward)(lambda: self.handed(src, sign).wait_send())

        self.each(act)


class Spread:
    def __init__(self, net, slot):
        self.net = net
        self.slot = slot
        self.along = Line(net, lambda z: slot(z * 2 + net.x))
        self.sent = net.alloc(net.line)
        self.got = net.alloc(net.line)

    def across(self, z):
        net = self.net
        block = self.slot(z * 2 + net.x)
        return net.copy(block, block, self.sent + z, self.got + z, net.side())

    def start(self):
        self.along.start()
        self.across(self.net.z).start()

    def arrive(self):
        self.along.arrive(lambda z: self.across(z).start())

    def finish(self):
        net = self.net
        for z in range(net.line):
            block = self.slot(z * 2 + 1 - net.x)
            net.copy(block, block, self.sent + z, self.got + z, net.side()).wait_recv()

    def drain(self):
        self.along.drain()
        for z in range(self.net.line):
            self.across(z).wait_send()


def spread_small(net, slot):
    recv = net.alloc(net.n_seq)
    sent = net.alloc(net.n_seq)

    def made(step):
        mine = slot(net.s)
        return net.copy(
            mine, mine, sent + step, recv + step, ((net.s + step) % net.n_seq, net.h)
        )

    for step in range(1, net.n_seq):
        made(step).start()
        net.pending.append(made(step).wait_send)

    def wait():
        for step in range(1, net.n_seq):
            src = slot((net.s - step + net.n_seq) % net.n_seq)
            net.copy(src, src, sent + step, recv + step, net.side()).wait_recv()

    return wait


def rows_of(first, count):
    return pl.ds(pl.multiple_of(first, 16), count)


def doc_starts(positions, doc_ref, docs):
    start = jnp.zeros(positions.shape, jnp.int32)
    end = jnp.int32(0)
    for k in range(docs - 1):
        end = end + doc_ref[k]
        start = jnp.where(positions >= end, end, start)
    return start


def forward_kernel(
    n_seq,
    docs,
    heads,
    tokens,
    gain_one,
    wq,
    wk,
    wv,
    wf,
    bias,
    wo_t,
    gain_two,
    wg,
    wu,
    wd_t,
    doc_ref,
    og,
    queries,
    keyval,
    offsets,
    mass,
    logit_t,
    mixed,
    exact,
    middle,
    normed_two,
    out_grads,
    w_attn,
    w_out,
    w_ffn,
    h_one,
    logs,
    allowed,
    proj,
    recv_low,
    recv_up,
    half_out,
    own_off,
    sems,
):
    net = Net(n_seq, sems)
    rows, width = tokens.shape
    half = rows // 2
    quarter = half // 2
    block = wq.shape[0]
    hc = wq.shape[1]
    hidden = wg.shape[1] // 2
    span = n_seq * half
    s, z, x, y, c = net.s, net.z, net.x, net.y, net.c

    def seq_rows(ref):
        return lambda j: ref.at[rows_of(j * block, block), :]

    attn_net = Spread(net, seq_rows(w_attn))
    out_net = Spread(net, seq_rows(w_out))
    ffn_net = Line(net, lambda j: w_ffn.at[rows_of(j * 2 * block, 2 * block), :])
    kv_net = Spread(net, lambda j: keyval.at[:, j])

    mine = rows_of(s * block, block)
    for index, ref in enumerate((wq, wk, wv)):
        w_attn[mine, index * hc : (index + 1) * hc] = ref[...]
    w_attn[mine, 3 * hc :] = wf[...]
    net.barrier()
    attn_net.start()

    w_out[mine, :] = wo_t[...]
    for index, ref in enumerate((wg, wu, wd_t)):
        cols = slice(index * hidden, (index + 1) * hidden)
        w_ffn[mine, cols] = ref[:, pl.ds(pl.multiple_of(x * hidden, LANES), hidden)]
        half_out[:, cols] = ref[:, pl.ds(pl.multiple_of((1 - x) * hidden, LANES), hidden)]

    values_in = tokens[...].astype(F32)
    inverse = lax.rsqrt(jnp.mean(values_in * values_in, axis=-1, keepdims=True) + EPSILON)
    h_one[...] = (values_in * inverse * gain_one[...]).astype(BF16)
    out_grads[rows_of(x * rows, rows), :] = og[...]

    def key_positions(shape, axis):
        at = lax.broadcasted_iota(jnp.int32, shape, axis)
        late = at // span
        owner = (at % span) // half
        return jnp.where(late == 0, owner, 2 * n_seq - 1 - owner) * half + at % half

    key_pos = key_positions((1, 2 * span), 1)
    for part in range(2):
        group = s if part == 0 else 2 * n_seq - 1 - s
        pos = group * half + lax.broadcasted_iota(jnp.int32, (half, 1), 0)
        start = doc_starts(pos, doc_ref, docs)
        seen = (key_pos <= pos) & (key_pos >= start)
        allowed[part * half : (part + 1) * half, :] = jnp.where(seen, 0.0, MASKED)

    attn_net.arrive()
    attn_net.finish()

    tile = 256
    for at in range(w_attn.shape[1] // tile):
        cols = slice(at * tile, (at + 1) * tile)
        proj[:, cols] = dot_nn(h_one[...], w_attn[:, cols])

    logit = proj[:, 3 * hc : 3 * hc + LANES] + bias[...]
    turned = logit.T[:8, :]
    logit_t[...] = turned
    logs[s] = jnp.minimum(turned, 0.0) - jnp.log(1.0 + jnp.exp(-jnp.abs(turned)))
    wait_logs = spread_small(net, lambda j: logs.at[j])
    for part in range(2):
        keyval[part, s] = proj[part * half : (part + 1) * half, hc : 3 * hc].astype(BF16)
    kv_net.start()
    queries[...] = (proj[:, :hc].astype(BF16).astype(F32) * HEAD_DIM ** (-0.5)).astype(BF16)

    wait_logs()
    upto = (
        lax.broadcasted_iota(jnp.int32, (half, half), 0)
        <= lax.broadcasted_iota(jnp.int32, (half, half), 1)
    ).astype(F32)
    before = jnp.zeros((8, 1), F32)
    for group in range(2 * n_seq):
        owner = group if group < n_seq else 2 * n_seq - 1 - group
        late = group // n_seq
        piece = logs[owner, :, late * half : (late + 1) * half]
        sums = jnp.dot(piece, upto, precision=HIGHEST, preferred_element_type=F32)
        at = (late * n_seq + owner) * half
        offsets[:, at : at + half] = sums + before
        before = before + jnp.sum(piece, axis=1, keepdims=True)

    kv_net.arrive()
    half_send = net.send(half_out, w_ffn.at[mine, :], net.side())
    out_net.start()
    kv_net.finish()

    lane = lax.broadcasted_iota(jnp.int32, (half, LANES), 1)
    masses = [jnp.zeros((half, LANES), F32), jnp.zeros((half, LANES), F32)]
    for pair in range(heads // 2):
        cols = slice(pair * LANES, (pair + 1) * LANES)
        vcols = slice(hc + pair * LANES, hc + (pair + 1) * LANES)
        for part in range(2):
            mine_rows = slice(part * half, (part + 1) * half)
            many = span * (part + 1)
            query_pair = queries[mine_rows, cols]
            key_pair = keyval[: part + 1, :, :, cols].reshape(many, LANES)
            value_pair = keyval[: part + 1, :, :, vcols].reshape(many, LANES)
            low_out, full_out = [], []
            for side in range(2):
                head = pair * 2 + side
                keep = (lane // HEAD_DIM) == side
                query = jnp.where(keep, query_pair, jnp.zeros_like(query_pair))
                scores = (
                    dot_nt(query, key_pair)
                    - offsets[head : head + 1, :many]
                    + allowed[mine_rows, :many]
                )
                top = jnp.max(scores, axis=1, keepdims=True)
                probs = jnp.exp(scores - top)
                total = jnp.sum(probs, axis=1, keepdims=True)
                high = probs.astype(BF16)
                rest = (probs - high.astype(F32)).astype(BF16)
                share = 1.0 / total
                rounded = dot_nn(high, value_pair)
                low_out.append(rounded * share)
                full_out.append((rounded + dot_nn(rest, value_pair)) * share)
                masses[part] = jnp.where(lane == head, top + jnp.log(total), masses[part])
            first = (lane // HEAD_DIM) == 0
            mixed[mine_rows, cols] = jnp.where(first, low_out[0], low_out[1]).astype(BF16)
            exact[mine_rows, cols] = jnp.where(first, full_out[0], full_out[1])
        if pair == 0:
            out_net.arrive()
            half_send.wait_recv()
            ffn_net.start()
            grads_send = net.send(
                out_grads.at[rows_of(x * rows, rows), :],
                out_grads.at[rows_of(x * rows, rows), :],
                net.side(),
            )
    for part in range(2):
        mass[part * half : (part + 1) * half, :] = masses[part]
    out_net.finish()

    for at in range(width // tile):
        cols = slice(at * tile, (at + 1) * tile)
        proj[:, cols] = dot_nt(mixed[...], w_out[cols, :])
    low_send = net.send(proj.at[rows_of((1 - c) * half, half), :], recv_low, net.lower())
    low_send.wait_recv()
    keep_low = rows_of(c * half, half)
    proj[keep_low, :] = proj[keep_low, :] + recv_low[...]
    up_send = net.send(
        proj.at[rows_of(c * half + (1 - y) * quarter, quarter), :], recv_up, net.upper()
    )
    up_send.wait_recv()
    kept = c * half + y * quarter
    own = rows_of(kept, quarter)
    total = tokens[own, :].astype(F32) + (proj[own, :] + recv_up[...])
    middle[...] = total
    inverse = lax.rsqrt(jnp.mean(total * total, axis=-1, keepdims=True) + EPSILON)
    here = rows_of(x * rows + kept, quarter)
    normed_two[here, :] = (total * inverse * gain_two[...]).astype(BF16)
    gather_rows(net, normed_two, rows)

    ffn_net.arrive()
    grads_send.wait_recv()
    for part in (attn_net, out_net, ffn_net, kv_net, net):
        part.drain()


def gather_rows(net, ref, rows):
    half, quarter = rows // 2, rows // 4
    base = net.x * rows + net.c * half
    piece = ref.at[rows_of(base + net.y * quarter, quarter), :]
    net.send(piece, piece, net.upper()).wait_recv()
    piece = ref.at[rows_of(base, half), :]
    across = net.send(piece, piece, net.side())
    first = net.send(piece, piece, net.lower())
    across.wait_recv()
    piece = ref.at[rows_of((1 - net.x) * rows + net.c * half, half), :]
    second = net.send(piece, piece, net.lower())
    first.wait_recv()
    second.wait_recv()


def run_forward(
    n_seq, heads, tokens, attn_gain, wq, wk, wv, wf, bias, wo_t, ffn_gain, wg, wu, wd_t, docs, og
):
    rows, width = tokens.shape
    hc = wq.shape[1]
    hidden = wg.shape[1] // 2
    half = rows // 2
    span = n_seq * half
    attn_cols = 3 * hc + LANES
    vmem = pl.BlockSpec(memory_space=pltpu.VMEM)
    outs = (
        ((rows, hc), BF16),
        ((2, n_seq, half, 2 * hc), BF16),
        ((8, 2 * span), F32),
        ((rows, LANES), F32),
        ((8, rows), F32),
        ((rows, hc), BF16),
        ((rows, hc), F32),
        ((rows // 4, width), F32),
        ((2 * rows, width), BF16),
        ((2 * rows, width), BF16),
        ((width, attn_cols), BF16),
        ((width, hc), BF16),
        ((width, 3 * hidden), BF16),
    )
    return pl.pallas_call(
        functools.partial(forward_kernel, n_seq, docs.shape[0], heads),
        out_shape=[jax.ShapeDtypeStruct(*o) for o in outs],
        in_specs=[vmem] * 12 + [pl.BlockSpec(memory_space=pltpu.SMEM), vmem],
        out_specs=[vmem] * len(outs),
        scratch_shapes=[
            pltpu.VMEM((rows, width), BF16),
            pltpu.VMEM((n_seq, 8, rows), F32),
            pltpu.VMEM((rows, 2 * span), F32),
            pltpu.VMEM((rows, width), F32),
            pltpu.VMEM((half, width), F32),
            pltpu.VMEM((half // 2, width), F32),
            pltpu.VMEM((wq.shape[0], 3 * hidden), BF16),
            pltpu.VMEM((rows, LANES), F32),
            pltpu.SemaphoreType.DMA((160,)),
        ],
        compiler_params=pltpu.CompilerParams(
            collective_id=0, has_side_effects=True, vmem_limit_bytes=58 << 20
        ),
    )(
        tokens,
        attn_gain.reshape(1, width),
        wq,
        wk,
        wv,
        jnp.pad(wf, ((0, 0), (0, LANES - heads))),
        jnp.pad(bias, (0, LANES - heads)).reshape(1, LANES),
        wo_t,
        ffn_gain.reshape(1, width),
        wg,
        wu,
        wd_t,
        docs,
        og,
    )


def dot_tn(left, right):
    return lax.dot_general(left, right, (((0,), (0,)), ((), ())), preferred_element_type=F32)


class LineReduce:
    def __init__(self, net, block, slots, relay):
        self.net = net
        self.block = block
        self.slots = slots
        self.relay = relay
        self.recv = net.alloc(4)
        self.sent = net.alloc(net.line)
        self.passing = net.alloc(2 * net.line)
        counts = {min(z, 2) + min(net.line - 1 - z, 2) for z in range(net.line)}
        self.counts = sorted(counts)
        self.count = jnp.minimum(net.z, 2) + jnp.minimum(net.line - 1 - net.z, 2)

    def held(self, sign, k):
        line = self.net.line
        if line <= 4:
            return 0
        return (0 if sign > 0 else line - 3) + k - 2

    def made(self, sign, k):
        net = self.net
        line = net.line
        to = (net.z + sign * k + 2 * line) % line
        if k <= 2:
            low = jnp.minimum(to, 2)
            place = low - k if sign > 0 else low + k - 1
            place = (place + 4) % 4
            last = self.slots.shape[0] - 1
            dst, recv, hop = self.slots.at[jnp.minimum(place, last)], self.recv + place, to
        else:
            index = self.held(sign, k - 1)
            dst, recv = self.relay.at[index], self.passing + index
            hop = (net.z + sign + line) % line
        return net.copy(self.block(to), dst, self.sent + to, recv, net.at_line(hop))

    def cases(self):
        net = self.net
        for k in range(net.line - 1, 0, -1):
            for sign in (1, -1):
                to = net.z + sign * k
                back = net.z - sign
                there = (to >= 0) & (to < net.line)
                behind = (back >= 0) & (back < net.line)
                yield sign, k, there, behind

    def start(self):
        for sign, k, there, behind in self.cases():
            ready = there if k == 1 else there & jnp.logical_not(behind)
            pl.when(ready)(lambda sign=sign, k=k: self.made(sign, k).start())

    def hand_on(self):
        net = self.net
        for sign, k, there, behind in self.cases():
            if k == 1:
                continue

            @pl.when(there & behind)
            def _(sign=sign, k=k):
                index = self.held(sign, k)
                came = self.relay.at[index]
                net.copy(came, came, self.sent, self.passing + index, net.side()).wait_recv()
                mine = self.block((net.z + sign * k + 2 * net.line) % net.line)
                mine[...] = (mine[...].astype(F32) + came[...].astype(F32)).astype(BF16)
                self.made(sign, k).start()

    def finish(self, use):
        net = self.net
        for many in self.counts:

            @pl.when(self.count == many)
            def _(many=many):
                for index in range(many):
                    slot = self.slots.at[index]
                    net.copy(slot, slot, self.sent, self.recv + index, net.side()).wait_recv()
                mine = self.block(net.z)

                def total(rows):
                    out = mine[rows, :].astype(F32)
                    for index in range(many):
                        out = out + self.slots[index, rows, :].astype(F32)
                    return out

                use(total)

    def drain(self):
        for sign, k, there, behind in self.cases():
            pl.when(there)(lambda sign=sign, k=k: self.made(sign, k).wait_send())


class SeqReduce:
    def __init__(self, net, grads, across, slots, relay):
        self.net = net
        self.grads = grads
        self.across = across
        self.block = across.shape[1]
        self.sent = net.alloc(net.line)
        self.got = net.alloc(net.line)
        self.along = LineReduce(net, lambda t: self.rows(t, net.x), slots, relay)

    def rows(self, z, x):
        return self.grads.at[rows_of((z * 2 + x) * self.block, self.block), :]

    def made(self, z):
        net = self.net
        return net.copy(
            self.rows(z, 1 - net.x), self.across.at[z], self.sent + z, self.got + z, net.side()
        )

    def start(self):
        for z in range(self.net.line):
            self.made(z).start()

    def turn(self):
        for z in range(self.net.line):
            self.made(z).wait_recv()
            mine = self.rows(z, self.net.x)
            mine[...] = (mine[...].astype(F32) + self.across[z].astype(F32)).astype(BF16)
        self.along.start()

    def drain(self):
        for z in range(self.net.line):
            self.made(z).wait_send()
        self.along.drain()


class RowReduce:
    def __init__(self, net, parts, recv_low, recv_side, recv_up):
        self.net = net
        self.parts = parts
        self.rows = parts.shape[0] // 2
        self.recv_low = recv_low
        self.recv_side = recv_side
        self.recv_up = recv_up

    def piece(self, x, first, count):
        return rows_of(x * self.rows + first, count)

    def start(self):
        net, half = self.net, self.rows // 2
        self.low = [
            net.send(
                self.parts.at[self.piece(x, (1 - net.c) * half, half), :],
                self.recv_low.at[x],
                net.lower(),
            )
            for x in range(2)
        ]

    def second(self):
        net, half = self.net, self.rows // 2
        for x in range(2):
            self.low[x].wait_recv()
            at = self.piece(x, net.c * half, half)
            self.parts[at, :] = (
                self.parts[at, :].astype(F32) + self.recv_low[x].astype(F32)
            ).astype(BF16)
        self.across = net.send(
            self.parts.at[self.piece(1 - net.x, net.c * half, half), :], self.recv_side, net.side()
        )

    def third(self):
        net, half = self.net, self.rows // 2
        self.across.wait_recv()
        at = self.piece(net.x, net.c * half, half)
        self.parts[at, :] = (
            self.parts[at, :].astype(F32) + self.recv_side[...].astype(F32)
        ).astype(BF16)
        away = net.c * half + (1 - net.y) * (half // 2)
        self.up = net.send(
            self.parts.at[self.piece(net.x, away, half // 2), :], self.recv_up, net.upper()
        )

    def result(self):
        net, half = self.net, self.rows // 2
        self.up.wait_recv()
        at = self.piece(net.x, net.c * half + net.y * (half // 2), half // 2)
        return self.parts[at, :].astype(F32) + self.recv_up[...].astype(F32)


def gather_quarters(net, ref):
    half = ref.shape[0] // 2
    base = net.c * half
    piece = ref.at[rows_of(base + net.y * (half // 2), half // 2), :]
    up = net.send(piece, piece, net.upper())

    def second():
        up.wait_recv()
        whole = ref.at[rows_of(base, half), :]
        return net.send(whole, whole, net.lower()).wait_recv

    return second


def norm_grad(grad_in, values_in, gain):
    inverse = lax.rsqrt(jnp.mean(values_in * values_in, axis=-1, keepdims=True) + EPSILON)
    normed = values_in * inverse
    scaled = grad_in * gain
    inner = jnp.mean(scaled * normed, axis=-1, keepdims=True)
    return inverse * (scaled - normed * inner), jnp.sum(grad_in * normed, axis=0, keepdims=True)


def to_columns(rows_in):
    many = rows_in.shape[1]
    return jnp.concatenate([rows_in, jnp.zeros((LANES - 8, many), F32)], axis=0).T


def backward_kernel(
    n_seq,
    docs,
    heads,
    tokens,
    gain_one,
    gain_two,
    queries,
    keyval,
    offsets,
    mass,
    logit_t,
    mixed,
    exact,
    middle,
    normed_two,
    out_grads,
    w_attn,
    w_out,
    w_ffn_far,
    doc_ref,
    layer_out,
    tokens_grad,
    gains,
    bias_grad,
    g_query,
    g_key,
    g_value,
    g_forget,
    g_out,
    g_gate,
    g_up,
    g_down,
    w_ffn,
    all_query,
    all_grad,
    allowed,
    ffn_grads,
    part_two,
    part_out,
    recv_two_low,
    recv_two_side,
    recv_two_up,
    recv_out_low,
    recv_out_side,
    recv_out_up,
    ffn_slots,
    ffn_relay,
    ffn_side,
    early_grads,
    early_across,
    early_slots,
    early_relay,
    late_grads,
    late_across,
    late_slots,
    late_relay,
    last_grads,
    last_across,
    last_slots,
    last_relay,
    h_one,
    grad_attn,
    grad_heads,
    stats,
    mass_rows,
    delta_rows,
    grad_qkv,
    grad_offs,
    one_parts,
    recv_one_low,
    recv_one_up,
    off_all,
    gain_swap,
    gain_peer,
    near_sem,
    sems,
):
    net = Net(n_seq, sems)
    s, z, x, y, c = net.s, net.z, net.x, net.y, net.c
    rows, width = tokens.shape
    half, quarter = rows // 2, rows // 4
    block = g_query.shape[0]
    hc = mixed.shape[1]
    hidden = w_ffn.shape[1] // 3
    span = n_seq * half
    tile = 256
    kept = c * half + y * quarter
    own = rows_of(kept, quarter)
    parts = [slice(p * half, (p + 1) * half) for p in range(2)]

    fetch = pltpu.make_async_copy(w_ffn_far, w_ffn, near_sem)
    fetch.start()
    query_net = Spread(net, lambda j: all_query.at[:, j])
    grad_net = Spread(net, lambda j: all_grad.at[:, j])
    ffn_net = LineReduce(
        net, lambda t: w_ffn.at[rows_of(t * 2 * block, 2 * block), :], ffn_slots, ffn_relay
    )
    early_net = SeqReduce(net, early_grads, early_across, early_slots, early_relay)
    late_net = SeqReduce(net, late_grads, late_across, late_slots, late_relay)
    last_net = SeqReduce(net, last_grads, last_across, last_slots, last_relay)
    for part in range(2):
        all_query[part, s] = queries[parts[part], :]
    net.barrier()
    query_net.start()
    fetch.wait()

    for at in range(2 * rows // tile):
        r = slice(at * tile, (at + 1) * tile)
        for col in range(hidden // tile):
            cc = [slice(k * hidden + col * tile, k * hidden + (col + 1) * tile) for k in range(3)]
            gate = dot_nn(normed_two[r, :], w_ffn[:, cc[0]])
            up = dot_nn(normed_two[r, :], w_ffn[:, cc[1]])
            grad_act = dot_nn(out_grads[r, :], w_ffn[:, cc[2]])
            sigmoid = 1.0 / (1.0 + jnp.exp(-gate))
            silu = gate * sigmoid
            ffn_grads[r, cc[0]] = (grad_act * up * sigmoid * (1.0 + gate * (1.0 - sigmoid))).astype(
                BF16
            )
            ffn_grads[r, cc[1]] = (grad_act * silu).astype(BF16)
            ffn_grads[r, cc[2]] = (silu * up).astype(BF16)
    for at in range(width // tile):
        cols = slice(at * tile, (at + 1) * tile)
        part_two[:, cols] = dot_nt(
            ffn_grads[:, : 2 * hidden], w_ffn[cols, : 2 * hidden]
        ).astype(BF16)
    two = RowReduce(net, part_two, recv_two_low, recv_two_side, recv_two_up)
    two.start()
    for at in range(width // tile):
        cols = slice(at * tile, (at + 1) * tile)
        part_out[:, cols] = dot_nt(ffn_grads[:, 2 * hidden :], w_ffn[cols, 2 * hidden :]).astype(
            BF16
        )
    two.second()
    out = RowReduce(net, part_out, recv_out_low, recv_out_side, recv_out_up)
    out.start()

    for at in range(width // tile):
        cols = slice(at * tile, (at + 1) * tile)
        w_ffn[cols, : 2 * hidden] = dot_tn(
            normed_two[:, cols], ffn_grads[:, : 2 * hidden]
        ).astype(BF16)
        w_ffn[cols, 2 * hidden :] = dot_tn(out_grads[:, cols], ffn_grads[:, 2 * hidden :]).astype(
            BF16
        )
    two.third()
    out.second()
    ffn_net.start()

    values_in = tokens[...].astype(F32)
    inverse = lax.rsqrt(jnp.mean(values_in * values_in, axis=-1, keepdims=True) + EPSILON)
    h_one[...] = (values_in * inverse * gain_one[...]).astype(BF16)

    def positions(shape, axis):
        at = lax.broadcasted_iota(jnp.int32, shape, axis)
        owner = (at % span) // half
        group = jnp.where(at // span == 0, owner, 2 * n_seq - 1 - owner)
        return group * half + at % half

    every_pos = positions((1, 2 * span), 1)
    own_pos = [
        (s if part == 0 else 2 * n_seq - 1 - s) * half
        + lax.broadcasted_iota(jnp.int32, (half, 1), 0)
        for part in range(2)
    ]
    for part in range(2):
        start = doc_starts(own_pos[part], doc_ref, docs)
        seen = (every_pos <= own_pos[part]) & (every_pos >= start)
        allowed[parts[part], :] = jnp.where(seen, 0.0, MASKED)

    grad_two = two.result()
    back_two, gain_two_part = norm_grad(grad_two, middle[...], gain_two[...])
    grad_middle = out_grads[rows_of(x * rows + kept, quarter), :].astype(F32) + back_two
    grad_attn[own, :] = grad_middle.astype(BF16)
    attn_second = gather_quarters(net, grad_attn)
    query_net.arrive()
    attn_second()()

    grad_heads[...] = dot_nn(grad_attn[...], w_out[...]).astype(BF16)
    for part in range(2):
        all_grad[part, s] = grad_heads[parts[part], :]
    grad_net.start()
    lane = lax.broadcasted_iota(jnp.int32, (rows, LANES), 1)
    delta = jnp.zeros((rows, LANES), F32)
    for pair in range(heads // 2):
        cols = slice(pair * LANES, (pair + 1) * LANES)
        product = grad_heads[:, cols].astype(F32) * exact[:, cols]
        for side in range(2):
            inner = jnp.sum(
                jnp.where(lane // HEAD_DIM == side, product, 0.0), axis=1, keepdims=True
            )
            delta = jnp.where(lane == pair * 2 + side, inner, delta)
    grad_offs[...] = delta
    stats[s, :8, :] = mass[...].T[:8, :]
    stats[s, 8:, :] = delta.T[:8, :]
    wait_stats = spread_small(net, lambda j: stats.at[j])
    out.third()

    lane = lax.broadcasted_iota(jnp.int32, (half, LANES), 1)
    first = (lane // HEAD_DIM) == 0
    score_sums = [jnp.zeros((half, LANES), F32), jnp.zeros((half, LANES), F32)]
    for pair in range(heads // 2):
        cols = slice(pair * LANES, (pair + 1) * LANES)
        vcols = slice(hc + pair * LANES, hc + (pair + 1) * LANES)
        for part in range(2):
            r = parts[part]
            many = span * (part + 1)
            key_pair = keyval[: part + 1, :, :, cols].reshape(many, LANES)
            value_pair = keyval[: part + 1, :, :, vcols].reshape(many, LANES)
            query_pair, grad_pair = queries[r, cols], grad_heads[r, cols]
            made = []
            for side in range(2):
                head = pair * 2 + side
                keep = (lane // HEAD_DIM) == side
                scores = (
                    dot_nt(jnp.where(keep, query_pair, jnp.zeros_like(query_pair)), key_pair)
                    - offsets[head : head + 1, :many]
                    + allowed[r, :many]
                )
                probs = jnp.exp(scores - mass[r, head : head + 1])
                grad_probs = dot_nt(
                    jnp.where(keep, grad_pair, jnp.zeros_like(grad_pair)), value_pair
                )
                grad_scores = (probs * (grad_probs - grad_offs[r, head : head + 1])).astype(BF16)
                made.append(dot_nn(grad_scores, key_pair))
                sums = jnp.sum(grad_scores.astype(F32), axis=1, keepdims=True)
                score_sums[part] = jnp.where(lane == head, sums, score_sums[part])
            grad_qkv[r, cols] = (jnp.where(first, made[0], made[1]) * HEAD_DIM ** (-0.5)).astype(
                BF16
            )
        if pair == 0:
            grad_net.arrive()
            query_net.finish()
    for part in range(2):
        grad_offs[parts[part], :] = score_sums[part]
    ffn_net.hand_on()

    for at in range(width // tile):
        cols = slice(at * tile, (at + 1) * tile)
        early_grads[cols, :hc] = dot_tn(h_one[:, cols], grad_qkv[:, :hc]).astype(BF16)
        early_grads[cols, hc:] = dot_tn(grad_attn[:, cols], mixed[...]).astype(BF16)
    grad_net.finish()
    early_net.start()
    ffn_sum_out = out.result()
    layer_out[own, :] = (middle[...] + ffn_sum_out).astype(BF16)
    layer_second = gather_quarters(net, layer_out)

    starts = doc_starts(every_pos, doc_ref, docs)
    for part in range(2):
        seen = (own_pos[part] <= every_pos) & (own_pos[part] >= starts)
        allowed[parts[part], :] = jnp.where(seen, 0.0, MASKED)
    wait_stats()
    for j in range(n_seq):
        for part in range(2):
            at = (part * n_seq + j) * half
            mass_rows[:, at : at + half] = stats[j, :8, parts[part]]
            delta_rows[:, at : at + half] = stats[j, 8:, parts[part]]

    score_sums = [jnp.zeros((half, LANES), F32), jnp.zeros((half, LANES), F32)]
    own_offs = [
        to_columns(offsets[:, pl.ds(pl.multiple_of((p * n_seq + s) * half, LANES), half)])
        for p in range(2)
    ]
    for pair in range(heads // 2):
        cols = slice(pair * LANES, (pair + 1) * LANES)
        vcols = slice(hc + pair * LANES, hc + (pair + 1) * LANES)
        for part in range(2):
            r = parts[part]
            many = span * (2 - part)
            lanes = slice(2 * span - many, 2 * span)
            query_all = all_query[part:, :, :, cols].reshape(many, LANES)
            grad_all = all_grad[part:, :, :, cols].reshape(many, LANES)
            key_pair, value_pair = keyval[part, s, :, cols], keyval[part, s, :, vcols]
            keys_made, values_made = [], []
            for side in range(2):
                head = pair * 2 + side
                keep = (lane // HEAD_DIM) == side
                scores = (
                    dot_nt(jnp.where(keep, key_pair, jnp.zeros_like(key_pair)), query_all)
                    - own_offs[part][:, head : head + 1]
                    + allowed[r, lanes]
                )
                probs = jnp.exp(scores - mass_rows[head : head + 1, lanes])
                grad_probs = dot_nt(
                    jnp.where(keep, value_pair, jnp.zeros_like(value_pair)), grad_all
                )
                grad_scores = (probs * (grad_probs - delta_rows[head : head + 1, lanes])).astype(
                    BF16
                )
                keys_made.append(dot_nn(grad_scores, query_all))
                values_made.append(dot_nn(probs.astype(BF16), grad_all))
                sums = jnp.sum(grad_scores.astype(F32), axis=1, keepdims=True)
                score_sums[part] = jnp.where(lane == head, sums, score_sums[part])
            grad_qkv[r, hc + pair * LANES : hc + (pair + 1) * LANES] = jnp.where(
                first, keys_made[0], keys_made[1]
            ).astype(BF16)
            grad_qkv[r, 2 * hc + pair * LANES : 2 * hc + (pair + 1) * LANES] = jnp.where(
                first, values_made[0], values_made[1]
            ).astype(BF16)
        if pair == 0:
            early_net.turn()
            layer_wait = layer_second()
    for part in range(2):
        grad_offs[parts[part], :] = grad_offs[parts[part], :] - score_sums[part]
    for at in range(width // tile):
        cols = slice(at * tile, (at + 1) * tile)
        late_grads[cols, :] = dot_tn(h_one[:, cols], grad_qkv[:, hc : 3 * hc]).astype(BF16)
    late_net.start()

    off_all[s] = grad_offs[...].T[:8, :]
    wait_offs = spread_small(net, lambda j: off_all.at[j])
    early_net.along.hand_on()
    wait_offs()
    after = (
        lax.broadcasted_iota(jnp.int32, (half, half), 0)
        >= lax.broadcasted_iota(jnp.int32, (half, half), 1)
    ).astype(F32)
    pieces = []
    for group in range(2 * n_seq):
        owner = group if group < n_seq else 2 * n_seq - 1 - group
        pieces.append(off_all[owner, :, parts[group // n_seq]])
    sums = jnp.dot(
        jnp.concatenate(pieces, axis=0), after, precision=HIGHEST, preferred_element_type=F32
    )
    later = jnp.zeros((8, 1), F32)
    own_sums = [jnp.zeros((8, half), F32), jnp.zeros((8, half), F32)]
    for group in range(2 * n_seq - 1, -1, -1):
        part = group // n_seq
        wanted = group == (s if part == 0 else 2 * n_seq - 1 - s)
        here = sums[group * 8 : (group + 1) * 8, :] + later
        own_sums[part] = jnp.where(wanted, here, own_sums[part])
        later = later + jnp.sum(pieces[group], axis=1, keepdims=True)
    grad_logit = jnp.concatenate(own_sums, axis=1) / (1.0 + jnp.exp(logit_t[...]))
    grad_qkv[:, 3 * hc :] = to_columns(grad_logit).astype(BF16)

    for at in range(width // tile):
        cols = slice(at * tile, (at + 1) * tile)
        last_grads[cols, :] = dot_tn(h_one[:, cols], grad_qkv[:, 3 * hc :]).astype(BF16)
    last_net.start()
    for at in range(width // tile):
        cols = slice(at * tile, (at + 1) * tile)
        for part in range(2):
            one_parts[part, :, cols] = dot_nt(grad_qkv[parts[part], :], w_attn[cols, :]).astype(
                BF16
            )
    low = net.send(one_parts.at[1 - c], recv_one_low, net.lower())
    late_net.turn()
    low.wait_recv()
    one_parts[c] = (one_parts[c].astype(F32) + recv_one_low[...].astype(F32)).astype(BF16)
    up = net.send(
        one_parts.at[c, rows_of((1 - y) * quarter, quarter), :], recv_one_up, net.upper()
    )
    last_net.turn()
    up.wait_recv()
    grad_one = one_parts[c, rows_of(y * quarter, quarter), :].astype(F32) + recv_one_up[
        ...
    ].astype(F32)
    back_one, gain_one_part = norm_grad(grad_one, tokens[own, :].astype(F32), gain_one[...])
    tokens_grad[own, :] = (grad_middle + back_one).astype(BF16)
    grad_second = gather_quarters(net, tokens_grad)
    line_row = lax.broadcasted_iota(jnp.int32, (8, width), 0)
    gain_peer[s, :, :width] = jnp.where(
        line_row == 0, gain_one_part, jnp.where(line_row == 1, gain_two_part, 0.0)
    )
    gain_peer[s, :, width:] = jnp.broadcast_to(
        jnp.sum(grad_logit, axis=1, keepdims=True), (8, LANES)
    )
    wait_gains = spread_small(net, lambda j: gain_peer.at[j])
    late_net.along.hand_on()
    last_net.along.hand_on()
    grad_wait = grad_second()

    def write_early(total):
        got = total(slice(0, block))
        g_query[...] = got[:, :hc]
        g_out[...] = got[:, hc:]

    early_net.along.finish(write_early)

    outs = (g_gate, g_up, g_down)
    side_rows = rows_of((1 - x) * block, block)

    def write_ffn(total):
        got = total(rows_of(x * block, block))
        for k, ref in enumerate(outs):
            ref[:, pl.ds(pl.multiple_of(x * hidden, LANES), hidden)] = got[
                :, k * hidden : (k + 1) * hidden
            ]
        ffn_side[0] = total(side_rows).astype(BF16)

    ffn_net.finish(write_ffn)
    across = net.send(ffn_side.at[0], ffn_side.at[1], net.side())

    wait_gains()
    total = gain_peer[0]
    for j in range(1, n_seq):
        total = total + gain_peer[j]
    bias_grad[...] = total[:, width:]
    for step, peer in enumerate((net.lower(), net.upper())):
        gain_swap[2 * step] = total[:, :width]
        swap = net.send(gain_swap.at[2 * step], gain_swap.at[2 * step + 1], peer)
        swap.wait_recv()
        total = gain_swap[2 * step] + gain_swap[2 * step + 1]
    gains[...] = total

    across.wait_recv()
    for k, ref in enumerate(outs):
        ref[:, pl.ds(pl.multiple_of((1 - x) * hidden, LANES), hidden)] = ffn_side[
            1, :, k * hidden : (k + 1) * hidden
        ].astype(F32)

    def write_late(total):
        got = total(slice(0, block))
        g_key[...] = got[:, :hc]
        g_value[...] = got[:, hc:]

    late_net.along.finish(write_late)

    def write_last(total):
        g_forget[...] = total(slice(0, block))

    last_net.along.finish(write_last)
    layer_wait()
    grad_wait()
    for part in (query_net, grad_net, ffn_net, early_net, late_net, last_net, net):
        part.drain()


def backward_shapes(n_seq, rows, width, hc, hidden, block):
    half, quarter = rows // 2, rows // 4
    line = n_seq // 2
    places = min(4, line - 1)
    relays = 1 if line <= 4 else 2 * (line - 3)

    def seq_reduce(columns):
        return [
            ((width, columns), BF16),
            ((line, block, columns), BF16),
            ((places, block, columns), BF16),
            ((relays, block, columns), BF16),
        ]

    ffn = 3 * hidden
    return [
        ((width, ffn), BF16),
        ((2, n_seq, half, hc), BF16),
        ((2, n_seq, half, hc), BF16),
        ((rows, 2 * n_seq * half), F32),
        ((2 * rows, ffn), BF16),
        ((2 * rows, width), BF16),
        ((2 * rows, width), BF16),
        ((2, half, width), BF16),
        ((half, width), BF16),
        ((quarter, width), BF16),
        ((2, half, width), BF16),
        ((half, width), BF16),
        ((quarter, width), BF16),
        ((places, 2 * block, ffn), BF16),
        ((relays, 2 * block, ffn), BF16),
        ((2, block, ffn), BF16),
        *seq_reduce(2 * hc),
        *seq_reduce(2 * hc),
        *seq_reduce(LANES),
        ((rows, width), BF16),
        ((rows, width), BF16),
        ((rows, hc), BF16),
        ((n_seq, 16, rows), F32),
        ((8, 2 * n_seq * half), F32),
        ((8, 2 * n_seq * half), F32),
        ((rows, 3 * hc + LANES), BF16),
        ((rows, LANES), F32),
        ((2, half, width), BF16),
        ((half, width), BF16),
        ((quarter, width), BF16),
        ((n_seq, 8, rows), F32),
        ((4, 8, width), F32),
        ((n_seq, 8, width + LANES), F32),
    ]


def run_backward(n_seq, heads, hidden, block, tokens, attn_gain, ffn_gain, docs, made):
    (
        queries,
        keyval,
        offsets,
        mass,
        logit_t,
        mixed,
        exact,
        middle,
        normed_two,
        out_grads,
        w_attn,
        w_out,
        w_ffn,
    ) = made
    rows, width = tokens.shape
    hc = mixed.shape[1]
    vmem = pl.BlockSpec(memory_space=pltpu.VMEM)
    outs = (
        ((rows, width), BF16),
        ((rows, width), BF16),
        ((8, width), F32),
        ((8, LANES), F32),
        ((block, hc), F32),
        ((block, hc), F32),
        ((block, hc), F32),
        ((block, LANES), F32),
        ((block, hc), F32),
        ((block, 2 * hidden), F32),
        ((block, 2 * hidden), F32),
        ((block, 2 * hidden), F32),
    )
    scratch = backward_shapes(n_seq, rows, width, hc, hidden, block)
    return pl.pallas_call(
        functools.partial(backward_kernel, n_seq, docs.shape[0], heads),
        out_shape=[jax.ShapeDtypeStruct(*o) for o in outs],
        in_specs=[vmem] * 15
        + [
            pl.BlockSpec(memory_space=pl.ANY),
            pl.BlockSpec(memory_space=pltpu.SMEM),
        ],
        out_specs=[vmem] * len(outs),
        scratch_shapes=[pltpu.VMEM(*o) for o in scratch]
        + [pltpu.SemaphoreType.DMA, pltpu.SemaphoreType.DMA((320,))],
        compiler_params=pltpu.CompilerParams(
            collective_id=1, has_side_effects=True, vmem_limit_bytes=62 << 20
        ),
    )(
        tokens,
        attn_gain.reshape(1, width),
        ffn_gain.reshape(1, width),
        queries,
        keyval,
        offsets,
        mass,
        logit_t,
        mixed,
        exact,
        middle,
        normed_two,
        out_grads,
        w_attn,
        w_out,
        w_ffn,
        docs,
    )


def kernel_body(
    tokens,
    attn_gain,
    query_weight,
    key_weight,
    value_weight,
    forget_weight,
    forget_bias,
    out_weight,
    ffn_gain,
    gate_weight,
    up_weight,
    down_weight,
    doc_lengths,
    out_grad,
):
    n_seq = lax.axis_size("seq")
    heads = forget_bias.shape[0]
    block = gate_weight.shape[0]
    hidden = gate_weight.shape[1] // 2
    made = run_forward(
        n_seq,
        heads,
        tokens,
        attn_gain,
        query_weight,
        key_weight,
        value_weight,
        forget_weight,
        forget_bias,
        out_weight.T,
        ffn_gain,
        gate_weight,
        up_weight,
        down_weight.T,
        doc_lengths,
        out_grad,
    )
    (
        layer_out,
        tokens_grad,
        gains,
        bias_grad,
        g_query,
        g_key,
        g_value,
        g_forget,
        g_out,
        g_gate,
        g_up,
        g_down,
    ) = run_backward(
        n_seq, heads, hidden, block, tokens, attn_gain, ffn_gain, doc_lengths, made
    )
    return (
        layer_out,
        tokens_grad,
        gains[0],
        g_query,
        g_key,
        g_value,
        g_forget[:, :heads],
        bias_grad[:heads, 0],
        g_out.T,
        gains[1],
        g_gate,
        g_up,
        g_down.T,
    )


def kernels_fit(tokens, forget_bias, out_weight, gate_weight):
    n_seq = lax.axis_size("seq")
    rows, width = tokens.shape
    hc = out_weight.shape[0]
    block, hidden = gate_weight.shape[0], gate_weight.shape[1] // 2
    shapes = backward_shapes(n_seq, rows, width, hc, hidden, block)
    size = sum(math.prod(shape) * jnp.dtype(kind).itemsize for shape, kind in shapes)
    return (
        size <= (48 << 20)
        and lax.axis_size("head") == 4
        and n_seq % 2 == 0
        and n_seq >= 8
        and rows == 2 * LANES
        and width % 256 == 0
        and hidden % 256 == 0
        and block % 16 == 0
        and forget_bias.shape[0] in (2, 4, 6)
    )


def unchanged(carried):
    return carried


def contract_rows(left, right):
    return lax.dot_general(
        left, right, (((0,), (0,)), ((), ())), preferred_element_type=jnp.float32
    )


def contract_cols(left, right):
    return lax.dot_general(
        left, right, (((1,), (1,)), ((), ())), preferred_element_type=jnp.float32
    )


def norm_rows(values_in, gain):
    inverse = lax.rsqrt(jnp.mean(values_in * values_in, axis=-1, keepdims=True) + EPSILON)
    normed = values_in * inverse
    return (normed, inverse, normed * gain)


def norm_back(grad_in, normed, inverse, gain):
    scaled = grad_in * gain
    inner = jnp.mean(scaled * normed, axis=-1, keepdims=True)
    return (inverse * (scaled - normed * inner), jnp.sum(grad_in * normed, axis=0))


def doc_index(positions, doc_ends):
    return jnp.sum((positions[:, None] >= doc_ends[None, :]).astype(jnp.int32), axis=1)


def stored_positions(rows, n_seq, local_rows):
    half_rows = local_rows // 2
    device_of = rows // local_rows
    within = rows % local_rows
    group_of = jnp.where(within < half_rows, device_of, 2 * n_seq - 1 - device_of)
    return group_of * half_rows + within % half_rows


def block_scores(
    query_heads, key_heads, query_offsets, key_offsets, query_pos, key_pos, query_docs, key_docs
):
    raw_scores = jnp.einsum(
        "qhd,khd->hqk", query_heads, key_heads, preferred_element_type=jnp.float32
    )
    scores = (
        raw_scores * HEAD_DIM ** (-0.5) + query_offsets.T[:, :, None] - key_offsets.T[:, None, :]
    )
    allowed = (query_docs[:, None] == key_docs[None, :]) & (key_pos[None, :] <= query_pos[:, None])
    return (jnp.where(allowed[None], scores, MASKED), allowed)


def piece_grads(
    query_heads,
    grad_heads,
    log_mass,
    row_delta,
    query_offsets,
    key_heads,
    value_heads,
    key_offsets,
    query_pos,
    key_pos,
    query_docs,
    key_docs,
):
    scores, allowed = block_scores(
        query_heads, key_heads, query_offsets, key_offsets, query_pos, key_pos, query_docs, key_docs
    )
    probs = jnp.where(allowed[None], jnp.exp(scores - log_mass[:, :, None]), 0.0)
    grad_probs = jnp.einsum(
        "qhd,khd->hqk", grad_heads, value_heads, preferred_element_type=jnp.float32
    )
    grad_scores = (probs * (grad_probs - row_delta[:, :, None])).astype(jnp.bfloat16)
    score_sums = grad_scores.astype(jnp.float32)
    query_rows = query_heads.shape[0]
    key_rows = key_heads.shape[0]
    grad_query = jnp.einsum(
        "hqk,khd->qhd", grad_scores, key_heads, preferred_element_type=jnp.float32
    ).reshape(query_rows, -1)
    grad_key = (
        jnp.einsum("hqk,qhd->khd", grad_scores, query_heads, preferred_element_type=jnp.float32)
        * HEAD_DIM ** (-0.5)
    ).reshape(key_rows, -1)
    grad_value = jnp.einsum(
        "hqk,qhd->khd", probs.astype(jnp.bfloat16), grad_heads, preferred_element_type=jnp.float32
    ).reshape(key_rows, -1)
    return (
        grad_query,
        jnp.sum(score_sums, axis=2).T,
        grad_key,
        grad_value,
        -jnp.sum(score_sums, axis=1).T,
    )


def plain_body(
    tokens,
    attn_gain,
    query_weight,
    key_weight,
    value_weight,
    forget_weight,
    forget_bias,
    out_weight,
    ffn_gain,
    gate_weight,
    up_weight,
    down_weight,
    doc_lengths,
    out_grad,
):
    local_rows = tokens.shape[0]
    local_heads = forget_bias.shape[0]
    head_cols = local_heads * HEAD_DIM
    n_seq = lax.axis_size("seq")
    my_index = lax.axis_index("seq")
    first_row = my_index * local_rows
    docs = doc_lengths.shape[0]
    doc_ends = jnp.sum(jnp.where(jnp.tri(docs, dtype=jnp.bool_), doc_lengths[None, :], 0), axis=1)
    local_pos = stored_positions(
        first_row + jnp.arange(local_rows, dtype=jnp.int32), n_seq, local_rows
    )
    local_docs = doc_index(local_pos, doc_ends)
    pos_low = jnp.min(local_pos)
    pos_high = jnp.max(local_pos)
    doc_low = jnp.min(local_docs)
    doc_high = jnp.max(local_docs)
    hidden = gate_weight.shape[1]
    forget_pad = jnp.pad(forget_weight, ((0, 0), (0, 128 - local_heads)))
    w_attn = lax.all_gather(
        jnp.concatenate([query_weight, key_weight, value_weight, forget_pad], axis=1),
        "seq",
        axis=0,
        tiled=True,
    )
    w_rest = lax.all_gather(
        jnp.concatenate([out_weight.T, gate_weight, up_weight, down_weight.T], axis=1),
        "seq",
        axis=0,
        tiled=True,
    )
    w_query = w_attn[:, :head_cols]
    w_key = w_attn[:, head_cols : 2 * head_cols]
    w_value = w_attn[:, 2 * head_cols : 3 * head_cols]
    w_forget = w_attn[:, 3 * head_cols : 3 * head_cols + local_heads]
    w_out_t = w_rest[:, :head_cols]
    w_gate = w_rest[:, head_cols : head_cols + hidden]
    w_up = w_rest[:, head_cols + hidden : head_cols + 2 * hidden]
    w_down_t = w_rest[:, head_cols + 2 * hidden :]
    inputs = tokens.astype(jnp.float32)
    normed_one, inverse_one, scaled_one = norm_rows(inputs, attn_gain)
    h_one = scaled_one.astype(jnp.bfloat16)
    query_flat = jnp.dot(h_one, w_query, preferred_element_type=jnp.float32).astype(jnp.bfloat16)
    key_flat = jnp.dot(h_one, w_key, preferred_element_type=jnp.float32).astype(jnp.bfloat16)
    value_flat = jnp.dot(h_one, w_value, preferred_element_type=jnp.float32).astype(jnp.bfloat16)
    forget_logit = jnp.dot(h_one, w_forget, preferred_element_type=jnp.float32) + forget_bias
    log_forget_all = lax.all_gather(jax.nn.log_sigmoid(forget_logit), "seq", axis=0, tiled=True)
    all_pos = stored_positions(
        jnp.arange(n_seq * local_rows, dtype=jnp.int32), n_seq, local_rows
    )
    earlier = (all_pos[None, :] <= all_pos[:, None]).astype(jnp.float32)
    offsets_all = jnp.dot(earlier, log_forget_all, precision=HIGHEST)
    offsets = lax.dynamic_slice_in_dim(offsets_all, first_row, local_rows, 0)
    query_heads = query_flat.reshape(local_rows, local_heads, HEAD_DIM)
    key_heads = key_flat.reshape(local_rows, local_heads, HEAD_DIM)
    value_heads = value_flat.reshape(local_rows, local_heads, HEAD_DIM)

    def key_range(piece_rows):
        key_pos = stored_positions(jnp.arange(piece_rows, dtype=jnp.int32), n_seq, local_rows)
        key_docs = doc_index(key_pos, doc_ends)
        is_live = (
            (jnp.min(key_pos) <= pos_high)
            & (jnp.max(key_docs) >= doc_low)
            & (jnp.min(key_docs) <= doc_high)
        )
        return (key_pos, key_docs, offsets_all, is_live)

    mass_state = (
        jnp.full((local_heads, local_rows), MASKED, jnp.float32),
        jnp.zeros((local_heads, local_rows), jnp.float32),
    )
    gathered = lax.all_gather(
        jnp.concatenate([key_flat, value_flat, query_flat], axis=1), "seq", axis=0, tiled=True
    )
    key_block = gathered[:, :head_cols]
    piece_rows = key_block.shape[0]
    key_pos, key_docs, key_offsets, is_live = key_range(piece_rows)

    def mass_update(carried_in):
        running_max, running_sum = carried_in
        scores, allowed = block_scores(
            query_heads,
            key_block.reshape(piece_rows, local_heads, HEAD_DIM),
            offsets,
            key_offsets,
            local_pos,
            key_pos,
            local_docs,
            key_docs,
        )
        new_max = jnp.maximum(running_max, jnp.max(scores, axis=2))
        weights = jnp.where(allowed[None], jnp.exp(scores - new_max[:, :, None]), 0.0)
        return (new_max, jnp.sum(weights, axis=2))

    running_max, running_sum = lax.cond(is_live, mass_update, unchanged, mass_state)
    log_mass = running_max + jnp.log(running_sum)
    start_state = (
        jnp.zeros((local_heads, local_rows, HEAD_DIM), jnp.float32),
        jnp.zeros((local_heads, local_rows, HEAD_DIM), jnp.float32),
    )
    attend_key_block = key_block
    value_block = gathered[:, head_cols : 2 * head_cols]
    attend_piece_rows = attend_key_block.shape[0]
    attend_key_pos, attend_key_docs, attend_key_offsets, is_live = key_range(attend_piece_rows)

    def attend_update(carried_in):
        scores, allowed = block_scores(
            query_heads,
            attend_key_block.reshape(attend_piece_rows, local_heads, HEAD_DIM),
            offsets,
            attend_key_offsets,
            local_pos,
            attend_key_pos,
            local_docs,
            attend_key_docs,
        )
        probs = jnp.where(allowed[None], jnp.exp(scores - log_mass[:, :, None]), 0.0)
        probs_low = probs.astype(jnp.bfloat16)
        remainder = (probs - probs_low.astype(jnp.float32)).astype(jnp.bfloat16)
        value_piece = value_block.reshape(attend_piece_rows, local_heads, HEAD_DIM)
        rounded_acc = jnp.einsum(
            "hqk,khd->hqd", probs_low, value_piece, preferred_element_type=jnp.float32
        )
        remainder_acc = jnp.einsum(
            "hqk,khd->hqd", remainder, value_piece, preferred_element_type=jnp.float32
        )
        return (rounded_acc, remainder_acc)

    rounded_acc, remainder_acc = lax.cond(is_live, attend_update, unchanged, start_state)
    attended_rows = rounded_acc.transpose(1, 0, 2)
    exact_rows = (rounded_acc + remainder_acc).transpose(1, 0, 2)
    mixed = attended_rows.reshape(local_rows, head_cols).astype(jnp.bfloat16)
    attn_part = contract_cols(mixed, w_out_t)
    middle = inputs + lax.psum(attn_part, "head")
    normed_two, inverse_two, scaled_two = norm_rows(middle, ffn_gain)
    h_two = scaled_two.astype(jnp.bfloat16)
    gate_value = jnp.dot(h_two, w_gate, preferred_element_type=jnp.float32)
    up_value = jnp.dot(h_two, w_up, preferred_element_type=jnp.float32)
    gate_sigmoid = jax.nn.sigmoid(gate_value)
    gate_silu = gate_value * gate_sigmoid
    activation = (gate_silu * up_value).astype(jnp.bfloat16)
    ffn_part = contract_cols(activation, w_down_t)
    layer_out = (
        middle + lax.psum(ffn_part.astype(jnp.bfloat16), "head").astype(jnp.float32)
    ).astype(jnp.bfloat16)
    grad_act = jnp.dot(out_grad, w_down_t, preferred_element_type=jnp.float32)
    grad_gate = (
        grad_act * up_value * gate_sigmoid * (1.0 + gate_value * (1.0 - gate_sigmoid))
    ).astype(jnp.bfloat16)
    grad_up = (grad_act * gate_silu).astype(jnp.bfloat16)
    part_two = contract_cols(grad_gate, w_gate) + contract_cols(grad_up, w_up)
    grad_two = lax.psum(part_two, "head")
    back_two, gain_two = norm_back(grad_two, normed_two, inverse_two, ffn_gain)
    grad_middle = out_grad.astype(jnp.float32) + back_two
    grad_attn = grad_middle.astype(jnp.bfloat16)
    grad_mixed = jnp.dot(grad_attn, w_out_t, preferred_element_type=jnp.float32).astype(
        jnp.bfloat16
    )
    grad_heads = grad_mixed.reshape(local_rows, local_heads, HEAD_DIM)
    row_delta = jnp.sum(grad_heads.astype(jnp.float32) * exact_rows, axis=2).T
    back_state = (
        jnp.zeros((local_rows, head_cols), jnp.float32),
        jnp.zeros((local_rows, local_heads), jnp.float32),
    )
    back_key_block = key_block
    back_value_block = value_block
    back_piece_rows = back_key_block.shape[0]
    back_key_pos, back_key_docs, back_key_offsets, is_live = key_range(back_piece_rows)

    def back_update(carried_in):
        terms = piece_grads(
            query_heads,
            grad_heads,
            log_mass,
            row_delta,
            offsets,
            back_key_block.reshape(back_piece_rows, local_heads, HEAD_DIM),
            back_value_block.reshape(back_piece_rows, local_heads, HEAD_DIM),
            back_key_offsets,
            local_pos,
            back_key_pos,
            local_docs,
            back_key_docs,
        )
        return (terms[0], terms[1])

    grad_query, grad_query_off = lax.cond(is_live, back_update, unchanged, back_state)
    stats = lax.all_gather(
        jnp.concatenate([log_mass.T, row_delta.T], axis=1), "seq", axis=0, tiled=True
    )
    stats_mass, stats_delta = stats[:, :local_heads], stats[:, local_heads:]
    key_state = (
        jnp.zeros((local_rows, head_cols), jnp.float32),
        jnp.zeros((local_rows, head_cols), jnp.float32),
        jnp.zeros((local_rows, local_heads), jnp.float32),
    )
    piece_query = gathered[:, 2 * head_cols :]
    piece_grad = lax.all_gather(grad_mixed, "seq", axis=0, tiled=True)
    key_piece_rows = piece_query.shape[0]
    piece_pos = stored_positions(jnp.arange(key_piece_rows, dtype=jnp.int32), n_seq, local_rows)
    piece_docs = doc_index(piece_pos, doc_ends)
    is_live = (
        (pos_low <= jnp.max(piece_pos))
        & (jnp.max(piece_docs) >= doc_low)
        & (jnp.min(piece_docs) <= doc_high)
    )

    def key_update(carried_in):
        piece_mass = stats_mass.T
        piece_delta = stats_delta.T
        terms = piece_grads(
            piece_query.reshape(key_piece_rows, local_heads, HEAD_DIM),
            piece_grad.reshape(key_piece_rows, local_heads, HEAD_DIM),
            piece_mass,
            piece_delta,
            offsets_all,
            key_heads,
            value_heads,
            offsets,
            piece_pos,
            local_pos,
            piece_docs,
            local_docs,
        )
        return (terms[2], terms[3], terms[4])

    grad_key, grad_value, grad_key_off = lax.cond(is_live, key_update, unchanged, key_state)
    grad_query_low = (grad_query * HEAD_DIM ** (-0.5)).astype(jnp.bfloat16)
    grad_key_low = grad_key.astype(jnp.bfloat16)
    grad_value_low = grad_value.astype(jnp.bfloat16)
    grad_offsets = grad_query_off + grad_key_off
    grad_off_all = lax.all_gather(grad_offsets, "seq", axis=0, tiled=True)
    later = (all_pos[None, :] >= local_pos[:, None]).astype(jnp.float32)
    grad_log = jnp.dot(later, grad_off_all, precision=HIGHEST)
    grad_logit = grad_log * jax.nn.sigmoid(-forget_logit)
    forget_table = w_forget.astype(jnp.float32)
    part_one = (
        contract_cols(grad_query_low, w_query)
        + contract_cols(grad_key_low, w_key)
        + contract_cols(grad_value_low, w_value)
        + lax.dot_general(grad_logit, forget_table, (((1,), (1,)), ((), ())), precision=HIGHEST)
    )
    grad_one = lax.psum(part_one.astype(jnp.bfloat16), "head").astype(jnp.float32)
    back_one, gain_one = norm_back(grad_one, normed_one, inverse_one, attn_gain)
    tokens_grad = (grad_middle + back_one).astype(jnp.bfloat16)
    forget_term = lax.dot_general(
        h_one.astype(jnp.float32), grad_logit, (((0,), (0,)), ((), ())), precision=HIGHEST
    )
    scatter_cols = [
        contract_rows(grad_attn, mixed),
        contract_rows(h_two, grad_gate),
        contract_rows(h_two, grad_up),
        contract_rows(out_grad, activation),
        contract_rows(h_one, grad_query_low),
        contract_rows(h_one, grad_key_low),
        contract_rows(h_one, grad_value_low),
        jnp.pad(forget_term, ((0, 0), (0, 128 - local_heads))),
    ]
    first_sum = lax.psum_scatter(
        jnp.concatenate([t.astype(jnp.bfloat16) for t in scatter_cols[:4]], axis=1),
        "seq",
        scatter_dimension=0,
        tiled=True,
    ).astype(jnp.float32)
    second_sum = lax.psum_scatter(
        jnp.concatenate([t.astype(jnp.bfloat16) for t in scatter_cols[4:]], axis=1),
        "seq",
        scatter_dimension=0,
        tiled=True,
    ).astype(jnp.float32)
    out_weight_grad = first_sum[:, :head_cols].T
    gate_weight_grad = first_sum[:, head_cols : head_cols + hidden]
    up_weight_grad = first_sum[:, head_cols + hidden : head_cols + 2 * hidden]
    down_weight_grad = first_sum[:, head_cols + 2 * hidden :].T
    query_weight_grad = second_sum[:, :head_cols]
    key_weight_grad = second_sum[:, head_cols : 2 * head_cols]
    value_weight_grad = second_sum[:, 2 * head_cols : 3 * head_cols]
    forget_weight_grad = second_sum[:, 3 * head_cols : 3 * head_cols + local_heads]
    attn_gain_grad, ffn_gain_grad, forget_bias_grad = lax.psum(
        (gain_one, gain_two, jnp.sum(grad_logit, axis=0)), "seq"
    )
    return (
        layer_out,
        tokens_grad,
        attn_gain_grad,
        query_weight_grad,
        key_weight_grad,
        value_weight_grad,
        forget_weight_grad,
        forget_bias_grad,
        out_weight_grad,
        ffn_gain_grad,
        gate_weight_grad,
        up_weight_grad,
        down_weight_grad,
    )


def body(*args):
    fits = kernels_fit(args[0], args[6], args[7], args[9])
    return (kernel_body if fits else plain_body)(*args)


def solution(mesh):
    return jax.shard_map(
        body,
        mesh=mesh,
        in_specs=(
            P("seq", None),
            P(),
            P("seq", "head"),
            P("seq", "head"),
            P("seq", "head"),
            P("seq", "head"),
            P("head"),
            P("head", "seq"),
            P(),
            P("seq", "head"),
            P("seq", "head"),
            P("head", "seq"),
            P(),
            P("seq", None),
        ),
        out_specs=(
            P("seq", None),
            P("seq", None),
            P(),
            P("seq", "head"),
            P("seq", "head"),
            P("seq", "head"),
            P("seq", "head"),
            P("head"),
            P("head", "seq"),
            P(),
            P("seq", "head"),
            P("seq", "head"),
            P("head", "seq"),
        ),
        check_vma=False,
    )
```

```python
import jax
import jax.numpy as jnp
from jax import lax
from jax.experimental import pallas as pl
from jax.experimental.pallas import tpu as pltpu
from jax.sharding import PartitionSpec as P

HEAD_DIM = 64
EPSILON = 1e-06
HIGHEST = lax.Precision.HIGHEST
MASKED = -1e30
MESH_ID = pl.DeviceIdType.MESH
F32 = jnp.float32
BF16 = jnp.bfloat16
LANES = 128
KEY_TILES = ((0, 0), (0, 1), (1, 0))
VALUE_TILES = ((1, 1), (2, 0), (2, 1))
OUT_TILES = ((0, 1), (1, 0), (1, 1))
NEAR_FIRST = (1, 3, 2)


def dot_nn(left, right):
    return jnp.dot(left, right, preferred_element_type=F32)


def dot_nt(left, right):
    return lax.dot_general(left, right, (((1,), (1,)), ((), ())), preferred_element_type=F32)


def dot_tn(left, right):
    return lax.dot_general(left, right, (((0,), (0,)), ((), ())), preferred_element_type=F32)


def rows_of(first, count):
    return pl.ds(pl.multiple_of(first, 16), count)


def add_to(ref, other):
    ref[...] = (ref[...].astype(F32) + other[...].astype(F32)).astype(BF16)


class Net:
    def __init__(self, sems):
        s = lax.axis_index("seq")
        h = lax.axis_index("head")
        self.line = 4
        self.z, self.x = s // 2, s % 2
        self.y, self.c = h // 2, h % 2
        self.sems = sems
        self.used = 0
        self.pending = []

    def alloc(self, count):
        first = self.used
        self.used += count
        return first

    def to(self, z=None, x=None, y=None, c=None):
        z = self.z if z is None else z
        x = self.x if x is None else x
        y = self.y if y is None else y
        c = self.c if c is None else c
        return (z * 2 + x, y * 2 + c)

    def side(self):
        return self.to(x=1 - self.x)

    def lower(self):
        return self.to(c=1 - self.c)

    def upper(self):
        return self.to(y=1 - self.y)

    def next(self, step):
        return (self.z + step) % self.line

    def barrier(self):
        sem = pltpu.get_barrier_semaphore()
        peers = [self.side(), self.lower(), self.upper(), self.to(x=1 - self.x, c=1 - self.c)]
        for step in range(1, self.line):
            peers.append(self.to(z=self.next(step)))
            peers.append(self.to(z=self.next(step), c=1 - self.c))
        for peer in peers:
            pl.semaphore_signal(sem, 1, device_id=peer, device_id_type=MESH_ID)
        pl.semaphore_wait(sem, len(peers))

    def copy(self, src, dst, send, recv, device):
        return pltpu.make_async_remote_copy(
            src_ref=src,
            dst_ref=dst,
            send_sem=self.sems.at[send],
            recv_sem=self.sems.at[recv],
            device_id=device,
            device_id_type=MESH_ID,
        )

    def begin(self, made):
        made.start()
        self.pending.append(made.wait_send)
        return made

    def send(self, src, dst, device):
        first = self.alloc(2)
        return self.begin(self.copy(src, dst, first, first + 1, device))

    def got(self, ref, recv):
        self.copy(ref, ref, recv, recv, self.side()).wait_recv()

    def drain(self):
        for wait in self.pending:
            wait()
        self.pending = []


class RowGather:
    def __init__(self, net, slot, lower=None):
        self.net = net
        self.slot = slot
        self.low = lower
        self.sent = net.alloc(4)
        self.came = net.alloc(4)
        self.up_sent = net.alloc(4)
        self.up_came = net.alloc(4)
        self.low_sent = net.alloc(8)
        self.low_came = net.alloc(8)

    def pass_low(self, y, z):
        if self.low is not None:
            net = self.net
            index = y * 4 + z
            block = self.slot(y, z)
            net.begin(
                net.copy(
                    block, block, self.low_sent + index, self.low_came + index, net.lower()
                )
            )

    def pass_up(self, z):
        net = self.net
        block = self.slot(net.y, z)
        net.begin(net.copy(block, block, self.up_sent + z, self.up_came + z, net.upper()))
        self.pass_low(net.y, z)

    def start(self):
        net = self.net
        mine = self.slot(net.y, net.z)
        for step in NEAR_FIRST:
            net.begin(
                net.copy(
                    mine, mine, self.sent + step, self.came + net.z, net.to(z=net.next(step))
                )
            )
        self.pass_up(net.z)

    def forward(self):
        net = self.net
        for step in NEAR_FIRST:
            src = net.next(step)
            net.got(self.slot(net.y, src), self.came + src)
            self.pass_up(src)

    def finish(self):
        net = self.net
        for step in (0,) + NEAR_FIRST:
            src = net.next(step)
            net.got(self.slot(1 - net.y, src), self.up_came + src)
            self.pass_low(1 - net.y, src)
        if self.low is not None:
            for y in range(2):
                for z in range(4):
                    net.got(self.low(y, z), self.low_came + y * 4 + z)


class RowSum:
    def __init__(self, net, slot, recv_up, recv_line):
        self.net = net
        self.slot = slot
        self.recv_up = recv_up
        self.recv_line = recv_line
        self.up_sent = net.alloc(4)
        self.up_came = net.alloc(4)
        self.sent = net.alloc(4)
        self.came = net.alloc(4)

    def start(self):
        net = self.net
        for step in (2, 1, 3, 0):
            z = net.next(step)
            net.begin(
                net.copy(
                    self.slot(1 - net.y, z),
                    self.recv_up.at[z],
                    self.up_sent + z,
                    self.up_came + z,
                    net.upper(),
                )
            )

    def middle(self):
        net = self.net
        for step in (2, 1, 3, 0):
            z = net.next(step)
            net.got(self.recv_up.at[z], self.up_came + z)
            mine = self.slot(net.y, z)
            add_to(mine, self.recv_up.at[z])
            if step:
                net.begin(
                    net.copy(
                        mine,
                        self.recv_line.at[net.z],
                        self.sent + step,
                        self.came + net.z,
                        net.to(z=z),
                    )
                )

    def result(self):
        net = self.net
        total = self.slot(net.y, net.z)[...].astype(F32)
        for step in NEAR_FIRST:
            src = net.next(step)
            net.got(self.recv_line.at[src], self.came + src)
            total = total + self.recv_line[src].astype(F32)
        return total


class CrossGather:
    def __init__(self, net, slot):
        self.net = net
        self.slot = slot

    def start(self):
        net = self.net
        mine = self.slot(net.x, net.c)
        self.across = net.send(mine, mine, net.side())
        self.low = net.send(mine, mine, net.lower())

    def forward(self):
        net = self.net
        self.across.wait_recv()
        other = self.slot(1 - net.x, net.c)
        self.both = net.send(other, other, net.lower())

    def finish(self):
        self.low.wait_recv()
        self.both.wait_recv()


class WeightSpread:
    def __init__(self, net, stage, full):
        self.net = net
        self.stage = stage
        self.full = full
        self.block = stage.shape[1]
        self.sent = net.alloc(2)
        self.came = net.alloc(4)
        self.side_sent = net.alloc(4)
        self.side_came = net.alloc(4)
        self.low_sent = net.alloc(8)
        self.low_came = net.alloc(8)
        self.first = (net.z // 2) == net.c

    def slot(self, z, x):
        return self.full.at[rows_of((z * 2 + x) * self.block, self.block), :]

    def away(self, u):
        net = self.net
        return net.copy(
            self.stage.at[u],
            self.slot(net.z, net.x),
            self.sent + u,
            self.came + net.z,
            net.to(z=2 * net.c + u),
        )

    def across(self, z):
        net = self.net
        block = self.slot(z, net.x)
        return net.copy(block, block, self.side_sent + z, self.side_came + z, net.side())

    def low(self, z, x):
        block = self.slot(z, x)
        index = z * 2 + x
        return self.net.copy(
            block, block, self.low_sent + index, self.low_came + index, self.net.lower()
        )

    def start(self):
        net = self.net
        for u in range(2):
            pl.when(2 * net.c + u != net.z)(lambda u=u: self.away(u).start())

        @pl.when(self.first)
        def _():
            self.slot(net.z, net.x)[...] = self.stage[net.z % 2]
            self.across(net.z).start()
            self.low(net.z, net.x).start()

    def forward(self):
        net = self.net

        @pl.when(self.first)
        def _():
            for step in NEAR_FIRST:
                src = net.next(step)
                net.got(self.slot(src, net.x), self.came + src)
                self.across(src).start()
                self.low(src, net.x).start()

    def finish(self):
        net = self.net

        @pl.when(self.first)
        def _():
            for step in (0,) + NEAR_FIRST:
                src = net.next(step)
                net.got(self.slot(src, 1 - net.x), self.side_came + src)
                self.low(src, 1 - net.x).start()

        @pl.when(jnp.logical_not(self.first))
        def _():
            for z in range(4):
                for x in range(2):
                    net.got(self.slot(z, x), self.low_came + z * 2 + x)

    def drain(self):
        net = self.net
        for u in range(2):
            pl.when(2 * net.c + u != net.z)(lambda u=u: self.away(u).wait_send())

        @pl.when(self.first)
        def _():
            for z in range(4):
                self.across(z).wait_send()
                for x in range(2):
                    self.low(z, x).wait_send()


class HiddenSpread:
    def __init__(self, net, stage, full):
        self.net = net
        self.stage = stage
        self.full = full
        self.block = stage.shape[1]
        self.sent = net.alloc(4)
        self.came = net.alloc(4)
        self.side_sent = net.alloc(4)
        self.side_came = net.alloc(4)

    def slot(self, z, x):
        return self.full.at[rows_of((z * 2 + x) * self.block, self.block), :]

    def across(self, z):
        net = self.net
        block = self.slot(z, net.x)
        net.begin(net.copy(block, block, self.side_sent + z, self.side_came + z, net.side()))

    def start(self):
        net = self.net
        self.slot(net.z, net.x)[...] = self.stage[net.z]
        for step in NEAR_FIRST:
            to = net.next(step)
            net.begin(
                net.copy(
                    self.stage.at[to],
                    self.slot(net.z, net.x),
                    self.sent + step,
                    self.came + net.z,
                    net.to(z=to),
                )
            )
        self.across(net.z)

    def forward(self):
        net = self.net
        for step in NEAR_FIRST:
            src = net.next(step)
            net.got(self.slot(src, net.x), self.came + src)
            self.across(src)

    def finish(self):
        net = self.net
        for z in range(4):
            net.got(self.slot(z, 1 - net.x), self.side_came + z)


class WeightSum:
    def __init__(self, net, grads, recv_low, recv_side, final):
        self.net = net
        self.grads = grads
        self.recv_low = recv_low
        self.recv_side = recv_side
        self.final = final
        self.block = final.shape[1]
        self.side_sent = net.alloc(2)
        self.side_came = net.alloc(2)
        self.sent = net.alloc(2)
        self.came = net.alloc(2)

    def rows(self, z, x):
        return self.grads.at[rows_of((z * 2 + x) * self.block, self.block), :]

    def start(self):
        net = self.net
        half = 4 * self.block
        self.low = net.send(
            self.grads.at[rows_of((1 - net.c) * half, half), :], self.recv_low, net.lower()
        )

    def second(self):
        net = self.net
        self.low.wait_recv()
        for x in (1 - net.x, net.x):
            for i in range(2):
                z = 2 * net.c + i
                add_to(
                    self.rows(z, x), self.recv_low.at[rows_of((i * 2 + x) * self.block, self.block)]
                )
        for i in range(2):
            net.begin(
                net.copy(
                    self.rows(2 * net.c + i, 1 - net.x),
                    self.recv_side.at[i],
                    self.side_sent + i,
                    self.side_came + i,
                    net.side(),
                )
            )

    def owner(self, i):
        net = self.net
        z = 2 * net.c + i
        made = net.copy(
            self.rows(z, net.x),
            self.final.at[net.z % 2],
            self.sent + i,
            self.came + net.z % 2,
            net.to(z=z, c=net.z // 2),
        )
        return (z == net.z) & (net.z // 2 == net.c), made

    def third(self):
        net = self.net
        for i in range(2):
            net.got(self.recv_side.at[i], self.side_came + i)
            mine = self.rows(2 * net.c + i, net.x)
            add_to(mine, self.recv_side.at[i])
            local, made = self.owner(i)

            @pl.when(local)
            def _():
                self.final[net.z % 2] = mine[...]

            pl.when(jnp.logical_not(local))(made.start)

    def finish(self):
        net = self.net
        for u in range(2):
            pl.when(2 * net.c + u != net.z)(
                lambda u=u: net.got(self.final.at[u], self.came + u)
            )

    def drain(self):
        for i in range(2):
            local, made = self.owner(i)
            pl.when(jnp.logical_not(local))(made.wait_send)


class HiddenSum:
    def __init__(self, net, grads, recv_side, final):
        self.net = net
        self.grads = grads
        self.recv_side = recv_side
        self.final = final
        self.block = final.shape[1]
        self.side_sent = net.alloc(4)
        self.side_came = net.alloc(4)
        self.sent = net.alloc(4)
        self.came = net.alloc(4)

    def rows(self, z, x):
        return self.grads.at[rows_of((z * 2 + x) * self.block, self.block), :]

    def start(self):
        net = self.net
        for step in (2, 1, 3, 0):
            z = net.next(step)
            net.begin(
                net.copy(
                    self.rows(z, 1 - net.x),
                    self.recv_side.at[z],
                    self.side_sent + z,
                    self.side_came + z,
                    net.side(),
                )
            )

    def second(self):
        net = self.net
        for step in (2, 1, 3, 0):
            z = net.next(step)
            net.got(self.recv_side.at[z], self.side_came + z)
            mine = self.rows(z, net.x)
            add_to(mine, self.recv_side.at[z])
            if step:
                net.begin(
                    net.copy(
                        mine,
                        self.final.at[net.z],
                        self.sent + step,
                        self.came + net.z,
                        net.to(z=z),
                    )
                )
            else:
                self.final[net.z] = mine[...]

    def finish(self):
        net = self.net
        for step in NEAR_FIRST:
            src = net.next(step)
            net.got(self.final.at[src], self.came + src)


class Places:
    def __init__(self, net, chunk):
        self.net = net
        self.chunk = chunk
        self.part = 4 * chunk
        self.all = 32 * chunk

    def position(self, at):
        chunk = self.chunk
        late = at // (16 * chunk)
        x = (at // (8 * chunk)) % 2
        c = (at // (4 * chunk)) % 2
        z = (at // chunk) % 4
        owner = 2 * z + x
        group = jnp.where(late == 0, owner, 15 - owner)
        return group * (2 * chunk) + c * chunk + at % chunk

    def own(self, late):
        return (late * 4 + self.net.x * 2 + self.net.c) * self.part

    def every(self, shape, axis):
        return self.position(lax.broadcasted_iota(jnp.int32, shape, axis))


def doc_starts(positions, doc_ref):
    start = jnp.zeros(positions.shape, jnp.int32)
    end = jnp.int32(0)
    for k in range(doc_ref.shape[0] - 1):
        end = end + doc_ref[k]
        start = jnp.where(positions >= end, end, start)
    return start


def running_sums(places, rows_in, spread, gather, backward):
    tiles = places.all // LANES
    chunk = places.chunk
    row = lax.broadcasted_iota(jnp.int32, (LANES, LANES), 0)
    col = lax.broadcasted_iota(jnp.int32, (LANES, LANES), 1)
    reach = row >= col if backward else row <= col
    within = ((row // chunk == col // chunk) & reach).astype(F32)
    stacked = jnp.concatenate(
        [rows_in[:, k * LANES : (k + 1) * LANES] for k in range(tiles)], axis=0
    )
    inside = jnp.dot(stacked, within, precision=HIGHEST, preferred_element_type=F32)
    outside = jnp.dot(rows_in, spread[...], precision=HIGHEST, preferred_element_type=F32)
    outside = outside[:, : gather.shape[0]]
    outside = jnp.dot(outside, gather[...], precision=HIGHEST, preferred_element_type=F32)
    return outside + jnp.concatenate(
        [inside[k * 8 : (k + 1) * 8, :] for k in range(tiles)], axis=1
    )


def order_tables(places, spread, gather, backward):
    order = places.every((places.all, LANES), 0) // places.chunk
    slot = lax.broadcasted_iota(jnp.int32, (places.all, LANES), 1)
    beyond = order > slot if backward else order < slot
    spread[...] = beyond.astype(F32)
    order = places.every(gather.shape, 1) // places.chunk
    slot = lax.broadcasted_iota(jnp.int32, gather.shape, 0)
    gather[...] = (order == slot).astype(F32)


def tile_of(ref, rows, tile):
    return ref[rows, tile * LANES : (tile + 1) * LANES]


def only(values_in, lane, side):
    return jnp.where(lane // HEAD_DIM == side, values_in, jnp.zeros_like(values_in))


def norm_grad(grad_in, values_in, gain):
    inverse = lax.rsqrt(jnp.mean(values_in * values_in, axis=-1, keepdims=True) + EPSILON)
    normed = values_in * inverse
    scaled = grad_in * gain
    inner = jnp.mean(scaled * normed, axis=-1, keepdims=True)
    return inverse * (scaled - normed * inner), jnp.sum(grad_in * normed, axis=0, keepdims=True)


def norm(values_in, gain):
    inverse = lax.rsqrt(jnp.mean(values_in * values_in, axis=-1, keepdims=True) + EPSILON)
    return (values_in * inverse * gain).astype(BF16)


def to_columns(rows_in, first=0):
    many = rows_in.shape[1]
    parts = [rows_in, jnp.zeros((LANES - 8 - first, many), F32)]
    if first:
        parts = [jnp.zeros((first, many), F32)] + parts
    return jnp.concatenate(parts, axis=0).T


def gather_quarters(net, ref):
    chunk = ref.shape[0] // 4

    def piece(y):
        return ref.at[rows_of((2 * y + net.c) * chunk, chunk), :]

    up = net.send(piece(net.y), piece(net.y), net.upper())
    first = net.send(piece(net.y), piece(net.y), net.lower())

    def second():
        up.wait_recv()
        other = net.send(piece(1 - net.y), piece(1 - net.y), net.lower())

        def last():
            first.wait_recv()
            other.wait_recv()

        return last

    return second


def forward_kernel(
    tokens,
    gain_one,
    gain_two,
    stage_attn,
    stage_out,
    stage_bias,
    wg,
    wu,
    wd_t,
    doc_ref,
    og,
    queries,
    keyval,
    offsets,
    mass,
    logits,
    mixed,
    exact,
    middle,
    normed_two,
    out_grads,
    w_attn,
    w_out,
    w_ffn,
    h_one,
    stage_ffn,
    rows_in,
    allowed,
    spread,
    gather,
    logit_parts,
    other_bias,
    proj,
    parts,
    recv_up,
    recv_line,
    sems,
):
    net = Net(sems)
    z, x, y, c = net.z, net.x, net.y, net.c
    width = tokens.shape[1]
    chunk = tokens.shape[0] // 4
    part = 4 * chunk
    places = Places(net, chunk)
    hidden = wg.shape[1] // 4
    own = rows_of((2 * y + c) * chunk, chunk)
    tile = 256

    token_net = RowGather(net, lambda yy, zz: rows_in.at[yy, zz])
    attn_net = WeightSpread(net, stage_attn, w_attn)
    out_net = WeightSpread(net, stage_out, w_out)
    ffn_net = HiddenSpread(net, stage_ffn, w_ffn)
    kv_net = CrossGather(net, lambda xx, cc: keyval.at[:, xx, cc])
    logit_net = CrossGather(net, lambda xx, cc: logit_parts.at[xx, cc])
    two_net = RowGather(
        net,
        lambda yy, zz: normed_two.at[c, yy, zz],
        lambda yy, zz: normed_two.at[1 - c, yy, zz],
    )
    grad_net = RowGather(
        net, lambda yy, zz: out_grads.at[c, yy, zz], lambda yy, zz: out_grads.at[1 - c, yy, zz]
    )
    attn_sum = RowSum(
        net, lambda yy, zz: parts.at[yy, rows_of(zz * chunk, chunk), :], recv_up, recv_line
    )

    rows_in[y, z] = tokens[own, :]
    net.barrier()
    attn_net.start()
    token_net.start()
    bias_send = net.send(stage_bias, other_bias, net.lower())

    out_grads[c, y, z] = og[own, :]
    for index, ref in enumerate((wg, wu, wd_t)):
        for zz in range(4):
            stage_ffn[zz, :, index * hidden : (index + 1) * hidden] = ref[
                :, zz * hidden : (zz + 1) * hidden
            ]
    order_tables(places, spread, gather, False)
    every = places.every((1, places.all), 1)
    for late in range(2):
        at = places.own(late) + lax.broadcasted_iota(jnp.int32, (part, 1), 0)
        pos = places.position(at)
        start = doc_starts(pos, doc_ref)
        seen = (every <= pos) & (every >= start)
        allowed[late * part : (late + 1) * part, :] = jnp.where(seen, 0.0, MASKED)

    token_net.forward()
    attn_net.forward()
    grad_net.start()
    h_one[y] = norm(rows_in[y].reshape(part, width).astype(F32), gain_one[...])
    token_net.finish()
    h_one[1 - y] = norm(rows_in[1 - y].reshape(part, width).astype(F32), gain_one[...])
    attn_net.finish()

    for late in range(2):
        r = slice(late * part, (late + 1) * part)
        for at in range(0, w_attn.shape[1], tile):
            cols = slice(at, min(at + tile, w_attn.shape[1]))
            proj[r, cols] = dot_nn(h_one[late], w_attn[:, cols])
        keyval[late, x, c] = proj[r, : 3 * LANES].astype(BF16)
    kv_net.start()
    bias_send.wait_recv()
    bias = jnp.where(attn_net.first, stage_bias[z % 2], other_bias[z % 2])[:, :1]
    logit_parts[x, c] = proj[:, 4 * LANES :].T[HEAD_DIM : HEAD_DIM + 8, :] + bias
    logit_net.start()
    out_net.start()
    ffn_net.start()
    queries[...] = (
        proj[:, 3 * LANES :].astype(BF16).astype(F32) * HEAD_DIM ** (-0.5)
    ).astype(BF16)

    logit_net.forward()
    grad_net.forward()
    logit_net.finish()
    for late in range(2):
        for xx in range(2):
            for cc in range(2):
                at = (late * 4 + xx * 2 + cc) * part
                logits[:, at : at + part] = logit_parts[xx, cc, :, late * part : (late + 1) * part]
    turned = logits[...]
    logs = jnp.minimum(turned, 0.0) - jnp.log(1.0 + jnp.exp(-jnp.abs(turned)))
    offsets[...] = running_sums(places, logs, spread, gather, False)
    kv_net.forward()
    out_net.forward()
    kv_net.finish()

    lane = lax.broadcasted_iota(jnp.int32, (LANES, LANES), 1)
    first = (lane // HEAD_DIM) == 0
    for block in range(2 * part // LANES):
        r = slice(block * LANES, (block + 1) * LANES)
        late = (block * LANES) // part
        many = places.all // 2 * (late + 1)
        made, kept = [], []
        masses = jnp.zeros((LANES, LANES), F32)
        for head in range(3):
            tile_k, side_k = KEY_TILES[head]
            tile_v, side_v = VALUE_TILES[head]
            keys = keyval[: late + 1, :, :, :, tile_k * LANES : (tile_k + 1) * LANES]
            values = keyval[: late + 1, :, :, :, tile_v * LANES : (tile_v + 1) * LANES]
            keys, values = keys.reshape(many, LANES), values.reshape(many, LANES)
            scores = (
                dot_nt(only(tile_of(queries, r, tile_k), lane, side_k), keys)
                - offsets[head : head + 1, :many]
                + allowed[r, :many]
            )
            top = jnp.max(scores, axis=1, keepdims=True)
            probs = jnp.exp(scores - top)
            total = jnp.sum(probs, axis=1, keepdims=True)
            high = probs.astype(BF16)
            rest = (probs - high.astype(F32)).astype(BF16)
            share = 1.0 / total
            rounded = dot_nn(high, values)
            made.append(rounded * share)
            kept.append((rounded + dot_nn(rest, values)) * share)
            masses = jnp.where(lane == head, top + jnp.log(total), masses)
        mass[r, :] = masses
        mixed[r, :LANES] = jnp.where(first, 0.0, made[0]).astype(BF16)
        mixed[r, LANES:] = jnp.where(first, made[1], made[2]).astype(BF16)
        exact[r, :LANES] = jnp.where(first, 0.0, kept[0])
        exact[r, LANES:] = jnp.where(first, kept[1], kept[2])
        if block == 1:
            out_net.finish()
            ffn_net.forward()

    def project(late):
        rows = rows_of(late * part, part)
        for at in range(0, width, tile):
            cols = slice(at, at + tile)
            parts[late, :, cols] = dot_nt(mixed[rows, :], w_out[cols, :]).astype(BF16)

    project(1 - y)
    attn_sum.start()
    project(y)
    attn_sum.middle()
    total = tokens[own, :].astype(F32) + attn_sum.result()
    middle[...] = total
    normed_two[c, y, z] = norm(total, gain_two[...])
    two_net.start()
    grad_net.finish()
    two_net.forward()
    ffn_net.finish()
    two_net.finish()
    attn_net.drain()
    out_net.drain()
    net.drain()


def backward_kernel(
    tokens,
    out_grad,
    gain_one,
    gain_two,
    queries,
    keyval,
    offsets,
    mass,
    logits,
    mixed,
    exact,
    middle,
    normed_two,
    out_grads,
    w_attn,
    w_out,
    w_ffn,
    h_one,
    doc_ref,
    layer_out,
    tokens_grad,
    gains,
    bias_grad,
    g_query,
    g_key,
    g_value,
    g_forget,
    g_out,
    g_gate,
    g_up,
    g_down,
    all_query,
    all_grad,
    allowed,
    spread,
    gather,
    ffn_grads,
    part_two,
    part_out,
    two_low,
    two_up,
    two_line,
    out_low,
    out_up,
    out_line,
    ffn_sum,
    ffn_side,
    ffn_final,
    late_sum,
    late_low,
    late_side,
    late_final,
    last_sum,
    last_low,
    last_side,
    last_final,
    early_sum,
    early_low,
    early_side,
    early_final,
    grad_attn,
    grad_heads,
    stats,
    off_parts,
    every_off,
    grad_qkv,
    grad_offs,
    part_one,
    one_up,
    one_line,
    gain_parts,
    gain_swap,
    sems,
):
    net = Net(sems)
    z, x, y, c = net.z, net.x, net.y, net.c
    width = tokens.shape[1]
    chunk = tokens.shape[0] // 4
    part = 4 * chunk
    places = Places(net, chunk)
    hidden = w_ffn.shape[1] // 3
    half_heads = g_query.shape[1] // 2
    own = rows_of((2 * y + c) * chunk, chunk)
    tile = 256
    tiles = [slice(at, at + tile) for at in range(0, width, tile)]

    query_net = CrossGather(net, lambda xx, cc: all_query.at[:, xx, cc])
    grad_net = CrossGather(net, lambda xx, cc: all_grad.at[:, xx, cc])
    stat_net = CrossGather(net, lambda xx, cc: stats.at[xx, cc])
    off_net = CrossGather(net, lambda xx, cc: off_parts.at[xx, cc])
    attn_net = RowGather(
        net, lambda yy, zz: grad_attn.at[yy, rows_of(zz * chunk, chunk), :]
    )

    def chunks_of(ref):
        return lambda yy, zz: ref.at[c, yy, rows_of(zz * chunk, chunk), :]

    two = RowSum(net, chunks_of(part_two), two_up, two_line)
    out = RowSum(net, chunks_of(part_out), out_up, out_line)
    one = RowSum(
        net, lambda yy, zz: part_one.at[yy, rows_of(zz * chunk, chunk), :], one_up, one_line
    )
    ffn_net = HiddenSum(net, ffn_sum, ffn_side, ffn_final)
    late_net = WeightSum(net, late_sum, late_low, late_side, late_final)
    last_net = WeightSum(net, last_sum, last_low, last_side, last_final)
    early_net = WeightSum(net, early_sum, early_low, early_side, early_final)

    for late in range(2):
        all_query[late, x, c] = queries[late * part : (late + 1) * part, :]
    net.barrier()
    query_net.start()

    for at in range(4):
        cc, late = at // 2, at % 2
        inputs = normed_two[cc, late].reshape(part, width)
        gate = dot_nn(inputs, w_ffn[:, :hidden])
        up = dot_nn(inputs, w_ffn[:, hidden : 2 * hidden])
        grad_act = dot_nn(out_grads[cc, late].reshape(part, width), w_ffn[:, 2 * hidden :])
        sigmoid = 1.0 / (1.0 + jnp.exp(-gate))
        silu = gate * sigmoid
        ffn_grads[cc, late, :, :hidden] = (
            grad_act * up * sigmoid * (1.0 + gate * (1.0 - sigmoid))
        ).astype(BF16)
        ffn_grads[cc, late, :, hidden : 2 * hidden] = (grad_act * silu).astype(BF16)
        ffn_grads[cc, late, :, 2 * hidden :] = (silu * up).astype(BF16)

    def project(parts, cc, late, cols):
        for r in tiles:
            parts[cc, late, :, r] = dot_nt(ffn_grads[cc, late, :, cols], w_ffn[r, cols]).astype(
                BF16
            )

    def lows(parts, recv, cols):
        project(parts, 1 - c, 1 - y, cols)
        first = net.send(parts.at[1 - c, 1 - y], recv.at[1 - y], net.lower())
        project(parts, 1 - c, y, cols)
        second = net.send(parts.at[1 - c, y], recv.at[y], net.lower())
        project(parts, c, 1 - y, cols)
        project(parts, c, y, cols)
        return first, second

    sends = lows(part_two, two_low, slice(0, 2 * hidden))
    sends[0].wait_recv()
    part_two[c, 1 - y] = (part_two[c, 1 - y].astype(F32) + two_low[1 - y].astype(F32)).astype(BF16)
    two.start()
    sends[1].wait_recv()
    part_two[c, y] = (part_two[c, y].astype(F32) + two_low[y].astype(F32)).astype(BF16)
    two.middle()

    both = 4 * part
    for cols in tiles:
        left = normed_two[:, :, :, :, cols].reshape(both, tile)
        right = ffn_grads[:, :, :, : 2 * hidden].reshape(both, 2 * hidden)
        ffn_sum[cols, : 2 * hidden] = dot_tn(left, right).astype(BF16)
        left = out_grads[:, :, :, :, cols].reshape(both, tile)
        right = ffn_grads[:, :, :, 2 * hidden :].reshape(both, hidden)
        ffn_sum[cols, 2 * hidden :] = dot_tn(left, right).astype(BF16)
    ffn_net.start()
    query_net.forward()

    grad_two = two.result()
    back_two, gain_two_part = norm_grad(grad_two, middle[...], gain_two[...])
    grad_middle = out_grad[own, :].astype(F32) + back_two
    grad_attn[y, rows_of(z * chunk, chunk), :] = grad_middle.astype(BF16)
    attn_net.start()
    out_sends = lows(part_out, out_low, slice(2 * hidden, 3 * hidden))
    every = places.every((1, places.all), 1)
    own_pos = [
        places.position(places.own(late) + lax.broadcasted_iota(jnp.int32, (part, 1), 0))
        for late in range(2)
    ]
    for late in range(2):
        start = doc_starts(own_pos[late], doc_ref)
        seen = (every <= own_pos[late]) & (every >= start)
        allowed[late * part : (late + 1) * part, :] = jnp.where(seen, 0.0, MASKED)
    attn_net.forward()
    ffn_net.second()
    query_net.finish()
    order_tables(places, spread, gather, True)
    attn_net.finish()

    lane = lax.broadcasted_iota(jnp.int32, (part, LANES), 1)
    for late in range(2):
        r = slice(late * part, (late + 1) * part)
        made = dot_nn(grad_attn[late], w_out[...])
        grad_heads[r, :] = made.astype(BF16)
        all_grad[late, x, c] = grad_heads[r, :]
    grad_net.start()
    for late in range(2):
        r = slice(late * part, (late + 1) * part)
        delta = jnp.zeros((part, LANES), F32)
        for head, (tile_o, side_o) in enumerate(OUT_TILES):
            product = tile_of(grad_heads, r, tile_o).astype(F32) * tile_of(exact, r, tile_o)
            inner = jnp.sum(only(product, lane, side_o), axis=1, keepdims=True)
            delta = jnp.where(lane == head, inner, delta)
        grad_offs[r, :] = delta
    stats[x, c, :8, :] = mass[...].T[:8, :]
    stats[x, c, 8:, :] = grad_offs[...].T[:8, :]
    stat_net.start()

    for cols in tiles:
        left = grad_attn[:, :, cols].reshape(2 * part, tile)
        early_sum[cols, :] = dot_tn(left, mixed[...]).astype(BF16)
    early_net.start()
    out_sends[0].wait_recv()
    part_out[c, 1 - y] = (part_out[c, 1 - y].astype(F32) + out_low[1 - y].astype(F32)).astype(BF16)
    out.start()
    out_sends[1].wait_recv()
    part_out[c, y] = (part_out[c, y].astype(F32) + out_low[y].astype(F32)).astype(BF16)

    lane = lax.broadcasted_iota(jnp.int32, (LANES, LANES), 1)
    first = (lane // HEAD_DIM) == 0
    for block in range(2 * part // LANES):
        r = slice(block * LANES, (block + 1) * LANES)
        late = (block * LANES) // part
        many = places.all // 2 * (late + 1)
        made = []
        sums = jnp.zeros((LANES, LANES), F32)
        for head in range(3):
            tile_k, side_k = KEY_TILES[head]
            tile_v, side_v = VALUE_TILES[head]
            tile_o, side_o = OUT_TILES[head]
            keys = keyval[: late + 1, :, :, :, tile_k * LANES : (tile_k + 1) * LANES]
            values = keyval[: late + 1, :, :, :, tile_v * LANES : (tile_v + 1) * LANES]
            keys, values = keys.reshape(many, LANES), values.reshape(many, LANES)
            scores = (
                dot_nt(only(tile_of(queries, r, tile_k), lane, side_k), keys)
                - offsets[head : head + 1, :many]
                + allowed[r, :many]
            )
            probs = jnp.exp(scores - mass[r, head : head + 1])
            grad_probs = dot_nt(only(tile_of(grad_heads, r, tile_o), lane, side_o), values)
            grad_scores = (probs * (grad_probs - grad_offs[r, head : head + 1])).astype(BF16)
            made.append(dot_nn(grad_scores, keys) * HEAD_DIM ** (-0.5))
            row_sum = jnp.sum(grad_scores.astype(F32), axis=1, keepdims=True)
            sums = jnp.where(lane == head, row_sum, sums)
        grad_qkv[r, 3 * LANES : 4 * LANES] = jnp.where(first, made[0], made[1]).astype(BF16)
        grad_qkv[r, 4 * LANES :] = jnp.where(first, made[2], 0.0).astype(BF16)
        grad_offs[r, :] = sums
        if block == 0:
            grad_net.forward()
            stat_net.forward()
        if block == 1:
            out.middle()
            early_net.second()

    starts = doc_starts(every, doc_ref)
    for late in range(2):
        seen = (own_pos[late] <= every) & (own_pos[late] >= starts)
        allowed[late * part : (late + 1) * part, :] = jnp.where(seen, 0.0, MASKED)
    stat_net.finish()
    grad_net.finish()
    for late in range(2):
        for xx in range(2):
            for cc in range(2):
                at = (late * 4 + xx * 2 + cc) * part
                piece = slice(late * part, (late + 1) * part)
                every_off[0, :, at : at + part] = stats[xx, cc, :8, piece]
                every_off[1, :, at : at + part] = stats[xx, cc, 8:, piece]

    own_offs = [
        to_columns(offsets[:, pl.ds(pl.multiple_of(places.own(late), LANES), part)])
        for late in range(2)
    ]
    for block in range(2 * part // LANES):
        r = slice(block * LANES, (block + 1) * LANES)
        late = (block * LANES) // part
        within = slice(block * LANES - late * part, (block + 1) * LANES - late * part)
        many = places.all // 2 * (2 - late)
        lanes = slice(places.all - many, places.all)
        keys_made, values_made = [], []
        sums = jnp.zeros((LANES, LANES), F32)
        for head in range(3):
            tile_k, side_k = KEY_TILES[head]
            tile_v, side_v = VALUE_TILES[head]
            tile_o, side_o = OUT_TILES[head]
            asked = all_query[late:, :, :, :, tile_k * LANES : (tile_k + 1) * LANES]
            given = all_grad[late:, :, :, :, tile_o * LANES : (tile_o + 1) * LANES]
            asked, given = asked.reshape(many, LANES), given.reshape(many, LANES)
            key = keyval[late, x, c, within, tile_k * LANES : (tile_k + 1) * LANES]
            value = keyval[late, x, c, within, tile_v * LANES : (tile_v + 1) * LANES]
            scores = (
                dot_nt(only(key, lane, side_k), asked)
                - own_offs[late][within, head : head + 1]
                + allowed[r, lanes]
            )
            probs = jnp.exp(scores - every_off[0, head : head + 1, lanes])
            grad_probs = dot_nt(only(value, lane, side_v), given)
            grad_scores = (probs * (grad_probs - every_off[1, head : head + 1, lanes])).astype(
                BF16
            )
            keys_made.append(dot_nn(grad_scores, asked))
            values_made.append(dot_nn(probs.astype(BF16), given))
            col_sum = jnp.sum(grad_scores.astype(F32), axis=1, keepdims=True)
            sums = jnp.where(lane == head, col_sum, sums)
        for at, (left, right) in enumerate(
            (
                (keys_made[0], keys_made[1]),
                (keys_made[2], values_made[0]),
                (values_made[1], values_made[2]),
            )
        ):
            grad_qkv[r, at * LANES : (at + 1) * LANES] = jnp.where(first, left, right).astype(BF16)
        grad_offs[r, :] = grad_offs[r, :] - sums
        if block == 1:
            early_net.third()
    off_parts[x, c] = grad_offs[...].T[:8, :]
    off_net.start()
    cut = late_sum.shape[1]
    for cols in tiles:
        left = h_one[:, :, cols].reshape(2 * part, tile)
        late_sum[cols, :] = dot_tn(left, grad_qkv[:, :cut]).astype(BF16)
    late_net.start()
    off_net.forward()
    off_net.finish()
    for late in range(2):
        for xx in range(2):
            for cc in range(2):
                at = (late * 4 + xx * 2 + cc) * part
                every_off[0, :, at : at + part] = off_parts[
                    xx, cc, :, late * part : (late + 1) * part
                ]
    late_net.second()
    grad_logs = running_sums(places, every_off[0], spread, gather, True)
    grad_logits = grad_logs / (1.0 + jnp.exp(logits[...]))
    every_off[1] = grad_logits
    for late in range(2):
        r = slice(late * part, (late + 1) * part)
        mine = every_off[1, :, pl.ds(pl.multiple_of(places.own(late), LANES), part)]
        held = grad_qkv[r, cut:]
        lane = lax.broadcasted_iota(jnp.int32, (part, LANES), 1)
        grad_qkv[r, cut:] = jnp.where(
            lane // HEAD_DIM == 0, held, to_columns(mine, HEAD_DIM).astype(BF16)
        )

    def back(late):
        rows = rows_of(late * part, part)
        for r in tiles:
            part_one[late, :, r] = dot_nt(grad_qkv[rows, :], w_attn[r, :]).astype(BF16)

    back(1 - y)
    one.start()
    back(y)
    for cols in tiles:
        left = h_one[:, :, cols].reshape(2 * part, tile)
        last_sum[cols, :] = dot_tn(left, grad_qkv[:, cut:]).astype(BF16)
    last_net.start()
    late_net.third()
    one.middle()
    last_net.second()
    layer_out[own, :] = (middle[...] + out.result()).astype(BF16)
    layer_second = gather_quarters(net, layer_out)
    grad_one = one.result()
    back_one, gain_one_part = norm_grad(grad_one, tokens[own, :].astype(F32), gain_one[...])
    tokens_grad[own, :] = (grad_middle + back_one).astype(BF16)
    grad_second = gather_quarters(net, tokens_grad)
    row = lax.broadcasted_iota(jnp.int32, (8, width), 0)
    gain_parts[z, :, :width] = jnp.where(
        row == 0, gain_one_part, jnp.where(row == 1, gain_two_part, 0.0)
    )
    gain_parts[z, :, width:] = jnp.broadcast_to(
        jnp.sum(grad_logits, axis=1, keepdims=True), (8, LANES)
    )
    came, sent = net.alloc(4), net.alloc(4)
    for step in NEAR_FIRST:
        net.begin(
            net.copy(
                gain_parts.at[z], gain_parts.at[z], sent + step, came + z, net.to(z=net.next(step))
            )
        )
    last_net.third()
    layer_last = layer_second()
    grad_last = grad_second()

    ffn_net.finish()
    for zz in range(4):
        cols = slice(zz * hidden, (zz + 1) * hidden)
        for index, ref in enumerate((g_gate, g_up, g_down)):
            ref[:, cols] = ffn_final[zz, :, index * hidden : (index + 1) * hidden].astype(F32)
    early_net.finish()
    for u in range(2):
        cols = slice(u * half_heads, (u + 1) * half_heads)
        g_out[:, cols] = early_final[u, :, HEAD_DIM:].astype(F32)

    total = jnp.zeros((8, width), F32)
    for step in (0,) + NEAR_FIRST:
        src = net.next(step)
        if step:
            net.got(gain_parts.at[src], came + src)
        total = total + gain_parts[src, :, :width]
    for u in range(2):
        bias_grad[u] = gain_parts[2 * c + u, :, width:]
    for step, peer in enumerate((net.lower(), net.upper(), net.side())):
        gain_swap[2 * step] = total
        swap = net.send(gain_swap.at[2 * step], gain_swap.at[2 * step + 1], peer)
        swap.wait_recv()
        total = total + gain_swap[2 * step + 1]
    gains[...] = total

    late_net.finish()
    last_net.finish()
    for u in range(2):
        cols = slice(u * half_heads, (u + 1) * half_heads)
        got = late_final[u].astype(F32)
        rest = last_final[u].astype(F32)
        g_key[:, cols] = got[:, :half_heads]
        g_value[:, cols] = got[:, half_heads : 2 * half_heads]
        g_query[:, cols] = jnp.concatenate(
            [got[:, 2 * half_heads :], rest[:, :HEAD_DIM]], axis=1
        )
        g_forget[u] = rest
    layer_last()
    grad_last()
    for part_net in (late_net, last_net, early_net, net):
        part_net.drain()


VMEM = pl.BlockSpec(memory_space=pltpu.VMEM)


def shapes_of(made):
    return [jax.ShapeDtypeStruct(*m) for m in made]


def forward_shapes(rows, width, heads, hidden):
    chunk = rows // 4
    part = 4 * chunk
    every = 32 * chunk
    attn = (3 * heads * HEAD_DIM // 2) + HEAD_DIM
    outs = [
        ((2 * part, 2 * LANES), BF16),
        ((2, 2, 2, part, 3 * LANES), BF16),
        ((8, every), F32),
        ((2 * part, LANES), F32),
        ((8, every), F32),
        ((2 * part, 2 * LANES), BF16),
        ((2 * part, 2 * LANES), F32),
        ((chunk, width), F32),
        ((2, 2, 4, chunk, width), BF16),
        ((2, 2, 4, chunk, width), BF16),
        ((width, attn), BF16),
        ((width, 2 * LANES), BF16),
        ((width, 3 * hidden), BF16),
        ((2, part, width), BF16),
    ]
    scratch = [
        ((4, width // 8, 3 * hidden), BF16),
        ((2, 4, chunk, width), BF16),
        ((2 * part, every), F32),
        ((every, LANES), F32),
        ((every // chunk, every), F32),
        ((2, 2, 8, 2 * part), F32),
        ((2, 8, LANES), F32),
        ((2 * part, attn), F32),
        ((2, part, width), BF16),
        ((4, chunk, width), BF16),
        ((4, chunk, width), BF16),
    ]
    return outs, scratch


def run_forward(heads, tokens, gain_one, gain_two, stages, ffn, doc_lengths, out_grad):
    rows, width = tokens.shape
    outs, scratch = forward_shapes(rows, width, heads, ffn[0].shape[1] // 4)
    return pl.pallas_call(
        forward_kernel,
        out_shape=shapes_of(outs),
        in_specs=[VMEM] * 9 + [pl.BlockSpec(memory_space=pltpu.SMEM), VMEM],
        out_specs=[VMEM] * len(outs),
        scratch_shapes=[pltpu.VMEM(*m) for m in scratch] + [pltpu.SemaphoreType.DMA((256,))],
        compiler_params=pltpu.CompilerParams(
            collective_id=0, has_side_effects=True, vmem_limit_bytes=60 << 20
        ),
    )(tokens, gain_one, gain_two, *stages, *ffn, doc_lengths, out_grad)


def backward_shapes(rows, width, heads, hidden):
    chunk = rows // 4
    part = 4 * chunk
    every = 32 * chunk
    block = width // 8
    attn = (3 * heads * HEAD_DIM // 2) + HEAD_DIM
    head_cols = heads * HEAD_DIM
    outs = [
        ((rows, width), BF16),
        ((rows, width), BF16),
        ((8, width), F32),
        ((2, 8, LANES), F32),
        ((block, head_cols), F32),
        ((block, head_cols), F32),
        ((block, head_cols), F32),
        ((2, block, LANES), F32),
        ((block, head_cols), F32),
        ((block, 4 * hidden), F32),
        ((block, 4 * hidden), F32),
        ((block, 4 * hidden), F32),
    ]

    def weight_sum(columns):
        return [
            ((width, columns), BF16),
            ((width // 2, columns), BF16),
            ((2, block, columns), BF16),
            ((2, block, columns), BF16),
        ]

    row_sum = [((2, part, width), BF16), ((4, chunk, width), BF16), ((4, chunk, width), BF16)]
    scratch = [
        ((2, 2, 2, part, 2 * LANES), BF16),
        ((2, 2, 2, part, 2 * LANES), BF16),
        ((2 * part, every), F32),
        ((every, LANES), F32),
        ((every // chunk, every), F32),
        ((2, 2, part, 3 * hidden), BF16),
        ((2, 2, part, width), BF16),
        ((2, 2, part, width), BF16),
        *row_sum,
        *row_sum,
        ((width, 3 * hidden), BF16),
        ((4, block, 3 * hidden), BF16),
        ((4, block, 3 * hidden), BF16),
        *weight_sum(attn - LANES),
        *weight_sum(LANES),
        *weight_sum(2 * LANES),
        ((2, part, width), BF16),
        ((2 * part, 2 * LANES), BF16),
        ((2, 2, 16, 2 * part), F32),
        ((2, 2, 8, 2 * part), F32),
        ((2, 8, every), F32),
        ((2 * part, attn), BF16),
        ((2 * part, LANES), F32),
        *row_sum,
        ((4, 8, width + LANES), F32),
        ((6, 8, width), F32),
    ]
    return outs, scratch


def run_backward(heads, hidden, tokens, out_grad, gain_one, gain_two, made, doc_lengths):
    rows, width = tokens.shape
    outs, scratch = backward_shapes(rows, width, heads, hidden)
    return pl.pallas_call(
        backward_kernel,
        out_shape=shapes_of(outs),
        in_specs=[VMEM] * 18 + [pl.BlockSpec(memory_space=pltpu.SMEM)],
        out_specs=[VMEM] * len(outs),
        scratch_shapes=[pltpu.VMEM(*m) for m in scratch] + [pltpu.SemaphoreType.DMA((320,))],
        compiler_params=pltpu.CompilerParams(
            collective_id=1, has_side_effects=True, vmem_limit_bytes=63 << 20
        ),
    )(tokens, out_grad, gain_one, gain_two, *made, doc_lengths)


def kernel_body(
    tokens,
    attn_gain,
    query_weight,
    key_weight,
    value_weight,
    forget_weight,
    forget_bias,
    out_weight,
    ffn_gain,
    gate_weight,
    up_weight,
    down_weight,
    doc_lengths,
    out_grad,
):
    heads = forget_bias.shape[0]
    width = tokens.shape[1]
    hidden = gate_weight.shape[1] // 4
    half_heads = heads // 2
    cols = half_heads * HEAD_DIM
    block = query_weight.shape[0]
    out_t = out_weight.T

    def halves(weight):
        return weight.reshape(block, 2, -1).transpose(1, 0, 2)

    stage_attn = jnp.concatenate(
        [
            halves(key_weight),
            halves(value_weight),
            halves(query_weight),
            halves(forget_weight),
            jnp.zeros((2, block, HEAD_DIM - half_heads), BF16),
        ],
        axis=2,
    )
    stage_out = jnp.pad(halves(out_t), ((0, 0), (0, 0), (2 * LANES - cols, 0)))
    stage_bias = jnp.broadcast_to(
        jnp.pad(forget_bias.reshape(2, half_heads), ((0, 0), (0, 8 - half_heads)))[:, :, None],
        (2, 8, LANES),
    )
    gain_one = attn_gain.reshape(1, width)
    gain_two = ffn_gain.reshape(1, width)
    made = run_forward(
        heads,
        tokens,
        gain_one,
        gain_two,
        (stage_attn, stage_out, stage_bias),
        (gate_weight, up_weight, down_weight.T),
        doc_lengths,
        out_grad,
    )
    (
        layer_out,
        tokens_grad,
        gains,
        bias_grad,
        g_query,
        g_key,
        g_value,
        g_forget,
        g_out,
        g_gate,
        g_up,
        g_down,
    ) = run_backward(heads, hidden, tokens, out_grad, gain_one, gain_two, made, doc_lengths)
    return (
        layer_out,
        tokens_grad,
        gains[0],
        g_query,
        g_key,
        g_value,
        g_forget[:, :, HEAD_DIM : HEAD_DIM + half_heads].transpose(1, 0, 2).reshape(block, heads),
        bias_grad[:, :half_heads, 0].reshape(heads),
        g_out.T,
        gains[1],
        g_gate,
        g_up,
        g_down.T,
    )


def kernels_fit(tokens, forget_bias, gate_weight):
    rows, width = tokens.shape
    heads = forget_bias.shape[0]
    return (
        lax.axis_size("seq") == 8
        and lax.axis_size("head") == 4
        and heads == 6
        and rows == 2 * LANES
        and width % 256 == 0
        and gate_weight.shape[1] % (4 * LANES) == 0
        and width * gate_weight.shape[1] <= (1536 * 1024)
    )


def unchanged(carried):
    return carried


def contract_rows(left, right):
    return lax.dot_general(
        left, right, (((0,), (0,)), ((), ())), preferred_element_type=jnp.float32
    )


def contract_cols(left, right):
    return lax.dot_general(
        left, right, (((1,), (1,)), ((), ())), preferred_element_type=jnp.float32
    )


def norm_rows(values_in, gain):
    inverse = lax.rsqrt(jnp.mean(values_in * values_in, axis=-1, keepdims=True) + EPSILON)
    normed = values_in * inverse
    return (normed, inverse, normed * gain)


def norm_back(grad_in, normed, inverse, gain):
    scaled = grad_in * gain
    inner = jnp.mean(scaled * normed, axis=-1, keepdims=True)
    return (inverse * (scaled - normed * inner), jnp.sum(grad_in * normed, axis=0))


def doc_index(positions, doc_ends):
    return jnp.sum((positions[:, None] >= doc_ends[None, :]).astype(jnp.int32), axis=1)


def stored_positions(rows, n_seq, local_rows):
    half_rows = local_rows // 2
    device_of = rows // local_rows
    within = rows % local_rows
    group_of = jnp.where(within < half_rows, device_of, 2 * n_seq - 1 - device_of)
    return group_of * half_rows + within % half_rows


def block_scores(
    query_heads, key_heads, query_offsets, key_offsets, query_pos, key_pos, query_docs, key_docs
):
    raw_scores = jnp.einsum(
        "qhd,khd->hqk", query_heads, key_heads, preferred_element_type=jnp.float32
    )
    scores = (
        raw_scores * HEAD_DIM ** (-0.5) + query_offsets.T[:, :, None] - key_offsets.T[:, None, :]
    )
    allowed = (query_docs[:, None] == key_docs[None, :]) & (key_pos[None, :] <= query_pos[:, None])
    return (jnp.where(allowed[None], scores, MASKED), allowed)


def piece_grads(
    query_heads,
    grad_heads,
    log_mass,
    row_delta,
    query_offsets,
    key_heads,
    value_heads,
    key_offsets,
    query_pos,
    key_pos,
    query_docs,
    key_docs,
):
    scores, allowed = block_scores(
        query_heads, key_heads, query_offsets, key_offsets, query_pos, key_pos, query_docs, key_docs
    )
    probs = jnp.where(allowed[None], jnp.exp(scores - log_mass[:, :, None]), 0.0)
    grad_probs = jnp.einsum(
        "qhd,khd->hqk", grad_heads, value_heads, preferred_element_type=jnp.float32
    )
    grad_scores = (probs * (grad_probs - row_delta[:, :, None])).astype(jnp.bfloat16)
    score_sums = grad_scores.astype(jnp.float32)
    query_rows = query_heads.shape[0]
    key_rows = key_heads.shape[0]
    grad_query = jnp.einsum(
        "hqk,khd->qhd", grad_scores, key_heads, preferred_element_type=jnp.float32
    ).reshape(query_rows, -1)
    grad_key = (
        jnp.einsum("hqk,qhd->khd", grad_scores, query_heads, preferred_element_type=jnp.float32)
        * HEAD_DIM ** (-0.5)
    ).reshape(key_rows, -1)
    grad_value = jnp.einsum(
        "hqk,qhd->khd", probs.astype(jnp.bfloat16), grad_heads, preferred_element_type=jnp.float32
    ).reshape(key_rows, -1)
    return (
        grad_query,
        jnp.sum(score_sums, axis=2).T,
        grad_key,
        grad_value,
        -jnp.sum(score_sums, axis=1).T,
    )


def plain_body(
    tokens,
    attn_gain,
    query_weight,
    key_weight,
    value_weight,
    forget_weight,
    forget_bias,
    out_weight,
    ffn_gain,
    gate_weight,
    up_weight,
    down_weight,
    doc_lengths,
    out_grad,
):
    local_rows = tokens.shape[0]
    local_heads = forget_bias.shape[0]
    head_cols = local_heads * HEAD_DIM
    n_seq = lax.axis_size("seq")
    my_index = lax.axis_index("seq")
    first_row = my_index * local_rows
    docs = doc_lengths.shape[0]
    doc_ends = jnp.sum(jnp.where(jnp.tri(docs, dtype=jnp.bool_), doc_lengths[None, :], 0), axis=1)
    local_pos = stored_positions(
        first_row + jnp.arange(local_rows, dtype=jnp.int32), n_seq, local_rows
    )
    local_docs = doc_index(local_pos, doc_ends)
    pos_low = jnp.min(local_pos)
    pos_high = jnp.max(local_pos)
    doc_low = jnp.min(local_docs)
    doc_high = jnp.max(local_docs)
    hidden = gate_weight.shape[1]
    forget_pad = jnp.pad(forget_weight, ((0, 0), (0, 128 - local_heads)))
    w_attn = lax.all_gather(
        jnp.concatenate([query_weight, key_weight, value_weight, forget_pad], axis=1),
        "seq",
        axis=0,
        tiled=True,
    )
    w_rest = lax.all_gather(
        jnp.concatenate([out_weight.T, gate_weight, up_weight, down_weight.T], axis=1),
        "seq",
        axis=0,
        tiled=True,
    )
    w_query = w_attn[:, :head_cols]
    w_key = w_attn[:, head_cols : 2 * head_cols]
    w_value = w_attn[:, 2 * head_cols : 3 * head_cols]
    w_forget = w_attn[:, 3 * head_cols : 3 * head_cols + local_heads]
    w_out_t = w_rest[:, :head_cols]
    w_gate = w_rest[:, head_cols : head_cols + hidden]
    w_up = w_rest[:, head_cols + hidden : head_cols + 2 * hidden]
    w_down_t = w_rest[:, head_cols + 2 * hidden :]
    inputs = tokens.astype(jnp.float32)
    normed_one, inverse_one, scaled_one = norm_rows(inputs, attn_gain)
    h_one = scaled_one.astype(jnp.bfloat16)
    query_flat = jnp.dot(h_one, w_query, preferred_element_type=jnp.float32).astype(jnp.bfloat16)
    key_flat = jnp.dot(h_one, w_key, preferred_element_type=jnp.float32).astype(jnp.bfloat16)
    value_flat = jnp.dot(h_one, w_value, preferred_element_type=jnp.float32).astype(jnp.bfloat16)
    forget_logit = jnp.dot(h_one, w_forget, preferred_element_type=jnp.float32) + forget_bias
    log_forget_all = lax.all_gather(jax.nn.log_sigmoid(forget_logit), "seq", axis=0, tiled=True)
    all_pos = stored_positions(
        jnp.arange(n_seq * local_rows, dtype=jnp.int32), n_seq, local_rows
    )
    earlier = (all_pos[None, :] <= all_pos[:, None]).astype(jnp.float32)
    offsets_all = jnp.dot(earlier, log_forget_all, precision=HIGHEST)
    offsets = lax.dynamic_slice_in_dim(offsets_all, first_row, local_rows, 0)
    query_heads = query_flat.reshape(local_rows, local_heads, HEAD_DIM)
    key_heads = key_flat.reshape(local_rows, local_heads, HEAD_DIM)
    value_heads = value_flat.reshape(local_rows, local_heads, HEAD_DIM)

    def key_range(piece_rows):
        key_pos = stored_positions(jnp.arange(piece_rows, dtype=jnp.int32), n_seq, local_rows)
        key_docs = doc_index(key_pos, doc_ends)
        is_live = (
            (jnp.min(key_pos) <= pos_high)
            & (jnp.max(key_docs) >= doc_low)
            & (jnp.min(key_docs) <= doc_high)
        )
        return (key_pos, key_docs, offsets_all, is_live)

    mass_state = (
        jnp.full((local_heads, local_rows), MASKED, jnp.float32),
        jnp.zeros((local_heads, local_rows), jnp.float32),
    )
    gathered = lax.all_gather(
        jnp.concatenate([key_flat, value_flat, query_flat], axis=1), "seq", axis=0, tiled=True
    )
    key_block = gathered[:, :head_cols]
    piece_rows = key_block.shape[0]
    key_pos, key_docs, key_offsets, is_live = key_range(piece_rows)

    def mass_update(carried_in):
        running_max, running_sum = carried_in
        scores, allowed = block_scores(
            query_heads,
            key_block.reshape(piece_rows, local_heads, HEAD_DIM),
            offsets,
            key_offsets,
            local_pos,
            key_pos,
            local_docs,
            key_docs,
        )
        new_max = jnp.maximum(running_max, jnp.max(scores, axis=2))
        weights = jnp.where(allowed[None], jnp.exp(scores - new_max[:, :, None]), 0.0)
        return (new_max, jnp.sum(weights, axis=2))

    running_max, running_sum = lax.cond(is_live, mass_update, unchanged, mass_state)
    log_mass = running_max + jnp.log(running_sum)
    start_state = (
        jnp.zeros((local_heads, local_rows, HEAD_DIM), jnp.float32),
        jnp.zeros((local_heads, local_rows, HEAD_DIM), jnp.float32),
    )
    attend_key_block = key_block
    value_block = gathered[:, head_cols : 2 * head_cols]
    attend_piece_rows = attend_key_block.shape[0]
    attend_key_pos, attend_key_docs, attend_key_offsets, is_live = key_range(attend_piece_rows)

    def attend_update(carried_in):
        scores, allowed = block_scores(
            query_heads,
            attend_key_block.reshape(attend_piece_rows, local_heads, HEAD_DIM),
            offsets,
            attend_key_offsets,
            local_pos,
            attend_key_pos,
            local_docs,
            attend_key_docs,
        )
        probs = jnp.where(allowed[None], jnp.exp(scores - log_mass[:, :, None]), 0.0)
        probs_low = probs.astype(jnp.bfloat16)
        remainder = (probs - probs_low.astype(jnp.float32)).astype(jnp.bfloat16)
        value_piece = value_block.reshape(attend_piece_rows, local_heads, HEAD_DIM)
        rounded_acc = jnp.einsum(
            "hqk,khd->hqd", probs_low, value_piece, preferred_element_type=jnp.float32
        )
        remainder_acc = jnp.einsum(
            "hqk,khd->hqd", remainder, value_piece, preferred_element_type=jnp.float32
        )
        return (rounded_acc, remainder_acc)

    rounded_acc, remainder_acc = lax.cond(is_live, attend_update, unchanged, start_state)
    attended_rows = rounded_acc.transpose(1, 0, 2)
    exact_rows = (rounded_acc + remainder_acc).transpose(1, 0, 2)
    mixed = attended_rows.reshape(local_rows, head_cols).astype(jnp.bfloat16)
    attn_part = contract_cols(mixed, w_out_t)
    middle = inputs + lax.psum(attn_part, "head")
    normed_two, inverse_two, scaled_two = norm_rows(middle, ffn_gain)
    h_two = scaled_two.astype(jnp.bfloat16)
    gate_value = jnp.dot(h_two, w_gate, preferred_element_type=jnp.float32)
    up_value = jnp.dot(h_two, w_up, preferred_element_type=jnp.float32)
    gate_sigmoid = jax.nn.sigmoid(gate_value)
    gate_silu = gate_value * gate_sigmoid
    activation = (gate_silu * up_value).astype(jnp.bfloat16)
    ffn_part = contract_cols(activation, w_down_t)
    layer_out = (
        middle + lax.psum(ffn_part.astype(jnp.bfloat16), "head").astype(jnp.float32)
    ).astype(jnp.bfloat16)
    grad_act = jnp.dot(out_grad, w_down_t, preferred_element_type=jnp.float32)
    grad_gate = (
        grad_act * up_value * gate_sigmoid * (1.0 + gate_value * (1.0 - gate_sigmoid))
    ).astype(jnp.bfloat16)
    grad_up = (grad_act * gate_silu).astype(jnp.bfloat16)
    part_two = contract_cols(grad_gate, w_gate) + contract_cols(grad_up, w_up)
    grad_two = lax.psum(part_two, "head")
    back_two, gain_two = norm_back(grad_two, normed_two, inverse_two, ffn_gain)
    grad_middle = out_grad.astype(jnp.float32) + back_two
    grad_attn = grad_middle.astype(jnp.bfloat16)
    grad_mixed = jnp.dot(grad_attn, w_out_t, preferred_element_type=jnp.float32).astype(
        jnp.bfloat16
    )
    grad_heads = grad_mixed.reshape(local_rows, local_heads, HEAD_DIM)
    row_delta = jnp.sum(grad_heads.astype(jnp.float32) * exact_rows, axis=2).T
    back_state = (
        jnp.zeros((local_rows, head_cols), jnp.float32),
        jnp.zeros((local_rows, local_heads), jnp.float32),
    )
    back_key_block = key_block
    back_value_block = value_block
    back_piece_rows = back_key_block.shape[0]
    back_key_pos, back_key_docs, back_key_offsets, is_live = key_range(back_piece_rows)

    def back_update(carried_in):
        terms = piece_grads(
            query_heads,
            grad_heads,
            log_mass,
            row_delta,
            offsets,
            back_key_block.reshape(back_piece_rows, local_heads, HEAD_DIM),
            back_value_block.reshape(back_piece_rows, local_heads, HEAD_DIM),
            back_key_offsets,
            local_pos,
            back_key_pos,
            local_docs,
            back_key_docs,
        )
        return (terms[0], terms[1])

    grad_query, grad_query_off = lax.cond(is_live, back_update, unchanged, back_state)
    stats = lax.all_gather(
        jnp.concatenate([log_mass.T, row_delta.T], axis=1), "seq", axis=0, tiled=True
    )
    stats_mass, stats_delta = stats[:, :local_heads], stats[:, local_heads:]
    key_state = (
        jnp.zeros((local_rows, head_cols), jnp.float32),
        jnp.zeros((local_rows, head_cols), jnp.float32),
        jnp.zeros((local_rows, local_heads), jnp.float32),
    )
    piece_query = gathered[:, 2 * head_cols :]
    piece_grad = lax.all_gather(grad_mixed, "seq", axis=0, tiled=True)
    key_piece_rows = piece_query.shape[0]
    piece_pos = stored_positions(jnp.arange(key_piece_rows, dtype=jnp.int32), n_seq, local_rows)
    piece_docs = doc_index(piece_pos, doc_ends)
    is_live = (
        (pos_low <= jnp.max(piece_pos))
        & (jnp.max(piece_docs) >= doc_low)
        & (jnp.min(piece_docs) <= doc_high)
    )

    def key_update(carried_in):
        piece_mass = stats_mass.T
        piece_delta = stats_delta.T
        terms = piece_grads(
            piece_query.reshape(key_piece_rows, local_heads, HEAD_DIM),
            piece_grad.reshape(key_piece_rows, local_heads, HEAD_DIM),
            piece_mass,
            piece_delta,
            offsets_all,
            key_heads,
            value_heads,
            offsets,
            piece_pos,
            local_pos,
            piece_docs,
            local_docs,
        )
        return (terms[2], terms[3], terms[4])

    grad_key, grad_value, grad_key_off = lax.cond(is_live, key_update, unchanged, key_state)
    grad_query_low = (grad_query * HEAD_DIM ** (-0.5)).astype(jnp.bfloat16)
    grad_key_low = grad_key.astype(jnp.bfloat16)
    grad_value_low = grad_value.astype(jnp.bfloat16)
    grad_offsets = grad_query_off + grad_key_off
    grad_off_all = lax.all_gather(grad_offsets, "seq", axis=0, tiled=True)
    later = (all_pos[None, :] >= local_pos[:, None]).astype(jnp.float32)
    grad_log = jnp.dot(later, grad_off_all, precision=HIGHEST)
    grad_logit = grad_log * jax.nn.sigmoid(-forget_logit)
    forget_table = w_forget.astype(jnp.float32)
    part_one = (
        contract_cols(grad_query_low, w_query)
        + contract_cols(grad_key_low, w_key)
        + contract_cols(grad_value_low, w_value)
        + lax.dot_general(grad_logit, forget_table, (((1,), (1,)), ((), ())), precision=HIGHEST)
    )
    grad_one = lax.psum(part_one.astype(jnp.bfloat16), "head").astype(jnp.float32)
    back_one, gain_one = norm_back(grad_one, normed_one, inverse_one, attn_gain)
    tokens_grad = (grad_middle + back_one).astype(jnp.bfloat16)
    forget_term = lax.dot_general(
        h_one.astype(jnp.float32), grad_logit, (((0,), (0,)), ((), ())), precision=HIGHEST
    )
    scatter_cols = [
        contract_rows(grad_attn, mixed),
        contract_rows(h_two, grad_gate),
        contract_rows(h_two, grad_up),
        contract_rows(out_grad, activation),
        contract_rows(h_one, grad_query_low),
        contract_rows(h_one, grad_key_low),
        contract_rows(h_one, grad_value_low),
        jnp.pad(forget_term, ((0, 0), (0, 128 - local_heads))),
    ]
    first_sum = lax.psum_scatter(
        jnp.concatenate([t.astype(jnp.bfloat16) for t in scatter_cols[:4]], axis=1),
        "seq",
        scatter_dimension=0,
        tiled=True,
    ).astype(jnp.float32)
    second_sum = lax.psum_scatter(
        jnp.concatenate([t.astype(jnp.bfloat16) for t in scatter_cols[4:]], axis=1),
        "seq",
        scatter_dimension=0,
        tiled=True,
    ).astype(jnp.float32)
    out_weight_grad = first_sum[:, :head_cols].T
    gate_weight_grad = first_sum[:, head_cols : head_cols + hidden]
    up_weight_grad = first_sum[:, head_cols + hidden : head_cols + 2 * hidden]
    down_weight_grad = first_sum[:, head_cols + 2 * hidden :].T
    query_weight_grad = second_sum[:, :head_cols]
    key_weight_grad = second_sum[:, head_cols : 2 * head_cols]
    value_weight_grad = second_sum[:, 2 * head_cols : 3 * head_cols]
    forget_weight_grad = second_sum[:, 3 * head_cols : 3 * head_cols + local_heads]
    attn_gain_grad, ffn_gain_grad, forget_bias_grad = lax.psum(
        (gain_one, gain_two, jnp.sum(grad_logit, axis=0)), "seq"
    )
    return (
        layer_out,
        tokens_grad,
        attn_gain_grad,
        query_weight_grad,
        key_weight_grad,
        value_weight_grad,
        forget_weight_grad,
        forget_bias_grad,
        out_weight_grad,
        ffn_gain_grad,
        gate_weight_grad,
        up_weight_grad,
        down_weight_grad,
    )


def body(*args):
    fits = kernels_fit(args[0], args[6], args[9])
    return (kernel_body if fits else plain_body)(*args)


def solution(mesh):
    return jax.shard_map(
        body,
        mesh=mesh,
        in_specs=(
            P("seq", None),
            P(),
            P("seq", "head"),
            P("seq", "head"),
            P("seq", "head"),
            P("seq", "head"),
            P("head"),
            P("head", "seq"),
            P(),
            P("seq", "head"),
            P("seq", "head"),
            P("head", "seq"),
            P(),
            P("seq", None),
        ),
        out_specs=(
            P("seq", None),
            P("seq", None),
            P(),
            P("seq", "head"),
            P("seq", "head"),
            P("seq", "head"),
            P("seq", "head"),
            P("head"),
            P("head", "seq"),
            P(),
            P("seq", "head"),
            P("seq", "head"),
            P("head", "seq"),
        ),
        check_vma=False,
    )
```

```python
import jax
import jax.numpy as jnp
from jax import lax
from jax.experimental import pallas as pl
from jax.experimental.pallas import tpu as pltpu
from jax.sharding import PartitionSpec as P

HEAD_DIM = 64
EPSILON = 1e-06
HIGHEST = lax.Precision.HIGHEST
MASKED = -1e30
MESH_ID = pl.DeviceIdType.MESH
F32 = jnp.float32
BF16 = jnp.bfloat16
LANES = 128
KEY_TILES = ((0, 0), (0, 1), (1, 0))
VALUE_TILES = ((1, 1), (2, 0), (2, 1))
OUT_TILES = ((0, 1), (1, 0), (1, 1))
NEAR_FIRST = (1, 3, 2)


def dot_nn(left, right):
    return jnp.dot(left, right, preferred_element_type=F32)


def dot_nt(left, right):
    return lax.dot_general(left, right, (((1,), (1,)), ((), ())), preferred_element_type=F32)


def dot_tn(left, right):
    return lax.dot_general(left, right, (((0,), (0,)), ((), ())), preferred_element_type=F32)


def rows_of(first, count):
    return pl.ds(pl.multiple_of(first, 16), count)


def add_to(ref, other):
    ref[...] = (ref[...].astype(F32) + other[...].astype(F32)).astype(BF16)


class Net:
    def __init__(self, sems):
        s = lax.axis_index("seq")
        h = lax.axis_index("head")
        self.line = 4
        self.z, self.x = s // 2, s % 2
        self.y, self.c = h // 2, h % 2
        self.sems = sems
        self.used = 0
        self.pending = []

    def alloc(self, count):
        first = self.used
        self.used += count
        return first

    def to(self, z=None, x=None, y=None, c=None):
        z = self.z if z is None else z
        x = self.x if x is None else x
        y = self.y if y is None else y
        c = self.c if c is None else c
        return (z * 2 + x, y * 2 + c)

    def side(self):
        return self.to(x=1 - self.x)

    def lower(self):
        return self.to(c=1 - self.c)

    def upper(self):
        return self.to(y=1 - self.y)

    def next(self, step):
        return (self.z + step) % self.line

    def barrier(self):
        sem = pltpu.get_barrier_semaphore()
        peers = [self.side(), self.lower(), self.upper(), self.to(x=1 - self.x, c=1 - self.c)]
        for step in range(1, self.line):
            peers.append(self.to(z=self.next(step)))
            peers.append(self.to(z=self.next(step), c=1 - self.c))
        for peer in peers:
            pl.semaphore_signal(sem, 1, device_id=peer, device_id_type=MESH_ID)
        pl.semaphore_wait(sem, len(peers))

    def copy(self, src, dst, send, recv, device):
        return pltpu.make_async_remote_copy(
            src_ref=src,
            dst_ref=dst,
            send_sem=self.sems.at[send],
            recv_sem=self.sems.at[recv],
            device_id=device,
            device_id_type=MESH_ID,
        )

    def begin(self, made):
        made.start()
        self.pending.append(made.wait_send)
        return made

    def send(self, src, dst, device):
        first = self.alloc(2)
        return self.begin(self.copy(src, dst, first, first + 1, device))

    def got(self, ref, recv):
        self.copy(ref, ref, recv, recv, self.side()).wait_recv()

    def drain(self):
        for wait in self.pending:
            wait()
        self.pending = []


class RowGather:
    def __init__(self, net, slot, lower=None):
        self.net = net
        self.slot = slot
        self.low = lower
        self.sent = net.alloc(4)
        self.came = net.alloc(4)
        self.up_sent = net.alloc(4)
        self.up_came = net.alloc(4)
        self.low_sent = net.alloc(8)
        self.low_came = net.alloc(8)

    def pass_low(self, y, z):
        if self.low is not None:
            net = self.net
            index = y * 4 + z
            block = self.slot(y, z)
            net.begin(
                net.copy(
                    block, block, self.low_sent + index, self.low_came + index, net.lower()
                )
            )

    def pass_up(self, z):
        net = self.net
        block = self.slot(net.y, z)
        net.begin(net.copy(block, block, self.up_sent + z, self.up_came + z, net.upper()))
        self.pass_low(net.y, z)

    def start(self):
        net = self.net
        mine = self.slot(net.y, net.z)
        for step in NEAR_FIRST:
            net.begin(
                net.copy(
                    mine, mine, self.sent + step, self.came + net.z, net.to(z=net.next(step))
                )
            )
        self.pass_up(net.z)

    def forward(self):
        net = self.net
        for step in NEAR_FIRST:
            src = net.next(step)
            net.got(self.slot(net.y, src), self.came + src)
            self.pass_up(src)

    def finish(self):
        net = self.net
        for step in (0,) + NEAR_FIRST:
            src = net.next(step)
            net.got(self.slot(1 - net.y, src), self.up_came + src)
            self.pass_low(1 - net.y, src)
        if self.low is not None:
            for y in range(2):
                for z in range(4):
                    net.got(self.low(y, z), self.low_came + y * 4 + z)


class RowSum:
    def __init__(self, net, slot, recv_up, recv_line):
        self.net = net
        self.slot = slot
        self.recv_up = recv_up
        self.recv_line = recv_line
        self.up_sent = net.alloc(4)
        self.up_came = net.alloc(4)
        self.sent = net.alloc(4)
        self.came = net.alloc(4)

    def start(self):
        net = self.net
        for step in (2, 1, 3, 0):
            z = net.next(step)
            net.begin(
                net.copy(
                    self.slot(1 - net.y, z),
                    self.recv_up.at[z],
                    self.up_sent + z,
                    self.up_came + z,
                    net.upper(),
                )
            )

    def middle(self):
        net = self.net
        for step in (2, 1, 3, 0):
            z = net.next(step)
            net.got(self.recv_up.at[z], self.up_came + z)
            mine = self.slot(net.y, z)
            add_to(mine, self.recv_up.at[z])
            if step:
                net.begin(
                    net.copy(
                        mine,
                        self.recv_line.at[net.z],
                        self.sent + step,
                        self.came + net.z,
                        net.to(z=z),
                    )
                )

    def result(self):
        net = self.net
        total = self.slot(net.y, net.z)[...].astype(F32)
        for step in NEAR_FIRST:
            src = net.next(step)
            net.got(self.recv_line.at[src], self.came + src)
            total = total + self.recv_line[src].astype(F32)
        return total


class CrossGather:
    def __init__(self, net, slot):
        self.net = net
        self.slot = slot

    def start(self):
        net = self.net
        mine = self.slot(net.x, net.c)
        self.across = net.send(mine, mine, net.side())
        self.low = net.send(mine, mine, net.lower())

    def forward(self):
        net = self.net
        self.across.wait_recv()
        other = self.slot(1 - net.x, net.c)
        self.both = net.send(other, other, net.lower())

    def finish(self):
        self.low.wait_recv()
        self.both.wait_recv()


class WeightSpread:
    def __init__(self, net, stage, full):
        self.net = net
        self.stage = stage
        self.full = full
        self.block = stage.shape[1]
        self.sent = net.alloc(2)
        self.came = net.alloc(4)
        self.side_sent = net.alloc(4)
        self.side_came = net.alloc(4)
        self.low_sent = net.alloc(8)
        self.low_came = net.alloc(8)
        self.first = (net.z // 2) == net.c

    def slot(self, z, x):
        return self.full.at[rows_of((z * 2 + x) * self.block, self.block), :]

    def away(self, u):
        net = self.net
        return net.copy(
            self.stage.at[u],
            self.slot(net.z, net.x),
            self.sent + u,
            self.came + net.z,
            net.to(z=2 * net.c + u),
        )

    def across(self, z):
        net = self.net
        block = self.slot(z, net.x)
        return net.copy(block, block, self.side_sent + z, self.side_came + z, net.side())

    def low(self, z, x):
        block = self.slot(z, x)
        index = z * 2 + x
        return self.net.copy(
            block, block, self.low_sent + index, self.low_came + index, self.net.lower()
        )

    def start(self):
        net = self.net
        for u in range(2):
            pl.when(2 * net.c + u != net.z)(lambda u=u: self.away(u).start())

        @pl.when(self.first)
        def _():
            self.slot(net.z, net.x)[...] = self.stage[net.z % 2]
            self.across(net.z).start()
            self.low(net.z, net.x).start()

    def forward(self):
        net = self.net

        @pl.when(self.first)
        def _():
            for step in NEAR_FIRST:
                src = net.next(step)
                net.got(self.slot(src, net.x), self.came + src)
                self.across(src).start()
                self.low(src, net.x).start()

    def finish(self):
        net = self.net

        @pl.when(self.first)
        def _():
            for step in (0,) + NEAR_FIRST:
                src = net.next(step)
                net.got(self.slot(src, 1 - net.x), self.side_came + src)
                self.low(src, 1 - net.x).start()

        @pl.when(jnp.logical_not(self.first))
        def _():
            for z in range(4):
                for x in range(2):
                    net.got(self.slot(z, x), self.low_came + z * 2 + x)

    def drain(self):
        net = self.net
        for u in range(2):
            pl.when(2 * net.c + u != net.z)(lambda u=u: self.away(u).wait_send())

        @pl.when(self.first)
        def _():
            for z in range(4):
                self.across(z).wait_send()
                for x in range(2):
                    self.low(z, x).wait_send()


class HiddenSpread:
    def __init__(self, net, stage, full):
        self.net = net
        self.stage = stage
        self.full = full
        self.block = stage.shape[1]
        self.sent = net.alloc(4)
        self.came = net.alloc(4)
        self.side_sent = net.alloc(4)
        self.side_came = net.alloc(4)

    def slot(self, z, x):
        return self.full.at[rows_of((z * 2 + x) * self.block, self.block), :]

    def across(self, z):
        net = self.net
        block = self.slot(z, net.x)
        net.begin(net.copy(block, block, self.side_sent + z, self.side_came + z, net.side()))

    def start(self):
        net = self.net
        self.slot(net.z, net.x)[...] = self.stage[net.z]
        for step in NEAR_FIRST:
            to = net.next(step)
            net.begin(
                net.copy(
                    self.stage.at[to],
                    self.slot(net.z, net.x),
                    self.sent + step,
                    self.came + net.z,
                    net.to(z=to),
                )
            )
        self.across(net.z)

    def forward(self):
        net = self.net
        for step in NEAR_FIRST:
            src = net.next(step)
            net.got(self.slot(src, net.x), self.came + src)
            self.across(src)

    def finish(self):
        net = self.net
        for z in range(4):
            net.got(self.slot(z, 1 - net.x), self.side_came + z)


class WeightSum:
    def __init__(self, net, grads, recv_low, recv_side, final):
        self.net = net
        self.grads = grads
        self.recv_low = recv_low
        self.recv_side = recv_side
        self.final = final
        self.block = final.shape[1]
        self.side_sent = net.alloc(2)
        self.side_came = net.alloc(2)
        self.sent = net.alloc(2)
        self.came = net.alloc(2)

    def rows(self, z, x):
        return self.grads.at[rows_of((z * 2 + x) * self.block, self.block), :]

    def start(self):
        net = self.net
        half = 4 * self.block
        self.low = net.send(
            self.grads.at[rows_of((1 - net.c) * half, half), :], self.recv_low, net.lower()
        )

    def second(self):
        net = self.net
        self.low.wait_recv()
        for x in (1 - net.x, net.x):
            for i in range(2):
                z = 2 * net.c + i
                add_to(
                    self.rows(z, x), self.recv_low.at[rows_of((i * 2 + x) * self.block, self.block)]
                )
        for i in range(2):
            net.begin(
                net.copy(
                    self.rows(2 * net.c + i, 1 - net.x),
                    self.recv_side.at[i],
                    self.side_sent + i,
                    self.side_came + i,
                    net.side(),
                )
            )

    def owner(self, i):
        net = self.net
        z = 2 * net.c + i
        made = net.copy(
            self.rows(z, net.x),
            self.final.at[net.z % 2],
            self.sent + i,
            self.came + net.z % 2,
            net.to(z=z, c=net.z // 2),
        )
        return (z == net.z) & (net.z // 2 == net.c), made

    def third(self):
        net = self.net
        for i in range(2):
            net.got(self.recv_side.at[i], self.side_came + i)
            mine = self.rows(2 * net.c + i, net.x)
            add_to(mine, self.recv_side.at[i])
            local, made = self.owner(i)

            @pl.when(local)
            def _():
                self.final[net.z % 2] = mine[...]

            pl.when(jnp.logical_not(local))(made.start)

    def finish(self):
        net = self.net
        for u in range(2):
            pl.when(2 * net.c + u != net.z)(
                lambda u=u: net.got(self.final.at[u], self.came + u)
            )

    def drain(self):
        for i in range(2):
            local, made = self.owner(i)
            pl.when(jnp.logical_not(local))(made.wait_send)


class HiddenSum:
    def __init__(self, net, grads, recv_side, final):
        self.net = net
        self.grads = grads
        self.recv_side = recv_side
        self.final = final
        self.block = final.shape[1]
        self.side_sent = net.alloc(4)
        self.side_came = net.alloc(4)
        self.sent = net.alloc(4)
        self.came = net.alloc(4)

    def rows(self, z, x):
        return self.grads.at[rows_of((z * 2 + x) * self.block, self.block), :]

    def start(self):
        net = self.net
        for step in (2, 1, 3, 0):
            z = net.next(step)
            net.begin(
                net.copy(
                    self.rows(z, 1 - net.x),
                    self.recv_side.at[z],
                    self.side_sent + z,
                    self.side_came + z,
                    net.side(),
                )
            )

    def second(self):
        net = self.net
        for step in (2, 1, 3, 0):
            z = net.next(step)
            net.got(self.recv_side.at[z], self.side_came + z)
            mine = self.rows(z, net.x)
            add_to(mine, self.recv_side.at[z])
            if step:
                net.begin(
                    net.copy(
                        mine,
                        self.final.at[net.z],
                        self.sent + step,
                        self.came + net.z,
                        net.to(z=z),
                    )
                )
            else:
                self.final[net.z] = mine[...]

    def finish(self):
        net = self.net
        for step in NEAR_FIRST:
            src = net.next(step)
            net.got(self.final.at[src], self.came + src)


class Places:
    def __init__(self, net, chunk):
        self.net = net
        self.chunk = chunk
        self.part = 4 * chunk
        self.all = 32 * chunk

    def position(self, at):
        chunk = self.chunk
        late = at // (16 * chunk)
        x = (at // (8 * chunk)) % 2
        c = (at // (4 * chunk)) % 2
        z = (at // chunk) % 4
        owner = 2 * z + x
        group = jnp.where(late == 0, owner, 15 - owner)
        return group * (2 * chunk) + c * chunk + at % chunk

    def own(self, late):
        return (late * 4 + self.net.x * 2 + self.net.c) * self.part

    def every(self, shape, axis):
        return self.position(lax.broadcasted_iota(jnp.int32, shape, axis))


def doc_starts(positions, doc_ref):
    start = jnp.zeros(positions.shape, jnp.int32)
    end = jnp.int32(0)
    for k in range(doc_ref.shape[0] - 1):
        end = end + doc_ref[k]
        start = jnp.where(positions >= end, end, start)
    return start


def running_sums(places, rows_in, spread, gather, backward):
    tiles = places.all // LANES
    chunk = places.chunk
    row = lax.broadcasted_iota(jnp.int32, (LANES, LANES), 0)
    col = lax.broadcasted_iota(jnp.int32, (LANES, LANES), 1)
    reach = row >= col if backward else row <= col
    within = ((row // chunk == col // chunk) & reach).astype(F32)
    stacked = jnp.concatenate(
        [rows_in[:, k * LANES : (k + 1) * LANES] for k in range(tiles)], axis=0
    )
    inside = jnp.dot(stacked, within, precision=HIGHEST, preferred_element_type=F32)
    outside = jnp.dot(rows_in, spread[...], precision=HIGHEST, preferred_element_type=F32)
    outside = outside[:, : gather.shape[0]]
    outside = jnp.dot(outside, gather[...], precision=HIGHEST, preferred_element_type=F32)
    return outside + jnp.concatenate(
        [inside[k * 8 : (k + 1) * 8, :] for k in range(tiles)], axis=1
    )


def order_tables(places, spread, gather, backward):
    order = places.every((places.all, LANES), 0) // places.chunk
    slot = lax.broadcasted_iota(jnp.int32, (places.all, LANES), 1)
    beyond = order > slot if backward else order < slot
    spread[...] = beyond.astype(F32)
    order = places.every(gather.shape, 1) // places.chunk
    slot = lax.broadcasted_iota(jnp.int32, gather.shape, 0)
    gather[...] = (order == slot).astype(F32)


def tile_of(ref, rows, tile):
    return ref[rows, tile * LANES : (tile + 1) * LANES]


def only(values_in, lane, side):
    return jnp.where(lane // HEAD_DIM == side, values_in, jnp.zeros_like(values_in))


def norm_grad(grad_in, values_in, gain):
    inverse = lax.rsqrt(jnp.mean(values_in * values_in, axis=-1, keepdims=True) + EPSILON)
    normed = values_in * inverse
    scaled = grad_in * gain
    inner = jnp.mean(scaled * normed, axis=-1, keepdims=True)
    return inverse * (scaled - normed * inner), jnp.sum(grad_in * normed, axis=0, keepdims=True)


def norm(values_in, gain):
    inverse = lax.rsqrt(jnp.mean(values_in * values_in, axis=-1, keepdims=True) + EPSILON)
    return (values_in * inverse * gain).astype(BF16)


def to_columns(rows_in, first=0):
    many = rows_in.shape[1]
    parts = [rows_in, jnp.zeros((LANES - 8 - first, many), F32)]
    if first:
        parts = [jnp.zeros((first, many), F32)] + parts
    return jnp.concatenate(parts, axis=0).T


def gather_quarters(net, ref):
    chunk = ref.shape[0] // 4

    def piece(y):
        return ref.at[rows_of((2 * y + net.c) * chunk, chunk), :]

    up = net.send(piece(net.y), piece(net.y), net.upper())
    first = net.send(piece(net.y), piece(net.y), net.lower())

    def second():
        up.wait_recv()
        other = net.send(piece(1 - net.y), piece(1 - net.y), net.lower())

        def last():
            first.wait_recv()
            other.wait_recv()

        return last

    return second


def layer_kernel(
    tokens,
    out_grad,
    gain_one,
    gain_two,
    wq,
    wk,
    wv,
    forget_t,
    bias_in,
    wo_t,
    wg,
    wu,
    wd_t,
    doc_ref,
    layer_out,
    tokens_grad,
    gains,
    bias_grad,
    late_final,
    last_final,
    early_final,
    ffn_final,
    stage_attn,
    stage_out,
    stage_bias,
    other_bias,
    h_one,
    allowed,
    spread,
    gather,
    logit_parts,
    queries,
    keyval,
    offsets,
    mass,
    logits,
    mixed,
    exact,
    middle,
    normed_two,
    out_grads,
    w_attn,
    w_out,
    w_ffn,
    all_query,
    all_grad,
    ffn_grads,
    part_two,
    part_out,
    two_low,
    two_up,
    two_line,
    out_low,
    out_up,
    out_line,
    ffn_sum,
    ffn_side,
    late_sum,
    late_low,
    late_side,
    last_sum,
    last_low,
    last_side,
    early_sum,
    early_low,
    early_side,
    grad_attn,
    grad_heads,
    stats,
    off_parts,
    every_off,
    grad_qkv,
    grad_offs,
    part_one,
    one_up,
    one_line,
    gain_parts,
    gain_swap,
    own_tokens,
    near_sems,
    sems,
):
    net = Net(sems)
    z, x, y, c = net.z, net.x, net.y, net.c
    width = tokens.shape[1]
    chunk = tokens.shape[0] // 4
    part = 4 * chunk
    places = Places(net, chunk)
    hidden = wg.shape[1] // 4
    own = rows_of((2 * y + c) * chunk, chunk)
    tile = 256
    scale_one = gain_one[...].reshape(1, width)
    scale_two = gain_two[...].reshape(1, width)

    token_net = RowGather(net, lambda yy, zz: grad_attn.at[yy, rows_of(zz * chunk, chunk), :])
    weight_net = WeightSpread(net, stage_attn, w_attn)
    out_net = WeightSpread(net, stage_out, w_out)
    units_net = HiddenSpread(net, ffn_side, w_ffn)
    kv_net = CrossGather(net, lambda xx, cc: keyval.at[:, xx, cc])
    logit_net = CrossGather(net, lambda xx, cc: logit_parts.at[xx, cc])
    two_net = RowGather(
        net,
        lambda yy, zz: normed_two.at[c, yy, zz],
        lambda yy, zz: normed_two.at[1 - c, yy, zz],
    )
    given_net = RowGather(
        net, lambda yy, zz: out_grads.at[c, yy, zz], lambda yy, zz: out_grads.at[1 - c, yy, zz]
    )
    attn_sum = RowSum(
        net, lambda yy, zz: part_one.at[yy, rows_of(zz * chunk, chunk), :], one_up, one_line
    )

    near = [
        (tokens.at[own, :], own_tokens),
        (tokens.at[own, :], grad_attn.at[y, rows_of(z * chunk, chunk), :]),
        (out_grad.at[own, :], out_grads.at[c, y, z]),
    ]
    for index, ref in enumerate((wg, wu, wd_t)):
        for zz in range(4):
            near.append(
                (
                    ref.at[:, zz * hidden : (zz + 1) * hidden],
                    ffn_side.at[zz, :, index * hidden : (index + 1) * hidden],
                )
            )
    fetched = [
        pltpu.make_async_copy(src, dst, near_sems.at[at]) for at, (src, dst) in enumerate(near)
    ]
    for copy in fetched:
        copy.start()
    half_cols = wq.shape[1] // 2
    half_heads = half_cols // HEAD_DIM
    block = wq.shape[0]
    forget = forget_t[...].astype(F32)
    row8 = lax.broadcasted_iota(jnp.int32, (8, LANES), 0)
    for u in range(2):
        cols = slice(u * half_cols, (u + 1) * half_cols)
        for index, ref in enumerate((wk, wv)):
            stage_attn[u, :, index * half_cols : (index + 1) * half_cols] = ref[:, cols]
        rows8 = jnp.concatenate(
            [
                forget[u * half_heads : (u + 1) * half_heads, :],
                jnp.zeros((8 - half_heads, block), F32),
            ],
            axis=0,
        )
        rows8 = jnp.concatenate([rows8, jnp.zeros((8, 2 * LANES - block), F32)], axis=1)
        stage_attn[u, :, 4 * LANES :] = to_columns(rows8, HEAD_DIM)[:block].astype(BF16)
        stage_attn[u, :, 2 * half_cols : 3 * half_cols] = wq[:, cols]
        biases = jnp.zeros((8, LANES), F32)
        for head in range(half_heads):
            biases = jnp.where(row8 == head, bias_in[u * half_heads + head], biases)
        stage_bias[u] = biases
    net.barrier()
    for copy in fetched[:3]:
        copy.wait()
    weight_net.start()
    token_net.start()
    bias_send = net.send(stage_bias, other_bias, net.lower())
    for u in range(2):
        stage_out[u, :, :HEAD_DIM] = jnp.zeros((block, HEAD_DIM), BF16)
        stage_out[u, :, HEAD_DIM:] = wo_t[:, u * half_cols : (u + 1) * half_cols]

    order_tables(places, spread, gather, False)
    every = places.every((1, places.all), 1)
    for late in range(2):
        at = places.own(late) + lax.broadcasted_iota(jnp.int32, (part, 1), 0)
        pos = places.position(at)
        start = doc_starts(pos, doc_ref)
        seen = (every <= pos) & (every >= start)
        allowed[late * part : (late + 1) * part, :] = jnp.where(seen, 0.0, MASKED).astype(BF16)

    token_net.forward()
    weight_net.forward()
    given_net.start()
    h_one[y] = norm(grad_attn[y].astype(F32), scale_one)
    token_net.finish()
    h_one[1 - y] = norm(grad_attn[1 - y].astype(F32), scale_one)
    weight_net.finish()

    for late in range(2):
        keyval[late, x, c] = dot_nn(h_one[late], w_attn[:, : 3 * LANES]).astype(BF16)
    kv_net.start()
    bias_send.wait_recv()
    bias = jnp.where(weight_net.first, stage_bias[z % 2], other_bias[z % 2])[:, :1]
    for late in range(2):
        r = slice(late * part, (late + 1) * part)
        made = dot_nn(h_one[late], w_attn[:, 3 * LANES :])
        logit_parts[x, c, :, r] = made[:, LANES:].T[HEAD_DIM : HEAD_DIM + 8, :] + bias
        queries[r, :] = (made.astype(BF16).astype(F32) * HEAD_DIM ** (-0.5)).astype(BF16)
    logit_net.start()
    out_net.start()
    for copy in fetched[3:]:
        copy.wait()
    units_net.start()

    logit_net.forward()
    given_net.forward()
    logit_net.finish()
    for late in range(2):
        for xx in range(2):
            for cc in range(2):
                at = (late * 4 + xx * 2 + cc) * part
                logits[:, at : at + part] = logit_parts[xx, cc, :, late * part : (late + 1) * part]
    turned = logits[...]
    logs = jnp.minimum(turned, 0.0) - jnp.log(1.0 + jnp.exp(-jnp.abs(turned)))
    offsets[...] = running_sums(places, logs, spread, gather, False)
    kv_net.forward()
    out_net.forward()
    kv_net.finish()

    lane = lax.broadcasted_iota(jnp.int32, (LANES, LANES), 1)
    first = (lane // HEAD_DIM) == 0
    for block in range(2 * part // LANES):
        r = slice(block * LANES, (block + 1) * LANES)
        late = (block * LANES) // part
        many = places.all // 2 * (late + 1)
        made, kept = [], []
        masses = jnp.zeros((LANES, LANES), F32)
        for head in range(3):
            tile_k, side_k = KEY_TILES[head]
            tile_v, side_v = VALUE_TILES[head]
            keys = keyval[: late + 1, :, :, :, tile_k * LANES : (tile_k + 1) * LANES]
            values = keyval[: late + 1, :, :, :, tile_v * LANES : (tile_v + 1) * LANES]
            keys, values = keys.reshape(many, LANES), values.reshape(many, LANES)
            scores = (
                dot_nt(only(tile_of(queries, r, tile_k), lane, side_k), keys)
                - offsets[head : head + 1, :many]
                + allowed[r, :many].astype(F32)
            )
            top = jnp.max(scores, axis=1, keepdims=True)
            probs = jnp.exp(scores - top)
            total = jnp.sum(probs, axis=1, keepdims=True)
            high = probs.astype(BF16)
            rest = (probs - high.astype(F32)).astype(BF16)
            share = 1.0 / total
            rounded = dot_nn(high, values)
            made.append(rounded * share)
            kept.append((rounded + dot_nn(rest, values)) * share)
            masses = jnp.where(lane == head, top + jnp.log(total), masses)
        mass[r, :] = masses
        mixed[r, :LANES] = jnp.where(first, 0.0, made[0]).astype(BF16)
        mixed[r, LANES:] = jnp.where(first, made[1], made[2]).astype(BF16)
        exact[r, :LANES] = jnp.where(first, 0.0, kept[0])
        exact[r, LANES:] = jnp.where(first, kept[1], kept[2])
        if block == 1:
            out_net.finish()
            units_net.forward()

    def project(late):
        rows = rows_of(late * part, part)
        for at in range(0, width, tile):
            cols = slice(at, at + tile)
            part_one[late, :, cols] = dot_nt(mixed[rows, :], w_out[cols, :]).astype(BF16)

    project(1 - y)
    attn_sum.start()
    project(y)
    attn_sum.middle()
    total = own_tokens[...].astype(F32) + attn_sum.result()
    middle[...] = total
    normed_two[c, y, z] = norm(total, scale_two)
    net.drain()
    two_net.start()
    given_net.finish()
    two_net.forward()
    units_net.finish()
    two_net.finish()

    half_heads = half_cols
    tiles = [slice(at, at + tile) for at in range(0, width, tile)]

    query_net = CrossGather(net, lambda xx, cc: all_query.at[:, xx, cc])
    grad_net = CrossGather(net, lambda xx, cc: all_grad.at[:, xx, cc])
    stat_net = CrossGather(net, lambda xx, cc: stats.at[xx, cc])
    off_net = CrossGather(net, lambda xx, cc: off_parts.at[xx, cc])
    attn_net = RowGather(
        net, lambda yy, zz: grad_attn.at[yy, rows_of(zz * chunk, chunk), :]
    )

    def chunks_of(ref):
        return lambda yy, zz: ref.at[c, yy, rows_of(zz * chunk, chunk), :]

    two = RowSum(net, chunks_of(part_two), two_up, two_line)
    out = RowSum(net, chunks_of(part_out), out_up, out_line)
    one = RowSum(
        net, lambda yy, zz: part_one.at[yy, rows_of(zz * chunk, chunk), :], one_up, one_line
    )
    ffn_net = HiddenSum(net, ffn_sum, ffn_side, ffn_final)
    late_net = WeightSum(net, late_sum, late_low, late_side, late_final)
    last_net = WeightSum(net, last_sum, last_low, last_side, last_final)
    early_net = WeightSum(net, early_sum, early_low, early_side, early_final)

    for late in range(2):
        all_query[late, x, c] = queries[late * part : (late + 1) * part, :]
    query_net.start()

    for at in range(4):
        cc, late = at // 2, at % 2
        inputs = normed_two[cc, late].reshape(part, width)
        gate = dot_nn(inputs, w_ffn[:, :hidden])
        up = dot_nn(inputs, w_ffn[:, hidden : 2 * hidden])
        grad_act = dot_nn(out_grads[cc, late].reshape(part, width), w_ffn[:, 2 * hidden :])
        sigmoid = 1.0 / (1.0 + jnp.exp(-gate))
        silu = gate * sigmoid
        ffn_grads[cc, late, :, :hidden] = (
            grad_act * up * sigmoid * (1.0 + gate * (1.0 - sigmoid))
        ).astype(BF16)
        ffn_grads[cc, late, :, hidden : 2 * hidden] = (grad_act * silu).astype(BF16)
        ffn_grads[cc, late, :, 2 * hidden :] = (silu * up).astype(BF16)

    def project(parts, cc, late, cols):
        for r in tiles:
            parts[cc, late, :, r] = dot_nt(ffn_grads[cc, late, :, cols], w_ffn[r, cols]).astype(
                BF16
            )

    def lows(parts, recv, cols):
        project(parts, 1 - c, 1 - y, cols)
        first = net.send(parts.at[1 - c, 1 - y], recv.at[1 - y], net.lower())
        project(parts, 1 - c, y, cols)
        second = net.send(parts.at[1 - c, y], recv.at[y], net.lower())
        project(parts, c, 1 - y, cols)
        project(parts, c, y, cols)
        return first, second

    sends = lows(part_two, two_low, slice(0, 2 * hidden))
    sends[0].wait_recv()
    part_two[c, 1 - y] = (part_two[c, 1 - y].astype(F32) + two_low[1 - y].astype(F32)).astype(BF16)
    two.start()
    sends[1].wait_recv()
    part_two[c, y] = (part_two[c, y].astype(F32) + two_low[y].astype(F32)).astype(BF16)
    two.middle()

    both = 4 * part
    for cols in tiles:
        left = normed_two[:, :, :, :, cols].reshape(both, tile)
        right = ffn_grads[:, :, :, : 2 * hidden].reshape(both, 2 * hidden)
        ffn_sum[cols, : 2 * hidden] = dot_tn(left, right).astype(BF16)
        left = out_grads[:, :, :, :, cols].reshape(both, tile)
        right = ffn_grads[:, :, :, 2 * hidden :].reshape(both, hidden)
        ffn_sum[cols, 2 * hidden :] = dot_tn(left, right).astype(BF16)
    query_net.forward()
    ffn_net.start()

    grad_two = two.result()
    back_two, gain_two_part = norm_grad(grad_two, middle[...], scale_two)
    grad_middle = out_grads[c, y, z].astype(F32) + back_two
    grad_attn[y, rows_of(z * chunk, chunk), :] = grad_middle.astype(BF16)
    attn_net.start()
    out_sends = lows(part_out, out_low, slice(2 * hidden, 3 * hidden))
    every = places.every((1, places.all), 1)
    own_pos = [
        places.position(places.own(late) + lax.broadcasted_iota(jnp.int32, (part, 1), 0))
        for late in range(2)
    ]
    for late in range(2):
        start = doc_starts(own_pos[late], doc_ref)
        seen = (every <= own_pos[late]) & (every >= start)
        allowed[late * part : (late + 1) * part, :] = jnp.where(seen, 0.0, MASKED).astype(BF16)
    attn_net.forward()
    ffn_net.second()
    query_net.finish()
    order_tables(places, spread, gather, True)
    attn_net.finish()

    lane = lax.broadcasted_iota(jnp.int32, (part, LANES), 1)
    for late in range(2):
        r = slice(late * part, (late + 1) * part)
        made = dot_nn(grad_attn[late], w_out[...])
        grad_heads[r, :] = made.astype(BF16)
        all_grad[late, x, c] = grad_heads[r, :]
    grad_net.start()
    for late in range(2):
        r = slice(late * part, (late + 1) * part)
        delta = jnp.zeros((part, LANES), F32)
        for head, (tile_o, side_o) in enumerate(OUT_TILES):
            product = tile_of(grad_heads, r, tile_o).astype(F32) * tile_of(exact, r, tile_o)
            inner = jnp.sum(only(product, lane, side_o), axis=1, keepdims=True)
            delta = jnp.where(lane == head, inner, delta)
        grad_offs[r, :] = delta
    stats[x, c, :8, :] = mass[...].T[:8, :]
    stats[x, c, 8:, :] = grad_offs[...].T[:8, :]
    stat_net.start()

    for cols in tiles:
        left = grad_attn[:, :, cols].reshape(2 * part, tile)
        early_sum[cols, :] = dot_tn(left, mixed[...]).astype(BF16)
    early_net.start()
    out_sends[0].wait_recv()
    part_out[c, 1 - y] = (part_out[c, 1 - y].astype(F32) + out_low[1 - y].astype(F32)).astype(BF16)
    out.start()
    out_sends[1].wait_recv()
    part_out[c, y] = (part_out[c, y].astype(F32) + out_low[y].astype(F32)).astype(BF16)

    lane = lax.broadcasted_iota(jnp.int32, (LANES, LANES), 1)
    first = (lane // HEAD_DIM) == 0
    for block in range(2 * part // LANES):
        r = slice(block * LANES, (block + 1) * LANES)
        late = (block * LANES) // part
        many = places.all // 2 * (late + 1)
        made = []
        sums = jnp.zeros((LANES, LANES), F32)
        for head in range(3):
            tile_k, side_k = KEY_TILES[head]
            tile_v, side_v = VALUE_TILES[head]
            tile_o, side_o = OUT_TILES[head]
            keys = keyval[: late + 1, :, :, :, tile_k * LANES : (tile_k + 1) * LANES]
            values = keyval[: late + 1, :, :, :, tile_v * LANES : (tile_v + 1) * LANES]
            keys, values = keys.reshape(many, LANES), values.reshape(many, LANES)
            scores = (
                dot_nt(only(tile_of(queries, r, tile_k), lane, side_k), keys)
                - offsets[head : head + 1, :many]
                + allowed[r, :many].astype(F32)
            )
            probs = jnp.exp(scores - mass[r, head : head + 1])
            grad_probs = dot_nt(only(tile_of(grad_heads, r, tile_o), lane, side_o), values)
            grad_scores = (probs * (grad_probs - grad_offs[r, head : head + 1])).astype(BF16)
            made.append(dot_nn(grad_scores, keys) * HEAD_DIM ** (-0.5))
            row_sum = jnp.sum(grad_scores.astype(F32), axis=1, keepdims=True)
            sums = jnp.where(lane == head, row_sum, sums)
        grad_qkv[r, 3 * LANES : 4 * LANES] = jnp.where(first, made[0], made[1]).astype(BF16)
        grad_qkv[r, 4 * LANES :] = jnp.where(first, made[2], 0.0).astype(BF16)
        grad_offs[r, :] = sums
        if block == 0:
            grad_net.forward()
            stat_net.forward()
        if block == 1:
            out.middle()
            early_net.second()

    starts = doc_starts(every, doc_ref)
    for late in range(2):
        seen = (own_pos[late] <= every) & (own_pos[late] >= starts)
        allowed[late * part : (late + 1) * part, :] = jnp.where(seen, 0.0, MASKED).astype(BF16)
    stat_net.finish()
    grad_net.finish()
    for late in range(2):
        for xx in range(2):
            for cc in range(2):
                at = (late * 4 + xx * 2 + cc) * part
                piece = slice(late * part, (late + 1) * part)
                every_off[0, :, at : at + part] = stats[xx, cc, :8, piece]
                every_off[1, :, at : at + part] = stats[xx, cc, 8:, piece]

    own_offs = [
        to_columns(offsets[:, pl.ds(pl.multiple_of(places.own(late), LANES), part)])
        for late in range(2)
    ]
    for block in range(2 * part // LANES):
        r = slice(block * LANES, (block + 1) * LANES)
        late = (block * LANES) // part
        within = slice(block * LANES - late * part, (block + 1) * LANES - late * part)
        many = places.all // 2 * (2 - late)
        lanes = slice(places.all - many, places.all)
        keys_made, values_made = [], []
        sums = jnp.zeros((LANES, LANES), F32)
        for head in range(3):
            tile_k, side_k = KEY_TILES[head]
            tile_v, side_v = VALUE_TILES[head]
            tile_o, side_o = OUT_TILES[head]
            asked = all_query[late:, :, :, :, tile_k * LANES : (tile_k + 1) * LANES]
            given = all_grad[late:, :, :, :, tile_o * LANES : (tile_o + 1) * LANES]
            asked, given = asked.reshape(many, LANES), given.reshape(many, LANES)
            key = keyval[late, x, c, within, tile_k * LANES : (tile_k + 1) * LANES]
            value = keyval[late, x, c, within, tile_v * LANES : (tile_v + 1) * LANES]
            scores = (
                dot_nt(only(key, lane, side_k), asked)
                - own_offs[late][within, head : head + 1]
                + allowed[r, lanes].astype(F32)
            )
            probs = jnp.exp(scores - every_off[0, head : head + 1, lanes])
            grad_probs = dot_nt(only(value, lane, side_v), given)
            grad_scores = (probs * (grad_probs - every_off[1, head : head + 1, lanes])).astype(
                BF16
            )
            keys_made.append(dot_nn(grad_scores, asked))
            values_made.append(dot_nn(probs.astype(BF16), given))
            col_sum = jnp.sum(grad_scores.astype(F32), axis=1, keepdims=True)
            sums = jnp.where(lane == head, col_sum, sums)
        for at, (left, right) in enumerate(
            (
                (keys_made[0], keys_made[1]),
                (keys_made[2], values_made[0]),
                (values_made[1], values_made[2]),
            )
        ):
            grad_qkv[r, at * LANES : (at + 1) * LANES] = jnp.where(first, left, right).astype(BF16)
        grad_offs[r, :] = grad_offs[r, :] - sums
        if block == 1:
            early_net.third()
    off_parts[x, c] = grad_offs[...].T[:8, :]
    off_net.start()
    cut = late_sum.shape[1]
    for cols in tiles:
        left = h_one[:, :, cols].reshape(2 * part, tile)
        late_sum[cols, :] = dot_tn(left, grad_qkv[:, :cut]).astype(BF16)
    late_net.start()
    off_net.forward()
    off_net.finish()
    for late in range(2):
        for xx in range(2):
            for cc in range(2):
                at = (late * 4 + xx * 2 + cc) * part
                every_off[0, :, at : at + part] = off_parts[
                    xx, cc, :, late * part : (late + 1) * part
                ]
    late_net.second()
    grad_logs = running_sums(places, every_off[0], spread, gather, True)
    grad_logits = grad_logs / (1.0 + jnp.exp(logits[...]))
    every_off[1] = grad_logits
    for late in range(2):
        r = slice(late * part, (late + 1) * part)
        mine = every_off[1, :, pl.ds(pl.multiple_of(places.own(late), LANES), part)]
        held = grad_qkv[r, cut:]
        lane = lax.broadcasted_iota(jnp.int32, (part, LANES), 1)
        grad_qkv[r, cut:] = jnp.where(
            lane // HEAD_DIM == 0, held, to_columns(mine, HEAD_DIM).astype(BF16)
        )

    def back(late):
        rows = rows_of(late * part, part)
        for r in tiles:
            part_one[late, :, r] = dot_nt(grad_qkv[rows, :], w_attn[r, :]).astype(BF16)

    back(1 - y)
    one.start()
    back(y)
    for cols in tiles:
        left = h_one[:, :, cols].reshape(2 * part, tile)
        last_sum[cols, :] = dot_tn(left, grad_qkv[:, cut:]).astype(BF16)
    last_net.start()
    late_net.third()
    one.middle()
    last_net.second()
    layer_out[own, :] = (middle[...] + out.result()).astype(BF16)
    layer_second = gather_quarters(net, layer_out)
    grad_one = one.result()
    back_one, gain_one_part = norm_grad(grad_one, own_tokens[...].astype(F32), scale_one)
    tokens_grad[own, :] = (grad_middle + back_one).astype(BF16)
    grad_second = gather_quarters(net, tokens_grad)
    row = lax.broadcasted_iota(jnp.int32, (8, width), 0)
    gain_parts[z, :, :width] = jnp.where(
        row == 0, gain_one_part, jnp.where(row == 1, gain_two_part, 0.0)
    )
    gain_parts[z, :, width:] = jnp.broadcast_to(
        jnp.sum(grad_logits, axis=1, keepdims=True), (8, LANES)
    )
    came, sent = net.alloc(4), net.alloc(4)
    for step in NEAR_FIRST:
        net.begin(
            net.copy(
                gain_parts.at[z], gain_parts.at[z], sent + step, came + z, net.to(z=net.next(step))
            )
        )
    last_net.third()
    layer_last = layer_second()
    grad_last = grad_second()

    ffn_net.finish()
    early_net.finish()

    total = jnp.zeros((8, width), F32)
    for step in (0,) + NEAR_FIRST:
        src = net.next(step)
        if step:
            net.got(gain_parts.at[src], came + src)
        total = total + gain_parts[src, :, :width]
    for u in range(2):
        bias_grad[u] = gain_parts[2 * c + u, :, width:]
    for step, peer in enumerate((net.lower(), net.upper(), net.side())):
        gain_swap[2 * step] = total
        swap = net.send(gain_swap.at[2 * step], gain_swap.at[2 * step + 1], peer)
        swap.wait_recv()
        total = total + gain_swap[2 * step + 1]
    gains[...] = total

    late_net.finish()
    last_net.finish()
    layer_last()
    grad_last()
    for part_net in (weight_net, out_net, late_net, last_net, early_net, net):
        part_net.drain()


def narrow_kernel(
    layer,
    tokens,
    gains,
    biases,
    late,
    last,
    early,
    units,
    layer_out,
    tokens_grad,
    gain_one,
    g_query,
    g_key,
    g_value,
    g_forget,
    g_bias,
    g_out,
    gain_two,
    g_gate,
    g_up,
    g_down,
):
    layer_out[...] = layer[...]
    tokens_grad[...] = tokens[...]
    gain_one[...] = gains[0]
    gain_two[...] = gains[1]
    half = g_query.shape[1] // 2
    heads = half // HEAD_DIM
    hidden = units.shape[2] // 3
    block = g_query.shape[0]
    for u in range(2):
        cols = slice(u * half, (u + 1) * half)
        got = late[u].astype(F32)
        rest = last[u].astype(F32)
        g_key[:, cols] = got[:, :half]
        g_value[:, cols] = got[:, half : 2 * half]
        g_query[:, cols] = jnp.concatenate([got[:, 2 * half :], rest[:, :HEAD_DIM]], axis=1)
        g_out[:, cols] = early[u, :, HEAD_DIM:].astype(F32)
        padded = jnp.concatenate([rest, jnp.zeros((2 * LANES - block, LANES), F32)], axis=0)
        g_forget[u * heads : (u + 1) * heads, :] = padded.T[HEAD_DIM : HEAD_DIM + heads, :block]
        g_bias[u * heads : (u + 1) * heads, :] = biases[u, :heads, :]
    for zz in range(4):
        cols = slice(zz * hidden, (zz + 1) * hidden)
        for index, ref in enumerate((g_gate, g_up, g_down)):
            ref[:, cols] = units[zz, :, index * hidden : (index + 1) * hidden].astype(F32)


VMEM = pl.BlockSpec(memory_space=pltpu.VMEM)
SMEM = pl.BlockSpec(memory_space=pltpu.SMEM)
HBM = pl.BlockSpec(memory_space=pl.ANY)


def shapes_of(made):
    return [jax.ShapeDtypeStruct(*m) for m in made]


def layer_shapes(rows, width, heads, hidden):
    chunk = rows // 4
    part = 4 * chunk
    every = 32 * chunk
    block = width // 8
    attn = (3 * heads * HEAD_DIM // 2) + HEAD_DIM
    cut = attn - LANES
    outs = [
        ((rows, width), BF16),
        ((rows, width), BF16),
        ((8, width), F32),
        ((2, 8, LANES), F32),
        ((2, block, cut), BF16),
        ((2, block, LANES), BF16),
        ((2, block, 2 * LANES), BF16),
        ((4, block, 3 * hidden), BF16),
    ]

    def weight_sum(columns):
        return [
            ((width, columns), BF16),
            ((width // 2, columns), BF16),
            ((2, block, columns), BF16),
        ]

    row_sum = [((2, part, width), BF16), ((4, chunk, width), BF16), ((4, chunk, width), BF16)]
    scratch = [
        ((2, block, attn), BF16),
        ((2, block, 2 * LANES), BF16),
        ((2, 8, LANES), F32),
        ((2, 8, LANES), F32),
        ((2, part, width), BF16),
        ((2 * part, every), BF16),
        ((every, LANES), F32),
        ((every // chunk, every), F32),
        ((2, 2, 8, 2 * part), F32),
        ((2 * part, 2 * LANES), BF16),
        ((2, 2, 2, part, 3 * LANES), BF16),
        ((8, every), F32),
        ((2 * part, LANES), F32),
        ((8, every), F32),
        ((2 * part, 2 * LANES), BF16),
        ((2 * part, 2 * LANES), F32),
        ((chunk, width), F32),
        ((2, 2, 4, chunk, width), BF16),
        ((2, 2, 4, chunk, width), BF16),
        ((width, attn), BF16),
        ((width, 2 * LANES), BF16),
        ((width, 3 * hidden), BF16),
        ((2, 2, 2, part, 2 * LANES), BF16),
        ((2, 2, 2, part, 2 * LANES), BF16),
        ((2, 2, part, 3 * hidden), BF16),
        ((2, 2, part, width), BF16),
        ((2, 2, part, width), BF16),
        *row_sum,
        *row_sum,
        ((width, 3 * hidden), BF16),
        ((4, block, 3 * hidden), BF16),
        *weight_sum(cut),
        *weight_sum(LANES),
        *weight_sum(2 * LANES),
        ((2, part, width), BF16),
        ((2 * part, 2 * LANES), BF16),
        ((2, 2, 16, 2 * part), F32),
        ((2, 2, 8, 2 * part), F32),
        ((2, 8, every), F32),
        ((2 * part, attn), BF16),
        ((2 * part, LANES), F32),
        *row_sum,
        ((4, 8, width + LANES), F32),
        ((6, 8, width), F32),
        ((chunk, width), BF16),
    ]
    return outs, scratch


def kernel_body(
    tokens,
    attn_gain,
    query_weight,
    key_weight,
    value_weight,
    forget_weight,
    forget_bias,
    out_weight,
    ffn_gain,
    gate_weight,
    up_weight,
    down_weight,
    doc_lengths,
    out_grad,
):
    heads = forget_bias.shape[0]
    rows, width = tokens.shape
    block, units = gate_weight.shape
    cols = query_weight.shape[1]
    outs, scratch = layer_shapes(rows, width, heads, units // 4)
    made = pl.pallas_call(
        layer_kernel,
        out_shape=shapes_of(outs),
        in_specs=[HBM] * 2 + [VMEM] * 6 + [SMEM] + [VMEM] + [HBM] * 3 + [SMEM],
        out_specs=[VMEM] * len(outs),
        scratch_shapes=[pltpu.VMEM(*m) for m in scratch] + [pltpu.SemaphoreType.DMA((15,)), pltpu.SemaphoreType.DMA((512,))],
        compiler_params=pltpu.CompilerParams(
            collective_id=0, has_side_effects=True, vmem_limit_bytes=63 << 20
        ),
    )(
        tokens,
        out_grad,
        attn_gain,
        ffn_gain,
        query_weight,
        key_weight,
        value_weight,
        forget_weight.T,
        forget_bias,
        out_weight.T,
        gate_weight,
        up_weight,
        down_weight.T,
        doc_lengths,
    )
    finals = [
        ((rows, width), BF16),
        ((rows, width), BF16),
        ((width,), F32),
        ((block, cols), F32),
        ((block, cols), F32),
        ((block, cols), F32),
        ((heads, block), F32),
        ((heads, LANES), F32),
        ((block, cols), F32),
        ((width,), F32),
        ((block, units), F32),
        ((block, units), F32),
        ((block, units), F32),
    ]
    final = pl.pallas_call(
        narrow_kernel,
        out_shape=shapes_of(finals),
        in_specs=[VMEM] * len(outs),
        out_specs=[VMEM] * len(finals),
        compiler_params=pltpu.CompilerParams(vmem_limit_bytes=63 << 20),
    )(*made)
    return (
        *final[:6],
        final[6].T,
        final[7][:, 0],
        final[8].T,
        *final[9:12],
        final[12].T,
    )


def kernels_fit(tokens, forget_bias, gate_weight):
    rows, width = tokens.shape
    heads = forget_bias.shape[0]
    return (
        lax.axis_size("seq") == 8
        and lax.axis_size("head") == 4
        and heads == 6
        and rows == 2 * LANES
        and width % 256 == 0
        and gate_weight.shape[1] % (4 * LANES) == 0
        and width * gate_weight.shape[1] <= (1536 * 1024)
    )


def unchanged(carried):
    return carried


def contract_rows(left, right):
    return lax.dot_general(
        left, right, (((0,), (0,)), ((), ())), preferred_element_type=jnp.float32
    )


def contract_cols(left, right):
    return lax.dot_general(
        left, right, (((1,), (1,)), ((), ())), preferred_element_type=jnp.float32
    )


def norm_rows(values_in, gain):
    inverse = lax.rsqrt(jnp.mean(values_in * values_in, axis=-1, keepdims=True) + EPSILON)
    normed = values_in * inverse
    return (normed, inverse, normed * gain)


def norm_back(grad_in, normed, inverse, gain):
    scaled = grad_in * gain
    inner = jnp.mean(scaled * normed, axis=-1, keepdims=True)
    return (inverse * (scaled - normed * inner), jnp.sum(grad_in * normed, axis=0))


def doc_index(positions, doc_ends):
    return jnp.sum((positions[:, None] >= doc_ends[None, :]).astype(jnp.int32), axis=1)


def stored_positions(rows, n_seq, local_rows):
    half_rows = local_rows // 2
    device_of = rows // local_rows
    within = rows % local_rows
    group_of = jnp.where(within < half_rows, device_of, 2 * n_seq - 1 - device_of)
    return group_of * half_rows + within % half_rows


def block_scores(
    query_heads, key_heads, query_offsets, key_offsets, query_pos, key_pos, query_docs, key_docs
):
    raw_scores = jnp.einsum(
        "qhd,khd->hqk", query_heads, key_heads, preferred_element_type=jnp.float32
    )
    scores = (
        raw_scores * HEAD_DIM ** (-0.5) + query_offsets.T[:, :, None] - key_offsets.T[:, None, :]
    )
    allowed = (query_docs[:, None] == key_docs[None, :]) & (key_pos[None, :] <= query_pos[:, None])
    return (jnp.where(allowed[None], scores, MASKED), allowed)


def piece_grads(
    query_heads,
    grad_heads,
    log_mass,
    row_delta,
    query_offsets,
    key_heads,
    value_heads,
    key_offsets,
    query_pos,
    key_pos,
    query_docs,
    key_docs,
):
    scores, allowed = block_scores(
        query_heads, key_heads, query_offsets, key_offsets, query_pos, key_pos, query_docs, key_docs
    )
    probs = jnp.where(allowed[None], jnp.exp(scores - log_mass[:, :, None]), 0.0)
    grad_probs = jnp.einsum(
        "qhd,khd->hqk", grad_heads, value_heads, preferred_element_type=jnp.float32
    )
    grad_scores = (probs * (grad_probs - row_delta[:, :, None])).astype(jnp.bfloat16)
    score_sums = grad_scores.astype(jnp.float32)
    query_rows = query_heads.shape[0]
    key_rows = key_heads.shape[0]
    grad_query = jnp.einsum(
        "hqk,khd->qhd", grad_scores, key_heads, preferred_element_type=jnp.float32
    ).reshape(query_rows, -1)
    grad_key = (
        jnp.einsum("hqk,qhd->khd", grad_scores, query_heads, preferred_element_type=jnp.float32)
        * HEAD_DIM ** (-0.5)
    ).reshape(key_rows, -1)
    grad_value = jnp.einsum(
        "hqk,qhd->khd", probs.astype(jnp.bfloat16), grad_heads, preferred_element_type=jnp.float32
    ).reshape(key_rows, -1)
    return (
        grad_query,
        jnp.sum(score_sums, axis=2).T,
        grad_key,
        grad_value,
        -jnp.sum(score_sums, axis=1).T,
    )


def plain_body(
    tokens,
    attn_gain,
    query_weight,
    key_weight,
    value_weight,
    forget_weight,
    forget_bias,
    out_weight,
    ffn_gain,
    gate_weight,
    up_weight,
    down_weight,
    doc_lengths,
    out_grad,
):
    local_rows = tokens.shape[0]
    local_heads = forget_bias.shape[0]
    head_cols = local_heads * HEAD_DIM
    n_seq = lax.axis_size("seq")
    my_index = lax.axis_index("seq")
    first_row = my_index * local_rows
    docs = doc_lengths.shape[0]
    doc_ends = jnp.sum(jnp.where(jnp.tri(docs, dtype=jnp.bool_), doc_lengths[None, :], 0), axis=1)
    local_pos = stored_positions(
        first_row + jnp.arange(local_rows, dtype=jnp.int32), n_seq, local_rows
    )
    local_docs = doc_index(local_pos, doc_ends)
    pos_low = jnp.min(local_pos)
    pos_high = jnp.max(local_pos)
    doc_low = jnp.min(local_docs)
    doc_high = jnp.max(local_docs)
    hidden = gate_weight.shape[1]
    forget_pad = jnp.pad(forget_weight, ((0, 0), (0, 128 - local_heads)))
    w_attn = lax.all_gather(
        jnp.concatenate([query_weight, key_weight, value_weight, forget_pad], axis=1),
        "seq",
        axis=0,
        tiled=True,
    )
    w_rest = lax.all_gather(
        jnp.concatenate([out_weight.T, gate_weight, up_weight, down_weight.T], axis=1),
        "seq",
        axis=0,
        tiled=True,
    )
    w_query = w_attn[:, :head_cols]
    w_key = w_attn[:, head_cols : 2 * head_cols]
    w_value = w_attn[:, 2 * head_cols : 3 * head_cols]
    w_forget = w_attn[:, 3 * head_cols : 3 * head_cols + local_heads]
    w_out_t = w_rest[:, :head_cols]
    w_gate = w_rest[:, head_cols : head_cols + hidden]
    w_up = w_rest[:, head_cols + hidden : head_cols + 2 * hidden]
    w_down_t = w_rest[:, head_cols + 2 * hidden :]
    inputs = tokens.astype(jnp.float32)
    normed_one, inverse_one, scaled_one = norm_rows(inputs, attn_gain)
    h_one = scaled_one.astype(jnp.bfloat16)
    query_flat = jnp.dot(h_one, w_query, preferred_element_type=jnp.float32).astype(jnp.bfloat16)
    key_flat = jnp.dot(h_one, w_key, preferred_element_type=jnp.float32).astype(jnp.bfloat16)
    value_flat = jnp.dot(h_one, w_value, preferred_element_type=jnp.float32).astype(jnp.bfloat16)
    forget_logit = jnp.dot(h_one, w_forget, preferred_element_type=jnp.float32) + forget_bias
    log_forget_all = lax.all_gather(jax.nn.log_sigmoid(forget_logit), "seq", axis=0, tiled=True)
    all_pos = stored_positions(
        jnp.arange(n_seq * local_rows, dtype=jnp.int32), n_seq, local_rows
    )
    earlier = (all_pos[None, :] <= all_pos[:, None]).astype(jnp.float32)
    offsets_all = jnp.dot(earlier, log_forget_all, precision=HIGHEST)
    offsets = lax.dynamic_slice_in_dim(offsets_all, first_row, local_rows, 0)
    query_heads = query_flat.reshape(local_rows, local_heads, HEAD_DIM)
    key_heads = key_flat.reshape(local_rows, local_heads, HEAD_DIM)
    value_heads = value_flat.reshape(local_rows, local_heads, HEAD_DIM)

    def key_range(piece_rows):
        key_pos = stored_positions(jnp.arange(piece_rows, dtype=jnp.int32), n_seq, local_rows)
        key_docs = doc_index(key_pos, doc_ends)
        is_live = (
            (jnp.min(key_pos) <= pos_high)
            & (jnp.max(key_docs) >= doc_low)
            & (jnp.min(key_docs) <= doc_high)
        )
        return (key_pos, key_docs, offsets_all, is_live)

    mass_state = (
        jnp.full((local_heads, local_rows), MASKED, jnp.float32),
        jnp.zeros((local_heads, local_rows), jnp.float32),
    )
    gathered = lax.all_gather(
        jnp.concatenate([key_flat, value_flat, query_flat], axis=1), "seq", axis=0, tiled=True
    )
    key_block = gathered[:, :head_cols]
    piece_rows = key_block.shape[0]
    key_pos, key_docs, key_offsets, is_live = key_range(piece_rows)

    def mass_update(carried_in):
        running_max, running_sum = carried_in
        scores, allowed = block_scores(
            query_heads,
            key_block.reshape(piece_rows, local_heads, HEAD_DIM),
            offsets,
            key_offsets,
            local_pos,
            key_pos,
            local_docs,
            key_docs,
        )
        new_max = jnp.maximum(running_max, jnp.max(scores, axis=2))
        weights = jnp.where(allowed[None], jnp.exp(scores - new_max[:, :, None]), 0.0)
        return (new_max, jnp.sum(weights, axis=2))

    running_max, running_sum = lax.cond(is_live, mass_update, unchanged, mass_state)
    log_mass = running_max + jnp.log(running_sum)
    start_state = (
        jnp.zeros((local_heads, local_rows, HEAD_DIM), jnp.float32),
        jnp.zeros((local_heads, local_rows, HEAD_DIM), jnp.float32),
    )
    attend_key_block = key_block
    value_block = gathered[:, head_cols : 2 * head_cols]
    attend_piece_rows = attend_key_block.shape[0]
    attend_key_pos, attend_key_docs, attend_key_offsets, is_live = key_range(attend_piece_rows)

    def attend_update(carried_in):
        scores, allowed = block_scores(
            query_heads,
            attend_key_block.reshape(attend_piece_rows, local_heads, HEAD_DIM),
            offsets,
            attend_key_offsets,
            local_pos,
            attend_key_pos,
            local_docs,
            attend_key_docs,
        )
        probs = jnp.where(allowed[None], jnp.exp(scores - log_mass[:, :, None]), 0.0)
        probs_low = probs.astype(jnp.bfloat16)
        remainder = (probs - probs_low.astype(jnp.float32)).astype(jnp.bfloat16)
        value_piece = value_block.reshape(attend_piece_rows, local_heads, HEAD_DIM)
        rounded_acc = jnp.einsum(
            "hqk,khd->hqd", probs_low, value_piece, preferred_element_type=jnp.float32
        )
        remainder_acc = jnp.einsum(
            "hqk,khd->hqd", remainder, value_piece, preferred_element_type=jnp.float32
        )
        return (rounded_acc, remainder_acc)

    rounded_acc, remainder_acc = lax.cond(is_live, attend_update, unchanged, start_state)
    attended_rows = rounded_acc.transpose(1, 0, 2)
    exact_rows = (rounded_acc + remainder_acc).transpose(1, 0, 2)
    mixed = attended_rows.reshape(local_rows, head_cols).astype(jnp.bfloat16)
    attn_part = contract_cols(mixed, w_out_t)
    middle = inputs + lax.psum(attn_part, "head")
    normed_two, inverse_two, scaled_two = norm_rows(middle, ffn_gain)
    h_two = scaled_two.astype(jnp.bfloat16)
    gate_value = jnp.dot(h_two, w_gate, preferred_element_type=jnp.float32)
    up_value = jnp.dot(h_two, w_up, preferred_element_type=jnp.float32)
    gate_sigmoid = jax.nn.sigmoid(gate_value)
    gate_silu = gate_value * gate_sigmoid
    activation = (gate_silu * up_value).astype(jnp.bfloat16)
    ffn_part = contract_cols(activation, w_down_t)
    layer_out = (
        middle + lax.psum(ffn_part.astype(jnp.bfloat16), "head").astype(jnp.float32)
    ).astype(jnp.bfloat16)
    grad_act = jnp.dot(out_grad, w_down_t, preferred_element_type=jnp.float32)
    grad_gate = (
        grad_act * up_value * gate_sigmoid * (1.0 + gate_value * (1.0 - gate_sigmoid))
    ).astype(jnp.bfloat16)
    grad_up = (grad_act * gate_silu).astype(jnp.bfloat16)
    part_two = contract_cols(grad_gate, w_gate) + contract_cols(grad_up, w_up)
    grad_two = lax.psum(part_two, "head")
    back_two, gain_two = norm_back(grad_two, normed_two, inverse_two, ffn_gain)
    grad_middle = out_grad.astype(jnp.float32) + back_two
    grad_attn = grad_middle.astype(jnp.bfloat16)
    grad_mixed = jnp.dot(grad_attn, w_out_t, preferred_element_type=jnp.float32).astype(
        jnp.bfloat16
    )
    grad_heads = grad_mixed.reshape(local_rows, local_heads, HEAD_DIM)
    row_delta = jnp.sum(grad_heads.astype(jnp.float32) * exact_rows, axis=2).T
    back_state = (
        jnp.zeros((local_rows, head_cols), jnp.float32),
        jnp.zeros((local_rows, local_heads), jnp.float32),
    )
    back_key_block = key_block
    back_value_block = value_block
    back_piece_rows = back_key_block.shape[0]
    back_key_pos, back_key_docs, back_key_offsets, is_live = key_range(back_piece_rows)

    def back_update(carried_in):
        terms = piece_grads(
            query_heads,
            grad_heads,
            log_mass,
            row_delta,
            offsets,
            back_key_block.reshape(back_piece_rows, local_heads, HEAD_DIM),
            back_value_block.reshape(back_piece_rows, local_heads, HEAD_DIM),
            back_key_offsets,
            local_pos,
            back_key_pos,
            local_docs,
            back_key_docs,
        )
        return (terms[0], terms[1])

    grad_query, grad_query_off = lax.cond(is_live, back_update, unchanged, back_state)
    stats = lax.all_gather(
        jnp.concatenate([log_mass.T, row_delta.T], axis=1), "seq", axis=0, tiled=True
    )
    stats_mass, stats_delta = stats[:, :local_heads], stats[:, local_heads:]
    key_state = (
        jnp.zeros((local_rows, head_cols), jnp.float32),
        jnp.zeros((local_rows, head_cols), jnp.float32),
        jnp.zeros((local_rows, local_heads), jnp.float32),
    )
    piece_query = gathered[:, 2 * head_cols :]
    piece_grad = lax.all_gather(grad_mixed, "seq", axis=0, tiled=True)
    key_piece_rows = piece_query.shape[0]
    piece_pos = stored_positions(jnp.arange(key_piece_rows, dtype=jnp.int32), n_seq, local_rows)
    piece_docs = doc_index(piece_pos, doc_ends)
    is_live = (
        (pos_low <= jnp.max(piece_pos))
        & (jnp.max(piece_docs) >= doc_low)
        & (jnp.min(piece_docs) <= doc_high)
    )

    def key_update(carried_in):
        piece_mass = stats_mass.T
        piece_delta = stats_delta.T
        terms = piece_grads(
            piece_query.reshape(key_piece_rows, local_heads, HEAD_DIM),
            piece_grad.reshape(key_piece_rows, local_heads, HEAD_DIM),
            piece_mass,
            piece_delta,
            offsets_all,
            key_heads,
            value_heads,
            offsets,
            piece_pos,
            local_pos,
            piece_docs,
            local_docs,
        )
        return (terms[2], terms[3], terms[4])

    grad_key, grad_value, grad_key_off = lax.cond(is_live, key_update, unchanged, key_state)
    grad_query_low = (grad_query * HEAD_DIM ** (-0.5)).astype(jnp.bfloat16)
    grad_key_low = grad_key.astype(jnp.bfloat16)
    grad_value_low = grad_value.astype(jnp.bfloat16)
    grad_offsets = grad_query_off + grad_key_off
    grad_off_all = lax.all_gather(grad_offsets, "seq", axis=0, tiled=True)
    later = (all_pos[None, :] >= local_pos[:, None]).astype(jnp.float32)
    grad_log = jnp.dot(later, grad_off_all, precision=HIGHEST)
    grad_logit = grad_log * jax.nn.sigmoid(-forget_logit)
    forget_table = w_forget.astype(jnp.float32)
    part_one = (
        contract_cols(grad_query_low, w_query)
        + contract_cols(grad_key_low, w_key)
        + contract_cols(grad_value_low, w_value)
        + lax.dot_general(grad_logit, forget_table, (((1,), (1,)), ((), ())), precision=HIGHEST)
    )
    grad_one = lax.psum(part_one.astype(jnp.bfloat16), "head").astype(jnp.float32)
    back_one, gain_one = norm_back(grad_one, normed_one, inverse_one, attn_gain)
    tokens_grad = (grad_middle + back_one).astype(jnp.bfloat16)
    forget_term = lax.dot_general(
        h_one.astype(jnp.float32), grad_logit, (((0,), (0,)), ((), ())), precision=HIGHEST
    )
    scatter_cols = [
        contract_rows(grad_attn, mixed),
        contract_rows(h_two, grad_gate),
        contract_rows(h_two, grad_up),
        contract_rows(out_grad, activation),
        contract_rows(h_one, grad_query_low),
        contract_rows(h_one, grad_key_low),
        contract_rows(h_one, grad_value_low),
        jnp.pad(forget_term, ((0, 0), (0, 128 - local_heads))),
    ]
    first_sum = lax.psum_scatter(
        jnp.concatenate([t.astype(jnp.bfloat16) for t in scatter_cols[:4]], axis=1),
        "seq",
        scatter_dimension=0,
        tiled=True,
    ).astype(jnp.float32)
    second_sum = lax.psum_scatter(
        jnp.concatenate([t.astype(jnp.bfloat16) for t in scatter_cols[4:]], axis=1),
        "seq",
        scatter_dimension=0,
        tiled=True,
    ).astype(jnp.float32)
    out_weight_grad = first_sum[:, :head_cols].T
    gate_weight_grad = first_sum[:, head_cols : head_cols + hidden]
    up_weight_grad = first_sum[:, head_cols + hidden : head_cols + 2 * hidden]
    down_weight_grad = first_sum[:, head_cols + 2 * hidden :].T
    query_weight_grad = second_sum[:, :head_cols]
    key_weight_grad = second_sum[:, head_cols : 2 * head_cols]
    value_weight_grad = second_sum[:, 2 * head_cols : 3 * head_cols]
    forget_weight_grad = second_sum[:, 3 * head_cols : 3 * head_cols + local_heads]
    attn_gain_grad, ffn_gain_grad, forget_bias_grad = lax.psum(
        (gain_one, gain_two, jnp.sum(grad_logit, axis=0)), "seq"
    )
    return (
        layer_out,
        tokens_grad,
        attn_gain_grad,
        query_weight_grad,
        key_weight_grad,
        value_weight_grad,
        forget_weight_grad,
        forget_bias_grad,
        out_weight_grad,
        ffn_gain_grad,
        gate_weight_grad,
        up_weight_grad,
        down_weight_grad,
    )


def body(*args):
    fits = kernels_fit(args[0], args[6], args[9])
    return (kernel_body if fits else plain_body)(*args)


def solution(mesh):
    return jax.shard_map(
        body,
        mesh=mesh,
        in_specs=(
            P("seq", None),
            P(),
            P("seq", "head"),
            P("seq", "head"),
            P("seq", "head"),
            P("seq", "head"),
            P("head"),
            P("head", "seq"),
            P(),
            P("seq", "head"),
            P("seq", "head"),
            P("head", "seq"),
            P(),
            P("seq", None),
        ),
        out_specs=(
            P("seq", None),
            P("seq", None),
            P(),
            P("seq", "head"),
            P("seq", "head"),
            P("seq", "head"),
            P("seq", "head"),
            P("head"),
            P("head", "seq"),
            P(),
            P("seq", "head"),
            P("seq", "head"),
            P("head", "seq"),
        ),
        check_vma=False,
    )
```

```python
import jax
import jax.numpy as jnp
from jax import lax
from jax.experimental import pallas as pl
from jax.experimental.pallas import tpu as pltpu
from jax.sharding import PartitionSpec as P

HEAD_DIM = 64
EPSILON = 1e-06
HIGHEST = lax.Precision.HIGHEST
MASKED = -1e30
MESH_ID = pl.DeviceIdType.MESH
F32 = jnp.float32
BF16 = jnp.bfloat16
LANES = 128
KEY_TILES = ((0, 0), (0, 1), (1, 0))
VALUE_TILES = ((1, 1), (2, 0), (2, 1))
OUT_TILES = ((0, 1), (1, 0), (1, 1))
NEAR_FIRST = (1, 3, 2)


def dot_nn(left, right):
    return jnp.dot(left, right, preferred_element_type=F32)


def dot_nt(left, right):
    return lax.dot_general(left, right, (((1,), (1,)), ((), ())), preferred_element_type=F32)


def dot_tn(left, right):
    return lax.dot_general(left, right, (((0,), (0,)), ((), ())), preferred_element_type=F32)


def rows_of(first, count):
    return pl.ds(pl.multiple_of(first, 16), count)


def add_to(ref, other):
    ref[...] = (ref[...].astype(F32) + other[...].astype(F32)).astype(BF16)


class Net:
    def __init__(self, sems):
        s = lax.axis_index("seq")
        h = lax.axis_index("head")
        self.line = 4
        self.z, self.x = s // 2, s % 2
        self.y, self.c = h // 2, h % 2
        self.inner = (self.z == 1) | (self.z == 2)
        self.group = self.z * 2 + self.y
        self.sems = sems
        self.used = 0
        self.pending = []

    def alloc(self, count):
        first = self.used
        self.used += count
        return first

    def to(self, z=None, x=None, y=None, c=None):
        z = self.z if z is None else z
        x = self.x if x is None else x
        y = self.y if y is None else y
        c = self.c if c is None else c
        return (z * 2 + x, y * 2 + c)

    def by_distance(self):
        low = self.z < 2
        nearest = self.z + 1 - 2 * (self.z % 2)
        return (nearest, jnp.where(low, 2, 1), jnp.where(low, 3, 0))

    def side(self):
        return self.to(x=1 - self.x)

    def lower(self):
        return self.to(c=1 - self.c)

    def upper(self):
        return self.to(y=1 - self.y)

    def next(self, step):
        return (self.z + step) % self.line

    def announce(self):
        sem = pltpu.get_barrier_semaphore()
        peers = [self.side(), self.lower(), self.upper()]
        peers.append(self.to(x=1 - self.x, c=1 - self.c))
        peers.append(self.to(y=1 - self.y, c=1 - self.c))
        for step in range(1, self.line):
            z = self.next(step)
            peers += [self.to(z=z), self.to(z=z, c=1 - self.c)]
            peers += [self.to(z=z, x=1 - self.x), self.to(z=z, y=1 - self.y)]
        for peer in peers:
            pl.semaphore_signal(sem, 1, device_id=peer, device_id_type=MESH_ID)
        self.peers = len(peers)

    def await_peers(self):
        pl.semaphore_wait(pltpu.get_barrier_semaphore(), self.peers)

    def copy(self, src, dst, send, recv, device):
        return pltpu.make_async_remote_copy(
            src_ref=src,
            dst_ref=dst,
            send_sem=self.sems.at[send],
            recv_sem=self.sems.at[recv],
            device_id=device,
            device_id_type=MESH_ID,
        )

    def begin(self, made):
        made.start()
        self.pending.append(made.wait_send)
        return made

    def begin_if(self, condition, made):
        pl.when(condition)(made.start)
        self.pending.append(lambda: pl.when(condition)(made.wait_send))

    def send(self, src, dst, device):
        first = self.alloc(2)
        return self.begin(self.copy(src, dst, first, first + 1, device))

    def got(self, ref, recv):
        self.copy(ref, ref, recv, recv, self.side()).wait_recv()

    def drain(self):
        for wait in self.pending:
            wait()
        self.pending = []


class RowGather:
    def __init__(self, net, slot, lower=None):
        self.net = net
        self.slot = slot
        self.low = lower
        self.sent = net.alloc(4)
        self.came = net.alloc(4)
        self.up_sent = net.alloc(4)
        self.up_came = net.alloc(4)
        self.low_sent = net.alloc(8)
        self.low_came = net.alloc(8)

    def pass_low(self, y, z):
        if self.low is not None:
            net = self.net
            index = y * 4 + z
            block = self.slot(y, z)
            net.begin(
                net.copy(
                    block, block, self.low_sent + index, self.low_came + index, net.lower()
                )
            )

    def pass_up(self, z):
        net = self.net
        block = self.slot(net.y, z)
        net.begin(net.copy(block, block, self.up_sent + z, self.up_came + z, net.upper()))
        self.pass_low(net.y, z)

    def along(self, src, to):
        net = self.net
        block = self.slot(net.y, src)
        return net.copy(block, block, self.sent + to, self.came + src, net.to(z=to))

    def start(self):
        net = self.net
        for to in range(net.line):
            gap = jnp.abs(to - net.z)
            net.begin_if((gap > 0) & (gap < 3), self.along(net.z, to))
        self.pass_up(net.z)

    def forward(self):
        net = self.net
        for src in net.by_distance():
            net.got(self.slot(net.y, src), self.came + src)
            self.pass_up(src)
        far = net.by_distance()[2]
        net.begin_if(net.inner, self.along(far, 3 - far))

    def finish(self):
        net = self.net
        for src in (net.z,) + net.by_distance():
            net.got(self.slot(1 - net.y, src), self.up_came + src)
            self.pass_low(1 - net.y, src)
        if self.low is not None:
            for y in range(2):
                for z in range(4):
                    net.got(self.low(y, z), self.low_came + y * 4 + z)


class RowSum:
    def __init__(self, net, slot, recv_up, recv_line):
        self.net = net
        self.slot = slot
        self.recv_up = recv_up
        self.recv_line = recv_line
        self.up_sent = net.alloc(4)
        self.up_came = net.alloc(4)
        self.sent = net.alloc(4)
        self.came = net.alloc(4)

    def start(self):
        net = self.net
        for z in net.by_distance()[::-1] + (net.z,):
            net.begin(
                net.copy(
                    self.slot(1 - net.y, z),
                    self.recv_up(z),
                    self.up_sent + z,
                    self.up_came + z,
                    net.upper(),
                )
            )

    def add_up(self, z):
        self.net.got(self.recv_up(z), self.up_came + z)
        add_to(self.slot(self.net.y, z), self.recv_up(z))

    def along(self, target, hop, place):
        net = self.net
        return net.copy(
            self.slot(net.y, target),
            self.recv_line(place),
            self.sent + target,
            self.came + place,
            net.to(z=hop),
        )

    def middle(self):
        net = self.net
        nearest, other, far = net.by_distance()
        self.add_up(far)
        net.begin_if(jnp.logical_not(net.inner), self.along(far, nearest, nearest))
        for z in (other, nearest):
            self.add_up(z)
            net.begin(self.along(z, z, net.z))

        @pl.when(net.inner)
        def _():
            net.got(self.recv_line(net.z), self.came + net.z)
            add_to(self.slot(net.y, far), self.recv_line(net.z))

        net.begin_if(net.inner, self.along(far, far, net.z))
        self.add_up(net.z)

    def result(self):
        net = self.net
        nearest, other, far = net.by_distance()

        @pl.when(jnp.logical_not(net.inner))
        def _():
            self.recv_line(far)[...] = jnp.zeros_like(self.recv_line(far))

        total = self.slot(net.y, net.z)[...].astype(F32)
        for z in (nearest, other):
            net.got(self.recv_line(z), self.came + z)
            total = total + self.recv_line(z)[...].astype(F32)
        pl.when(net.inner)(lambda: net.got(self.recv_line(far), self.came + far))
        return total + self.recv_line(far)[...].astype(F32)


class CrossGather:
    def __init__(self, net, slot):
        self.net = net
        self.slot = slot

    def start(self):
        net = self.net
        mine = self.slot(net.x, net.c)
        self.across = net.send(mine, mine, net.side())
        self.low = net.send(mine, mine, net.lower())

    def forward(self):
        net = self.net
        self.across.wait_recv()
        other = self.slot(1 - net.x, net.c)
        self.both = net.send(other, other, net.lower())

    def finish(self):
        self.low.wait_recv()
        self.both.wait_recv()


class Direct:
    def __init__(self, net, me, peers):
        self.net = net
        self.me = me
        self.peers = peers
        self.sent = net.alloc(8)
        self.came = net.alloc(8)

    def start(self, made, slot):
        net = self.net
        for at, (index, device) in enumerate(self.peers):
            net.begin(
                net.copy(
                    made(index), slot(self.me), self.sent + at, self.came + self.me, device
                )
            )

    def finish(self, slot):
        for index, _ in self.peers:
            self.net.got(slot(index), self.came + index)


class WeightSpread:
    def __init__(self, net, stage, full):
        self.net = net
        self.stage = stage
        self.full = full
        self.block = stage.shape[1]
        self.sent = net.alloc(2)
        self.came = net.alloc(4)
        self.side_sent = net.alloc(4)
        self.side_came = net.alloc(4)
        self.low_sent = net.alloc(8)
        self.low_came = net.alloc(8)
        self.first = (net.z // 2) == net.c

    def slot(self, z, x):
        return self.full.at[rows_of((z * 2 + x) * self.block, self.block), :]

    def away(self, u):
        net = self.net
        return net.copy(
            self.stage.at[u],
            self.slot(net.z, net.x),
            self.sent + u,
            self.came + net.z,
            net.to(z=2 * net.c + u),
        )

    def across(self, z):
        net = self.net
        block = self.slot(z, net.x)
        return net.copy(block, block, self.side_sent + z, self.side_came + z, net.side())

    def low(self, z, x):
        block = self.slot(z, x)
        index = z * 2 + x
        return self.net.copy(
            block, block, self.low_sent + index, self.low_came + index, self.net.lower()
        )

    def start(self):
        net = self.net
        for u in range(2):
            pl.when(2 * net.c + u != net.z)(lambda u=u: self.away(u).start())

        @pl.when(self.first)
        def _():
            self.slot(net.z, net.x)[...] = self.stage[net.z % 2]
            self.across(net.z).start()
            self.low(net.z, net.x).start()

    def forward(self):
        net = self.net

        @pl.when(self.first)
        def _():
            for step in NEAR_FIRST:
                src = net.next(step)
                net.got(self.slot(src, net.x), self.came + src)
                self.across(src).start()
                self.low(src, net.x).start()

    def finish(self):
        net = self.net

        @pl.when(self.first)
        def _():
            for step in (0,) + NEAR_FIRST:
                src = net.next(step)
                net.got(self.slot(src, 1 - net.x), self.side_came + src)
                self.low(src, 1 - net.x).start()

        @pl.when(jnp.logical_not(self.first))
        def _():
            for z in range(4):
                for x in range(2):
                    net.got(self.slot(z, x), self.low_came + z * 2 + x)

    def drain(self):
        net = self.net
        for u in range(2):
            pl.when(2 * net.c + u != net.z)(lambda u=u: self.away(u).wait_send())

        @pl.when(self.first)
        def _():
            for z in range(4):
                self.across(z).wait_send()
                for x in range(2):
                    self.low(z, x).wait_send()


class HiddenSpread:
    def __init__(self, net, stage, full):
        self.net = net
        self.stage = stage
        self.full = full
        self.block = stage.shape[1]
        self.sent = net.alloc(4)
        self.came = net.alloc(4)
        self.side_sent = net.alloc(4)
        self.side_came = net.alloc(4)

    def slot(self, z, x):
        return self.full.at[rows_of((z * 2 + x) * self.block, self.block), :]

    def across(self, z):
        net = self.net
        block = self.slot(z, net.x)
        net.begin(net.copy(block, block, self.side_sent + z, self.side_came + z, net.side()))

    def start(self):
        net = self.net
        self.slot(net.z, net.x)[...] = self.stage[net.z]
        for step in NEAR_FIRST:
            to = net.next(step)
            net.begin(
                net.copy(
                    self.stage.at[to],
                    self.slot(net.z, net.x),
                    self.sent + step,
                    self.came + net.z,
                    net.to(z=to),
                )
            )
        self.across(net.z)

    def forward(self):
        net = self.net
        for step in NEAR_FIRST:
            src = net.next(step)
            net.got(self.slot(src, net.x), self.came + src)
            self.across(src)

    def finish(self):
        net = self.net
        for z in range(4):
            net.got(self.slot(z, 1 - net.x), self.side_came + z)


class WeightSum:
    def __init__(self, net, grads, recv_low, recv_side, final):
        self.net = net
        self.grads = grads
        self.recv_low = recv_low
        self.recv_side = recv_side
        self.final = final
        self.block = final.shape[1]
        self.side_sent = net.alloc(2)
        self.side_came = net.alloc(2)
        self.sent = net.alloc(2)
        self.came = net.alloc(2)

    def rows(self, z, x):
        return self.grads.at[rows_of((z * 2 + x) * self.block, self.block), :]

    def start(self):
        net = self.net
        half = 4 * self.block
        self.low = net.send(
            self.grads.at[rows_of((1 - net.c) * half, half), :], self.recv_low, net.lower()
        )

    def second(self):
        net = self.net
        self.low.wait_recv()
        for x in (1 - net.x, net.x):
            for i in range(2):
                z = 2 * net.c + i
                add_to(
                    self.rows(z, x), self.recv_low.at[rows_of((i * 2 + x) * self.block, self.block)]
                )
        for i in range(2):
            net.begin(
                net.copy(
                    self.rows(2 * net.c + i, 1 - net.x),
                    self.recv_side.at[i],
                    self.side_sent + i,
                    self.side_came + i,
                    net.side(),
                )
            )

    def owner(self, i):
        net = self.net
        z = 2 * net.c + i
        made = net.copy(
            self.rows(z, net.x),
            self.final.at[net.z % 2],
            self.sent + i,
            self.came + net.z % 2,
            net.to(z=z, c=net.z // 2),
        )
        return (z == net.z) & (net.z // 2 == net.c), made

    def third(self):
        net = self.net
        for i in range(2):
            net.got(self.recv_side.at[i], self.side_came + i)
            mine = self.rows(2 * net.c + i, net.x)
            add_to(mine, self.recv_side.at[i])
            local, made = self.owner(i)

            @pl.when(local)
            def _():
                self.final[net.z % 2] = mine[...]

            pl.when(jnp.logical_not(local))(made.start)

    def finish(self):
        net = self.net
        for u in range(2):
            pl.when(2 * net.c + u != net.z)(
                lambda u=u: net.got(self.final.at[u], self.came + u)
            )

    def drain(self):
        for i in range(2):
            local, made = self.owner(i)
            pl.when(jnp.logical_not(local))(made.wait_send)


class HiddenSum:
    def __init__(self, net, grads, recv_side, final):
        self.net = net
        self.grads = grads
        self.recv_side = recv_side
        self.final = final
        self.block = final.shape[1]
        self.side_sent = net.alloc(4)
        self.side_came = net.alloc(4)
        self.sent = net.alloc(4)
        self.came = net.alloc(4)

    def rows(self, z, x):
        return self.grads.at[rows_of((z * 2 + x) * self.block, self.block), :]

    def start(self):
        net = self.net
        for step in (2, 1, 3, 0):
            z = net.next(step)
            net.begin(
                net.copy(
                    self.rows(z, 1 - net.x),
                    self.recv_side.at[z],
                    self.side_sent + z,
                    self.side_came + z,
                    net.side(),
                )
            )

    def second(self):
        net = self.net
        for step in (2, 1, 3, 0):
            z = net.next(step)
            net.got(self.recv_side.at[z], self.side_came + z)
            mine = self.rows(z, net.x)
            add_to(mine, self.recv_side.at[z])
            if step:
                net.begin(
                    net.copy(
                        mine,
                        self.final.at[net.z],
                        self.sent + step,
                        self.came + net.z,
                        net.to(z=z),
                    )
                )
            else:
                self.final[net.z] = mine[...]

    def finish(self):
        net = self.net
        for step in NEAR_FIRST:
            src = net.next(step)
            net.got(self.final.at[src], self.came + src)


class Places:
    def __init__(self, net, chunk):
        self.net = net
        self.chunk = chunk
        self.part = 4 * chunk
        self.all = 32 * chunk

    def position(self, at):
        chunk = self.chunk
        late = at // (16 * chunk)
        x = (at // (8 * chunk)) % 2
        c = (at // (4 * chunk)) % 2
        z = (at // chunk) % 4
        owner = 2 * z + x
        group = jnp.where(late == 0, owner, 15 - owner)
        return group * (2 * chunk) + c * chunk + at % chunk

    def own(self, late):
        return (late * 4 + self.net.x * 2 + self.net.c) * self.part

    def every(self, shape, axis):
        return self.position(lax.broadcasted_iota(jnp.int32, shape, axis))


def doc_starts(positions, doc_ref):
    start = jnp.zeros(positions.shape, jnp.int32)
    end = jnp.int32(0)
    for k in range(doc_ref.shape[0] - 1):
        end = end + doc_ref[k]
        start = jnp.where(positions >= end, end, start)
    return start


def running_sums(places, rows_in, spread, gather):
    tiles = places.all // LANES
    chunk = places.chunk
    row = lax.broadcasted_iota(jnp.int32, (LANES, LANES), 0)
    col = lax.broadcasted_iota(jnp.int32, (LANES, LANES), 1)
    within = ((row // chunk == col // chunk) & (row <= col)).astype(F32)
    stacked = jnp.concatenate(
        [rows_in[:, k * LANES : (k + 1) * LANES] for k in range(tiles)], axis=0
    )
    inside = jnp.dot(stacked, within, precision=HIGHEST, preferred_element_type=F32)
    outside = jnp.dot(rows_in, spread[...], precision=HIGHEST, preferred_element_type=F32)
    outside = outside[:, : gather.shape[0]]
    outside = jnp.dot(outside, gather[...], precision=HIGHEST, preferred_element_type=F32)
    return outside + jnp.concatenate(
        [inside[k * 8 : (k + 1) * 8, :] for k in range(tiles)], axis=1
    )


def order_tables(places, spread, gather):
    order = places.every((places.all, LANES), 0) // places.chunk
    slot = lax.broadcasted_iota(jnp.int32, (places.all, LANES), 1)
    spread[...] = (order < slot).astype(F32)
    order = places.every(gather.shape, 1) // places.chunk
    slot = lax.broadcasted_iota(jnp.int32, gather.shape, 0)
    gather[...] = (order == slot).astype(F32)


def tile_of(ref, rows, tile):
    return ref[rows, tile * LANES : (tile + 1) * LANES]


def only(values_in, lane, side):
    return jnp.where(lane // HEAD_DIM == side, values_in, jnp.zeros_like(values_in))


def norm_grad(grad_in, values_in, gain):
    inverse = lax.rsqrt(jnp.mean(values_in * values_in, axis=-1, keepdims=True) + EPSILON)
    normed = values_in * inverse
    scaled = grad_in * gain
    inner = jnp.mean(scaled * normed, axis=-1, keepdims=True)
    return inverse * (scaled - normed * inner), jnp.sum(grad_in * normed, axis=0, keepdims=True)


def norm(values_in, gain):
    inverse = lax.rsqrt(jnp.mean(values_in * values_in, axis=-1, keepdims=True) + EPSILON)
    return (values_in * inverse * gain).astype(BF16)


def to_columns(rows_in, first=0):
    many = rows_in.shape[1]
    parts = [rows_in, jnp.zeros((LANES - 8 - first, many), F32)]
    if first:
        parts = [jnp.zeros((first, many), F32)] + parts
    return jnp.concatenate(parts, axis=0).T


def gather_quarters(net, ref):
    chunk = ref.shape[0] // 4

    def piece(y):
        return ref.at[rows_of((2 * y + net.c) * chunk, chunk), :]

    up = net.send(piece(net.y), piece(net.y), net.upper())
    first = net.send(piece(net.y), piece(net.y), net.lower())

    def second():
        up.wait_recv()
        other = net.send(piece(1 - net.y), piece(1 - net.y), net.lower())

        def last():
            first.wait_recv()
            other.wait_recv()

        return last

    return second


def layer_kernel(
    tokens,
    out_grad,
    gain_one,
    gain_two,
    wq,
    wk,
    wv,
    forget_t,
    bias_in,
    wo_t,
    wg,
    wu,
    wd_t,
    doc_ref,
    layer_out,
    tokens_grad,
    gains,
    bias_grad,
    late_final,
    last_final,
    early_final,
    ffn_final,
    stage_attn,
    stage_out,
    stage_bias,
    other_bias,
    h_one,
    allowed,
    spread,
    gather,
    logit_parts,
    queries,
    keyval,
    offsets,
    mass,
    logits,
    mixed,
    exact,
    middle,
    normed_two,
    out_grads,
    w_attn,
    w_out,
    w_ffn,
    all_query,
    all_grad,
    ffn_grads,
    part_two,
    part_out,
    two_low,
    two_up,
    two_line,
    out_low,
    out_up,
    out_line,
    ffn_sum,
    ffn_side,
    late_sum,
    late_low,
    late_side,
    last_sum,
    last_low,
    last_side,
    early_sum,
    early_low,
    early_side,
    grad_attn,
    grad_heads,
    stats,
    off_parts,
    every_off,
    grad_qkv,
    grad_offs,
    part_one,
    one_up,
    one_line,
    gain_parts,
    gain_swap,
    own_tokens,
    all_forget,
    own_logits,
    near_sems,
    sems,
):
    net = Net(sems)
    net.announce()
    z, x, y, c = net.z, net.x, net.y, net.c
    width = tokens.shape[1]
    chunk = tokens.shape[0] // 4
    part = 4 * chunk
    places = Places(net, chunk)
    hidden = wg.shape[1] // 4
    own = rows_of((2 * y + c) * chunk, chunk)
    tile = 256
    scale_one = gain_one[...].reshape(1, width)
    scale_two = gain_two[...].reshape(1, width)

    token_net = RowGather(net, lambda yy, zz: grad_attn.at[yy, rows_of(zz * chunk, chunk), :])
    weight_net = WeightSpread(net, stage_attn, w_attn)
    out_net = WeightSpread(net, stage_out, w_out)
    units_net = HiddenSpread(net, ffn_side, w_ffn)
    kv_nets = [
        CrossGather(net, lambda xx, cc, late=late: keyval.at[late, xx, cc]) for late in range(2)
    ]
    sub = chunk // 2
    pieces = [slice(0, sub), slice(sub, chunk)]

    def piece_of(ref, k):
        return lambda zz: ref.at[zz, pieces[k], :]

    def rows_at(ref, k):
        return lambda yy, zz: ref.at[yy, rows_of(zz * chunk + k * sub, sub), :]

    logit_net = CrossGather(net, lambda xx, cc: logit_parts.at[xx, cc])
    two_nets = [
        RowGather(
            net,
            lambda yy, zz, k=k: normed_two.at[c, yy, zz, pieces[k], :],
            lambda yy, zz, k=k: normed_two.at[1 - c, yy, zz, pieces[k], :],
        )
        for k in range(2)
    ]
    given_net = RowGather(
        net, lambda yy, zz: out_grads.at[c, yy, zz], lambda yy, zz: out_grads.at[1 - c, yy, zz]
    )
    attn_sums = [
        RowSum(net, rows_at(part_one, k), piece_of(one_up, k), piece_of(one_line, k))
        for k in range(2)
    ]

    def groups():
        found = [(z * 2 + 1 - y, net.upper())]
        for step in range(1, 4):
            far = net.next(step)
            found.append((far * 2 + y, net.to(z=far)))
            found.append((far * 2 + 1 - y, net.to(z=far, y=1 - y)))
        return found

    forget_net = Direct(net, net.group, groups())
    logit_back = Direct(net, net.group, groups())
    rest = [(z * 2 + 1 - x, net.side())]
    for step in range(1, 4):
        far = net.next(step)
        rest.append((far * 2 + x, net.to(z=far)))
        rest.append((far * 2 + 1 - x, net.to(z=far, x=1 - x)))
    gain_net = Direct(net, z * 2 + x, rest)
    corner = net.to(y=1 - y, c=1 - c)
    last_gain = Direct(
        net,
        y * 2 + c,
        [(y * 2 + 1 - c, net.lower()), (2 - 2 * y + c, net.upper()), (3 - 2 * y - c, corner)],
    )

    near = [
        (tokens.at[own, :], own_tokens),
        (tokens.at[own, :], grad_attn.at[y, rows_of(z * chunk, chunk), :]),
        (out_grad.at[own, :], out_grads.at[c, y, z]),
    ]
    for index, ref in enumerate((wg, wu, wd_t)):
        for zz in range(4):
            near.append(
                (
                    ref.at[:, zz * hidden : (zz + 1) * hidden],
                    ffn_side.at[zz, :, index * hidden : (index + 1) * hidden],
                )
            )
    fetched = [
        pltpu.make_async_copy(src, dst, near_sems.at[at]) for at, (src, dst) in enumerate(near)
    ]
    for copy in fetched:
        copy.start()
    half_cols = wq.shape[1] // 2
    half_heads = half_cols // HEAD_DIM
    block = wq.shape[0]
    forget = forget_t[...].astype(F32)
    row8 = lax.broadcasted_iota(jnp.int32, (8, LANES), 0)
    for u in range(2):
        cols = slice(u * half_cols, (u + 1) * half_cols)
        for index, ref in enumerate((wk, wv)):
            stage_attn[u, :, index * half_cols : (index + 1) * half_cols] = ref[:, cols]
        rows8 = jnp.concatenate(
            [
                forget[u * half_heads : (u + 1) * half_heads, :],
                jnp.zeros((8 - half_heads, block), F32),
            ],
            axis=0,
        )
        rows8 = jnp.concatenate([rows8, jnp.zeros((8, 2 * LANES - block), F32)], axis=1)
        stage_attn[u, :, 4 * LANES :] = to_columns(rows8, HEAD_DIM)[:block].astype(BF16)
        stage_attn[u, :, 2 * half_cols : 3 * half_cols] = wq[:, cols]
        biases = jnp.zeros((8, LANES), F32)
        for head in range(half_heads):
            biases = jnp.where(row8 == head, bias_in[u * half_heads + head], biases)
        stage_bias[u] = biases
    net.await_peers()
    for copy in fetched[:3]:
        copy.wait()
    weight_net.start()
    token_net.start()
    bias_send = net.send(stage_bias, other_bias, net.lower())
    for u in range(2):
        stage_out[u, :, :HEAD_DIM] = jnp.zeros((block, HEAD_DIM), BF16)
        stage_out[u, :, HEAD_DIM:] = wo_t[:, u * half_cols : (u + 1) * half_cols]

    order_tables(places, spread, gather)
    every = places.every((1, places.all), 1)
    for late in range(2):
        at = places.own(late) + lax.broadcasted_iota(jnp.int32, (part, 1), 0)
        pos = places.position(at)
        start = doc_starts(pos, doc_ref)
        seen = (every <= pos) & (every >= start)
        allowed[late * part : (late + 1) * part, :] = jnp.where(seen, 0.0, MASKED).astype(BF16)

    weight_net.forward()
    token_net.forward()
    given_net.start()
    h_one[y] = norm(grad_attn[y].astype(F32), scale_one)
    token_net.finish()
    h_one[1 - y] = norm(grad_attn[1 - y].astype(F32), scale_one)
    weight_net.finish()

    for late in range(2):
        keyval[late, x, c] = dot_nn(h_one[late], w_attn[:, : 3 * LANES]).astype(BF16)
        kv_nets[late].start()
    bias_send.wait_recv()
    bias = jnp.where(weight_net.first, stage_bias[z % 2], other_bias[z % 2])[:, :1]
    for late in range(2):
        r = slice(late * part, (late + 1) * part)
        made = dot_nn(h_one[late], w_attn[:, 3 * LANES :])
        logit_parts[x, c, :, r] = made[:, LANES:].T[HEAD_DIM : HEAD_DIM + 8, :] + bias
        queries[r, :] = (made.astype(BF16).astype(F32) * HEAD_DIM ** (-0.5)).astype(BF16)
    logit_net.start()
    all_forget[net.group] = w_attn[:, 4 * LANES :].astype(F32).T[HEAD_DIM : HEAD_DIM + 8, :]
    forget_net.start(lambda index: all_forget.at[net.group], lambda index: all_forget.at[index])
    out_net.start()
    for copy in fetched[3:]:
        copy.wait()
    units_net.start()

    logit_net.forward()
    given_net.forward()
    logit_net.finish()
    for late in range(2):
        for xx in range(2):
            for cc in range(2):
                at = (late * 4 + xx * 2 + cc) * part
                logits[:, at : at + part] = logit_parts[xx, cc, :, late * part : (late + 1) * part]
    turned = logits[...]
    logs = jnp.minimum(turned, 0.0) - jnp.log(1.0 + jnp.exp(-jnp.abs(turned)))
    offsets[...] = running_sums(places, logs, spread, gather)
    kv_nets[0].forward()
    kv_nets[1].forward()
    out_net.forward()
    kv_nets[0].finish()

    lane = lax.broadcasted_iota(jnp.int32, (LANES, LANES), 1)
    first = (lane // HEAD_DIM) == 0
    for block in range(2 * part // LANES):
        r = slice(block * LANES, (block + 1) * LANES)
        late = (block * LANES) // part
        many = places.all // 2 * (late + 1)
        made, kept = [], []
        masses = jnp.zeros((LANES, LANES), F32)
        for head in range(3):
            tile_k, side_k = KEY_TILES[head]
            tile_v, side_v = VALUE_TILES[head]
            keys = keyval[: late + 1, :, :, :, tile_k * LANES : (tile_k + 1) * LANES]
            values = keyval[: late + 1, :, :, :, tile_v * LANES : (tile_v + 1) * LANES]
            keys, values = keys.reshape(many, LANES), values.reshape(many, LANES)
            scores = (
                dot_nt(only(tile_of(queries, r, tile_k), lane, side_k), keys)
                - offsets[head : head + 1, :many]
                + allowed[r, :many].astype(F32)
            )
            top = jnp.max(scores, axis=1, keepdims=True)
            probs = jnp.exp(scores - top)
            total = jnp.sum(probs, axis=1, keepdims=True)
            high = probs.astype(BF16)
            rest = (probs - high.astype(F32)).astype(BF16)
            share = 1.0 / total
            rounded = dot_nn(high, values)
            made.append(rounded * share)
            kept.append((rounded + dot_nn(rest, values)) * share)
            masses = jnp.where(lane == head, top + jnp.log(total), masses)
        mass[r, :] = masses
        mixed[r, :LANES] = jnp.where(first, 0.0, made[0]).astype(BF16)
        mixed[r, LANES:] = jnp.where(first, made[1], made[2]).astype(BF16)
        exact[r, :LANES] = jnp.where(first, 0.0, kept[0])
        exact[r, LANES:] = jnp.where(first, kept[1], kept[2])
        if block == 1:
            out_net.finish()
            units_net.forward()
            kv_nets[1].finish()

    def project(late):
        rows = rows_of(late * part, part)
        for at in range(0, width, tile):
            cols = slice(at, at + tile)
            part_one[late, :, cols] = dot_nt(mixed[rows, :], w_out[cols, :]).astype(BF16)

    project(1 - y)
    for attn_sum in attn_sums:
        attn_sum.start()
    project(y)
    for attn_sum in attn_sums:
        attn_sum.middle()
    net.drain()
    for k in range(2):
        total = own_tokens[pieces[k], :].astype(F32) + attn_sums[k].result()
        middle[pieces[k], :] = total
        normed_two[c, y, z, pieces[k], :] = norm(total, scale_two)
        two_nets[k].start()
    given_net.finish()
    two_nets[0].forward()
    units_net.finish()
    two_nets[0].finish()

    half_heads = half_cols
    tiles = [slice(at, at + tile) for at in range(0, width, tile)]

    query_net = CrossGather(net, lambda xx, cc: all_query.at[:, xx, cc])
    grad_net = CrossGather(net, lambda xx, cc: all_grad.at[:, xx, cc])
    stat_net = CrossGather(net, lambda xx, cc: stats.at[xx, cc])
    off_net = CrossGather(net, lambda xx, cc: off_parts.at[xx, cc])
    attn_nets = [RowGather(net, rows_at(grad_attn, k)) for k in range(2)]

    def own_parts(ref, k):
        return lambda yy, zz: ref.at[k, c, rows_of(yy * 4 * sub + zz * sub, sub), :]

    twos = [
        RowSum(net, own_parts(part_two, k), piece_of(two_up, k), piece_of(two_line, k))
        for k in range(2)
    ]
    outs = [
        RowSum(net, own_parts(part_out, k), piece_of(out_up, k), piece_of(out_line, k))
        for k in range(2)
    ]
    ones = [
        RowSum(net, rows_at(part_one, k), piece_of(one_up, k), piece_of(one_line, k))
        for k in range(2)
    ]
    ffn_net = HiddenSum(net, ffn_sum, ffn_side, ffn_final)
    late_net = WeightSum(net, late_sum, late_low, late_side, late_final)
    last_net = WeightSum(net, last_sum, last_low, last_side, last_final)
    early_net = WeightSum(net, early_sum, early_low, early_side, early_final)

    for late in range(2):
        all_query[late, x, c] = queries[late * part : (late + 1) * part, :]
    query_net.start()

    def units_of(k):
        for cc in range(2):
            inputs = normed_two[cc, :, :, pieces[k], :].reshape(part, width)
            given = out_grads[cc, :, :, pieces[k], :].reshape(part, width)
            gate = dot_nn(inputs, w_ffn[:, :hidden])
            up = dot_nn(inputs, w_ffn[:, hidden : 2 * hidden])
            grad_act = dot_nn(given, w_ffn[:, 2 * hidden :])
            sigmoid = 1.0 / (1.0 + jnp.exp(-gate))
            silu = gate * sigmoid
            ffn_grads[k, cc, :, :hidden] = (
                grad_act * up * sigmoid * (1.0 + gate * (1.0 - sigmoid))
            ).astype(BF16)
            ffn_grads[k, cc, :, hidden : 2 * hidden] = (grad_act * silu).astype(BF16)
            ffn_grads[k, cc, :, 2 * hidden :] = (silu * up).astype(BF16)

    def lower_of(parts, recv, k, cols):
        def back(cc):
            for r in tiles:
                parts[k, cc, :, r] = dot_nt(ffn_grads[k, cc, :, cols], w_ffn[r, cols]).astype(BF16)

        back(1 - c)
        made = net.send(parts.at[k, 1 - c], recv.at[k], net.lower())
        back(c)
        return made

    def upper_of(made, parts, recv, k, sums):
        made.wait_recv()
        parts[k, c] = (parts[k, c].astype(F32) + recv[k].astype(F32)).astype(BF16)
        sums[k].start()

    def unit_grads(some):
        for cols in some:
            both = [0.0, 0.0]
            for k in range(2):
                left = normed_two[:, :, :, pieces[k], cols].reshape(2 * part, tile)
                right = ffn_grads[k].reshape(2 * part, 3 * hidden)
                both[0] = both[0] + dot_tn(left, right[:, : 2 * hidden])
                left = out_grads[:, :, :, pieces[k], cols].reshape(2 * part, tile)
                both[1] = both[1] + dot_tn(left, right[:, 2 * hidden :])
            ffn_sum[cols, : 2 * hidden] = both[0].astype(BF16)
            ffn_sum[cols, 2 * hidden :] = both[1].astype(BF16)

    units_of(0)
    two_nets[1].forward()
    to_lower = slice(0, 2 * hidden)
    first_low = lower_of(part_two, two_low, 0, to_lower)
    two_nets[1].finish()
    units_of(1)
    upper_of(first_low, part_two, two_low, 0, twos)
    second_low = lower_of(part_two, two_low, 1, to_lower)
    twos[0].middle()
    upper_of(second_low, part_two, two_low, 1, twos)
    unit_grads(tiles[:3])
    twos[1].middle()
    unit_grads(tiles[3:])
    query_net.forward()
    ffn_net.start()
    grad_middle = []
    gain_two_part = 0.0
    for k in range(2):
        back_two, part_gain = norm_grad(twos[k].result(), middle[pieces[k], :], scale_two)
        gain_two_part = gain_two_part + part_gain
        grad_middle.append(out_grads[c, y, z, pieces[k], :].astype(F32) + back_two)
        grad_attn[y, rows_of(z * chunk + k * sub, sub), :] = grad_middle[k].astype(BF16)
        attn_nets[k].start()
    to_out = slice(2 * hidden, 3 * hidden)
    out_sends = [lower_of(part_out, out_low, 0, to_out), None]
    attn_nets[0].forward()
    out_sends[1] = lower_of(part_out, out_low, 1, to_out)
    every = places.every((1, places.all), 1)
    own_pos = [
        places.position(places.own(late) + lax.broadcasted_iota(jnp.int32, (part, 1), 0))
        for late in range(2)
    ]
    attn_nets[1].forward()
    attn_nets[0].finish()
    query_net.finish()
    attn_nets[1].finish()

    lane = lax.broadcasted_iota(jnp.int32, (part, LANES), 1)
    for late in range(2):
        r = slice(late * part, (late + 1) * part)
        made = dot_nn(grad_attn[late], w_out[...])
        grad_heads[r, :] = made.astype(BF16)
        all_grad[late, x, c] = grad_heads[r, :]
    grad_net.start()
    for late in range(2):
        r = slice(late * part, (late + 1) * part)
        delta = jnp.zeros((part, LANES), F32)
        for head, (tile_o, side_o) in enumerate(OUT_TILES):
            product = tile_of(grad_heads, r, tile_o).astype(F32) * tile_of(exact, r, tile_o)
            inner = jnp.sum(only(product, lane, side_o), axis=1, keepdims=True)
            delta = jnp.where(lane == head, inner, delta)
        grad_offs[r, :] = delta
    stats[x, c, :8, :] = mass[...].T[:8, :]
    stats[x, c, 8:, :] = grad_offs[...].T[:8, :]
    stat_net.start()

    for cols in tiles:
        left = grad_attn[:, :, cols].reshape(2 * part, tile)
        early_sum[cols, :] = dot_tn(left, mixed[...]).astype(BF16)
    early_net.start()
    for k in range(2):
        upper_of(out_sends[k], part_out, out_low, k, outs)
    ffn_net.second()

    lane = lax.broadcasted_iota(jnp.int32, (LANES, LANES), 1)
    first = (lane // HEAD_DIM) == 0
    for block in range(2 * part // LANES):
        r = slice(block * LANES, (block + 1) * LANES)
        late = (block * LANES) // part
        many = places.all // 2 * (late + 1)
        made = []
        sums = jnp.zeros((LANES, LANES), F32)
        for head in range(3):
            tile_k, side_k = KEY_TILES[head]
            tile_v, side_v = VALUE_TILES[head]
            tile_o, side_o = OUT_TILES[head]
            keys = keyval[: late + 1, :, :, :, tile_k * LANES : (tile_k + 1) * LANES]
            values = keyval[: late + 1, :, :, :, tile_v * LANES : (tile_v + 1) * LANES]
            keys, values = keys.reshape(many, LANES), values.reshape(many, LANES)
            scores = (
                dot_nt(only(tile_of(queries, r, tile_k), lane, side_k), keys)
                - offsets[head : head + 1, :many]
                + allowed[r, :many].astype(F32)
            )
            probs = jnp.exp(scores - mass[r, head : head + 1])
            grad_probs = dot_nt(only(tile_of(grad_heads, r, tile_o), lane, side_o), values)
            grad_scores = (probs * (grad_probs - grad_offs[r, head : head + 1])).astype(BF16)
            made.append(dot_nn(grad_scores, keys) * HEAD_DIM ** (-0.5))
            row_sum = jnp.sum(grad_scores.astype(F32), axis=1, keepdims=True)
            sums = jnp.where(lane == head, row_sum, sums)
        grad_qkv[r, 3 * LANES : 4 * LANES] = jnp.where(first, made[0], made[1]).astype(BF16)
        grad_qkv[r, 4 * LANES :] = jnp.where(first, made[2], 0.0).astype(BF16)
        grad_offs[r, :] = sums
        if block == 0:
            grad_net.forward()
            stat_net.forward()
        if block == 1:
            for out in outs:
                out.middle()
            early_net.second()

    starts = doc_starts(every, doc_ref)
    for late in range(2):
        seen = (own_pos[late] <= every) & (own_pos[late] >= starts)
        allowed[late * part : (late + 1) * part, :] = jnp.where(seen, 0.0, MASKED).astype(BF16)
    stat_net.finish()
    grad_net.finish()
    for late in range(2):
        for xx in range(2):
            for cc in range(2):
                at = (late * 4 + xx * 2 + cc) * part
                piece = slice(late * part, (late + 1) * part)
                every_off[0, :, at : at + part] = stats[xx, cc, :8, piece]
                every_off[1, :, at : at + part] = stats[xx, cc, 8:, piece]

    own_offs = [
        to_columns(offsets[:, pl.ds(pl.multiple_of(places.own(late), LANES), part)])
        for late in range(2)
    ]
    for block in range(2 * part // LANES):
        r = slice(block * LANES, (block + 1) * LANES)
        late = (block * LANES) // part
        within = slice(block * LANES - late * part, (block + 1) * LANES - late * part)
        many = places.all // 2 * (2 - late)
        lanes = slice(places.all - many, places.all)
        keys_made, values_made = [], []
        sums = jnp.zeros((LANES, LANES), F32)
        for head in range(3):
            tile_k, side_k = KEY_TILES[head]
            tile_v, side_v = VALUE_TILES[head]
            tile_o, side_o = OUT_TILES[head]
            asked = all_query[late:, :, :, :, tile_k * LANES : (tile_k + 1) * LANES]
            given = all_grad[late:, :, :, :, tile_o * LANES : (tile_o + 1) * LANES]
            asked, given = asked.reshape(many, LANES), given.reshape(many, LANES)
            key = keyval[late, x, c, within, tile_k * LANES : (tile_k + 1) * LANES]
            value = keyval[late, x, c, within, tile_v * LANES : (tile_v + 1) * LANES]
            scores = (
                dot_nt(only(key, lane, side_k), asked)
                - own_offs[late][within, head : head + 1]
                + allowed[r, lanes].astype(F32)
            )
            probs = jnp.exp(scores - every_off[0, head : head + 1, lanes])
            grad_probs = dot_nt(only(value, lane, side_v), given)
            grad_scores = (probs * (grad_probs - every_off[1, head : head + 1, lanes])).astype(
                BF16
            )
            keys_made.append(dot_nn(grad_scores, asked))
            values_made.append(dot_nn(probs.astype(BF16), given))
            col_sum = jnp.sum(grad_scores.astype(F32), axis=1, keepdims=True)
            sums = jnp.where(lane == head, col_sum, sums)
        for at, (left, right) in enumerate(
            (
                (keys_made[0], keys_made[1]),
                (keys_made[2], values_made[0]),
                (values_made[1], values_made[2]),
            )
        ):
            grad_qkv[r, at * LANES : (at + 1) * LANES] = jnp.where(first, left, right).astype(BF16)
        grad_offs[r, :] = grad_offs[r, :] - sums
        if block == 1:
            early_net.third()
    off_parts[x, c] = grad_offs[...].T[:8, :]
    off_net.start()

    def back(late):
        rows = rows_of(late * part, part)
        for r in tiles:
            part_one[late, :, r] = dot_nt(grad_qkv[rows, :], w_attn[r, :]).astype(BF16)

    back(1 - y)
    for one in ones:
        one.start()
    back(y)
    off_net.forward()
    cut = late_sum.shape[1]
    for cols in tiles:
        left = h_one[:, :, cols].reshape(2 * part, tile)
        late_sum[cols, :] = dot_tn(left, grad_qkv[:, :cut]).astype(BF16)
    late_net.start()
    ones[0].middle()
    off_net.finish()
    for late in range(2):
        for xx in range(2):
            for cc in range(2):
                at = (late * 4 + xx * 2 + cc) * part
                every_off[0, :, at : at + part] = off_parts[
                    xx, cc, :, late * part : (late + 1) * part
                ]
    given = every_off[0]
    whole = jnp.sum(given, axis=1, keepdims=True)
    grad_logs = whole - running_sums(places, given, spread, gather) + given
    grad_logits = grad_logs / (1.0 + jnp.exp(logits[...]))
    every_off[1] = grad_logits

    def rows_for(index):
        at = places.own(index % 2) + (index // 4) * LANES
        return every_off.at[1, :, pl.ds(pl.multiple_of(at, LANES), LANES)]

    logit_back.start(rows_for, lambda index: own_logits.at[index])
    own_logits[net.group] = rows_for(net.group)[...]
    ones[1].middle()
    late_net.second()
    for late in range(2):
        r = slice(late * part, (late + 1) * part)
        mine = every_off[1, :, pl.ds(pl.multiple_of(places.own(late), LANES), part)]
        held = grad_qkv[r, cut:]
        lane = lax.broadcasted_iota(jnp.int32, (part, LANES), 1)
        grad_qkv[r, cut:] = jnp.where(
            lane // HEAD_DIM == 0, held, to_columns(mine, HEAD_DIM).astype(BF16)
        )
    for cols in tiles:
        left = h_one[:, :, cols].reshape(2 * part, tile)
        last_sum[cols, :] = dot_tn(left, grad_qkv[:, cut:]).astype(BF16)
    last_net.start()
    late_net.third()
    logit_back.finish(lambda index: own_logits.at[index])
    forget_net.finish(lambda index: all_forget.at[index])
    held = own_logits[...].reshape(8 * 8, LANES)
    held = jnp.where(z % 2 == 0, held[:, :chunk], held[:, chunk:]).astype(BF16)
    forget_part = dot_tn(held, all_forget[...].reshape(8 * 8, width).astype(BF16))
    last_net.second()
    for k in range(2):
        layer_out[rows_of((2 * y + c) * chunk + k * sub, sub), :] = (
            middle[pieces[k], :] + outs[k].result()
        ).astype(BF16)
    layer_second = gather_quarters(net, layer_out)
    gain_one_part = 0.0
    for k in range(2):
        back_one, part_gain = norm_grad(
            ones[k].result() + forget_part[pieces[k], :],
            own_tokens[pieces[k], :].astype(F32),
            scale_one,
        )
        gain_one_part = gain_one_part + part_gain
        tokens_grad[rows_of((2 * y + c) * chunk + k * sub, sub), :] = (
            grad_middle[k] + back_one
        ).astype(BF16)
    grad_second = gather_quarters(net, tokens_grad)
    cells = width // 4
    gain_mine = gain_parts.at[z * 2 + x]
    gain_mine[:, :cells] = jnp.concatenate(
        [g[:, k * cells : (k + 1) * cells] for g in (gain_one_part, gain_two_part) for k in range(4)],
        axis=0,
    )
    gain_mine[:, cells:] = jnp.broadcast_to(
        jnp.sum(grad_logits, axis=1, keepdims=True), (8, LANES)
    )
    gain_net.start(lambda index: gain_mine, lambda index: gain_parts.at[index])
    last_net.third()
    layer_last = layer_second()
    grad_last = grad_second()

    gain_net.finish(lambda index: gain_parts.at[index])
    total = gain_parts[0, :, :cells]
    for index in range(1, 8):
        total = total + gain_parts[index, :, :cells]
    gain_swap[y * 2 + c] = total
    last_gain.start(lambda index: gain_swap.at[y * 2 + c], lambda index: gain_swap.at[index])
    for u in range(2):
        bias_grad[u] = gain_parts[(2 * c + u) * 2 + x, :, cells:]

    ffn_net.finish()
    early_net.finish()
    last_gain.finish(lambda index: gain_swap.at[index])
    total = gain_swap[0]
    for index in range(1, 4):
        total = total + gain_swap[index]
    gains[...] = total

    late_net.finish()
    last_net.finish()
    layer_last()
    grad_last()
    for part_net in (weight_net, out_net, late_net, last_net, early_net, net):
        part_net.drain()


def narrow_kernel(
    layer,
    tokens,
    gains,
    biases,
    late,
    last,
    early,
    units,
    layer_out,
    tokens_grad,
    gain_one,
    g_query,
    g_key,
    g_value,
    g_forget,
    g_bias,
    g_out,
    gain_two,
    g_gate,
    g_up,
    g_down,
):
    layer_out[...] = layer[...]
    tokens_grad[...] = tokens[...]
    for k, ref in enumerate((gain_one, gain_two)):
        ref[...] = jnp.concatenate(
            [gains[4 * k + at : 4 * k + at + 1, :] for at in range(4)], axis=1
        )[0]
    half = g_query.shape[1] // 2
    heads = half // HEAD_DIM
    hidden = units.shape[2] // 3
    block = g_query.shape[0]
    for u in range(2):
        cols = slice(u * half, (u + 1) * half)
        got = late[u].astype(F32)
        rest = last[u].astype(F32)
        g_key[:, cols] = got[:, :half]
        g_value[:, cols] = got[:, half : 2 * half]
        g_query[:, cols] = jnp.concatenate([got[:, 2 * half :], rest[:, :HEAD_DIM]], axis=1)
        g_out[:, cols] = early[u, :, HEAD_DIM:].astype(F32)
        padded = jnp.concatenate([rest, jnp.zeros((2 * LANES - block, LANES), F32)], axis=0)
        g_forget[u * heads : (u + 1) * heads, :] = padded.T[HEAD_DIM : HEAD_DIM + heads, :block]
    each = jnp.concatenate([biases[0, :heads, :], biases[1, :heads, :]], axis=0)
    g_bias[...] = each
    for zz in range(4):
        cols = slice(zz * hidden, (zz + 1) * hidden)
        for index, ref in enumerate((g_gate, g_up, g_down)):
            ref[:, cols] = units[zz, :, index * hidden : (index + 1) * hidden].astype(F32)


VMEM = pl.BlockSpec(memory_space=pltpu.VMEM)
SMEM = pl.BlockSpec(memory_space=pltpu.SMEM)
HBM = pl.BlockSpec(memory_space=pl.ANY)


def shapes_of(made):
    return [jax.ShapeDtypeStruct(*m) for m in made]


def layer_shapes(rows, width, heads, hidden):
    chunk = rows // 4
    part = 4 * chunk
    every = 32 * chunk
    block = width // 8
    attn = (3 * heads * HEAD_DIM // 2) + HEAD_DIM
    cut = attn - LANES
    outs = [
        ((rows, width), BF16),
        ((rows, width), BF16),
        ((8, width // 4), F32),
        ((2, 8, LANES), F32),
        ((2, block, cut), BF16),
        ((2, block, LANES), BF16),
        ((2, block, 2 * LANES), BF16),
        ((4, block, 3 * hidden), BF16),
    ]

    def weight_sum(columns):
        return [
            ((width, columns), BF16),
            ((width // 2, columns), BF16),
            ((2, block, columns), BF16),
        ]

    row_sum = [((2, part, width), BF16), ((4, chunk, width), BF16), ((4, chunk, width), BF16)]
    scratch = [
        ((2, block, attn), BF16),
        ((2, block, 2 * LANES), BF16),
        ((2, 8, LANES), F32),
        ((2, 8, LANES), F32),
        ((2, part, width), BF16),
        ((2 * part, every), BF16),
        ((every, LANES), F32),
        ((every // chunk, every), F32),
        ((2, 2, 8, 2 * part), F32),
        ((2 * part, 2 * LANES), BF16),
        ((2, 2, 2, part, 3 * LANES), BF16),
        ((8, every), F32),
        ((2 * part, LANES), F32),
        ((8, every), F32),
        ((2 * part, 2 * LANES), BF16),
        ((2 * part, 2 * LANES), F32),
        ((chunk, width), F32),
        ((2, 2, 4, chunk, width), BF16),
        ((2, 2, 4, chunk, width), BF16),
        ((width, attn), BF16),
        ((width, 2 * LANES), BF16),
        ((width, 3 * hidden), BF16),
        ((2, 2, 2, part, 2 * LANES), BF16),
        ((2, 2, 2, part, 2 * LANES), BF16),
        ((2, 2, part, 3 * hidden), BF16),
        ((2, 2, part, width), BF16),
        ((2, 2, part, width), BF16),
        *row_sum,
        *row_sum,
        ((width, 3 * hidden), BF16),
        ((4, block, 3 * hidden), BF16),
        *weight_sum(cut),
        *weight_sum(LANES),
        *weight_sum(2 * LANES),
        ((2, part, width), BF16),
        ((2 * part, 2 * LANES), BF16),
        ((2, 2, 16, 2 * part), F32),
        ((2, 2, 8, 2 * part), F32),
        ((2, 8, every), F32),
        ((2 * part, attn), BF16),
        ((2 * part, LANES), F32),
        *row_sum,
        ((8, 8, width // 4 + LANES), F32),
        ((4, 8, width // 4), F32),
        ((chunk, width), BF16),
        ((8, 8, width), F32),
        ((8, 8, LANES), F32),
    ]
    return outs, scratch


def kernel_body(
    tokens,
    attn_gain,
    query_weight,
    key_weight,
    value_weight,
    forget_weight,
    forget_bias,
    out_weight,
    ffn_gain,
    gate_weight,
    up_weight,
    down_weight,
    doc_lengths,
    out_grad,
):
    heads = forget_bias.shape[0]
    rows, width = tokens.shape
    block, units = gate_weight.shape
    cols = query_weight.shape[1]
    outs, scratch = layer_shapes(rows, width, heads, units // 4)
    made = pl.pallas_call(
        layer_kernel,
        out_shape=shapes_of(outs),
        in_specs=[HBM] * 2 + [VMEM] * 6 + [SMEM] + [VMEM] + [HBM] * 3 + [SMEM],
        out_specs=[VMEM] * len(outs),
        scratch_shapes=[pltpu.VMEM(*m) for m in scratch] + [pltpu.SemaphoreType.DMA((15,)), pltpu.SemaphoreType.DMA((640,))],
        compiler_params=pltpu.CompilerParams(
            collective_id=0, has_side_effects=True, vmem_limit_bytes=63 << 20
        ),
    )(
        tokens,
        out_grad,
        attn_gain,
        ffn_gain,
        query_weight,
        key_weight,
        value_weight,
        forget_weight.T,
        forget_bias,
        out_weight.T,
        gate_weight,
        up_weight,
        down_weight.T,
        doc_lengths,
    )
    finals = [
        ((rows, width), BF16),
        ((rows, width), BF16),
        ((width,), F32),
        ((block, cols), F32),
        ((block, cols), F32),
        ((block, cols), F32),
        ((heads, block), F32),
        ((heads, LANES), F32),
        ((block, cols), F32),
        ((width,), F32),
        ((block, units), F32),
        ((block, units), F32),
        ((block, units), F32),
    ]
    final = pl.pallas_call(
        narrow_kernel,
        out_shape=shapes_of(finals),
        in_specs=[VMEM] * len(outs),
        out_specs=[VMEM] * len(finals),
        compiler_params=pltpu.CompilerParams(vmem_limit_bytes=63 << 20),
    )(*made)
    return (
        *final[:6],
        final[6].T,
        final[7][:, 0],
        final[8].T,
        *final[9:12],
        final[12].T,
    )


def kernels_fit(tokens, forget_bias, gate_weight):
    rows, width = tokens.shape
    heads = forget_bias.shape[0]
    return (
        lax.axis_size("seq") == 8
        and lax.axis_size("head") == 4
        and heads == 6
        and rows == 2 * LANES
        and width % 256 == 0
        and gate_weight.shape[1] % (4 * LANES) == 0
        and width * gate_weight.shape[1] <= (1536 * 1024)
    )


def unchanged(carried):
    return carried


def contract_rows(left, right):
    return lax.dot_general(
        left, right, (((0,), (0,)), ((), ())), preferred_element_type=jnp.float32
    )


def contract_cols(left, right):
    return lax.dot_general(
        left, right, (((1,), (1,)), ((), ())), preferred_element_type=jnp.float32
    )


def norm_rows(values_in, gain):
    inverse = lax.rsqrt(jnp.mean(values_in * values_in, axis=-1, keepdims=True) + EPSILON)
    normed = values_in * inverse
    return (normed, inverse, normed * gain)


def norm_back(grad_in, normed, inverse, gain):
    scaled = grad_in * gain
    inner = jnp.mean(scaled * normed, axis=-1, keepdims=True)
    return (inverse * (scaled - normed * inner), jnp.sum(grad_in * normed, axis=0))


def doc_index(positions, doc_ends):
    return jnp.sum((positions[:, None] >= doc_ends[None, :]).astype(jnp.int32), axis=1)


def stored_positions(rows, n_seq, local_rows):
    half_rows = local_rows // 2
    device_of = rows // local_rows
    within = rows % local_rows
    group_of = jnp.where(within < half_rows, device_of, 2 * n_seq - 1 - device_of)
    return group_of * half_rows + within % half_rows


def block_scores(
    query_heads, key_heads, query_offsets, key_offsets, query_pos, key_pos, query_docs, key_docs
):
    raw_scores = jnp.einsum(
        "qhd,khd->hqk", query_heads, key_heads, preferred_element_type=jnp.float32
    )
    scores = (
        raw_scores * HEAD_DIM ** (-0.5) + query_offsets.T[:, :, None] - key_offsets.T[:, None, :]
    )
    allowed = (query_docs[:, None] == key_docs[None, :]) & (key_pos[None, :] <= query_pos[:, None])
    return (jnp.where(allowed[None], scores, MASKED), allowed)


def piece_grads(
    query_heads,
    grad_heads,
    log_mass,
    row_delta,
    query_offsets,
    key_heads,
    value_heads,
    key_offsets,
    query_pos,
    key_pos,
    query_docs,
    key_docs,
):
    scores, allowed = block_scores(
        query_heads, key_heads, query_offsets, key_offsets, query_pos, key_pos, query_docs, key_docs
    )
    probs = jnp.where(allowed[None], jnp.exp(scores - log_mass[:, :, None]), 0.0)
    grad_probs = jnp.einsum(
        "qhd,khd->hqk", grad_heads, value_heads, preferred_element_type=jnp.float32
    )
    grad_scores = (probs * (grad_probs - row_delta[:, :, None])).astype(jnp.bfloat16)
    score_sums = grad_scores.astype(jnp.float32)
    query_rows = query_heads.shape[0]
    key_rows = key_heads.shape[0]
    grad_query = jnp.einsum(
        "hqk,khd->qhd", grad_scores, key_heads, preferred_element_type=jnp.float32
    ).reshape(query_rows, -1)
    grad_key = (
        jnp.einsum("hqk,qhd->khd", grad_scores, query_heads, preferred_element_type=jnp.float32)
        * HEAD_DIM ** (-0.5)
    ).reshape(key_rows, -1)
    grad_value = jnp.einsum(
        "hqk,qhd->khd", probs.astype(jnp.bfloat16), grad_heads, preferred_element_type=jnp.float32
    ).reshape(key_rows, -1)
    return (
        grad_query,
        jnp.sum(score_sums, axis=2).T,
        grad_key,
        grad_value,
        -jnp.sum(score_sums, axis=1).T,
    )


def plain_body(
    tokens,
    attn_gain,
    query_weight,
    key_weight,
    value_weight,
    forget_weight,
    forget_bias,
    out_weight,
    ffn_gain,
    gate_weight,
    up_weight,
    down_weight,
    doc_lengths,
    out_grad,
):
    local_rows = tokens.shape[0]
    local_heads = forget_bias.shape[0]
    head_cols = local_heads * HEAD_DIM
    n_seq = lax.axis_size("seq")
    my_index = lax.axis_index("seq")
    first_row = my_index * local_rows
    docs = doc_lengths.shape[0]
    doc_ends = jnp.sum(jnp.where(jnp.tri(docs, dtype=jnp.bool_), doc_lengths[None, :], 0), axis=1)
    local_pos = stored_positions(
        first_row + jnp.arange(local_rows, dtype=jnp.int32), n_seq, local_rows
    )
    local_docs = doc_index(local_pos, doc_ends)
    pos_low = jnp.min(local_pos)
    pos_high = jnp.max(local_pos)
    doc_low = jnp.min(local_docs)
    doc_high = jnp.max(local_docs)
    hidden = gate_weight.shape[1]
    forget_pad = jnp.pad(forget_weight, ((0, 0), (0, 128 - local_heads)))
    w_attn = lax.all_gather(
        jnp.concatenate([query_weight, key_weight, value_weight, forget_pad], axis=1),
        "seq",
        axis=0,
        tiled=True,
    )
    w_rest = lax.all_gather(
        jnp.concatenate([out_weight.T, gate_weight, up_weight, down_weight.T], axis=1),
        "seq",
        axis=0,
        tiled=True,
    )
    w_query = w_attn[:, :head_cols]
    w_key = w_attn[:, head_cols : 2 * head_cols]
    w_value = w_attn[:, 2 * head_cols : 3 * head_cols]
    w_forget = w_attn[:, 3 * head_cols : 3 * head_cols + local_heads]
    w_out_t = w_rest[:, :head_cols]
    w_gate = w_rest[:, head_cols : head_cols + hidden]
    w_up = w_rest[:, head_cols + hidden : head_cols + 2 * hidden]
    w_down_t = w_rest[:, head_cols + 2 * hidden :]
    inputs = tokens.astype(jnp.float32)
    normed_one, inverse_one, scaled_one = norm_rows(inputs, attn_gain)
    h_one = scaled_one.astype(jnp.bfloat16)
    query_flat = jnp.dot(h_one, w_query, preferred_element_type=jnp.float32).astype(jnp.bfloat16)
    key_flat = jnp.dot(h_one, w_key, preferred_element_type=jnp.float32).astype(jnp.bfloat16)
    value_flat = jnp.dot(h_one, w_value, preferred_element_type=jnp.float32).astype(jnp.bfloat16)
    forget_logit = jnp.dot(h_one, w_forget, preferred_element_type=jnp.float32) + forget_bias
    log_forget_all = lax.all_gather(jax.nn.log_sigmoid(forget_logit), "seq", axis=0, tiled=True)
    all_pos = stored_positions(
        jnp.arange(n_seq * local_rows, dtype=jnp.int32), n_seq, local_rows
    )
    earlier = (all_pos[None, :] <= all_pos[:, None]).astype(jnp.float32)
    offsets_all = jnp.dot(earlier, log_forget_all, precision=HIGHEST)
    offsets = lax.dynamic_slice_in_dim(offsets_all, first_row, local_rows, 0)
    query_heads = query_flat.reshape(local_rows, local_heads, HEAD_DIM)
    key_heads = key_flat.reshape(local_rows, local_heads, HEAD_DIM)
    value_heads = value_flat.reshape(local_rows, local_heads, HEAD_DIM)

    def key_range(piece_rows):
        key_pos = stored_positions(jnp.arange(piece_rows, dtype=jnp.int32), n_seq, local_rows)
        key_docs = doc_index(key_pos, doc_ends)
        is_live = (
            (jnp.min(key_pos) <= pos_high)
            & (jnp.max(key_docs) >= doc_low)
            & (jnp.min(key_docs) <= doc_high)
        )
        return (key_pos, key_docs, offsets_all, is_live)

    mass_state = (
        jnp.full((local_heads, local_rows), MASKED, jnp.float32),
        jnp.zeros((local_heads, local_rows), jnp.float32),
    )
    gathered = lax.all_gather(
        jnp.concatenate([key_flat, value_flat, query_flat], axis=1), "seq", axis=0, tiled=True
    )
    key_block = gathered[:, :head_cols]
    piece_rows = key_block.shape[0]
    key_pos, key_docs, key_offsets, is_live = key_range(piece_rows)

    def mass_update(carried_in):
        running_max, running_sum = carried_in
        scores, allowed = block_scores(
            query_heads,
            key_block.reshape(piece_rows, local_heads, HEAD_DIM),
            offsets,
            key_offsets,
            local_pos,
            key_pos,
            local_docs,
            key_docs,
        )
        new_max = jnp.maximum(running_max, jnp.max(scores, axis=2))
        weights = jnp.where(allowed[None], jnp.exp(scores - new_max[:, :, None]), 0.0)
        return (new_max, jnp.sum(weights, axis=2))

    running_max, running_sum = lax.cond(is_live, mass_update, unchanged, mass_state)
    log_mass = running_max + jnp.log(running_sum)
    start_state = (
        jnp.zeros((local_heads, local_rows, HEAD_DIM), jnp.float32),
        jnp.zeros((local_heads, local_rows, HEAD_DIM), jnp.float32),
    )
    attend_key_block = key_block
    value_block = gathered[:, head_cols : 2 * head_cols]
    attend_piece_rows = attend_key_block.shape[0]
    attend_key_pos, attend_key_docs, attend_key_offsets, is_live = key_range(attend_piece_rows)

    def attend_update(carried_in):
        scores, allowed = block_scores(
            query_heads,
            attend_key_block.reshape(attend_piece_rows, local_heads, HEAD_DIM),
            offsets,
            attend_key_offsets,
            local_pos,
            attend_key_pos,
            local_docs,
            attend_key_docs,
        )
        probs = jnp.where(allowed[None], jnp.exp(scores - log_mass[:, :, None]), 0.0)
        probs_low = probs.astype(jnp.bfloat16)
        remainder = (probs - probs_low.astype(jnp.float32)).astype(jnp.bfloat16)
        value_piece = value_block.reshape(attend_piece_rows, local_heads, HEAD_DIM)
        rounded_acc = jnp.einsum(
            "hqk,khd->hqd", probs_low, value_piece, preferred_element_type=jnp.float32
        )
        remainder_acc = jnp.einsum(
            "hqk,khd->hqd", remainder, value_piece, preferred_element_type=jnp.float32
        )
        return (rounded_acc, remainder_acc)

    rounded_acc, remainder_acc = lax.cond(is_live, attend_update, unchanged, start_state)
    attended_rows = rounded_acc.transpose(1, 0, 2)
    exact_rows = (rounded_acc + remainder_acc).transpose(1, 0, 2)
    mixed = attended_rows.reshape(local_rows, head_cols).astype(jnp.bfloat16)
    attn_part = contract_cols(mixed, w_out_t)
    middle = inputs + lax.psum(attn_part, "head")
    normed_two, inverse_two, scaled_two = norm_rows(middle, ffn_gain)
    h_two = scaled_two.astype(jnp.bfloat16)
    gate_value = jnp.dot(h_two, w_gate, preferred_element_type=jnp.float32)
    up_value = jnp.dot(h_two, w_up, preferred_element_type=jnp.float32)
    gate_sigmoid = jax.nn.sigmoid(gate_value)
    gate_silu = gate_value * gate_sigmoid
    activation = (gate_silu * up_value).astype(jnp.bfloat16)
    ffn_part = contract_cols(activation, w_down_t)
    layer_out = (
        middle + lax.psum(ffn_part.astype(jnp.bfloat16), "head").astype(jnp.float32)
    ).astype(jnp.bfloat16)
    grad_act = jnp.dot(out_grad, w_down_t, preferred_element_type=jnp.float32)
    grad_gate = (
        grad_act * up_value * gate_sigmoid * (1.0 + gate_value * (1.0 - gate_sigmoid))
    ).astype(jnp.bfloat16)
    grad_up = (grad_act * gate_silu).astype(jnp.bfloat16)
    part_two = contract_cols(grad_gate, w_gate) + contract_cols(grad_up, w_up)
    grad_two = lax.psum(part_two, "head")
    back_two, gain_two = norm_back(grad_two, normed_two, inverse_two, ffn_gain)
    grad_middle = out_grad.astype(jnp.float32) + back_two
    grad_attn = grad_middle.astype(jnp.bfloat16)
    grad_mixed = jnp.dot(grad_attn, w_out_t, preferred_element_type=jnp.float32).astype(
        jnp.bfloat16
    )
    grad_heads = grad_mixed.reshape(local_rows, local_heads, HEAD_DIM)
    row_delta = jnp.sum(grad_heads.astype(jnp.float32) * exact_rows, axis=2).T
    back_state = (
        jnp.zeros((local_rows, head_cols), jnp.float32),
        jnp.zeros((local_rows, local_heads), jnp.float32),
    )
    back_key_block = key_block
    back_value_block = value_block
    back_piece_rows = back_key_block.shape[0]
    back_key_pos, back_key_docs, back_key_offsets, is_live = key_range(back_piece_rows)

    def back_update(carried_in):
        terms = piece_grads(
            query_heads,
            grad_heads,
            log_mass,
            row_delta,
            offsets,
            back_key_block.reshape(back_piece_rows, local_heads, HEAD_DIM),
            back_value_block.reshape(back_piece_rows, local_heads, HEAD_DIM),
            back_key_offsets,
            local_pos,
            back_key_pos,
            local_docs,
            back_key_docs,
        )
        return (terms[0], terms[1])

    grad_query, grad_query_off = lax.cond(is_live, back_update, unchanged, back_state)
    stats = lax.all_gather(
        jnp.concatenate([log_mass.T, row_delta.T], axis=1), "seq", axis=0, tiled=True
    )
    stats_mass, stats_delta = stats[:, :local_heads], stats[:, local_heads:]
    key_state = (
        jnp.zeros((local_rows, head_cols), jnp.float32),
        jnp.zeros((local_rows, head_cols), jnp.float32),
        jnp.zeros((local_rows, local_heads), jnp.float32),
    )
    piece_query = gathered[:, 2 * head_cols :]
    piece_grad = lax.all_gather(grad_mixed, "seq", axis=0, tiled=True)
    key_piece_rows = piece_query.shape[0]
    piece_pos = stored_positions(jnp.arange(key_piece_rows, dtype=jnp.int32), n_seq, local_rows)
    piece_docs = doc_index(piece_pos, doc_ends)
    is_live = (
        (pos_low <= jnp.max(piece_pos))
        & (jnp.max(piece_docs) >= doc_low)
        & (jnp.min(piece_docs) <= doc_high)
    )

    def key_update(carried_in):
        piece_mass = stats_mass.T
        piece_delta = stats_delta.T
        terms = piece_grads(
            piece_query.reshape(key_piece_rows, local_heads, HEAD_DIM),
            piece_grad.reshape(key_piece_rows, local_heads, HEAD_DIM),
            piece_mass,
            piece_delta,
            offsets_all,
            key_heads,
            value_heads,
            offsets,
            piece_pos,
            local_pos,
            piece_docs,
            local_docs,
        )
        return (terms[2], terms[3], terms[4])

    grad_key, grad_value, grad_key_off = lax.cond(is_live, key_update, unchanged, key_state)
    grad_query_low = (grad_query * HEAD_DIM ** (-0.5)).astype(jnp.bfloat16)
    grad_key_low = grad_key.astype(jnp.bfloat16)
    grad_value_low = grad_value.astype(jnp.bfloat16)
    grad_offsets = grad_query_off + grad_key_off
    grad_off_all = lax.all_gather(grad_offsets, "seq", axis=0, tiled=True)
    later = (all_pos[None, :] >= local_pos[:, None]).astype(jnp.float32)
    grad_log = jnp.dot(later, grad_off_all, precision=HIGHEST)
    grad_logit = grad_log * jax.nn.sigmoid(-forget_logit)
    forget_table = w_forget.astype(jnp.float32)
    part_one = (
        contract_cols(grad_query_low, w_query)
        + contract_cols(grad_key_low, w_key)
        + contract_cols(grad_value_low, w_value)
        + lax.dot_general(grad_logit, forget_table, (((1,), (1,)), ((), ())), precision=HIGHEST)
    )
    grad_one = lax.psum(part_one.astype(jnp.bfloat16), "head").astype(jnp.float32)
    back_one, gain_one = norm_back(grad_one, normed_one, inverse_one, attn_gain)
    tokens_grad = (grad_middle + back_one).astype(jnp.bfloat16)
    forget_term = lax.dot_general(
        h_one.astype(jnp.float32), grad_logit, (((0,), (0,)), ((), ())), precision=HIGHEST
    )
    scatter_cols = [
        contract_rows(grad_attn, mixed),
        contract_rows(h_two, grad_gate),
        contract_rows(h_two, grad_up),
        contract_rows(out_grad, activation),
        contract_rows(h_one, grad_query_low),
        contract_rows(h_one, grad_key_low),
        contract_rows(h_one, grad_value_low),
        jnp.pad(forget_term, ((0, 0), (0, 128 - local_heads))),
    ]
    first_sum = lax.psum_scatter(
        jnp.concatenate([t.astype(jnp.bfloat16) for t in scatter_cols[:4]], axis=1),
        "seq",
        scatter_dimension=0,
        tiled=True,
    ).astype(jnp.float32)
    second_sum = lax.psum_scatter(
        jnp.concatenate([t.astype(jnp.bfloat16) for t in scatter_cols[4:]], axis=1),
        "seq",
        scatter_dimension=0,
        tiled=True,
    ).astype(jnp.float32)
    out_weight_grad = first_sum[:, :head_cols].T
    gate_weight_grad = first_sum[:, head_cols : head_cols + hidden]
    up_weight_grad = first_sum[:, head_cols + hidden : head_cols + 2 * hidden]
    down_weight_grad = first_sum[:, head_cols + 2 * hidden :].T
    query_weight_grad = second_sum[:, :head_cols]
    key_weight_grad = second_sum[:, head_cols : 2 * head_cols]
    value_weight_grad = second_sum[:, 2 * head_cols : 3 * head_cols]
    forget_weight_grad = second_sum[:, 3 * head_cols : 3 * head_cols + local_heads]
    attn_gain_grad, ffn_gain_grad, forget_bias_grad = lax.psum(
        (gain_one, gain_two, jnp.sum(grad_logit, axis=0)), "seq"
    )
    return (
        layer_out,
        tokens_grad,
        attn_gain_grad,
        query_weight_grad,
        key_weight_grad,
        value_weight_grad,
        forget_weight_grad,
        forget_bias_grad,
        out_weight_grad,
        ffn_gain_grad,
        gate_weight_grad,
        up_weight_grad,
        down_weight_grad,
    )


def body(*args):
    fits = kernels_fit(args[0], args[6], args[9])
    return (kernel_body if fits else plain_body)(*args)


def solution(mesh):
    return jax.shard_map(
        body,
        mesh=mesh,
        in_specs=(
            P("seq", None),
            P(),
            P("seq", "head"),
            P("seq", "head"),
            P("seq", "head"),
            P("seq", "head"),
            P("head"),
            P("head", "seq"),
            P(),
            P("seq", "head"),
            P("seq", "head"),
            P("head", "seq"),
            P(),
            P("seq", None),
        ),
        out_specs=(
            P("seq", None),
            P("seq", None),
            P(),
            P("seq", "head"),
            P("seq", "head"),
            P("seq", "head"),
            P("seq", "head"),
            P("head"),
            P("head", "seq"),
            P(),
            P("seq", "head"),
            P("seq", "head"),
            P("head", "seq"),
        ),
        check_vma=False,
    )
```

```python
import jax
import jax.numpy as jnp
from jax import lax
from jax.experimental import pallas as pl
from jax.experimental.pallas import tpu as pltpu
from jax.sharding import PartitionSpec as P

HEAD_DIM = 64
EPSILON = 1e-06
HIGHEST = lax.Precision.HIGHEST
MASKED = -1e30
MESH_ID = pl.DeviceIdType.MESH
F32 = jnp.float32
BF16 = jnp.bfloat16
LANES = 128
KEY_TILES = ((0, 0), (0, 1), (1, 0))
VALUE_TILES = ((1, 1), (2, 0), (2, 1))
OUT_TILES = ((0, 1), (1, 0), (1, 1))
NEAR_FIRST = (1, 3, 2)


def dot_nn(left, right):
    return jnp.dot(left, right, preferred_element_type=F32)


def dot_nt(left, right):
    return lax.dot_general(left, right, (((1,), (1,)), ((), ())), preferred_element_type=F32)


def dot_tn(left, right):
    return lax.dot_general(left, right, (((0,), (0,)), ((), ())), preferred_element_type=F32)


def rows_of(first, count):
    return pl.ds(pl.multiple_of(first, 16), count)


def add_to(ref, other):
    ref[...] = (ref[...].astype(F32) + other[...].astype(F32)).astype(BF16)


class Net:
    def __init__(self, sems):
        s = lax.axis_index("seq")
        h = lax.axis_index("head")
        self.line = 4
        self.z, self.x = s // 2, s % 2
        self.y, self.c = h // 2, h % 2
        self.inner = (self.z == 1) | (self.z == 2)
        self.group = self.z * 2 + self.y
        self.sems = sems
        self.used = 0
        self.pending = []

    def alloc(self, count):
        first = self.used
        self.used += count
        return first

    def to(self, z=None, x=None, y=None, c=None):
        z = self.z if z is None else z
        x = self.x if x is None else x
        y = self.y if y is None else y
        c = self.c if c is None else c
        return (z * 2 + x, y * 2 + c)

    def by_distance(self):
        low = self.z < 2
        nearest = self.z + 1 - 2 * (self.z % 2)
        return (nearest, jnp.where(low, 2, 1), jnp.where(low, 3, 0))

    def side(self):
        return self.to(x=1 - self.x)

    def lower(self):
        return self.to(c=1 - self.c)

    def upper(self):
        return self.to(y=1 - self.y)

    def next(self, step):
        return (self.z + step) % self.line

    def announce(self):
        sem = pltpu.get_barrier_semaphore()
        peers = [self.side(), self.lower(), self.upper()]
        peers.append(self.to(x=1 - self.x, c=1 - self.c))
        peers.append(self.to(y=1 - self.y, c=1 - self.c))
        for step in range(1, self.line):
            z = self.next(step)
            peers += [self.to(z=z), self.to(z=z, c=1 - self.c)]
            peers += [self.to(z=z, x=1 - self.x), self.to(z=z, y=1 - self.y)]
        for peer in peers:
            pl.semaphore_signal(sem, 1, device_id=peer, device_id_type=MESH_ID)
        self.peers = len(peers)

    def await_peers(self):
        pl.semaphore_wait(pltpu.get_barrier_semaphore(), self.peers)

    def copy(self, src, dst, send, recv, device):
        return pltpu.make_async_remote_copy(
            src_ref=src,
            dst_ref=dst,
            send_sem=self.sems.at[send],
            recv_sem=self.sems.at[recv],
            device_id=device,
            device_id_type=MESH_ID,
        )

    def begin(self, made):
        made.start()
        self.pending.append(made.wait_send)
        return made

    def begin_if(self, condition, made):
        pl.when(condition)(made.start)
        self.pending.append(lambda: pl.when(condition)(made.wait_send))

    def send(self, src, dst, device):
        first = self.alloc(2)
        return self.begin(self.copy(src, dst, first, first + 1, device))

    def got(self, ref, recv):
        self.copy(ref, ref, recv, recv, self.side()).wait_recv()

    def drain(self):
        for wait in self.pending:
            wait()
        self.pending = []


class RowGather:
    def __init__(self, net, slot, lower=None):
        self.net = net
        self.slot = slot
        self.low = lower
        self.sent = net.alloc(4)
        self.came = net.alloc(4)
        self.up_sent = net.alloc(4)
        self.up_came = net.alloc(4)
        self.low_sent = net.alloc(8)
        self.low_came = net.alloc(8)

    def pass_low(self, y, z):
        if self.low is not None:
            net = self.net
            index = y * 4 + z
            block = self.slot(y, z)
            net.begin(
                net.copy(
                    block, block, self.low_sent + index, self.low_came + index, net.lower()
                )
            )

    def pass_up(self, z):
        net = self.net
        block = self.slot(net.y, z)
        net.begin(net.copy(block, block, self.up_sent + z, self.up_came + z, net.upper()))
        self.pass_low(net.y, z)

    def along(self, src, to):
        net = self.net
        block = self.slot(net.y, src)
        return net.copy(block, block, self.sent + to, self.came + src, net.to(z=to))

    def start(self):
        net = self.net
        for to in range(net.line):
            gap = jnp.abs(to - net.z)
            net.begin_if((gap > 0) & (gap < 3), self.along(net.z, to))
        self.pass_up(net.z)

    def forward(self):
        net = self.net
        for src in net.by_distance():
            net.got(self.slot(net.y, src), self.came + src)
            self.pass_up(src)
        far = net.by_distance()[2]
        net.begin_if(net.inner, self.along(far, 3 - far))

    def finish(self):
        net = self.net
        for src in (net.z,) + net.by_distance():
            net.got(self.slot(1 - net.y, src), self.up_came + src)
            self.pass_low(1 - net.y, src)
        if self.low is not None:
            for y in range(2):
                for z in range(4):
                    net.got(self.low(y, z), self.low_came + y * 4 + z)


class RowSum:
    def __init__(self, net, slot, recv_up, recv_line):
        self.net = net
        self.slot = slot
        self.recv_up = recv_up
        self.recv_line = recv_line
        self.up_sent = net.alloc(4)
        self.up_came = net.alloc(4)
        self.sent = net.alloc(4)
        self.came = net.alloc(4)

    def start(self):
        net = self.net
        for z in net.by_distance()[::-1] + (net.z,):
            net.begin(
                net.copy(
                    self.slot(1 - net.y, z),
                    self.recv_up(z),
                    self.up_sent + z,
                    self.up_came + z,
                    net.upper(),
                )
            )

    def add_up(self, z):
        self.net.got(self.recv_up(z), self.up_came + z)
        add_to(self.slot(self.net.y, z), self.recv_up(z))

    def along(self, target, hop, place):
        net = self.net
        return net.copy(
            self.slot(net.y, target),
            self.recv_line(place),
            self.sent + target,
            self.came + place,
            net.to(z=hop),
        )

    def middle(self):
        net = self.net
        nearest, other, far = net.by_distance()
        self.add_up(far)
        net.begin_if(jnp.logical_not(net.inner), self.along(far, nearest, nearest))
        for z in (other, nearest):
            self.add_up(z)
            net.begin(self.along(z, z, net.z))

        @pl.when(net.inner)
        def _():
            net.got(self.recv_line(net.z), self.came + net.z)
            add_to(self.slot(net.y, far), self.recv_line(net.z))

        net.begin_if(net.inner, self.along(far, far, net.z))
        self.add_up(net.z)

    def result(self):
        net = self.net
        nearest, other, far = net.by_distance()

        @pl.when(jnp.logical_not(net.inner))
        def _():
            self.recv_line(far)[...] = jnp.zeros_like(self.recv_line(far))

        total = self.slot(net.y, net.z)[...].astype(F32)
        for z in (nearest, other):
            net.got(self.recv_line(z), self.came + z)
            total = total + self.recv_line(z)[...].astype(F32)
        pl.when(net.inner)(lambda: net.got(self.recv_line(far), self.came + far))
        return total + self.recv_line(far)[...].astype(F32)


class CrossGather:
    def __init__(self, net, slot):
        self.net = net
        self.slot = slot

    def start(self):
        net = self.net
        mine = self.slot(net.x, net.c)
        self.across = net.send(mine, mine, net.side())
        self.low = net.send(mine, mine, net.lower())

    def forward(self):
        net = self.net
        self.across.wait_recv()
        other = self.slot(1 - net.x, net.c)
        self.both = net.send(other, other, net.lower())

    def finish(self):
        self.low.wait_recv()
        self.both.wait_recv()


class Direct:
    def __init__(self, net, me, peers):
        self.net = net
        self.me = me
        self.peers = peers
        self.sent = net.alloc(8)
        self.came = net.alloc(8)

    def start(self, made, slot):
        net = self.net
        for at, (index, device) in enumerate(self.peers):
            net.begin(
                net.copy(
                    made(index), slot(self.me), self.sent + at, self.came + self.me, device
                )
            )

    def finish(self, slot):
        for index, _ in self.peers:
            self.net.got(slot(index), self.came + index)


class WeightSpread:
    def __init__(self, net, stage, full):
        self.net = net
        self.stage = stage
        self.full = full
        self.block = stage.shape[1]
        self.sent = net.alloc(2)
        self.came = net.alloc(4)
        self.side_sent = net.alloc(4)
        self.side_came = net.alloc(4)
        self.low_sent = net.alloc(8)
        self.low_came = net.alloc(8)
        self.first = (net.z // 2) == net.c

    def slot(self, z, x):
        return self.full.at[rows_of((z * 2 + x) * self.block, self.block), :]

    def away(self, u):
        net = self.net
        return net.copy(
            self.stage.at[u],
            self.slot(net.z, net.x),
            self.sent + u,
            self.came + net.z,
            net.to(z=2 * net.c + u),
        )

    def across(self, z):
        net = self.net
        block = self.slot(z, net.x)
        return net.copy(block, block, self.side_sent + z, self.side_came + z, net.side())

    def low(self, z, x):
        block = self.slot(z, x)
        index = z * 2 + x
        return self.net.copy(
            block, block, self.low_sent + index, self.low_came + index, self.net.lower()
        )

    def start(self):
        net = self.net
        for u in range(2):
            pl.when(2 * net.c + u != net.z)(lambda u=u: self.away(u).start())

        @pl.when(self.first)
        def _():
            self.slot(net.z, net.x)[...] = self.stage[net.z % 2]
            self.across(net.z).start()
            self.low(net.z, net.x).start()

    def forward(self):
        net = self.net

        @pl.when(self.first)
        def _():
            for step in NEAR_FIRST:
                src = net.next(step)
                net.got(self.slot(src, net.x), self.came + src)
                self.across(src).start()
                self.low(src, net.x).start()

    def finish(self):
        net = self.net

        @pl.when(self.first)
        def _():
            for step in (0,) + NEAR_FIRST:
                src = net.next(step)
                net.got(self.slot(src, 1 - net.x), self.side_came + src)
                self.low(src, 1 - net.x).start()

        @pl.when(jnp.logical_not(self.first))
        def _():
            for z in range(4):
                for x in range(2):
                    net.got(self.slot(z, x), self.low_came + z * 2 + x)

    def drain(self):
        net = self.net
        for u in range(2):
            pl.when(2 * net.c + u != net.z)(lambda u=u: self.away(u).wait_send())

        @pl.when(self.first)
        def _():
            for z in range(4):
                self.across(z).wait_send()
                for x in range(2):
                    self.low(z, x).wait_send()


class HiddenSpread:
    def __init__(self, net, stage, full):
        self.net = net
        self.stage = stage
        self.full = full
        self.block = stage.shape[1]
        self.sent = net.alloc(4)
        self.came = net.alloc(4)
        self.side_sent = net.alloc(4)
        self.side_came = net.alloc(4)

    def slot(self, z, x):
        return self.full.at[rows_of((z * 2 + x) * self.block, self.block), :]

    def across(self, z):
        net = self.net
        block = self.slot(z, net.x)
        net.begin(net.copy(block, block, self.side_sent + z, self.side_came + z, net.side()))

    def start(self):
        net = self.net
        self.slot(net.z, net.x)[...] = self.stage[net.z]
        for step in NEAR_FIRST:
            to = net.next(step)
            net.begin(
                net.copy(
                    self.stage.at[to],
                    self.slot(net.z, net.x),
                    self.sent + step,
                    self.came + net.z,
                    net.to(z=to),
                )
            )
        self.across(net.z)

    def forward(self):
        net = self.net
        for step in NEAR_FIRST:
            src = net.next(step)
            net.got(self.slot(src, net.x), self.came + src)
            self.across(src)

    def finish(self):
        net = self.net
        for z in range(4):
            net.got(self.slot(z, 1 - net.x), self.side_came + z)


class WeightSum:
    def __init__(self, net, grads, recv_low, recv_side, final):
        self.net = net
        self.grads = grads
        self.recv_low = recv_low
        self.recv_side = recv_side
        self.final = final
        self.block = final.shape[1]
        self.side_sent = net.alloc(2)
        self.side_came = net.alloc(2)
        self.sent = net.alloc(2)
        self.came = net.alloc(2)

    def rows(self, z, x):
        return self.grads.at[rows_of((z * 2 + x) * self.block, self.block), :]

    def start(self):
        net = self.net
        half = 4 * self.block
        self.low = net.send(
            self.grads.at[rows_of((1 - net.c) * half, half), :], self.recv_low, net.lower()
        )

    def second(self):
        net = self.net
        self.low.wait_recv()
        for x in (1 - net.x, net.x):
            for i in range(2):
                z = 2 * net.c + i
                add_to(
                    self.rows(z, x), self.recv_low.at[rows_of((i * 2 + x) * self.block, self.block)]
                )
        for i in range(2):
            net.begin(
                net.copy(
                    self.rows(2 * net.c + i, 1 - net.x),
                    self.recv_side.at[i],
                    self.side_sent + i,
                    self.side_came + i,
                    net.side(),
                )
            )

    def owner(self, i):
        net = self.net
        z = 2 * net.c + i
        made = net.copy(
            self.rows(z, net.x),
            self.final.at[net.z % 2],
            self.sent + i,
            self.came + net.z % 2,
            net.to(z=z, c=net.z // 2),
        )
        return (z == net.z) & (net.z // 2 == net.c), made

    def third(self):
        net = self.net
        for i in range(2):
            net.got(self.recv_side.at[i], self.side_came + i)
            mine = self.rows(2 * net.c + i, net.x)
            add_to(mine, self.recv_side.at[i])
            local, made = self.owner(i)

            @pl.when(local)
            def _():
                self.final[net.z % 2] = mine[...]

            pl.when(jnp.logical_not(local))(made.start)

    def finish(self):
        net = self.net
        for u in range(2):
            pl.when(2 * net.c + u != net.z)(
                lambda u=u: net.got(self.final.at[u], self.came + u)
            )

    def drain(self):
        for i in range(2):
            local, made = self.owner(i)
            pl.when(jnp.logical_not(local))(made.wait_send)


class HiddenSum:
    def __init__(self, net, grads, recv_side, final):
        self.net = net
        self.grads = grads
        self.recv_side = recv_side
        self.final = final
        self.block = final.shape[1]
        self.side_sent = net.alloc(4)
        self.side_came = net.alloc(4)
        self.sent = net.alloc(4)
        self.came = net.alloc(4)

    def rows(self, z, x):
        return self.grads.at[rows_of((z * 2 + x) * self.block, self.block), :]

    def start(self):
        net = self.net
        for step in (2, 1, 3, 0):
            z = net.next(step)
            net.begin(
                net.copy(
                    self.rows(z, 1 - net.x),
                    self.recv_side.at[z],
                    self.side_sent + z,
                    self.side_came + z,
                    net.side(),
                )
            )

    def second(self):
        net = self.net
        for step in (2, 1, 3, 0):
            z = net.next(step)
            net.got(self.recv_side.at[z], self.side_came + z)
            mine = self.rows(z, net.x)
            add_to(mine, self.recv_side.at[z])
            if step:
                net.begin(
                    net.copy(
                        mine,
                        self.final.at[net.z],
                        self.sent + step,
                        self.came + net.z,
                        net.to(z=z),
                    )
                )
            else:
                self.final[net.z] = mine[...]

    def finish(self):
        net = self.net
        for step in NEAR_FIRST:
            src = net.next(step)
            net.got(self.final.at[src], self.came + src)


class Places:
    def __init__(self, net, chunk):
        self.net = net
        self.chunk = chunk
        self.part = 4 * chunk
        self.all = 32 * chunk

    def position(self, at):
        chunk = self.chunk
        late = at // (16 * chunk)
        x = (at // (8 * chunk)) % 2
        c = (at // (4 * chunk)) % 2
        z = (at // chunk) % 4
        owner = 2 * z + x
        group = jnp.where(late == 0, owner, 15 - owner)
        return group * (2 * chunk) + c * chunk + at % chunk

    def own(self, late):
        return (late * 4 + self.net.x * 2 + self.net.c) * self.part

    def every(self, shape, axis):
        return self.position(lax.broadcasted_iota(jnp.int32, shape, axis))


def doc_starts(positions, doc_ref):
    start = jnp.zeros(positions.shape, jnp.int32)
    end = jnp.int32(0)
    for k in range(doc_ref.shape[0] - 1):
        end = end + doc_ref[k]
        start = jnp.where(positions >= end, end, start)
    return start


def running_sums(places, rows_in, spread, gather):
    tiles = places.all // LANES
    chunk = places.chunk
    row = lax.broadcasted_iota(jnp.int32, (LANES, LANES), 0)
    col = lax.broadcasted_iota(jnp.int32, (LANES, LANES), 1)
    within = ((row // chunk == col // chunk) & (row <= col)).astype(F32)
    stacked = jnp.concatenate(
        [rows_in[:, k * LANES : (k + 1) * LANES] for k in range(tiles)], axis=0
    )
    inside = jnp.dot(stacked, within, precision=HIGHEST, preferred_element_type=F32)
    outside = jnp.dot(rows_in, spread[...], precision=HIGHEST, preferred_element_type=F32)
    outside = outside[:, : gather.shape[0]]
    outside = jnp.dot(outside, gather[...], precision=HIGHEST, preferred_element_type=F32)
    return outside + jnp.concatenate(
        [inside[k * 8 : (k + 1) * 8, :] for k in range(tiles)], axis=1
    )


def order_tables(places, spread, gather):
    order = places.every((places.all, LANES), 0) // places.chunk
    slot = lax.broadcasted_iota(jnp.int32, (places.all, LANES), 1)
    spread[...] = (order < slot).astype(F32)
    order = places.every(gather.shape, 1) // places.chunk
    slot = lax.broadcasted_iota(jnp.int32, gather.shape, 0)
    gather[...] = (order == slot).astype(F32)


def tile_of(ref, rows, tile):
    return ref[rows, tile * LANES : (tile + 1) * LANES]


def only(values_in, lane, side):
    return jnp.where(lane // HEAD_DIM == side, values_in, jnp.zeros_like(values_in))


def norm_grad(grad_in, values_in, gain):
    inverse = lax.rsqrt(jnp.mean(values_in * values_in, axis=-1, keepdims=True) + EPSILON)
    normed = values_in * inverse
    scaled = grad_in * gain
    inner = jnp.mean(scaled * normed, axis=-1, keepdims=True)
    return inverse * (scaled - normed * inner), jnp.sum(grad_in * normed, axis=0, keepdims=True)


def norm(values_in, gain):
    inverse = lax.rsqrt(jnp.mean(values_in * values_in, axis=-1, keepdims=True) + EPSILON)
    return (values_in * inverse * gain).astype(BF16)


def to_columns(rows_in, first=0):
    many = rows_in.shape[1]
    parts = [rows_in, jnp.zeros((LANES - 8 - first, many), F32)]
    if first:
        parts = [jnp.zeros((first, many), F32)] + parts
    return jnp.concatenate(parts, axis=0).T


def gather_quarters(net, ref):
    chunk = ref.shape[0] // 4

    def piece(y):
        return ref.at[rows_of((2 * y + net.c) * chunk, chunk), :]

    up = net.send(piece(net.y), piece(net.y), net.upper())
    first = net.send(piece(net.y), piece(net.y), net.lower())

    def second():
        up.wait_recv()
        other = net.send(piece(1 - net.y), piece(1 - net.y), net.lower())

        def last():
            first.wait_recv()
            other.wait_recv()

        return last

    return second


def layer_kernel(
    tokens,
    out_grad,
    gain_one,
    gain_two,
    wq,
    wk,
    wv,
    forget_t,
    bias_in,
    wo_t,
    wg,
    wu,
    wd_t,
    doc_ref,
    layer_out,
    tokens_grad,
    gains,
    bias_grad,
    late_final,
    last_final,
    early_final,
    ffn_final,
    stage_attn,
    stage_out,
    stage_bias,
    other_bias,
    h_one,
    allowed,
    spread,
    gather,
    logit_parts,
    queries,
    keyval,
    offsets,
    mass,
    logits,
    mixed,
    exact,
    middle,
    normed_two,
    out_grads,
    w_attn,
    w_out,
    w_ffn,
    all_query,
    all_grad,
    ffn_grads,
    part_two,
    part_out,
    two_low,
    two_up,
    two_line,
    out_low,
    out_up,
    out_line,
    ffn_sum,
    ffn_side,
    late_sum,
    late_low,
    late_side,
    last_sum,
    last_low,
    last_side,
    early_sum,
    early_low,
    early_side,
    grad_attn,
    grad_heads,
    stats,
    off_parts,
    every_off,
    grad_qkv,
    grad_offs,
    part_one,
    one_up,
    one_line,
    gain_parts,
    gain_swap,
    own_tokens,
    all_forget,
    own_logits,
    near_sems,
    sems,
):
    net = Net(sems)
    net.announce()
    z, x, y, c = net.z, net.x, net.y, net.c
    width = tokens.shape[1]
    chunk = tokens.shape[0] // 4
    part = 4 * chunk
    places = Places(net, chunk)
    hidden = wg.shape[1] // 4
    own = rows_of((2 * y + c) * chunk, chunk)
    tile = 256
    scale_one = gain_one[...].reshape(1, width)
    scale_two = gain_two[...].reshape(1, width)

    token_net = RowGather(net, lambda yy, zz: grad_attn.at[yy, rows_of(zz * chunk, chunk), :])
    weight_net = WeightSpread(net, stage_attn, w_attn)
    out_net = WeightSpread(net, stage_out, w_out)
    units_net = HiddenSpread(net, ffn_side, w_ffn)
    kv_nets = [
        CrossGather(net, lambda xx, cc, late=late: keyval.at[late, xx, cc]) for late in range(2)
    ]
    sub = chunk // 2
    pieces = [slice(0, sub), slice(sub, chunk)]

    def piece_of(ref, k):
        return lambda zz: ref.at[zz, pieces[k], :]

    def rows_at(ref, k):
        return lambda yy, zz: ref.at[yy, rows_of(zz * chunk + k * sub, sub), :]

    logit_net = CrossGather(net, lambda xx, cc: logit_parts.at[xx, cc])
    two_nets = [
        RowGather(
            net,
            lambda yy, zz, k=k: normed_two.at[c, yy, zz, pieces[k], :],
            lambda yy, zz, k=k: normed_two.at[1 - c, yy, zz, pieces[k], :],
        )
        for k in range(2)
    ]
    given_net = RowGather(
        net, lambda yy, zz: out_grads.at[c, yy, zz], lambda yy, zz: out_grads.at[1 - c, yy, zz]
    )
    attn_sums = [
        RowSum(net, rows_at(part_one, k), piece_of(one_up, k), piece_of(one_line, k))
        for k in range(2)
    ]

    def groups():
        found = [(z * 2 + 1 - y, net.upper())]
        for step in range(1, 4):
            far = net.next(step)
            found.append((far * 2 + y, net.to(z=far)))
            found.append((far * 2 + 1 - y, net.to(z=far, y=1 - y)))
        return found

    forget_net = Direct(net, net.group, groups())
    logit_back = Direct(net, net.group, groups())
    rest = [(z * 2 + 1 - x, net.side())]
    for step in range(1, 4):
        far = net.next(step)
        rest.append((far * 2 + x, net.to(z=far)))
        rest.append((far * 2 + 1 - x, net.to(z=far, x=1 - x)))
    gain_net = Direct(net, z * 2 + x, rest)
    corner = net.to(y=1 - y, c=1 - c)
    last_gain = Direct(
        net,
        y * 2 + c,
        [(y * 2 + 1 - c, net.lower()), (2 - 2 * y + c, net.upper()), (3 - 2 * y - c, corner)],
    )

    near = [
        (tokens.at[own, :], own_tokens),
        (tokens.at[own, :], grad_attn.at[y, rows_of(z * chunk, chunk), :]),
        (out_grad.at[own, :], out_grads.at[c, y, z]),
    ]
    for index, ref in enumerate((wg, wu, wd_t)):
        for zz in range(4):
            near.append(
                (
                    ref.at[:, zz * hidden : (zz + 1) * hidden],
                    ffn_side.at[zz, :, index * hidden : (index + 1) * hidden],
                )
            )
    fetched = [
        pltpu.make_async_copy(src, dst, near_sems.at[at]) for at, (src, dst) in enumerate(near)
    ]
    for copy in fetched:
        copy.start()
    half_cols = wq.shape[1] // 2
    half_heads = half_cols // HEAD_DIM
    block = wq.shape[0]
    forget = forget_t[...].astype(F32)
    row8 = lax.broadcasted_iota(jnp.int32, (8, LANES), 0)
    for u in range(2):
        cols = slice(u * half_cols, (u + 1) * half_cols)
        for index, ref in enumerate((wk, wv)):
            stage_attn[u, :, index * half_cols : (index + 1) * half_cols] = ref[:, cols]
        rows8 = jnp.concatenate(
            [
                forget[u * half_heads : (u + 1) * half_heads, :],
                jnp.zeros((8 - half_heads, block), F32),
            ],
            axis=0,
        )
        rows8 = jnp.concatenate([rows8, jnp.zeros((8, 2 * LANES - block), F32)], axis=1)
        stage_attn[u, :, 4 * LANES :] = to_columns(rows8, HEAD_DIM)[:block].astype(BF16)
        stage_attn[u, :, 2 * half_cols : 3 * half_cols] = wq[:, cols]
        biases = jnp.zeros((8, LANES), F32)
        for head in range(half_heads):
            biases = jnp.where(row8 == head, bias_in[u * half_heads + head], biases)
        stage_bias[u] = biases
    net.await_peers()
    for copy in fetched[:3]:
        copy.wait()
    weight_net.start()
    token_net.start()
    bias_send = net.send(stage_bias, other_bias, net.lower())
    for u in range(2):
        stage_out[u, :, :HEAD_DIM] = jnp.zeros((block, HEAD_DIM), BF16)
        stage_out[u, :, HEAD_DIM:] = wo_t[:, u * half_cols : (u + 1) * half_cols]

    order_tables(places, spread, gather)
    every = places.every((1, places.all), 1)
    for late in range(2):
        at = places.own(late) + lax.broadcasted_iota(jnp.int32, (part, 1), 0)
        pos = places.position(at)
        start = doc_starts(pos, doc_ref)
        seen = (every <= pos) & (every >= start)
        allowed[late * part : (late + 1) * part, :] = jnp.where(seen, 0.0, MASKED).astype(BF16)

    weight_net.forward()
    token_net.forward()
    given_net.start()
    h_one[y] = norm(grad_attn[y].astype(F32), scale_one)
    token_net.finish()
    h_one[1 - y] = norm(grad_attn[1 - y].astype(F32), scale_one)
    weight_net.finish()

    for late in range(2):
        keyval[late, x, c] = dot_nn(h_one[late], w_attn[:, : 3 * LANES]).astype(BF16)
        kv_nets[late].start()
    bias_send.wait_recv()
    bias = jnp.where(weight_net.first, stage_bias[z % 2], other_bias[z % 2])[:, :1]
    for late in range(2):
        r = slice(late * part, (late + 1) * part)
        made = dot_nn(h_one[late], w_attn[:, 3 * LANES :])
        logit_parts[x, c, :, r] = made[:, LANES:].T[HEAD_DIM : HEAD_DIM + 8, :] + bias
        queries[r, :] = (made.astype(BF16).astype(F32) * HEAD_DIM ** (-0.5)).astype(BF16)
    logit_net.start()
    all_forget[net.group] = w_attn[:, 4 * LANES :].astype(F32).T[HEAD_DIM : HEAD_DIM + 8, :]
    forget_net.start(lambda index: all_forget.at[net.group], lambda index: all_forget.at[index])
    out_net.start()
    for copy in fetched[3:]:
        copy.wait()
    units_net.start()

    logit_net.forward()
    given_net.forward()
    logit_net.finish()
    for late in range(2):
        for xx in range(2):
            for cc in range(2):
                at = (late * 4 + xx * 2 + cc) * part
                logits[:, at : at + part] = logit_parts[xx, cc, :, late * part : (late + 1) * part]
    turned = logits[...]
    logs = jnp.minimum(turned, 0.0) - jnp.log(1.0 + jnp.exp(-jnp.abs(turned)))
    offsets[...] = running_sums(places, logs, spread, gather)
    kv_nets[0].forward()
    kv_nets[1].forward()
    out_net.forward()
    kv_nets[0].finish()

    lane = lax.broadcasted_iota(jnp.int32, (LANES, LANES), 1)
    first = (lane // HEAD_DIM) == 0
    for block in range(2 * part // LANES):
        r = slice(block * LANES, (block + 1) * LANES)
        late = (block * LANES) // part
        many = places.all // 2 * (late + 1)
        made, kept = [], []
        masses = jnp.zeros((LANES, LANES), F32)
        for head in range(3):
            tile_k, side_k = KEY_TILES[head]
            tile_v, side_v = VALUE_TILES[head]
            keys = keyval[: late + 1, :, :, :, tile_k * LANES : (tile_k + 1) * LANES]
            values = keyval[: late + 1, :, :, :, tile_v * LANES : (tile_v + 1) * LANES]
            keys, values = keys.reshape(many, LANES), values.reshape(many, LANES)
            scores = (
                dot_nt(only(tile_of(queries, r, tile_k), lane, side_k), keys)
                - offsets[head : head + 1, :many]
                + allowed[r, :many].astype(F32)
            )
            top = jnp.max(scores, axis=1, keepdims=True)
            probs = jnp.exp(scores - top)
            total = jnp.sum(probs, axis=1, keepdims=True)
            high = probs.astype(BF16)
            rest = (probs - high.astype(F32)).astype(BF16)
            share = 1.0 / total
            rounded = dot_nn(high, values)
            made.append(rounded * share)
            kept.append((rounded + dot_nn(rest, values)) * share)
            masses = jnp.where(lane == head, top + jnp.log(total), masses)
        mass[r, :] = masses
        mixed[r, :LANES] = jnp.where(first, 0.0, made[0]).astype(BF16)
        mixed[r, LANES:] = jnp.where(first, made[1], made[2]).astype(BF16)
        exact[r, :LANES] = jnp.where(first, 0.0, kept[0])
        exact[r, LANES:] = jnp.where(first, kept[1], kept[2])
        if block == 1:
            out_net.finish()
            kv_nets[1].finish()

    def project(late):
        rows = rows_of(late * part, part)
        for at in range(0, width, tile):
            cols = slice(at, at + tile)
            part_one[late, :, cols] = dot_nt(mixed[rows, :], w_out[cols, :]).astype(BF16)

    project(1 - y)
    for attn_sum in attn_sums:
        attn_sum.start()
    project(y)
    for attn_sum in attn_sums:
        attn_sum.middle()
    units_net.forward()
    earlier, net.pending = net.pending, []
    for k in range(2):
        total = own_tokens[pieces[k], :].astype(F32) + attn_sums[k].result()
        middle[pieces[k], :] = total
        normed_two[c, y, z, pieces[k], :] = norm(total, scale_two)
        two_nets[k].start()
    given_net.finish()
    two_nets[0].forward()
    units_net.finish()
    two_nets[0].finish()

    half_heads = half_cols
    tiles = [slice(at, at + tile) for at in range(0, width, tile)]

    query_net = CrossGather(net, lambda xx, cc: all_query.at[:, xx, cc])
    grad_net = CrossGather(net, lambda xx, cc: all_grad.at[:, xx, cc])
    stat_net = CrossGather(net, lambda xx, cc: stats.at[xx, cc])
    off_net = CrossGather(net, lambda xx, cc: off_parts.at[xx, cc])
    attn_nets = [RowGather(net, rows_at(grad_attn, k)) for k in range(2)]

    def own_parts(ref, k):
        return lambda yy, zz: ref.at[k, c, rows_of(yy * 4 * sub + zz * sub, sub), :]

    twos = [
        RowSum(net, own_parts(part_two, k), piece_of(two_up, k), piece_of(two_line, k))
        for k in range(2)
    ]
    outs = [
        RowSum(net, own_parts(part_out, k), piece_of(out_up, k), piece_of(out_line, k))
        for k in range(2)
    ]
    ones = [
        RowSum(net, rows_at(part_one, k), piece_of(one_up, k), piece_of(one_line, k))
        for k in range(2)
    ]
    ffn_net = HiddenSum(net, ffn_sum, ffn_side, ffn_final)
    late_net = WeightSum(net, late_sum, late_low, late_side, late_final)
    last_net = WeightSum(net, last_sum, last_low, last_side, last_final)
    early_net = WeightSum(net, early_sum, early_low, early_side, early_final)

    for late in range(2):
        all_query[late, x, c] = queries[late * part : (late + 1) * part, :]
    for wait in earlier:
        wait()
    query_net.start()

    def units_of(k):
        for cc in range(2):
            inputs = normed_two[cc, :, :, pieces[k], :].reshape(part, width)
            given = out_grads[cc, :, :, pieces[k], :].reshape(part, width)
            gate = dot_nn(inputs, w_ffn[:, :hidden])
            up = dot_nn(inputs, w_ffn[:, hidden : 2 * hidden])
            grad_act = dot_nn(given, w_ffn[:, 2 * hidden :])
            sigmoid = 1.0 / (1.0 + jnp.exp(-gate))
            silu = gate * sigmoid
            ffn_grads[k, cc, :, :hidden] = (
                grad_act * up * sigmoid * (1.0 + gate * (1.0 - sigmoid))
            ).astype(BF16)
            ffn_grads[k, cc, :, hidden : 2 * hidden] = (grad_act * silu).astype(BF16)
            ffn_grads[k, cc, :, 2 * hidden :] = (silu * up).astype(BF16)

    def lower_of(parts, recv, k, cols):
        def back(cc):
            for r in tiles:
                parts[k, cc, :, r] = dot_nt(ffn_grads[k, cc, :, cols], w_ffn[r, cols]).astype(BF16)

        back(1 - c)
        made = net.send(parts.at[k, 1 - c], recv.at[k], net.lower())
        back(c)
        return made

    def upper_of(made, parts, recv, k, sums):
        made.wait_recv()
        parts[k, c] = (parts[k, c].astype(F32) + recv[k].astype(F32)).astype(BF16)
        sums[k].start()

    def unit_grads(some):
        for cols in some:
            both = [0.0, 0.0]
            for k in range(2):
                left = normed_two[:, :, :, pieces[k], cols].reshape(2 * part, tile)
                right = ffn_grads[k].reshape(2 * part, 3 * hidden)
                both[0] = both[0] + dot_tn(left, right[:, : 2 * hidden])
                left = out_grads[:, :, :, pieces[k], cols].reshape(2 * part, tile)
                both[1] = both[1] + dot_tn(left, right[:, 2 * hidden :])
            ffn_sum[cols, : 2 * hidden] = both[0].astype(BF16)
            ffn_sum[cols, 2 * hidden :] = both[1].astype(BF16)

    units_of(0)
    two_nets[1].forward()
    to_lower = slice(0, 2 * hidden)
    first_low = lower_of(part_two, two_low, 0, to_lower)
    two_nets[1].finish()
    units_of(1)
    upper_of(first_low, part_two, two_low, 0, twos)
    second_low = lower_of(part_two, two_low, 1, to_lower)
    twos[0].middle()
    upper_of(second_low, part_two, two_low, 1, twos)
    unit_grads(tiles[:3])
    twos[1].middle()
    unit_grads(tiles[3:])
    query_net.forward()
    ffn_net.start()
    grad_middle = []
    gain_two_part = 0.0
    for k in range(2):
        back_two, part_gain = norm_grad(twos[k].result(), middle[pieces[k], :], scale_two)
        gain_two_part = gain_two_part + part_gain
        grad_middle.append(out_grads[c, y, z, pieces[k], :].astype(F32) + back_two)
        grad_attn[y, rows_of(z * chunk + k * sub, sub), :] = grad_middle[k].astype(BF16)
        attn_nets[k].start()
    to_out = slice(2 * hidden, 3 * hidden)
    out_sends = [lower_of(part_out, out_low, 0, to_out), None]
    attn_nets[0].forward()
    out_sends[1] = lower_of(part_out, out_low, 1, to_out)
    every = places.every((1, places.all), 1)
    own_pos = [
        places.position(places.own(late) + lax.broadcasted_iota(jnp.int32, (part, 1), 0))
        for late in range(2)
    ]
    attn_nets[1].forward()
    attn_nets[0].finish()
    query_net.finish()
    attn_nets[1].finish()

    lane = lax.broadcasted_iota(jnp.int32, (part, LANES), 1)
    for late in range(2):
        r = slice(late * part, (late + 1) * part)
        made = dot_nn(grad_attn[late], w_out[...])
        grad_heads[r, :] = made.astype(BF16)
        all_grad[late, x, c] = grad_heads[r, :]
    grad_net.start()
    for late in range(2):
        r = slice(late * part, (late + 1) * part)
        delta = jnp.zeros((part, LANES), F32)
        for head, (tile_o, side_o) in enumerate(OUT_TILES):
            product = tile_of(grad_heads, r, tile_o).astype(F32) * tile_of(exact, r, tile_o)
            inner = jnp.sum(only(product, lane, side_o), axis=1, keepdims=True)
            delta = jnp.where(lane == head, inner, delta)
        grad_offs[r, :] = delta
    stats[x, c, :8, :] = mass[...].T[:8, :]
    stats[x, c, 8:, :] = grad_offs[...].T[:8, :]
    stat_net.start()

    for cols in tiles:
        left = grad_attn[:, :, cols].reshape(2 * part, tile)
        early_sum[cols, :] = dot_tn(left, mixed[...]).astype(BF16)
    early_net.start()
    for k in range(2):
        upper_of(out_sends[k], part_out, out_low, k, outs)
    ffn_net.second()

    lane = lax.broadcasted_iota(jnp.int32, (LANES, LANES), 1)
    first = (lane // HEAD_DIM) == 0
    for block in range(2 * part // LANES):
        r = slice(block * LANES, (block + 1) * LANES)
        late = (block * LANES) // part
        many = places.all // 2 * (late + 1)
        made = []
        sums = jnp.zeros((LANES, LANES), F32)
        for head in range(3):
            tile_k, side_k = KEY_TILES[head]
            tile_v, side_v = VALUE_TILES[head]
            tile_o, side_o = OUT_TILES[head]
            keys = keyval[: late + 1, :, :, :, tile_k * LANES : (tile_k + 1) * LANES]
            values = keyval[: late + 1, :, :, :, tile_v * LANES : (tile_v + 1) * LANES]
            keys, values = keys.reshape(many, LANES), values.reshape(many, LANES)
            scores = (
                dot_nt(only(tile_of(queries, r, tile_k), lane, side_k), keys)
                - offsets[head : head + 1, :many]
                + allowed[r, :many].astype(F32)
            )
            probs = jnp.exp(scores - mass[r, head : head + 1])
            grad_probs = dot_nt(only(tile_of(grad_heads, r, tile_o), lane, side_o), values)
            grad_scores = (probs * (grad_probs - grad_offs[r, head : head + 1])).astype(BF16)
            made.append(dot_nn(grad_scores, keys) * HEAD_DIM ** (-0.5))
            row_sum = jnp.sum(grad_scores.astype(F32), axis=1, keepdims=True)
            sums = jnp.where(lane == head, row_sum, sums)
        grad_qkv[r, 3 * LANES : 4 * LANES] = jnp.where(first, made[0], made[1]).astype(BF16)
        grad_qkv[r, 4 * LANES :] = jnp.where(first, made[2], 0.0).astype(BF16)
        grad_offs[r, :] = sums
        if block == 0:
            grad_net.forward()
            stat_net.forward()
        if block == 1:
            for out in outs:
                out.middle()
            early_net.second()

    starts = doc_starts(every, doc_ref)
    for late in range(2):
        seen = (own_pos[late] <= every) & (own_pos[late] >= starts)
        allowed[late * part : (late + 1) * part, :] = jnp.where(seen, 0.0, MASKED).astype(BF16)
    stat_net.finish()
    grad_net.finish()
    for late in range(2):
        for xx in range(2):
            for cc in range(2):
                at = (late * 4 + xx * 2 + cc) * part
                piece = slice(late * part, (late + 1) * part)
                every_off[0, :, at : at + part] = stats[xx, cc, :8, piece]
                every_off[1, :, at : at + part] = stats[xx, cc, 8:, piece]

    own_offs = [
        to_columns(offsets[:, pl.ds(pl.multiple_of(places.own(late), LANES), part)])
        for late in range(2)
    ]
    for block in range(2 * part // LANES):
        r = slice(block * LANES, (block + 1) * LANES)
        late = (block * LANES) // part
        within = slice(block * LANES - late * part, (block + 1) * LANES - late * part)
        many = places.all // 2 * (2 - late)
        lanes = slice(places.all - many, places.all)
        keys_made, values_made = [], []
        sums = jnp.zeros((LANES, LANES), F32)
        for head in range(3):
            tile_k, side_k = KEY_TILES[head]
            tile_v, side_v = VALUE_TILES[head]
            tile_o, side_o = OUT_TILES[head]
            asked = all_query[late:, :, :, :, tile_k * LANES : (tile_k + 1) * LANES]
            given = all_grad[late:, :, :, :, tile_o * LANES : (tile_o + 1) * LANES]
            asked, given = asked.reshape(many, LANES), given.reshape(many, LANES)
            key = keyval[late, x, c, within, tile_k * LANES : (tile_k + 1) * LANES]
            value = keyval[late, x, c, within, tile_v * LANES : (tile_v + 1) * LANES]
            scores = (
                dot_nt(only(key, lane, side_k), asked)
                - own_offs[late][within, head : head + 1]
                + allowed[r, lanes].astype(F32)
            )
            probs = jnp.exp(scores - every_off[0, head : head + 1, lanes])
            grad_probs = dot_nt(only(value, lane, side_v), given)
            grad_scores = (probs * (grad_probs - every_off[1, head : head + 1, lanes])).astype(
                BF16
            )
            keys_made.append(dot_nn(grad_scores, asked))
            values_made.append(dot_nn(probs.astype(BF16), given))
            col_sum = jnp.sum(grad_scores.astype(F32), axis=1, keepdims=True)
            sums = jnp.where(lane == head, col_sum, sums)
        for at, (left, right) in enumerate(
            (
                (keys_made[0], keys_made[1]),
                (keys_made[2], values_made[0]),
                (values_made[1], values_made[2]),
            )
        ):
            grad_qkv[r, at * LANES : (at + 1) * LANES] = jnp.where(first, left, right).astype(BF16)
        grad_offs[r, :] = grad_offs[r, :] - sums
        if block == 1:
            early_net.third()
    off_parts[x, c] = grad_offs[...].T[:8, :]
    off_net.start()

    def back(late):
        rows = rows_of(late * part, part)
        for r in tiles:
            part_one[late, :, r] = dot_nt(grad_qkv[rows, :], w_attn[r, :]).astype(BF16)

    back(1 - y)
    for one in ones:
        one.start()
    back(y)
    off_net.forward()
    cut = late_sum.shape[1]
    for cols in tiles:
        left = h_one[:, :, cols].reshape(2 * part, tile)
        late_sum[cols, :] = dot_tn(left, grad_qkv[:, :cut]).astype(BF16)
    late_net.start()
    ones[0].middle()
    off_net.finish()
    for late in range(2):
        for xx in range(2):
            for cc in range(2):
                at = (late * 4 + xx * 2 + cc) * part
                every_off[0, :, at : at + part] = off_parts[
                    xx, cc, :, late * part : (late + 1) * part
                ]
    given = every_off[0]
    whole = jnp.sum(given, axis=1, keepdims=True)
    grad_logs = whole - running_sums(places, given, spread, gather) + given
    grad_logits = grad_logs / (1.0 + jnp.exp(logits[...]))
    every_off[1] = grad_logits

    def rows_for(index):
        at = places.own(index % 2) + (index // 4) * LANES
        return every_off.at[1, :, pl.ds(pl.multiple_of(at, LANES), LANES)]

    logit_back.start(rows_for, lambda index: own_logits.at[index])
    own_logits[net.group] = rows_for(net.group)[...]
    ones[1].middle()
    late_net.second()
    for late in range(2):
        r = slice(late * part, (late + 1) * part)
        mine = every_off[1, :, pl.ds(pl.multiple_of(places.own(late), LANES), part)]
        held = grad_qkv[r, cut:]
        lane = lax.broadcasted_iota(jnp.int32, (part, LANES), 1)
        grad_qkv[r, cut:] = jnp.where(
            lane // HEAD_DIM == 0, held, to_columns(mine, HEAD_DIM).astype(BF16)
        )
    for cols in tiles:
        left = h_one[:, :, cols].reshape(2 * part, tile)
        last_sum[cols, :] = dot_tn(left, grad_qkv[:, cut:]).astype(BF16)
    last_net.start()
    late_net.third()
    logit_back.finish(lambda index: own_logits.at[index])
    forget_net.finish(lambda index: all_forget.at[index])
    held = own_logits[...].reshape(8 * 8, LANES)
    held = jnp.where(z % 2 == 0, held[:, :chunk], held[:, chunk:]).astype(BF16)
    forget_part = dot_tn(held, all_forget[...].reshape(8 * 8, width).astype(BF16))
    last_net.second()
    for k in range(2):
        layer_out[rows_of((2 * y + c) * chunk + k * sub, sub), :] = (
            middle[pieces[k], :] + outs[k].result()
        ).astype(BF16)
    layer_second = gather_quarters(net, layer_out)
    gain_one_part = 0.0
    for k in range(2):
        back_one, part_gain = norm_grad(
            ones[k].result() + forget_part[pieces[k], :],
            own_tokens[pieces[k], :].astype(F32),
            scale_one,
        )
        gain_one_part = gain_one_part + part_gain
        tokens_grad[rows_of((2 * y + c) * chunk + k * sub, sub), :] = (
            grad_middle[k] + back_one
        ).astype(BF16)
    grad_second = gather_quarters(net, tokens_grad)
    cells = width // 4
    gain_mine = gain_parts.at[z * 2 + x]
    gain_mine[:, :cells] = jnp.concatenate(
        [g[:, k * cells : (k + 1) * cells] for g in (gain_one_part, gain_two_part) for k in range(4)],
        axis=0,
    )
    gain_mine[:, cells:] = jnp.broadcast_to(
        jnp.sum(grad_logits, axis=1, keepdims=True), (8, LANES)
    )
    gain_net.start(lambda index: gain_mine, lambda index: gain_parts.at[index])
    last_net.third()
    layer_last = layer_second()
    grad_last = grad_second()

    gain_net.finish(lambda index: gain_parts.at[index])
    total = gain_parts[0, :, :cells]
    for index in range(1, 8):
        total = total + gain_parts[index, :, :cells]
    gain_swap[y * 2 + c] = total
    last_gain.start(lambda index: gain_swap.at[y * 2 + c], lambda index: gain_swap.at[index])
    for u in range(2):
        bias_grad[u] = gain_parts[(2 * c + u) * 2 + x, :, cells:]

    ffn_net.finish()
    early_net.finish()
    last_gain.finish(lambda index: gain_swap.at[index])
    total = gain_swap[0]
    for index in range(1, 4):
        total = total + gain_swap[index]
    gains[...] = total

    late_net.finish()
    last_net.finish()
    layer_last()
    grad_last()
    for part_net in (weight_net, out_net, late_net, last_net, early_net, net):
        part_net.drain()


def narrow_kernel(
    layer,
    tokens,
    gains,
    biases,
    late,
    last,
    early,
    units,
    layer_out,
    tokens_grad,
    gain_one,
    g_query,
    g_key,
    g_value,
    g_forget,
    g_bias,
    g_out,
    gain_two,
    g_gate,
    g_up,
    g_down,
):
    layer_out[...] = layer[...]
    tokens_grad[...] = tokens[...]
    for k, ref in enumerate((gain_one, gain_two)):
        ref[...] = jnp.concatenate(
            [gains[4 * k + at : 4 * k + at + 1, :] for at in range(4)], axis=1
        )[0]
    half = g_query.shape[1] // 2
    heads = half // HEAD_DIM
    hidden = units.shape[2] // 3
    block = g_query.shape[0]
    for u in range(2):
        cols = slice(u * half, (u + 1) * half)
        got = late[u].astype(F32)
        rest = last[u].astype(F32)
        g_key[:, cols] = got[:, :half]
        g_value[:, cols] = got[:, half : 2 * half]
        g_query[:, cols] = jnp.concatenate([got[:, 2 * half :], rest[:, :HEAD_DIM]], axis=1)
        g_out[:, cols] = early[u, :, HEAD_DIM:].astype(F32)
        padded = jnp.concatenate([rest, jnp.zeros((2 * LANES - block, LANES), F32)], axis=0)
        g_forget[u * heads : (u + 1) * heads, :] = padded.T[HEAD_DIM : HEAD_DIM + heads, :block]
    each = jnp.concatenate([biases[0, :heads, :], biases[1, :heads, :]], axis=0)
    g_bias[...] = each
    for zz in range(4):
        cols = slice(zz * hidden, (zz + 1) * hidden)
        for index, ref in enumerate((g_gate, g_up, g_down)):
            ref[:, cols] = units[zz, :, index * hidden : (index + 1) * hidden].astype(F32)


VMEM = pl.BlockSpec(memory_space=pltpu.VMEM)
SMEM = pl.BlockSpec(memory_space=pltpu.SMEM)
HBM = pl.BlockSpec(memory_space=pl.ANY)


def shapes_of(made):
    return [jax.ShapeDtypeStruct(*m) for m in made]


def layer_shapes(rows, width, heads, hidden):
    chunk = rows // 4
    part = 4 * chunk
    every = 32 * chunk
    block = width // 8
    attn = (3 * heads * HEAD_DIM // 2) + HEAD_DIM
    cut = attn - LANES
    outs = [
        ((rows, width), BF16),
        ((rows, width), BF16),
        ((8, width // 4), F32),
        ((2, 8, LANES), F32),
        ((2, block, cut), BF16),
        ((2, block, LANES), BF16),
        ((2, block, 2 * LANES), BF16),
        ((4, block, 3 * hidden), BF16),
    ]

    def weight_sum(columns):
        return [
            ((width, columns), BF16),
            ((width // 2, columns), BF16),
            ((2, block, columns), BF16),
        ]

    row_sum = [((2, part, width), BF16), ((4, chunk, width), BF16), ((4, chunk, width), BF16)]
    scratch = [
        ((2, block, attn), BF16),
        ((2, block, 2 * LANES), BF16),
        ((2, 8, LANES), F32),
        ((2, 8, LANES), F32),
        ((2, part, width), BF16),
        ((2 * part, every), BF16),
        ((every, LANES), F32),
        ((every // chunk, every), F32),
        ((2, 2, 8, 2 * part), F32),
        ((2 * part, 2 * LANES), BF16),
        ((2, 2, 2, part, 3 * LANES), BF16),
        ((8, every), F32),
        ((2 * part, LANES), F32),
        ((8, every), F32),
        ((2 * part, 2 * LANES), BF16),
        ((2 * part, 2 * LANES), F32),
        ((chunk, width), F32),
        ((2, 2, 4, chunk, width), BF16),
        ((2, 2, 4, chunk, width), BF16),
        ((width, attn), BF16),
        ((width, 2 * LANES), BF16),
        ((width, 3 * hidden), BF16),
        ((2, 2, 2, part, 2 * LANES), BF16),
        ((2, 2, 2, part, 2 * LANES), BF16),
        ((2, 2, part, 3 * hidden), BF16),
        ((2, 2, part, width), BF16),
        ((2, 2, part, width), BF16),
        *row_sum,
        *row_sum,
        ((width, 3 * hidden), BF16),
        ((4, block, 3 * hidden), BF16),
        *weight_sum(cut),
        *weight_sum(LANES),
        *weight_sum(2 * LANES),
        ((2, part, width), BF16),
        ((2 * part, 2 * LANES), BF16),
        ((2, 2, 16, 2 * part), F32),
        ((2, 2, 8, 2 * part), F32),
        ((2, 8, every), F32),
        ((2 * part, attn), BF16),
        ((2 * part, LANES), F32),
        *row_sum,
        ((8, 8, width // 4 + LANES), F32),
        ((4, 8, width // 4), F32),
        ((chunk, width), BF16),
        ((8, 8, width), F32),
        ((8, 8, LANES), F32),
    ]
    return outs, scratch


def kernel_body(
    tokens,
    attn_gain,
    query_weight,
    key_weight,
    value_weight,
    forget_weight,
    forget_bias,
    out_weight,
    ffn_gain,
    gate_weight,
    up_weight,
    down_weight,
    doc_lengths,
    out_grad,
):
    heads = forget_bias.shape[0]
    rows, width = tokens.shape
    block, units = gate_weight.shape
    cols = query_weight.shape[1]
    outs, scratch = layer_shapes(rows, width, heads, units // 4)
    made = pl.pallas_call(
        layer_kernel,
        out_shape=shapes_of(outs),
        in_specs=[HBM] * 2 + [VMEM] * 6 + [SMEM] + [VMEM] + [HBM] * 3 + [SMEM],
        out_specs=[VMEM] * len(outs),
        scratch_shapes=[pltpu.VMEM(*m) for m in scratch] + [pltpu.SemaphoreType.DMA((15,)), pltpu.SemaphoreType.DMA((640,))],
        compiler_params=pltpu.CompilerParams(
            collective_id=0, has_side_effects=True, vmem_limit_bytes=63 << 20
        ),
    )(
        tokens,
        out_grad,
        attn_gain,
        ffn_gain,
        query_weight,
        key_weight,
        value_weight,
        forget_weight.T,
        forget_bias,
        out_weight.T,
        gate_weight,
        up_weight,
        down_weight.T,
        doc_lengths,
    )
    finals = [
        ((rows, width), BF16),
        ((rows, width), BF16),
        ((width,), F32),
        ((block, cols), F32),
        ((block, cols), F32),
        ((block, cols), F32),
        ((heads, block), F32),
        ((heads, LANES), F32),
        ((block, cols), F32),
        ((width,), F32),
        ((block, units), F32),
        ((block, units), F32),
        ((block, units), F32),
    ]
    final = pl.pallas_call(
        narrow_kernel,
        out_shape=shapes_of(finals),
        in_specs=[VMEM] * len(outs),
        out_specs=[VMEM] * len(finals),
        compiler_params=pltpu.CompilerParams(vmem_limit_bytes=63 << 20),
    )(*made)
    return (
        *final[:6],
        final[6].T,
        final[7][:, 0],
        final[8].T,
        *final[9:12],
        final[12].T,
    )


def kernels_fit(tokens, forget_bias, gate_weight):
    rows, width = tokens.shape
    heads = forget_bias.shape[0]
    return (
        lax.axis_size("seq") == 8
        and lax.axis_size("head") == 4
        and heads == 6
        and rows == 2 * LANES
        and width % 256 == 0
        and gate_weight.shape[1] % (4 * LANES) == 0
        and width * gate_weight.shape[1] <= (1536 * 1024)
    )


def unchanged(carried):
    return carried


def contract_rows(left, right):
    return lax.dot_general(
        left, right, (((0,), (0,)), ((), ())), preferred_element_type=jnp.float32
    )


def contract_cols(left, right):
    return lax.dot_general(
        left, right, (((1,), (1,)), ((), ())), preferred_element_type=jnp.float32
    )


def norm_rows(values_in, gain):
    inverse = lax.rsqrt(jnp.mean(values_in * values_in, axis=-1, keepdims=True) + EPSILON)
    normed = values_in * inverse
    return (normed, inverse, normed * gain)


def norm_back(grad_in, normed, inverse, gain):
    scaled = grad_in * gain
    inner = jnp.mean(scaled * normed, axis=-1, keepdims=True)
    return (inverse * (scaled - normed * inner), jnp.sum(grad_in * normed, axis=0))


def doc_index(positions, doc_ends):
    return jnp.sum((positions[:, None] >= doc_ends[None, :]).astype(jnp.int32), axis=1)


def stored_positions(rows, n_seq, local_rows):
    half_rows = local_rows // 2
    device_of = rows // local_rows
    within = rows % local_rows
    group_of = jnp.where(within < half_rows, device_of, 2 * n_seq - 1 - device_of)
    return group_of * half_rows + within % half_rows


def block_scores(
    query_heads, key_heads, query_offsets, key_offsets, query_pos, key_pos, query_docs, key_docs
):
    raw_scores = jnp.einsum(
        "qhd,khd->hqk", query_heads, key_heads, preferred_element_type=jnp.float32
    )
    scores = (
        raw_scores * HEAD_DIM ** (-0.5) + query_offsets.T[:, :, None] - key_offsets.T[:, None, :]
    )
    allowed = (query_docs[:, None] == key_docs[None, :]) & (key_pos[None, :] <= query_pos[:, None])
    return (jnp.where(allowed[None], scores, MASKED), allowed)


def piece_grads(
    query_heads,
    grad_heads,
    log_mass,
    row_delta,
    query_offsets,
    key_heads,
    value_heads,
    key_offsets,
    query_pos,
    key_pos,
    query_docs,
    key_docs,
):
    scores, allowed = block_scores(
        query_heads, key_heads, query_offsets, key_offsets, query_pos, key_pos, query_docs, key_docs
    )
    probs = jnp.where(allowed[None], jnp.exp(scores - log_mass[:, :, None]), 0.0)
    grad_probs = jnp.einsum(
        "qhd,khd->hqk", grad_heads, value_heads, preferred_element_type=jnp.float32
    )
    grad_scores = (probs * (grad_probs - row_delta[:, :, None])).astype(jnp.bfloat16)
    score_sums = grad_scores.astype(jnp.float32)
    query_rows = query_heads.shape[0]
    key_rows = key_heads.shape[0]
    grad_query = jnp.einsum(
        "hqk,khd->qhd", grad_scores, key_heads, preferred_element_type=jnp.float32
    ).reshape(query_rows, -1)
    grad_key = (
        jnp.einsum("hqk,qhd->khd", grad_scores, query_heads, preferred_element_type=jnp.float32)
        * HEAD_DIM ** (-0.5)
    ).reshape(key_rows, -1)
    grad_value = jnp.einsum(
        "hqk,qhd->khd", probs.astype(jnp.bfloat16), grad_heads, preferred_element_type=jnp.float32
    ).reshape(key_rows, -1)
    return (
        grad_query,
        jnp.sum(score_sums, axis=2).T,
        grad_key,
        grad_value,
        -jnp.sum(score_sums, axis=1).T,
    )


def plain_body(
    tokens,
    attn_gain,
    query_weight,
    key_weight,
    value_weight,
    forget_weight,
    forget_bias,
    out_weight,
    ffn_gain,
    gate_weight,
    up_weight,
    down_weight,
    doc_lengths,
    out_grad,
):
    local_rows = tokens.shape[0]
    local_heads = forget_bias.shape[0]
    head_cols = local_heads * HEAD_DIM
    n_seq = lax.axis_size("seq")
    my_index = lax.axis_index("seq")
    first_row = my_index * local_rows
    docs = doc_lengths.shape[0]
    doc_ends = jnp.sum(jnp.where(jnp.tri(docs, dtype=jnp.bool_), doc_lengths[None, :], 0), axis=1)
    local_pos = stored_positions(
        first_row + jnp.arange(local_rows, dtype=jnp.int32), n_seq, local_rows
    )
    local_docs = doc_index(local_pos, doc_ends)
    pos_low = jnp.min(local_pos)
    pos_high = jnp.max(local_pos)
    doc_low = jnp.min(local_docs)
    doc_high = jnp.max(local_docs)
    hidden = gate_weight.shape[1]
    forget_pad = jnp.pad(forget_weight, ((0, 0), (0, 128 - local_heads)))
    w_attn = lax.all_gather(
        jnp.concatenate([query_weight, key_weight, value_weight, forget_pad], axis=1),
        "seq",
        axis=0,
        tiled=True,
    )
    w_rest = lax.all_gather(
        jnp.concatenate([out_weight.T, gate_weight, up_weight, down_weight.T], axis=1),
        "seq",
        axis=0,
        tiled=True,
    )
    w_query = w_attn[:, :head_cols]
    w_key = w_attn[:, head_cols : 2 * head_cols]
    w_value = w_attn[:, 2 * head_cols : 3 * head_cols]
    w_forget = w_attn[:, 3 * head_cols : 3 * head_cols + local_heads]
    w_out_t = w_rest[:, :head_cols]
    w_gate = w_rest[:, head_cols : head_cols + hidden]
    w_up = w_rest[:, head_cols + hidden : head_cols + 2 * hidden]
    w_down_t = w_rest[:, head_cols + 2 * hidden :]
    inputs = tokens.astype(jnp.float32)
    normed_one, inverse_one, scaled_one = norm_rows(inputs, attn_gain)
    h_one = scaled_one.astype(jnp.bfloat16)
    query_flat = jnp.dot(h_one, w_query, preferred_element_type=jnp.float32).astype(jnp.bfloat16)
    key_flat = jnp.dot(h_one, w_key, preferred_element_type=jnp.float32).astype(jnp.bfloat16)
    value_flat = jnp.dot(h_one, w_value, preferred_element_type=jnp.float32).astype(jnp.bfloat16)
    forget_logit = jnp.dot(h_one, w_forget, preferred_element_type=jnp.float32) + forget_bias
    log_forget_all = lax.all_gather(jax.nn.log_sigmoid(forget_logit), "seq", axis=0, tiled=True)
    all_pos = stored_positions(
        jnp.arange(n_seq * local_rows, dtype=jnp.int32), n_seq, local_rows
    )
    earlier = (all_pos[None, :] <= all_pos[:, None]).astype(jnp.float32)
    offsets_all = jnp.dot(earlier, log_forget_all, precision=HIGHEST)
    offsets = lax.dynamic_slice_in_dim(offsets_all, first_row, local_rows, 0)
    query_heads = query_flat.reshape(local_rows, local_heads, HEAD_DIM)
    key_heads = key_flat.reshape(local_rows, local_heads, HEAD_DIM)
    value_heads = value_flat.reshape(local_rows, local_heads, HEAD_DIM)

    def key_range(piece_rows):
        key_pos = stored_positions(jnp.arange(piece_rows, dtype=jnp.int32), n_seq, local_rows)
        key_docs = doc_index(key_pos, doc_ends)
        is_live = (
            (jnp.min(key_pos) <= pos_high)
            & (jnp.max(key_docs) >= doc_low)
            & (jnp.min(key_docs) <= doc_high)
        )
        return (key_pos, key_docs, offsets_all, is_live)

    mass_state = (
        jnp.full((local_heads, local_rows), MASKED, jnp.float32),
        jnp.zeros((local_heads, local_rows), jnp.float32),
    )
    gathered = lax.all_gather(
        jnp.concatenate([key_flat, value_flat, query_flat], axis=1), "seq", axis=0, tiled=True
    )
    key_block = gathered[:, :head_cols]
    piece_rows = key_block.shape[0]
    key_pos, key_docs, key_offsets, is_live = key_range(piece_rows)

    def mass_update(carried_in):
        running_max, running_sum = carried_in
        scores, allowed = block_scores(
            query_heads,
            key_block.reshape(piece_rows, local_heads, HEAD_DIM),
            offsets,
            key_offsets,
            local_pos,
            key_pos,
            local_docs,
            key_docs,
        )
        new_max = jnp.maximum(running_max, jnp.max(scores, axis=2))
        weights = jnp.where(allowed[None], jnp.exp(scores - new_max[:, :, None]), 0.0)
        return (new_max, jnp.sum(weights, axis=2))

    running_max, running_sum = lax.cond(is_live, mass_update, unchanged, mass_state)
    log_mass = running_max + jnp.log(running_sum)
    start_state = (
        jnp.zeros((local_heads, local_rows, HEAD_DIM), jnp.float32),
        jnp.zeros((local_heads, local_rows, HEAD_DIM), jnp.float32),
    )
    attend_key_block = key_block
    value_block = gathered[:, head_cols : 2 * head_cols]
    attend_piece_rows = attend_key_block.shape[0]
    attend_key_pos, attend_key_docs, attend_key_offsets, is_live = key_range(attend_piece_rows)

    def attend_update(carried_in):
        scores, allowed = block_scores(
            query_heads,
            attend_key_block.reshape(attend_piece_rows, local_heads, HEAD_DIM),
            offsets,
            attend_key_offsets,
            local_pos,
            attend_key_pos,
            local_docs,
            attend_key_docs,
        )
        probs = jnp.where(allowed[None], jnp.exp(scores - log_mass[:, :, None]), 0.0)
        probs_low = probs.astype(jnp.bfloat16)
        remainder = (probs - probs_low.astype(jnp.float32)).astype(jnp.bfloat16)
        value_piece = value_block.reshape(attend_piece_rows, local_heads, HEAD_DIM)
        rounded_acc = jnp.einsum(
            "hqk,khd->hqd", probs_low, value_piece, preferred_element_type=jnp.float32
        )
        remainder_acc = jnp.einsum(
            "hqk,khd->hqd", remainder, value_piece, preferred_element_type=jnp.float32
        )
        return (rounded_acc, remainder_acc)

    rounded_acc, remainder_acc = lax.cond(is_live, attend_update, unchanged, start_state)
    attended_rows = rounded_acc.transpose(1, 0, 2)
    exact_rows = (rounded_acc + remainder_acc).transpose(1, 0, 2)
    mixed = attended_rows.reshape(local_rows, head_cols).astype(jnp.bfloat16)
    attn_part = contract_cols(mixed, w_out_t)
    middle = inputs + lax.psum(attn_part, "head")
    normed_two, inverse_two, scaled_two = norm_rows(middle, ffn_gain)
    h_two = scaled_two.astype(jnp.bfloat16)
    gate_value = jnp.dot(h_two, w_gate, preferred_element_type=jnp.float32)
    up_value = jnp.dot(h_two, w_up, preferred_element_type=jnp.float32)
    gate_sigmoid = jax.nn.sigmoid(gate_value)
    gate_silu = gate_value * gate_sigmoid
    activation = (gate_silu * up_value).astype(jnp.bfloat16)
    ffn_part = contract_cols(activation, w_down_t)
    layer_out = (
        middle + lax.psum(ffn_part.astype(jnp.bfloat16), "head").astype(jnp.float32)
    ).astype(jnp.bfloat16)
    grad_act = jnp.dot(out_grad, w_down_t, preferred_element_type=jnp.float32)
    grad_gate = (
        grad_act * up_value * gate_sigmoid * (1.0 + gate_value * (1.0 - gate_sigmoid))
    ).astype(jnp.bfloat16)
    grad_up = (grad_act * gate_silu).astype(jnp.bfloat16)
    part_two = contract_cols(grad_gate, w_gate) + contract_cols(grad_up, w_up)
    grad_two = lax.psum(part_two, "head")
    back_two, gain_two = norm_back(grad_two, normed_two, inverse_two, ffn_gain)
    grad_middle = out_grad.astype(jnp.float32) + back_two
    grad_attn = grad_middle.astype(jnp.bfloat16)
    grad_mixed = jnp.dot(grad_attn, w_out_t, preferred_element_type=jnp.float32).astype(
        jnp.bfloat16
    )
    grad_heads = grad_mixed.reshape(local_rows, local_heads, HEAD_DIM)
    row_delta = jnp.sum(grad_heads.astype(jnp.float32) * exact_rows, axis=2).T
    back_state = (
        jnp.zeros((local_rows, head_cols), jnp.float32),
        jnp.zeros((local_rows, local_heads), jnp.float32),
    )
    back_key_block = key_block
    back_value_block = value_block
    back_piece_rows = back_key_block.shape[0]
    back_key_pos, back_key_docs, back_key_offsets, is_live = key_range(back_piece_rows)

    def back_update(carried_in):
        terms = piece_grads(
            query_heads,
            grad_heads,
            log_mass,
            row_delta,
            offsets,
            back_key_block.reshape(back_piece_rows, local_heads, HEAD_DIM),
            back_value_block.reshape(back_piece_rows, local_heads, HEAD_DIM),
            back_key_offsets,
            local_pos,
            back_key_pos,
            local_docs,
            back_key_docs,
        )
        return (terms[0], terms[1])

    grad_query, grad_query_off = lax.cond(is_live, back_update, unchanged, back_state)
    stats = lax.all_gather(
        jnp.concatenate([log_mass.T, row_delta.T], axis=1), "seq", axis=0, tiled=True
    )
    stats_mass, stats_delta = stats[:, :local_heads], stats[:, local_heads:]
    key_state = (
        jnp.zeros((local_rows, head_cols), jnp.float32),
        jnp.zeros((local_rows, head_cols), jnp.float32),
        jnp.zeros((local_rows, local_heads), jnp.float32),
    )
    piece_query = gathered[:, 2 * head_cols :]
    piece_grad = lax.all_gather(grad_mixed, "seq", axis=0, tiled=True)
    key_piece_rows = piece_query.shape[0]
    piece_pos = stored_positions(jnp.arange(key_piece_rows, dtype=jnp.int32), n_seq, local_rows)
    piece_docs = doc_index(piece_pos, doc_ends)
    is_live = (
        (pos_low <= jnp.max(piece_pos))
        & (jnp.max(piece_docs) >= doc_low)
        & (jnp.min(piece_docs) <= doc_high)
    )

    def key_update(carried_in):
        piece_mass = stats_mass.T
        piece_delta = stats_delta.T
        terms = piece_grads(
            piece_query.reshape(key_piece_rows, local_heads, HEAD_DIM),
            piece_grad.reshape(key_piece_rows, local_heads, HEAD_DIM),
            piece_mass,
            piece_delta,
            offsets_all,
            key_heads,
            value_heads,
            offsets,
            piece_pos,
            local_pos,
            piece_docs,
            local_docs,
        )
        return (terms[2], terms[3], terms[4])

    grad_key, grad_value, grad_key_off = lax.cond(is_live, key_update, unchanged, key_state)
    grad_query_low = (grad_query * HEAD_DIM ** (-0.5)).astype(jnp.bfloat16)
    grad_key_low = grad_key.astype(jnp.bfloat16)
    grad_value_low = grad_value.astype(jnp.bfloat16)
    grad_offsets = grad_query_off + grad_key_off
    grad_off_all = lax.all_gather(grad_offsets, "seq", axis=0, tiled=True)
    later = (all_pos[None, :] >= local_pos[:, None]).astype(jnp.float32)
    grad_log = jnp.dot(later, grad_off_all, precision=HIGHEST)
    grad_logit = grad_log * jax.nn.sigmoid(-forget_logit)
    forget_table = w_forget.astype(jnp.float32)
    part_one = (
        contract_cols(grad_query_low, w_query)
        + contract_cols(grad_key_low, w_key)
        + contract_cols(grad_value_low, w_value)
        + lax.dot_general(grad_logit, forget_table, (((1,), (1,)), ((), ())), precision=HIGHEST)
    )
    grad_one = lax.psum(part_one.astype(jnp.bfloat16), "head").astype(jnp.float32)
    back_one, gain_one = norm_back(grad_one, normed_one, inverse_one, attn_gain)
    tokens_grad = (grad_middle + back_one).astype(jnp.bfloat16)
    forget_term = lax.dot_general(
        h_one.astype(jnp.float32), grad_logit, (((0,), (0,)), ((), ())), precision=HIGHEST
    )
    scatter_cols = [
        contract_rows(grad_attn, mixed),
        contract_rows(h_two, grad_gate),
        contract_rows(h_two, grad_up),
        contract_rows(out_grad, activation),
        contract_rows(h_one, grad_query_low),
        contract_rows(h_one, grad_key_low),
        contract_rows(h_one, grad_value_low),
        jnp.pad(forget_term, ((0, 0), (0, 128 - local_heads))),
    ]
    first_sum = lax.psum_scatter(
        jnp.concatenate([t.astype(jnp.bfloat16) for t in scatter_cols[:4]], axis=1),
        "seq",
        scatter_dimension=0,
        tiled=True,
    ).astype(jnp.float32)
    second_sum = lax.psum_scatter(
        jnp.concatenate([t.astype(jnp.bfloat16) for t in scatter_cols[4:]], axis=1),
        "seq",
        scatter_dimension=0,
        tiled=True,
    ).astype(jnp.float32)
    out_weight_grad = first_sum[:, :head_cols].T
    gate_weight_grad = first_sum[:, head_cols : head_cols + hidden]
    up_weight_grad = first_sum[:, head_cols + hidden : head_cols + 2 * hidden]
    down_weight_grad = first_sum[:, head_cols + 2 * hidden :].T
    query_weight_grad = second_sum[:, :head_cols]
    key_weight_grad = second_sum[:, head_cols : 2 * head_cols]
    value_weight_grad = second_sum[:, 2 * head_cols : 3 * head_cols]
    forget_weight_grad = second_sum[:, 3 * head_cols : 3 * head_cols + local_heads]
    attn_gain_grad, ffn_gain_grad, forget_bias_grad = lax.psum(
        (gain_one, gain_two, jnp.sum(grad_logit, axis=0)), "seq"
    )
    return (
        layer_out,
        tokens_grad,
        attn_gain_grad,
        query_weight_grad,
        key_weight_grad,
        value_weight_grad,
        forget_weight_grad,
        forget_bias_grad,
        out_weight_grad,
        ffn_gain_grad,
        gate_weight_grad,
        up_weight_grad,
        down_weight_grad,
    )


def body(*args):
    fits = kernels_fit(args[0], args[6], args[9])
    return (kernel_body if fits else plain_body)(*args)


def solution(mesh):
    return jax.shard_map(
        body,
        mesh=mesh,
        in_specs=(
            P("seq", None),
            P(),
            P("seq", "head"),
            P("seq", "head"),
            P("seq", "head"),
            P("seq", "head"),
            P("head"),
            P("head", "seq"),
            P(),
            P("seq", "head"),
            P("seq", "head"),
            P("head", "seq"),
            P(),
            P("seq", None),
        ),
        out_specs=(
            P("seq", None),
            P("seq", None),
            P(),
            P("seq", "head"),
            P("seq", "head"),
            P("seq", "head"),
            P("seq", "head"),
            P("head"),
            P("head", "seq"),
            P(),
            P("seq", "head"),
            P("seq", "head"),
            P("head", "seq"),
        ),
        check_vma=False,
    )
```

```python
import jax
import jax.numpy as jnp
from jax import lax
from jax.experimental import pallas as pl
from jax.experimental.pallas import tpu as pltpu
from jax.sharding import PartitionSpec as P

HEAD_DIM = 64
EPSILON = 1e-06
HIGHEST = lax.Precision.HIGHEST
MASKED = -1e30
MESH_ID = pl.DeviceIdType.MESH
F32 = jnp.float32
BF16 = jnp.bfloat16
LANES = 128
KEY_TILES = ((0, 0), (0, 1), (1, 0))
VALUE_TILES = ((1, 1), (2, 0), (2, 1))
OUT_TILES = ((0, 1), (1, 0), (1, 1))
NEAR_FIRST = (1, 3, 2)


def dot_nn(left, right):
    return jnp.dot(left, right, preferred_element_type=F32)


def dot_nt(left, right):
    return lax.dot_general(left, right, (((1,), (1,)), ((), ())), preferred_element_type=F32)


def dot_tn(left, right):
    return lax.dot_general(left, right, (((0,), (0,)), ((), ())), preferred_element_type=F32)


def rows_of(first, count):
    return pl.ds(pl.multiple_of(first, 16), count)


def add_to(ref, other):
    ref[...] = (ref[...].astype(F32) + other[...].astype(F32)).astype(BF16)


class Net:
    def __init__(self, sems):
        s = lax.axis_index("seq")
        h = lax.axis_index("head")
        self.line = 4
        self.z, self.x = s // 2, s % 2
        self.y, self.c = h // 2, h % 2
        self.inner = (self.z == 1) | (self.z == 2)
        self.group = self.z * 2 + self.y
        self.sems = sems
        self.used = 0
        self.pending = []

    def alloc(self, count):
        first = self.used
        self.used += count
        return first

    def to(self, z=None, x=None, y=None, c=None):
        z = self.z if z is None else z
        x = self.x if x is None else x
        y = self.y if y is None else y
        c = self.c if c is None else c
        return (z * 2 + x, y * 2 + c)

    def by_distance(self):
        low = self.z < 2
        nearest = self.z + 1 - 2 * (self.z % 2)
        return (nearest, jnp.where(low, 2, 1), jnp.where(low, 3, 0))

    def side(self):
        return self.to(x=1 - self.x)

    def lower(self):
        return self.to(c=1 - self.c)

    def upper(self):
        return self.to(y=1 - self.y)

    def next(self, step):
        return (self.z + step) % self.line

    def announce(self):
        sem = pltpu.get_barrier_semaphore()
        peers = [self.side(), self.lower(), self.upper()]
        peers.append(self.to(x=1 - self.x, c=1 - self.c))
        peers.append(self.to(y=1 - self.y, c=1 - self.c))
        for step in range(1, self.line):
            z = self.next(step)
            peers += [self.to(z=z), self.to(z=z, c=1 - self.c)]
            peers += [self.to(z=z, x=1 - self.x), self.to(z=z, y=1 - self.y)]
        for peer in peers:
            pl.semaphore_signal(sem, 1, device_id=peer, device_id_type=MESH_ID)
        self.peers = len(peers)

    def await_peers(self):
        pl.semaphore_wait(pltpu.get_barrier_semaphore(), self.peers)

    def copy(self, src, dst, send, recv, device):
        return pltpu.make_async_remote_copy(
            src_ref=src,
            dst_ref=dst,
            send_sem=self.sems.at[send],
            recv_sem=self.sems.at[recv],
            device_id=device,
            device_id_type=MESH_ID,
        )

    def begin(self, made):
        made.start()
        self.pending.append(made.wait_send)
        return made

    def begin_if(self, condition, made):
        pl.when(condition)(made.start)
        self.pending.append(lambda: pl.when(condition)(made.wait_send))

    def send(self, src, dst, device):
        first = self.alloc(2)
        return self.begin(self.copy(src, dst, first, first + 1, device))

    def got(self, ref, recv):
        self.copy(ref, ref, recv, recv, self.side()).wait_recv()

    def drain(self):
        for wait in self.pending:
            wait()
        self.pending = []


class RowGather:
    def __init__(self, net, slot, lower=None):
        self.net = net
        self.slot = slot
        self.low = lower
        self.sent = net.alloc(4)
        self.came = net.alloc(4)
        self.up_sent = net.alloc(4)
        self.up_came = net.alloc(4)
        self.low_sent = net.alloc(8)
        self.low_came = net.alloc(8)

    def pass_low(self, y, z):
        if self.low is not None:
            net = self.net
            index = y * 4 + z
            block = self.slot(y, z)
            net.begin(
                net.copy(
                    block, block, self.low_sent + index, self.low_came + index, net.lower()
                )
            )

    def pass_up(self, z):
        net = self.net
        block = self.slot(net.y, z)
        net.begin(net.copy(block, block, self.up_sent + z, self.up_came + z, net.upper()))
        self.pass_low(net.y, z)

    def along(self, src, to):
        net = self.net
        block = self.slot(net.y, src)
        return net.copy(block, block, self.sent + to, self.came + src, net.to(z=to))

    def start(self):
        net = self.net
        for to in range(net.line):
            gap = jnp.abs(to - net.z)
            net.begin_if((gap > 0) & (gap < 3), self.along(net.z, to))
        self.pass_up(net.z)

    def forward(self):
        net = self.net
        for src in net.by_distance():
            net.got(self.slot(net.y, src), self.came + src)
            self.pass_up(src)
        far = net.by_distance()[2]
        net.begin_if(net.inner, self.along(far, 3 - far))

    def finish(self):
        net = self.net
        for src in (net.z,) + net.by_distance():
            net.got(self.slot(1 - net.y, src), self.up_came + src)
            self.pass_low(1 - net.y, src)
        if self.low is not None:
            for y in range(2):
                for z in range(4):
                    net.got(self.low(y, z), self.low_came + y * 4 + z)


class RowSum:
    def __init__(self, net, slot, recv_up, recv_line):
        self.net = net
        self.slot = slot
        self.recv_up = recv_up
        self.recv_line = recv_line
        self.up_sent = net.alloc(4)
        self.up_came = net.alloc(4)
        self.sent = net.alloc(4)
        self.came = net.alloc(4)

    def start(self):
        net = self.net
        for z in net.by_distance()[::-1] + (net.z,):
            net.begin(
                net.copy(
                    self.slot(1 - net.y, z),
                    self.recv_up(z),
                    self.up_sent + z,
                    self.up_came + z,
                    net.upper(),
                )
            )

    def add_up(self, z):
        self.net.got(self.recv_up(z), self.up_came + z)
        add_to(self.slot(self.net.y, z), self.recv_up(z))

    def along(self, target, hop, place):
        net = self.net
        return net.copy(
            self.slot(net.y, target),
            self.recv_line(place),
            self.sent + target,
            self.came + place,
            net.to(z=hop),
        )

    def middle(self):
        net = self.net
        nearest, other, far = net.by_distance()
        self.add_up(far)
        net.begin_if(jnp.logical_not(net.inner), self.along(far, nearest, nearest))
        for z in (other, nearest):
            self.add_up(z)
            net.begin(self.along(z, z, net.z))

        @pl.when(net.inner)
        def _():
            net.got(self.recv_line(net.z), self.came + net.z)
            add_to(self.slot(net.y, far), self.recv_line(net.z))

        net.begin_if(net.inner, self.along(far, far, net.z))
        self.add_up(net.z)

    def result(self):
        net = self.net
        nearest, other, far = net.by_distance()

        @pl.when(jnp.logical_not(net.inner))
        def _():
            self.recv_line(far)[...] = jnp.zeros_like(self.recv_line(far))

        total = self.slot(net.y, net.z)[...].astype(F32)
        for z in (nearest, other):
            net.got(self.recv_line(z), self.came + z)
            total = total + self.recv_line(z)[...].astype(F32)
        pl.when(net.inner)(lambda: net.got(self.recv_line(far), self.came + far))
        return total + self.recv_line(far)[...].astype(F32)


class CrossGather:
    def __init__(self, net, slot):
        self.net = net
        self.slot = slot

    def start(self):
        net = self.net
        mine = self.slot(net.x, net.c)
        self.across = net.send(mine, mine, net.side())
        self.low = net.send(mine, mine, net.lower())

    def forward(self):
        net = self.net
        self.across.wait_recv()
        other = self.slot(1 - net.x, net.c)
        self.both = net.send(other, other, net.lower())

    def finish(self):
        self.low.wait_recv()
        self.both.wait_recv()


class Direct:
    def __init__(self, net, me, peers):
        self.net = net
        self.me = me
        self.peers = peers
        self.sent = net.alloc(8)
        self.came = net.alloc(8)

    def start(self, made, slot):
        net = self.net
        for at, (index, device) in enumerate(self.peers):
            net.begin(
                net.copy(
                    made(index), slot(self.me), self.sent + at, self.came + self.me, device
                )
            )

    def finish(self, slot):
        for index, _ in self.peers:
            self.net.got(slot(index), self.came + index)


class WeightSpread:
    def __init__(self, net, stage, full):
        self.net = net
        self.stage = stage
        self.full = full
        self.block = stage.shape[1]
        self.sent = net.alloc(2)
        self.came = net.alloc(4)
        self.side_sent = net.alloc(4)
        self.side_came = net.alloc(4)
        self.low_sent = net.alloc(8)
        self.low_came = net.alloc(8)
        self.first = (net.z // 2) == net.c

    def slot(self, z, x):
        return self.full.at[rows_of((z * 2 + x) * self.block, self.block), :]

    def away(self, u):
        net = self.net
        return net.copy(
            self.stage.at[u],
            self.slot(net.z, net.x),
            self.sent + u,
            self.came + net.z,
            net.to(z=2 * net.c + u),
        )

    def across(self, z):
        net = self.net
        block = self.slot(z, net.x)
        return net.copy(block, block, self.side_sent + z, self.side_came + z, net.side())

    def low(self, z, x):
        block = self.slot(z, x)
        index = z * 2 + x
        return self.net.copy(
            block, block, self.low_sent + index, self.low_came + index, self.net.lower()
        )

    def start(self):
        net = self.net
        for u in range(2):
            pl.when(2 * net.c + u != net.z)(lambda u=u: self.away(u).start())

        @pl.when(self.first)
        def _():
            self.slot(net.z, net.x)[...] = self.stage[net.z % 2]
            self.across(net.z).start()
            self.low(net.z, net.x).start()

    def forward(self):
        net = self.net

        @pl.when(self.first)
        def _():
            for step in NEAR_FIRST:
                src = net.next(step)
                net.got(self.slot(src, net.x), self.came + src)
                self.across(src).start()
                self.low(src, net.x).start()

    def finish(self):
        net = self.net

        @pl.when(self.first)
        def _():
            for step in (0,) + NEAR_FIRST:
                src = net.next(step)
                net.got(self.slot(src, 1 - net.x), self.side_came + src)
                self.low(src, 1 - net.x).start()

        @pl.when(jnp.logical_not(self.first))
        def _():
            for z in range(4):
                for x in range(2):
                    net.got(self.slot(z, x), self.low_came + z * 2 + x)

    def drain(self):
        net = self.net
        for u in range(2):
            pl.when(2 * net.c + u != net.z)(lambda u=u: self.away(u).wait_send())

        @pl.when(self.first)
        def _():
            for z in range(4):
                self.across(z).wait_send()
                for x in range(2):
                    self.low(z, x).wait_send()


class HiddenSpread:
    def __init__(self, net, stage, full):
        self.net = net
        self.stage = stage
        self.full = full
        self.block = stage.shape[1]
        self.sent = net.alloc(4)
        self.came = net.alloc(4)
        self.side_sent = net.alloc(4)
        self.side_came = net.alloc(4)

    def slot(self, z, x):
        return self.full.at[rows_of((z * 2 + x) * self.block, self.block), :]

    def across(self, z):
        net = self.net
        block = self.slot(z, net.x)
        net.begin(net.copy(block, block, self.side_sent + z, self.side_came + z, net.side()))

    def start(self):
        net = self.net
        self.slot(net.z, net.x)[...] = self.stage[net.z]
        for step in NEAR_FIRST:
            to = net.next(step)
            net.begin(
                net.copy(
                    self.stage.at[to],
                    self.slot(net.z, net.x),
                    self.sent + step,
                    self.came + net.z,
                    net.to(z=to),
                )
            )
        self.across(net.z)

    def forward(self):
        net = self.net
        for step in NEAR_FIRST:
            src = net.next(step)
            net.got(self.slot(src, net.x), self.came + src)
            self.across(src)

    def finish(self):
        net = self.net
        for z in range(4):
            net.got(self.slot(z, 1 - net.x), self.side_came + z)


class WeightSum:
    def __init__(self, net, grads, recv_low, recv_side, final):
        self.net = net
        self.grads = grads
        self.recv_low = recv_low
        self.recv_side = recv_side
        self.final = final
        self.block = final.shape[1]
        self.side_sent = net.alloc(2)
        self.side_came = net.alloc(2)
        self.sent = net.alloc(2)
        self.came = net.alloc(2)

    def rows(self, z, x):
        return self.grads.at[rows_of((z * 2 + x) * self.block, self.block), :]

    def start(self):
        net = self.net
        half = 4 * self.block
        self.low = net.send(
            self.grads.at[rows_of((1 - net.c) * half, half), :], self.recv_low, net.lower()
        )

    def second(self):
        net = self.net
        self.low.wait_recv()
        for x in (1 - net.x, net.x):
            for i in range(2):
                z = 2 * net.c + i
                add_to(
                    self.rows(z, x), self.recv_low.at[rows_of((i * 2 + x) * self.block, self.block)]
                )
        for i in range(2):
            net.begin(
                net.copy(
                    self.rows(2 * net.c + i, 1 - net.x),
                    self.recv_side.at[i],
                    self.side_sent + i,
                    self.side_came + i,
                    net.side(),
                )
            )

    def owner(self, i):
        net = self.net
        z = 2 * net.c + i
        made = net.copy(
            self.rows(z, net.x),
            self.final.at[net.z % 2],
            self.sent + i,
            self.came + net.z % 2,
            net.to(z=z, c=net.z // 2),
        )
        return (z == net.z) & (net.z // 2 == net.c), made

    def third(self):
        net = self.net
        for i in range(2):
            net.got(self.recv_side.at[i], self.side_came + i)
            mine = self.rows(2 * net.c + i, net.x)
            add_to(mine, self.recv_side.at[i])
            local, made = self.owner(i)

            @pl.when(local)
            def _():
                self.final[net.z % 2] = mine[...]

            pl.when(jnp.logical_not(local))(made.start)

    def finish(self):
        net = self.net
        for u in range(2):
            pl.when(2 * net.c + u != net.z)(
                lambda u=u: net.got(self.final.at[u], self.came + u)
            )

    def drain(self):
        for i in range(2):
            local, made = self.owner(i)
            pl.when(jnp.logical_not(local))(made.wait_send)


class HiddenSum:
    def __init__(self, net, grads, recv_side, final):
        self.net = net
        self.grads = grads
        self.recv_side = recv_side
        self.final = final
        self.block = final.shape[1]
        self.side_sent = net.alloc(4)
        self.side_came = net.alloc(4)
        self.sent = net.alloc(4)
        self.came = net.alloc(4)

    def rows(self, z, x):
        return self.grads.at[rows_of((z * 2 + x) * self.block, self.block), :]

    def start(self):
        net = self.net
        for step in (2, 1, 3, 0):
            z = net.next(step)
            net.begin(
                net.copy(
                    self.rows(z, 1 - net.x),
                    self.recv_side.at[z],
                    self.side_sent + z,
                    self.side_came + z,
                    net.side(),
                )
            )

    def second(self):
        net = self.net
        for step in (2, 1, 3, 0):
            z = net.next(step)
            net.got(self.recv_side.at[z], self.side_came + z)
            mine = self.rows(z, net.x)
            add_to(mine, self.recv_side.at[z])
            if step:
                net.begin(
                    net.copy(
                        mine,
                        self.final.at[net.z],
                        self.sent + step,
                        self.came + net.z,
                        net.to(z=z),
                    )
                )
            else:
                self.final[net.z] = mine[...]

    def finish(self):
        net = self.net
        for step in NEAR_FIRST:
            src = net.next(step)
            net.got(self.final.at[src], self.came + src)


class Places:
    def __init__(self, net, chunk):
        self.net = net
        self.chunk = chunk
        self.part = 4 * chunk
        self.all = 32 * chunk

    def position(self, at):
        chunk = self.chunk
        late = at // (16 * chunk)
        x = (at // (8 * chunk)) % 2
        c = (at // (4 * chunk)) % 2
        z = (at // chunk) % 4
        owner = 2 * z + x
        group = jnp.where(late == 0, owner, 15 - owner)
        return group * (2 * chunk) + c * chunk + at % chunk

    def own(self, late):
        return (late * 4 + self.net.x * 2 + self.net.c) * self.part

    def every(self, shape, axis):
        return self.position(lax.broadcasted_iota(jnp.int32, shape, axis))


def doc_starts(positions, doc_ref):
    start = jnp.zeros(positions.shape, jnp.int32)
    end = jnp.int32(0)
    for k in range(doc_ref.shape[0] - 1):
        end = end + doc_ref[k]
        start = jnp.where(positions >= end, end, start)
    return start


def running_sums(places, rows_in, spread, gather):
    tiles = places.all // LANES
    chunk = places.chunk
    row = lax.broadcasted_iota(jnp.int32, (LANES, LANES), 0)
    col = lax.broadcasted_iota(jnp.int32, (LANES, LANES), 1)
    within = ((row // chunk == col // chunk) & (row <= col)).astype(F32)
    stacked = jnp.concatenate(
        [rows_in[:, k * LANES : (k + 1) * LANES] for k in range(tiles)], axis=0
    )
    inside = jnp.dot(stacked, within, precision=HIGHEST, preferred_element_type=F32)
    outside = jnp.dot(rows_in, spread[...], precision=HIGHEST, preferred_element_type=F32)
    outside = outside[:, : gather.shape[0]]
    outside = jnp.dot(outside, gather[...], precision=HIGHEST, preferred_element_type=F32)
    return outside + jnp.concatenate(
        [inside[k * 8 : (k + 1) * 8, :] for k in range(tiles)], axis=1
    )


def order_tables(places, spread, gather):
    order = places.every((places.all, LANES), 0) // places.chunk
    slot = lax.broadcasted_iota(jnp.int32, (places.all, LANES), 1)
    spread[...] = (order < slot).astype(F32)
    order = places.every(gather.shape, 1) // places.chunk
    slot = lax.broadcasted_iota(jnp.int32, gather.shape, 0)
    gather[...] = (order == slot).astype(F32)


def tile_of(ref, rows, tile):
    return ref[rows, tile * LANES : (tile + 1) * LANES]


def only(values_in, lane, side):
    return jnp.where(lane // HEAD_DIM == side, values_in, jnp.zeros_like(values_in))


def norm_grad(grad_in, values_in, gain):
    inverse = lax.rsqrt(jnp.mean(values_in * values_in, axis=-1, keepdims=True) + EPSILON)
    normed = values_in * inverse
    scaled = grad_in * gain
    inner = jnp.mean(scaled * normed, axis=-1, keepdims=True)
    return inverse * (scaled - normed * inner), jnp.sum(grad_in * normed, axis=0, keepdims=True)


def norm(values_in, gain):
    inverse = lax.rsqrt(jnp.mean(values_in * values_in, axis=-1, keepdims=True) + EPSILON)
    return (values_in * inverse * gain).astype(BF16)


def to_columns(rows_in, first=0):
    many = rows_in.shape[1]
    parts = [rows_in, jnp.zeros((LANES - 8 - first, many), F32)]
    if first:
        parts = [jnp.zeros((first, many), F32)] + parts
    return jnp.concatenate(parts, axis=0).T


def gather_quarters(net, ref):
    chunk = ref.shape[0] // 4

    def piece(y):
        return ref.at[rows_of((2 * y + net.c) * chunk, chunk), :]

    up = net.send(piece(net.y), piece(net.y), net.upper())
    first = net.send(piece(net.y), piece(net.y), net.lower())

    def second():
        up.wait_recv()
        other = net.send(piece(1 - net.y), piece(1 - net.y), net.lower())

        def last():
            first.wait_recv()
            other.wait_recv()

        return last

    return second


def layer_kernel(
    tokens,
    out_grad,
    gain_one,
    gain_two,
    wq,
    wk,
    wv,
    forget_t,
    bias_in,
    wo_t,
    wg,
    wu,
    wd_t,
    doc_ref,
    layer_out,
    tokens_grad,
    gains,
    bias_grad,
    late_final,
    last_final,
    early_final,
    ffn_final,
    stage_attn,
    stage_out,
    stage_bias,
    other_bias,
    h_one,
    allowed,
    spread,
    gather,
    logit_parts,
    queries,
    keyval,
    offsets,
    mass,
    logits,
    mixed,
    exact,
    middle,
    normed_two,
    out_grads,
    w_attn,
    w_out,
    w_ffn,
    all_query,
    all_grad,
    ffn_grads,
    part_two,
    part_out,
    two_low,
    two_up,
    two_line,
    out_low,
    out_up,
    out_line,
    ffn_sum,
    ffn_side,
    late_sum,
    late_low,
    late_side,
    last_sum,
    last_low,
    last_side,
    early_sum,
    early_low,
    early_side,
    grad_attn,
    grad_heads,
    stats,
    off_parts,
    every_off,
    grad_qkv,
    grad_offs,
    part_one,
    one_up,
    one_line,
    gain_parts,
    gain_swap,
    own_tokens,
    all_forget,
    own_logits,
    near_sems,
    sems,
):
    net = Net(sems)
    net.announce()
    z, x, y, c = net.z, net.x, net.y, net.c
    width = tokens.shape[1]
    chunk = tokens.shape[0] // 4
    part = 4 * chunk
    places = Places(net, chunk)
    hidden = wg.shape[1] // 4
    own = rows_of((2 * y + c) * chunk, chunk)
    tile = 256
    scale_one = gain_one[...].reshape(1, width)
    scale_two = gain_two[...].reshape(1, width)

    token_net = RowGather(net, lambda yy, zz: grad_attn.at[yy, rows_of(zz * chunk, chunk), :])
    weight_net = WeightSpread(net, stage_attn, w_attn)
    out_net = WeightSpread(net, stage_out, w_out)
    units_net = HiddenSpread(net, ffn_side, w_ffn)
    kv_nets = [
        CrossGather(net, lambda xx, cc, late=late: keyval.at[late, xx, cc]) for late in range(2)
    ]
    sub = chunk // 2
    pieces = [slice(0, sub), slice(sub, chunk)]

    def piece_of(ref, k):
        return lambda zz: ref.at[zz, pieces[k], :]

    def rows_at(ref, k):
        return lambda yy, zz: ref.at[yy, rows_of(zz * chunk + k * sub, sub), :]

    logit_net = CrossGather(net, lambda xx, cc: logit_parts.at[xx, cc])
    two_nets = [
        RowGather(
            net,
            lambda yy, zz, k=k: normed_two.at[c, yy, zz, pieces[k], :],
            lambda yy, zz, k=k: normed_two.at[1 - c, yy, zz, pieces[k], :],
        )
        for k in range(2)
    ]
    given_net = RowGather(
        net, lambda yy, zz: out_grads.at[c, yy, zz], lambda yy, zz: out_grads.at[1 - c, yy, zz]
    )
    attn_sums = [
        RowSum(net, rows_at(part_one, k), piece_of(one_up, k), piece_of(one_line, k))
        for k in range(2)
    ]

    def groups():
        found = [(z * 2 + 1 - y, net.upper())]
        for step in range(1, 4):
            far = net.next(step)
            found.append((far * 2 + y, net.to(z=far)))
            found.append((far * 2 + 1 - y, net.to(z=far, y=1 - y)))
        return found

    forget_net = Direct(net, net.group, groups())
    logit_back = Direct(net, net.group, groups())
    rest = [(z * 2 + 1 - x, net.side())]
    for step in range(1, 4):
        far = net.next(step)
        rest.append((far * 2 + x, net.to(z=far)))
        rest.append((far * 2 + 1 - x, net.to(z=far, x=1 - x)))
    gain_net = Direct(net, z * 2 + x, rest)
    corner = net.to(y=1 - y, c=1 - c)
    last_gain = Direct(
        net,
        y * 2 + c,
        [(y * 2 + 1 - c, net.lower()), (2 - 2 * y + c, net.upper()), (3 - 2 * y - c, corner)],
    )

    near = [
        (tokens.at[own, :], own_tokens),
        (tokens.at[own, :], grad_attn.at[y, rows_of(z * chunk, chunk), :]),
        (out_grad.at[own, :], out_grads.at[c, y, z]),
    ]
    for index, ref in enumerate((wg, wu, wd_t)):
        for zz in range(4):
            near.append(
                (
                    ref.at[:, zz * hidden : (zz + 1) * hidden],
                    ffn_side.at[zz, :, index * hidden : (index + 1) * hidden],
                )
            )
    fetched = [
        pltpu.make_async_copy(src, dst, near_sems.at[at]) for at, (src, dst) in enumerate(near)
    ]
    for copy in fetched:
        copy.start()
    half_cols = wq.shape[1] // 2
    half_heads = half_cols // HEAD_DIM
    block = wq.shape[0]
    forget = forget_t[...].astype(F32)
    row8 = lax.broadcasted_iota(jnp.int32, (8, LANES), 0)
    for u in range(2):
        cols = slice(u * half_cols, (u + 1) * half_cols)
        for index, ref in enumerate((wk, wv)):
            stage_attn[u, :, index * half_cols : (index + 1) * half_cols] = ref[:, cols]
        rows8 = jnp.concatenate(
            [
                forget[u * half_heads : (u + 1) * half_heads, :],
                jnp.zeros((8 - half_heads, block), F32),
            ],
            axis=0,
        )
        rows8 = jnp.concatenate([rows8, jnp.zeros((8, 2 * LANES - block), F32)], axis=1)
        stage_attn[u, :, 4 * LANES :] = to_columns(rows8, HEAD_DIM)[:block].astype(BF16)
        stage_attn[u, :, 2 * half_cols : 3 * half_cols] = wq[:, cols]
        biases = jnp.zeros((8, LANES), F32)
        for head in range(half_heads):
            biases = jnp.where(row8 == head, bias_in[u * half_heads + head], biases)
        stage_bias[u] = biases
    net.await_peers()
    for copy in fetched[:3]:
        copy.wait()
    weight_net.start()
    token_net.start()
    bias_send = net.send(stage_bias, other_bias, net.lower())
    for u in range(2):
        stage_out[u, :, :HEAD_DIM] = jnp.zeros((block, HEAD_DIM), BF16)
        stage_out[u, :, HEAD_DIM:] = wo_t[:, u * half_cols : (u + 1) * half_cols]

    order_tables(places, spread, gather)
    every = places.every((1, places.all), 1)
    for late in range(2):
        at = places.own(late) + lax.broadcasted_iota(jnp.int32, (part, 1), 0)
        pos = places.position(at)
        start = doc_starts(pos, doc_ref)
        seen = (every <= pos) & (every >= start)
        allowed[late * part : (late + 1) * part, :] = jnp.where(seen, 0.0, MASKED).astype(BF16)

    weight_net.forward()
    token_net.forward()
    given_net.start()
    h_one[y] = norm(grad_attn[y].astype(F32), scale_one)
    token_net.finish()
    h_one[1 - y] = norm(grad_attn[1 - y].astype(F32), scale_one)
    weight_net.finish()

    for late in range(2):
        keyval[late, x, c] = dot_nn(h_one[late], w_attn[:, : 3 * LANES]).astype(BF16)
        kv_nets[late].start()
    bias_send.wait_recv()
    bias = jnp.where(weight_net.first, stage_bias[z % 2], other_bias[z % 2])[:, :1]
    for late in range(2):
        r = slice(late * part, (late + 1) * part)
        made = dot_nn(h_one[late], w_attn[:, 3 * LANES :])
        logit_parts[x, c, :, r] = made[:, LANES:].T[HEAD_DIM : HEAD_DIM + 8, :] + bias
        queries[r, :] = (made.astype(BF16).astype(F32) * HEAD_DIM ** (-0.5)).astype(BF16)
    logit_net.start()
    all_forget[net.group] = w_attn[:, 4 * LANES :].astype(F32).T[HEAD_DIM : HEAD_DIM + 8, :]
    forget_net.start(lambda index: all_forget.at[net.group], lambda index: all_forget.at[index])
    out_net.start()
    for copy in fetched[3:]:
        copy.wait()
    units_net.start()

    logit_net.forward()
    given_net.forward()
    logit_net.finish()
    for late in range(2):
        for xx in range(2):
            for cc in range(2):
                at = (late * 4 + xx * 2 + cc) * part
                logits[:, at : at + part] = logit_parts[xx, cc, :, late * part : (late + 1) * part]
    turned = logits[...]
    logs = jnp.minimum(turned, 0.0) - jnp.log(1.0 + jnp.exp(-jnp.abs(turned)))
    offsets[...] = running_sums(places, logs, spread, gather)
    kv_nets[0].forward()
    kv_nets[1].forward()
    out_net.forward()
    kv_nets[0].finish()

    lane = lax.broadcasted_iota(jnp.int32, (LANES, LANES), 1)
    first = (lane // HEAD_DIM) == 0
    for block in range(2 * part // LANES):
        r = slice(block * LANES, (block + 1) * LANES)
        late = (block * LANES) // part
        many = places.all // 2 * (late + 1)
        made, kept = [], []
        masses = jnp.zeros((LANES, LANES), F32)
        for head in range(3):
            tile_k, side_k = KEY_TILES[head]
            tile_v, side_v = VALUE_TILES[head]
            keys = keyval[: late + 1, :, :, :, tile_k * LANES : (tile_k + 1) * LANES]
            values = keyval[: late + 1, :, :, :, tile_v * LANES : (tile_v + 1) * LANES]
            keys, values = keys.reshape(many, LANES), values.reshape(many, LANES)
            scores = (
                dot_nt(only(tile_of(queries, r, tile_k), lane, side_k), keys)
                - offsets[head : head + 1, :many]
                + allowed[r, :many].astype(F32)
            )
            top = jnp.max(scores, axis=1, keepdims=True)
            probs = jnp.exp(scores - top)
            total = jnp.sum(probs, axis=1, keepdims=True)
            high = probs.astype(BF16)
            rest = (probs - high.astype(F32)).astype(BF16)
            share = 1.0 / total
            rounded = dot_nn(high, values)
            made.append(rounded * share)
            kept.append((rounded + dot_nn(rest, values)) * share)
            masses = jnp.where(lane == head, top + jnp.log(total), masses)
        mass[r, :] = masses
        mixed[r, :LANES] = jnp.where(first, 0.0, made[0]).astype(BF16)
        mixed[r, LANES:] = jnp.where(first, made[1], made[2]).astype(BF16)
        exact[r, :LANES] = jnp.where(first, 0.0, kept[0])
        exact[r, LANES:] = jnp.where(first, kept[1], kept[2])
        if block == 1:
            out_net.finish()
            kv_nets[1].finish()

    def project(late):
        rows = rows_of(late * part, part)
        for at in range(0, width, tile):
            cols = slice(at, at + tile)
            part_one[late, :, cols] = dot_nt(mixed[rows, :], w_out[cols, :]).astype(BF16)

    project(1 - y)
    for attn_sum in attn_sums:
        attn_sum.start()
    project(y)
    for attn_sum in attn_sums:
        attn_sum.middle()
    units_net.forward()
    earlier, net.pending = net.pending, []
    for k in range(2):
        total = own_tokens[pieces[k], :].astype(F32) + attn_sums[k].result()
        middle[pieces[k], :] = total
        normed_two[c, y, z, pieces[k], :] = norm(total, scale_two)
        two_nets[k].start()
    given_net.finish()
    two_nets[0].forward()
    units_net.finish()
    two_nets[0].finish()

    half_heads = half_cols
    tiles = [slice(at, at + tile) for at in range(0, width, tile)]

    query_net = CrossGather(net, lambda xx, cc: all_query.at[:, xx, cc])
    grad_net = CrossGather(net, lambda xx, cc: all_grad.at[:, xx, cc])
    stat_net = CrossGather(net, lambda xx, cc: stats.at[xx, cc])
    off_net = CrossGather(net, lambda xx, cc: off_parts.at[xx, cc])
    attn_nets = [RowGather(net, rows_at(grad_attn, k)) for k in range(2)]

    def own_parts(ref, k):
        return lambda yy, zz: ref.at[k, c, rows_of(yy * 4 * sub + zz * sub, sub), :]

    twos = [
        RowSum(net, own_parts(part_two, k), piece_of(two_up, k), piece_of(two_line, k))
        for k in range(2)
    ]
    outs = [
        RowSum(net, own_parts(part_out, k), piece_of(out_up, k), piece_of(out_line, k))
        for k in range(2)
    ]
    ones = [
        RowSum(net, rows_at(part_one, k), piece_of(one_up, k), piece_of(one_line, k))
        for k in range(2)
    ]
    ffn_net = HiddenSum(net, ffn_sum, ffn_side, ffn_final)
    late_net = WeightSum(net, late_sum, late_low, late_side, late_final)
    last_net = WeightSum(net, last_sum, last_low, last_side, last_final)
    early_net = WeightSum(net, early_sum, early_low, early_side, early_final)

    for late in range(2):
        all_query[late, x, c] = queries[late * part : (late + 1) * part, :]
    for wait in earlier:
        wait()
    query_net.start()

    def units_of(k):
        for cc in range(2):
            inputs = normed_two[cc, :, :, pieces[k], :].reshape(part, width)
            given = out_grads[cc, :, :, pieces[k], :].reshape(part, width)
            gate = dot_nn(inputs, w_ffn[:, :hidden])
            up = dot_nn(inputs, w_ffn[:, hidden : 2 * hidden])
            grad_act = dot_nn(given, w_ffn[:, 2 * hidden :])
            sigmoid = 1.0 / (1.0 + jnp.exp(-gate))
            silu = gate * sigmoid
            ffn_grads[k, cc, :, :hidden] = (
                grad_act * up * sigmoid * (1.0 + gate * (1.0 - sigmoid))
            ).astype(BF16)
            ffn_grads[k, cc, :, hidden : 2 * hidden] = (grad_act * silu).astype(BF16)
            ffn_grads[k, cc, :, 2 * hidden :] = (silu * up).astype(BF16)

    def lower_of(parts, recv, k, cols):
        def back(cc):
            for r in tiles:
                parts[k, cc, :, r] = dot_nt(ffn_grads[k, cc, :, cols], w_ffn[r, cols]).astype(BF16)

        back(1 - c)
        made = net.send(parts.at[k, 1 - c], recv.at[k], net.lower())
        back(c)
        return made

    def upper_of(made, parts, recv, k, sums):
        made.wait_recv()
        parts[k, c] = (parts[k, c].astype(F32) + recv[k].astype(F32)).astype(BF16)
        sums[k].start()

    def unit_grads(some):
        for cols in some:
            both = [0.0, 0.0]
            for k in range(2):
                left = normed_two[:, :, :, pieces[k], cols].reshape(2 * part, tile)
                right = ffn_grads[k].reshape(2 * part, 3 * hidden)
                both[0] = both[0] + dot_tn(left, right[:, : 2 * hidden])
                left = out_grads[:, :, :, pieces[k], cols].reshape(2 * part, tile)
                both[1] = both[1] + dot_tn(left, right[:, 2 * hidden :])
            ffn_sum[cols, : 2 * hidden] = both[0].astype(BF16)
            ffn_sum[cols, 2 * hidden :] = both[1].astype(BF16)

    units_of(0)
    two_nets[1].forward()
    to_lower = slice(0, 2 * hidden)
    first_low = lower_of(part_two, two_low, 0, to_lower)
    two_nets[1].finish()
    units_of(1)
    upper_of(first_low, part_two, two_low, 0, twos)
    second_low = lower_of(part_two, two_low, 1, to_lower)
    twos[0].middle()
    upper_of(second_low, part_two, two_low, 1, twos)
    unit_grads(tiles[:3])
    twos[1].middle()
    unit_grads(tiles[3:])
    query_net.forward()
    ffn_net.start()
    grad_middle = []
    gain_two_part = 0.0
    for k in range(2):
        back_two, part_gain = norm_grad(twos[k].result(), middle[pieces[k], :], scale_two)
        gain_two_part = gain_two_part + part_gain
        grad_middle.append(out_grads[c, y, z, pieces[k], :].astype(F32) + back_two)
        grad_attn[y, rows_of(z * chunk + k * sub, sub), :] = grad_middle[k].astype(BF16)
        attn_nets[k].start()
    to_out = slice(2 * hidden, 3 * hidden)
    attn_nets[0].forward()
    every = places.every((1, places.all), 1)
    own_pos = [
        places.position(places.own(late) + lax.broadcasted_iota(jnp.int32, (part, 1), 0))
        for late in range(2)
    ]
    attn_nets[1].forward()
    out_sends = [lower_of(part_out, out_low, k, to_out) for k in range(2)]
    attn_nets[0].finish()
    query_net.finish()
    attn_nets[1].finish()
    for k in range(2):
        upper_of(out_sends[k], part_out, out_low, k, outs)

    lane = lax.broadcasted_iota(jnp.int32, (part, LANES), 1)
    for late in range(2):
        r = slice(late * part, (late + 1) * part)
        made = dot_nn(grad_attn[late], w_out[...])
        grad_heads[r, :] = made.astype(BF16)
        all_grad[late, x, c] = grad_heads[r, :]
    grad_net.start()
    for late in range(2):
        r = slice(late * part, (late + 1) * part)
        delta = jnp.zeros((part, LANES), F32)
        for head, (tile_o, side_o) in enumerate(OUT_TILES):
            product = tile_of(grad_heads, r, tile_o).astype(F32) * tile_of(exact, r, tile_o)
            inner = jnp.sum(only(product, lane, side_o), axis=1, keepdims=True)
            delta = jnp.where(lane == head, inner, delta)
        grad_offs[r, :] = delta
    stats[x, c, :8, :] = mass[...].T[:8, :]
    stats[x, c, 8:, :] = grad_offs[...].T[:8, :]
    stat_net.start()

    for cols in tiles:
        left = grad_attn[:, :, cols].reshape(2 * part, tile)
        early_sum[cols, :] = dot_tn(left, mixed[...]).astype(BF16)
    early_net.start()
    for out in outs:
        out.middle()
    ffn_net.second()

    lane = lax.broadcasted_iota(jnp.int32, (LANES, LANES), 1)
    first = (lane // HEAD_DIM) == 0
    for block in range(2 * part // LANES):
        r = slice(block * LANES, (block + 1) * LANES)
        late = (block * LANES) // part
        many = places.all // 2 * (late + 1)
        made = []
        sums = jnp.zeros((LANES, LANES), F32)
        for head in range(3):
            tile_k, side_k = KEY_TILES[head]
            tile_v, side_v = VALUE_TILES[head]
            tile_o, side_o = OUT_TILES[head]
            keys = keyval[: late + 1, :, :, :, tile_k * LANES : (tile_k + 1) * LANES]
            values = keyval[: late + 1, :, :, :, tile_v * LANES : (tile_v + 1) * LANES]
            keys, values = keys.reshape(many, LANES), values.reshape(many, LANES)
            scores = (
                dot_nt(only(tile_of(queries, r, tile_k), lane, side_k), keys)
                - offsets[head : head + 1, :many]
                + allowed[r, :many].astype(F32)
            )
            probs = jnp.exp(scores - mass[r, head : head + 1])
            grad_probs = dot_nt(only(tile_of(grad_heads, r, tile_o), lane, side_o), values)
            grad_scores = (probs * (grad_probs - grad_offs[r, head : head + 1])).astype(BF16)
            made.append(dot_nn(grad_scores, keys) * HEAD_DIM ** (-0.5))
            row_sum = jnp.sum(grad_scores.astype(F32), axis=1, keepdims=True)
            sums = jnp.where(lane == head, row_sum, sums)
        grad_qkv[r, 3 * LANES : 4 * LANES] = jnp.where(first, made[0], made[1]).astype(BF16)
        grad_qkv[r, 4 * LANES :] = jnp.where(first, made[2], 0.0).astype(BF16)
        grad_offs[r, :] = sums
        if block == 0:
            grad_net.forward()
            stat_net.forward()
        if block == 1:
            pass
            early_net.second()

    starts = doc_starts(every, doc_ref)
    for late in range(2):
        seen = (own_pos[late] <= every) & (own_pos[late] >= starts)
        allowed[late * part : (late + 1) * part, :] = jnp.where(seen, 0.0, MASKED).astype(BF16)
    stat_net.finish()
    grad_net.finish()
    for late in range(2):
        for xx in range(2):
            for cc in range(2):
                at = (late * 4 + xx * 2 + cc) * part
                piece = slice(late * part, (late + 1) * part)
                every_off[0, :, at : at + part] = stats[xx, cc, :8, piece]
                every_off[1, :, at : at + part] = stats[xx, cc, 8:, piece]

    own_offs = [
        to_columns(offsets[:, pl.ds(pl.multiple_of(places.own(late), LANES), part)])
        for late in range(2)
    ]
    for block in range(2 * part // LANES):
        r = slice(block * LANES, (block + 1) * LANES)
        late = (block * LANES) // part
        within = slice(block * LANES - late * part, (block + 1) * LANES - late * part)
        many = places.all // 2 * (2 - late)
        lanes = slice(places.all - many, places.all)
        keys_made, values_made = [], []
        sums = jnp.zeros((LANES, LANES), F32)
        for head in range(3):
            tile_k, side_k = KEY_TILES[head]
            tile_v, side_v = VALUE_TILES[head]
            tile_o, side_o = OUT_TILES[head]
            asked = all_query[late:, :, :, :, tile_k * LANES : (tile_k + 1) * LANES]
            given = all_grad[late:, :, :, :, tile_o * LANES : (tile_o + 1) * LANES]
            asked, given = asked.reshape(many, LANES), given.reshape(many, LANES)
            key = keyval[late, x, c, within, tile_k * LANES : (tile_k + 1) * LANES]
            value = keyval[late, x, c, within, tile_v * LANES : (tile_v + 1) * LANES]
            scores = (
                dot_nt(only(key, lane, side_k), asked)
                - own_offs[late][within, head : head + 1]
                + allowed[r, lanes].astype(F32)
            )
            probs = jnp.exp(scores - every_off[0, head : head + 1, lanes])
            grad_probs = dot_nt(only(value, lane, side_v), given)
            grad_scores = (probs * (grad_probs - every_off[1, head : head + 1, lanes])).astype(
                BF16
            )
            keys_made.append(dot_nn(grad_scores, asked))
            values_made.append(dot_nn(probs.astype(BF16), given))
            col_sum = jnp.sum(grad_scores.astype(F32), axis=1, keepdims=True)
            sums = jnp.where(lane == head, col_sum, sums)
        for at, (left, right) in enumerate(
            (
                (keys_made[0], keys_made[1]),
                (keys_made[2], values_made[0]),
                (values_made[1], values_made[2]),
            )
        ):
            grad_qkv[r, at * LANES : (at + 1) * LANES] = jnp.where(first, left, right).astype(BF16)
        grad_offs[r, :] = grad_offs[r, :] - sums
        if block == 1:
            early_net.third()
    off_parts[x, c] = grad_offs[...].T[:8, :]
    off_net.start()

    def back(late):
        rows = rows_of(late * part, part)
        for r in tiles:
            part_one[late, :, r] = dot_nt(grad_qkv[rows, :], w_attn[r, :]).astype(BF16)

    back(1 - y)
    for one in ones:
        one.start()
    back(y)
    off_net.forward()
    cut = late_sum.shape[1]
    for cols in tiles:
        left = h_one[:, :, cols].reshape(2 * part, tile)
        late_sum[cols, :] = dot_tn(left, grad_qkv[:, :cut]).astype(BF16)
    late_net.start()
    ones[0].middle()
    off_net.finish()
    for late in range(2):
        for xx in range(2):
            for cc in range(2):
                at = (late * 4 + xx * 2 + cc) * part
                every_off[0, :, at : at + part] = off_parts[
                    xx, cc, :, late * part : (late + 1) * part
                ]
    given = every_off[0]
    whole = jnp.sum(given, axis=1, keepdims=True)
    grad_logs = whole - running_sums(places, given, spread, gather) + given
    grad_logits = grad_logs / (1.0 + jnp.exp(logits[...]))
    every_off[1] = grad_logits

    def rows_for(index):
        at = places.own(index % 2) + (index // 4) * LANES
        return every_off.at[1, :, pl.ds(pl.multiple_of(at, LANES), LANES)]

    logit_back.start(rows_for, lambda index: own_logits.at[index])
    own_logits[net.group] = rows_for(net.group)[...]
    ones[1].middle()
    late_net.second()
    for late in range(2):
        r = slice(late * part, (late + 1) * part)
        mine = every_off[1, :, pl.ds(pl.multiple_of(places.own(late), LANES), part)]
        held = grad_qkv[r, cut:]
        lane = lax.broadcasted_iota(jnp.int32, (part, LANES), 1)
        grad_qkv[r, cut:] = jnp.where(
            lane // HEAD_DIM == 0, held, to_columns(mine, HEAD_DIM).astype(BF16)
        )
    for cols in tiles:
        left = h_one[:, :, cols].reshape(2 * part, tile)
        last_sum[cols, :] = dot_tn(left, grad_qkv[:, cut:]).astype(BF16)
    last_net.start()
    late_net.third()
    logit_back.finish(lambda index: own_logits.at[index])
    forget_net.finish(lambda index: all_forget.at[index])
    held = own_logits[...].reshape(8 * 8, LANES)
    held = jnp.where(z % 2 == 0, held[:, :chunk], held[:, chunk:]).astype(BF16)
    forget_part = dot_tn(held, all_forget[...].reshape(8 * 8, width).astype(BF16))
    last_net.second()
    for k in range(2):
        layer_out[rows_of((2 * y + c) * chunk + k * sub, sub), :] = (
            middle[pieces[k], :] + outs[k].result()
        ).astype(BF16)
    layer_second = gather_quarters(net, layer_out)
    gain_one_part = 0.0
    for k in range(2):
        back_one, part_gain = norm_grad(
            ones[k].result() + forget_part[pieces[k], :],
            own_tokens[pieces[k], :].astype(F32),
            scale_one,
        )
        gain_one_part = gain_one_part + part_gain
        tokens_grad[rows_of((2 * y + c) * chunk + k * sub, sub), :] = (
            grad_middle[k] + back_one
        ).astype(BF16)
    grad_second = gather_quarters(net, tokens_grad)
    cells = width // 4
    gain_mine = gain_parts.at[z * 2 + x]
    gain_mine[:, :cells] = jnp.concatenate(
        [g[:, k * cells : (k + 1) * cells] for g in (gain_one_part, gain_two_part) for k in range(4)],
        axis=0,
    )
    gain_mine[:, cells:] = jnp.broadcast_to(
        jnp.sum(grad_logits, axis=1, keepdims=True), (8, LANES)
    )
    gain_net.start(lambda index: gain_mine, lambda index: gain_parts.at[index])
    last_net.third()
    layer_last = layer_second()
    grad_last = grad_second()

    gain_net.finish(lambda index: gain_parts.at[index])
    total = gain_parts[0, :, :cells]
    for index in range(1, 8):
        total = total + gain_parts[index, :, :cells]
    gain_swap[y * 2 + c] = total
    last_gain.start(lambda index: gain_swap.at[y * 2 + c], lambda index: gain_swap.at[index])
    for u in range(2):
        bias_grad[u] = gain_parts[(2 * c + u) * 2 + x, :, cells:]

    ffn_net.finish()
    early_net.finish()
    last_gain.finish(lambda index: gain_swap.at[index])
    total = gain_swap[0]
    for index in range(1, 4):
        total = total + gain_swap[index]
    gains[...] = total

    late_net.finish()
    last_net.finish()
    layer_last()
    grad_last()
    for part_net in (weight_net, out_net, late_net, last_net, early_net, net):
        part_net.drain()


def narrow_kernel(
    layer,
    tokens,
    gains,
    biases,
    late,
    last,
    early,
    units,
    layer_out,
    tokens_grad,
    gain_one,
    g_query,
    g_key,
    g_value,
    g_forget,
    g_bias,
    g_out,
    gain_two,
    g_gate,
    g_up,
    g_down,
):
    layer_out[...] = layer[...]
    tokens_grad[...] = tokens[...]
    for k, ref in enumerate((gain_one, gain_two)):
        ref[...] = jnp.concatenate(
            [gains[4 * k + at : 4 * k + at + 1, :] for at in range(4)], axis=1
        )[0]
    half = g_query.shape[1] // 2
    heads = half // HEAD_DIM
    hidden = units.shape[2] // 3
    block = g_query.shape[0]
    for u in range(2):
        cols = slice(u * half, (u + 1) * half)
        got = late[u].astype(F32)
        rest = last[u].astype(F32)
        g_key[:, cols] = got[:, :half]
        g_value[:, cols] = got[:, half : 2 * half]
        g_query[:, cols] = jnp.concatenate([got[:, 2 * half :], rest[:, :HEAD_DIM]], axis=1)
        g_out[:, cols] = early[u, :, HEAD_DIM:].astype(F32)
        padded = jnp.concatenate([rest, jnp.zeros((2 * LANES - block, LANES), F32)], axis=0)
        g_forget[u * heads : (u + 1) * heads, :] = padded.T[HEAD_DIM : HEAD_DIM + heads, :block]
    each = jnp.concatenate([biases[0, :heads, :], biases[1, :heads, :]], axis=0)
    g_bias[...] = each
    for zz in range(4):
        cols = slice(zz * hidden, (zz + 1) * hidden)
        for index, ref in enumerate((g_gate, g_up, g_down)):
            ref[:, cols] = units[zz, :, index * hidden : (index + 1) * hidden].astype(F32)


VMEM = pl.BlockSpec(memory_space=pltpu.VMEM)
SMEM = pl.BlockSpec(memory_space=pltpu.SMEM)
HBM = pl.BlockSpec(memory_space=pl.ANY)


def shapes_of(made):
    return [jax.ShapeDtypeStruct(*m) for m in made]


def layer_shapes(rows, width, heads, hidden):
    chunk = rows // 4
    part = 4 * chunk
    every = 32 * chunk
    block = width // 8
    attn = (3 * heads * HEAD_DIM // 2) + HEAD_DIM
    cut = attn - LANES
    outs = [
        ((rows, width), BF16),
        ((rows, width), BF16),
        ((8, width // 4), F32),
        ((2, 8, LANES), F32),
        ((2, block, cut), BF16),
        ((2, block, LANES), BF16),
        ((2, block, 2 * LANES), BF16),
        ((4, block, 3 * hidden), BF16),
    ]

    def weight_sum(columns):
        return [
            ((width, columns), BF16),
            ((width // 2, columns), BF16),
            ((2, block, columns), BF16),
        ]

    row_sum = [((2, part, width), BF16), ((4, chunk, width), BF16), ((4, chunk, width), BF16)]
    scratch = [
        ((2, block, attn), BF16),
        ((2, block, 2 * LANES), BF16),
        ((2, 8, LANES), F32),
        ((2, 8, LANES), F32),
        ((2, part, width), BF16),
        ((2 * part, every), BF16),
        ((every, LANES), F32),
        ((every // chunk, every), F32),
        ((2, 2, 8, 2 * part), F32),
        ((2 * part, 2 * LANES), BF16),
        ((2, 2, 2, part, 3 * LANES), BF16),
        ((8, every), F32),
        ((2 * part, LANES), F32),
        ((8, every), F32),
        ((2 * part, 2 * LANES), BF16),
        ((2 * part, 2 * LANES), F32),
        ((chunk, width), F32),
        ((2, 2, 4, chunk, width), BF16),
        ((2, 2, 4, chunk, width), BF16),
        ((width, attn), BF16),
        ((width, 2 * LANES), BF16),
        ((width, 3 * hidden), BF16),
        ((2, 2, 2, part, 2 * LANES), BF16),
        ((2, 2, 2, part, 2 * LANES), BF16),
        ((2, 2, part, 3 * hidden), BF16),
        ((2, 2, part, width), BF16),
        ((2, 2, part, width), BF16),
        *row_sum,
        *row_sum,
        ((width, 3 * hidden), BF16),
        ((4, block, 3 * hidden), BF16),
        *weight_sum(cut),
        *weight_sum(LANES),
        *weight_sum(2 * LANES),
        ((2, part, width), BF16),
        ((2 * part, 2 * LANES), BF16),
        ((2, 2, 16, 2 * part), F32),
        ((2, 2, 8, 2 * part), F32),
        ((2, 8, every), F32),
        ((2 * part, attn), BF16),
        ((2 * part, LANES), F32),
        *row_sum,
        ((8, 8, width // 4 + LANES), F32),
        ((4, 8, width // 4), F32),
        ((chunk, width), BF16),
        ((8, 8, width), F32),
        ((8, 8, LANES), F32),
    ]
    return outs, scratch


def kernel_body(
    tokens,
    attn_gain,
    query_weight,
    key_weight,
    value_weight,
    forget_weight,
    forget_bias,
    out_weight,
    ffn_gain,
    gate_weight,
    up_weight,
    down_weight,
    doc_lengths,
    out_grad,
):
    heads = forget_bias.shape[0]
    rows, width = tokens.shape
    block, units = gate_weight.shape
    cols = query_weight.shape[1]
    outs, scratch = layer_shapes(rows, width, heads, units // 4)
    made = pl.pallas_call(
        layer_kernel,
        out_shape=shapes_of(outs),
        in_specs=[HBM] * 2 + [VMEM] * 6 + [SMEM] + [VMEM] + [HBM] * 3 + [SMEM],
        out_specs=[VMEM] * len(outs),
        scratch_shapes=[pltpu.VMEM(*m) for m in scratch] + [pltpu.SemaphoreType.DMA((15,)), pltpu.SemaphoreType.DMA((640,))],
        compiler_params=pltpu.CompilerParams(
            collective_id=0, has_side_effects=True, vmem_limit_bytes=63 << 20
        ),
    )(
        tokens,
        out_grad,
        attn_gain,
        ffn_gain,
        query_weight,
        key_weight,
        value_weight,
        forget_weight.T,
        forget_bias,
        out_weight.T,
        gate_weight,
        up_weight,
        down_weight.T,
        doc_lengths,
    )
    finals = [
        ((rows, width), BF16),
        ((rows, width), BF16),
        ((width,), F32),
        ((block, cols), F32),
        ((block, cols), F32),
        ((block, cols), F32),
        ((heads, block), F32),
        ((heads, LANES), F32),
        ((block, cols), F32),
        ((width,), F32),
        ((block, units), F32),
        ((block, units), F32),
        ((block, units), F32),
    ]
    final = pl.pallas_call(
        narrow_kernel,
        out_shape=shapes_of(finals),
        in_specs=[VMEM] * len(outs),
        out_specs=[VMEM] * len(finals),
        compiler_params=pltpu.CompilerParams(vmem_limit_bytes=63 << 20),
    )(*made)
    return (
        *final[:6],
        final[6].T,
        final[7][:, 0],
        final[8].T,
        *final[9:12],
        final[12].T,
    )


def kernels_fit(tokens, forget_bias, gate_weight):
    rows, width = tokens.shape
    heads = forget_bias.shape[0]
    return (
        lax.axis_size("seq") == 8
        and lax.axis_size("head") == 4
        and heads == 6
        and rows == 2 * LANES
        and width % 256 == 0
        and gate_weight.shape[1] % (4 * LANES) == 0
        and width * gate_weight.shape[1] <= (1536 * 1024)
    )


def unchanged(carried):
    return carried


def contract_rows(left, right):
    return lax.dot_general(
        left, right, (((0,), (0,)), ((), ())), preferred_element_type=jnp.float32
    )


def contract_cols(left, right):
    return lax.dot_general(
        left, right, (((1,), (1,)), ((), ())), preferred_element_type=jnp.float32
    )


def norm_rows(values_in, gain):
    inverse = lax.rsqrt(jnp.mean(values_in * values_in, axis=-1, keepdims=True) + EPSILON)
    normed = values_in * inverse
    return (normed, inverse, normed * gain)


def norm_back(grad_in, normed, inverse, gain):
    scaled = grad_in * gain
    inner = jnp.mean(scaled * normed, axis=-1, keepdims=True)
    return (inverse * (scaled - normed * inner), jnp.sum(grad_in * normed, axis=0))


def doc_index(positions, doc_ends):
    return jnp.sum((positions[:, None] >= doc_ends[None, :]).astype(jnp.int32), axis=1)


def stored_positions(rows, n_seq, local_rows):
    half_rows = local_rows // 2
    device_of = rows // local_rows
    within = rows % local_rows
    group_of = jnp.where(within < half_rows, device_of, 2 * n_seq - 1 - device_of)
    return group_of * half_rows + within % half_rows


def block_scores(
    query_heads, key_heads, query_offsets, key_offsets, query_pos, key_pos, query_docs, key_docs
):
    raw_scores = jnp.einsum(
        "qhd,khd->hqk", query_heads, key_heads, preferred_element_type=jnp.float32
    )
    scores = (
        raw_scores * HEAD_DIM ** (-0.5) + query_offsets.T[:, :, None] - key_offsets.T[:, None, :]
    )
    allowed = (query_docs[:, None] == key_docs[None, :]) & (key_pos[None, :] <= query_pos[:, None])
    return (jnp.where(allowed[None], scores, MASKED), allowed)


def piece_grads(
    query_heads,
    grad_heads,
    log_mass,
    row_delta,
    query_offsets,
    key_heads,
    value_heads,
    key_offsets,
    query_pos,
    key_pos,
    query_docs,
    key_docs,
):
    scores, allowed = block_scores(
        query_heads, key_heads, query_offsets, key_offsets, query_pos, key_pos, query_docs, key_docs
    )
    probs = jnp.where(allowed[None], jnp.exp(scores - log_mass[:, :, None]), 0.0)
    grad_probs = jnp.einsum(
        "qhd,khd->hqk", grad_heads, value_heads, preferred_element_type=jnp.float32
    )
    grad_scores = (probs * (grad_probs - row_delta[:, :, None])).astype(jnp.bfloat16)
    score_sums = grad_scores.astype(jnp.float32)
    query_rows = query_heads.shape[0]
    key_rows = key_heads.shape[0]
    grad_query = jnp.einsum(
        "hqk,khd->qhd", grad_scores, key_heads, preferred_element_type=jnp.float32
    ).reshape(query_rows, -1)
    grad_key = (
        jnp.einsum("hqk,qhd->khd", grad_scores, query_heads, preferred_element_type=jnp.float32)
        * HEAD_DIM ** (-0.5)
    ).reshape(key_rows, -1)
    grad_value = jnp.einsum(
        "hqk,qhd->khd", probs.astype(jnp.bfloat16), grad_heads, preferred_element_type=jnp.float32
    ).reshape(key_rows, -1)
    return (
        grad_query,
        jnp.sum(score_sums, axis=2).T,
        grad_key,
        grad_value,
        -jnp.sum(score_sums, axis=1).T,
    )


def plain_body(
    tokens,
    attn_gain,
    query_weight,
    key_weight,
    value_weight,
    forget_weight,
    forget_bias,
    out_weight,
    ffn_gain,
    gate_weight,
    up_weight,
    down_weight,
    doc_lengths,
    out_grad,
):
    local_rows = tokens.shape[0]
    local_heads = forget_bias.shape[0]
    head_cols = local_heads * HEAD_DIM
    n_seq = lax.axis_size("seq")
    my_index = lax.axis_index("seq")
    first_row = my_index * local_rows
    docs = doc_lengths.shape[0]
    doc_ends = jnp.sum(jnp.where(jnp.tri(docs, dtype=jnp.bool_), doc_lengths[None, :], 0), axis=1)
    local_pos = stored_positions(
        first_row + jnp.arange(local_rows, dtype=jnp.int32), n_seq, local_rows
    )
    local_docs = doc_index(local_pos, doc_ends)
    pos_low = jnp.min(local_pos)
    pos_high = jnp.max(local_pos)
    doc_low = jnp.min(local_docs)
    doc_high = jnp.max(local_docs)
    hidden = gate_weight.shape[1]
    forget_pad = jnp.pad(forget_weight, ((0, 0), (0, 128 - local_heads)))
    w_attn = lax.all_gather(
        jnp.concatenate([query_weight, key_weight, value_weight, forget_pad], axis=1),
        "seq",
        axis=0,
        tiled=True,
    )
    w_rest = lax.all_gather(
        jnp.concatenate([out_weight.T, gate_weight, up_weight, down_weight.T], axis=1),
        "seq",
        axis=0,
        tiled=True,
    )
    w_query = w_attn[:, :head_cols]
    w_key = w_attn[:, head_cols : 2 * head_cols]
    w_value = w_attn[:, 2 * head_cols : 3 * head_cols]
    w_forget = w_attn[:, 3 * head_cols : 3 * head_cols + local_heads]
    w_out_t = w_rest[:, :head_cols]
    w_gate = w_rest[:, head_cols : head_cols + hidden]
    w_up = w_rest[:, head_cols + hidden : head_cols + 2 * hidden]
    w_down_t = w_rest[:, head_cols + 2 * hidden :]
    inputs = tokens.astype(jnp.float32)
    normed_one, inverse_one, scaled_one = norm_rows(inputs, attn_gain)
    h_one = scaled_one.astype(jnp.bfloat16)
    query_flat = jnp.dot(h_one, w_query, preferred_element_type=jnp.float32).astype(jnp.bfloat16)
    key_flat = jnp.dot(h_one, w_key, preferred_element_type=jnp.float32).astype(jnp.bfloat16)
    value_flat = jnp.dot(h_one, w_value, preferred_element_type=jnp.float32).astype(jnp.bfloat16)
    forget_logit = jnp.dot(h_one, w_forget, preferred_element_type=jnp.float32) + forget_bias
    log_forget_all = lax.all_gather(jax.nn.log_sigmoid(forget_logit), "seq", axis=0, tiled=True)
    all_pos = stored_positions(
        jnp.arange(n_seq * local_rows, dtype=jnp.int32), n_seq, local_rows
    )
    earlier = (all_pos[None, :] <= all_pos[:, None]).astype(jnp.float32)
    offsets_all = jnp.dot(earlier, log_forget_all, precision=HIGHEST)
    offsets = lax.dynamic_slice_in_dim(offsets_all, first_row, local_rows, 0)
    query_heads = query_flat.reshape(local_rows, local_heads, HEAD_DIM)
    key_heads = key_flat.reshape(local_rows, local_heads, HEAD_DIM)
    value_heads = value_flat.reshape(local_rows, local_heads, HEAD_DIM)

    def key_range(piece_rows):
        key_pos = stored_positions(jnp.arange(piece_rows, dtype=jnp.int32), n_seq, local_rows)
        key_docs = doc_index(key_pos, doc_ends)
        is_live = (
            (jnp.min(key_pos) <= pos_high)
            & (jnp.max(key_docs) >= doc_low)
            & (jnp.min(key_docs) <= doc_high)
        )
        return (key_pos, key_docs, offsets_all, is_live)

    mass_state = (
        jnp.full((local_heads, local_rows), MASKED, jnp.float32),
        jnp.zeros((local_heads, local_rows), jnp.float32),
    )
    gathered = lax.all_gather(
        jnp.concatenate([key_flat, value_flat, query_flat], axis=1), "seq", axis=0, tiled=True
    )
    key_block = gathered[:, :head_cols]
    piece_rows = key_block.shape[0]
    key_pos, key_docs, key_offsets, is_live = key_range(piece_rows)

    def mass_update(carried_in):
        running_max, running_sum = carried_in
        scores, allowed = block_scores(
            query_heads,
            key_block.reshape(piece_rows, local_heads, HEAD_DIM),
            offsets,
            key_offsets,
            local_pos,
            key_pos,
            local_docs,
            key_docs,
        )
        new_max = jnp.maximum(running_max, jnp.max(scores, axis=2))
        weights = jnp.where(allowed[None], jnp.exp(scores - new_max[:, :, None]), 0.0)
        return (new_max, jnp.sum(weights, axis=2))

    running_max, running_sum = lax.cond(is_live, mass_update, unchanged, mass_state)
    log_mass = running_max + jnp.log(running_sum)
    start_state = (
        jnp.zeros((local_heads, local_rows, HEAD_DIM), jnp.float32),
        jnp.zeros((local_heads, local_rows, HEAD_DIM), jnp.float32),
    )
    attend_key_block = key_block
    value_block = gathered[:, head_cols : 2 * head_cols]
    attend_piece_rows = attend_key_block.shape[0]
    attend_key_pos, attend_key_docs, attend_key_offsets, is_live = key_range(attend_piece_rows)

    def attend_update(carried_in):
        scores, allowed = block_scores(
            query_heads,
            attend_key_block.reshape(attend_piece_rows, local_heads, HEAD_DIM),
            offsets,
            attend_key_offsets,
            local_pos,
            attend_key_pos,
            local_docs,
            attend_key_docs,
        )
        probs = jnp.where(allowed[None], jnp.exp(scores - log_mass[:, :, None]), 0.0)
        probs_low = probs.astype(jnp.bfloat16)
        remainder = (probs - probs_low.astype(jnp.float32)).astype(jnp.bfloat16)
        value_piece = value_block.reshape(attend_piece_rows, local_heads, HEAD_DIM)
        rounded_acc = jnp.einsum(
            "hqk,khd->hqd", probs_low, value_piece, preferred_element_type=jnp.float32
        )
        remainder_acc = jnp.einsum(
            "hqk,khd->hqd", remainder, value_piece, preferred_element_type=jnp.float32
        )
        return (rounded_acc, remainder_acc)

    rounded_acc, remainder_acc = lax.cond(is_live, attend_update, unchanged, start_state)
    attended_rows = rounded_acc.transpose(1, 0, 2)
    exact_rows = (rounded_acc + remainder_acc).transpose(1, 0, 2)
    mixed = attended_rows.reshape(local_rows, head_cols).astype(jnp.bfloat16)
    attn_part = contract_cols(mixed, w_out_t)
    middle = inputs + lax.psum(attn_part, "head")
    normed_two, inverse_two, scaled_two = norm_rows(middle, ffn_gain)
    h_two = scaled_two.astype(jnp.bfloat16)
    gate_value = jnp.dot(h_two, w_gate, preferred_element_type=jnp.float32)
    up_value = jnp.dot(h_two, w_up, preferred_element_type=jnp.float32)
    gate_sigmoid = jax.nn.sigmoid(gate_value)
    gate_silu = gate_value * gate_sigmoid
    activation = (gate_silu * up_value).astype(jnp.bfloat16)
    ffn_part = contract_cols(activation, w_down_t)
    layer_out = (
        middle + lax.psum(ffn_part.astype(jnp.bfloat16), "head").astype(jnp.float32)
    ).astype(jnp.bfloat16)
    grad_act = jnp.dot(out_grad, w_down_t, preferred_element_type=jnp.float32)
    grad_gate = (
        grad_act * up_value * gate_sigmoid * (1.0 + gate_value * (1.0 - gate_sigmoid))
    ).astype(jnp.bfloat16)
    grad_up = (grad_act * gate_silu).astype(jnp.bfloat16)
    part_two = contract_cols(grad_gate, w_gate) + contract_cols(grad_up, w_up)
    grad_two = lax.psum(part_two, "head")
    back_two, gain_two = norm_back(grad_two, normed_two, inverse_two, ffn_gain)
    grad_middle = out_grad.astype(jnp.float32) + back_two
    grad_attn = grad_middle.astype(jnp.bfloat16)
    grad_mixed = jnp.dot(grad_attn, w_out_t, preferred_element_type=jnp.float32).astype(
        jnp.bfloat16
    )
    grad_heads = grad_mixed.reshape(local_rows, local_heads, HEAD_DIM)
    row_delta = jnp.sum(grad_heads.astype(jnp.float32) * exact_rows, axis=2).T
    back_state = (
        jnp.zeros((local_rows, head_cols), jnp.float32),
        jnp.zeros((local_rows, local_heads), jnp.float32),
    )
    back_key_block = key_block
    back_value_block = value_block
    back_piece_rows = back_key_block.shape[0]
    back_key_pos, back_key_docs, back_key_offsets, is_live = key_range(back_piece_rows)

    def back_update(carried_in):
        terms = piece_grads(
            query_heads,
            grad_heads,
            log_mass,
            row_delta,
            offsets,
            back_key_block.reshape(back_piece_rows, local_heads, HEAD_DIM),
            back_value_block.reshape(back_piece_rows, local_heads, HEAD_DIM),
            back_key_offsets,
            local_pos,
            back_key_pos,
            local_docs,
            back_key_docs,
        )
        return (terms[0], terms[1])

    grad_query, grad_query_off = lax.cond(is_live, back_update, unchanged, back_state)
    stats = lax.all_gather(
        jnp.concatenate([log_mass.T, row_delta.T], axis=1), "seq", axis=0, tiled=True
    )
    stats_mass, stats_delta = stats[:, :local_heads], stats[:, local_heads:]
    key_state = (
        jnp.zeros((local_rows, head_cols), jnp.float32),
        jnp.zeros((local_rows, head_cols), jnp.float32),
        jnp.zeros((local_rows, local_heads), jnp.float32),
    )
    piece_query = gathered[:, 2 * head_cols :]
    piece_grad = lax.all_gather(grad_mixed, "seq", axis=0, tiled=True)
    key_piece_rows = piece_query.shape[0]
    piece_pos = stored_positions(jnp.arange(key_piece_rows, dtype=jnp.int32), n_seq, local_rows)
    piece_docs = doc_index(piece_pos, doc_ends)
    is_live = (
        (pos_low <= jnp.max(piece_pos))
        & (jnp.max(piece_docs) >= doc_low)
        & (jnp.min(piece_docs) <= doc_high)
    )

    def key_update(carried_in):
        piece_mass = stats_mass.T
        piece_delta = stats_delta.T
        terms = piece_grads(
            piece_query.reshape(key_piece_rows, local_heads, HEAD_DIM),
            piece_grad.reshape(key_piece_rows, local_heads, HEAD_DIM),
            piece_mass,
            piece_delta,
            offsets_all,
            key_heads,
            value_heads,
            offsets,
            piece_pos,
            local_pos,
            piece_docs,
            local_docs,
        )
        return (terms[2], terms[3], terms[4])

    grad_key, grad_value, grad_key_off = lax.cond(is_live, key_update, unchanged, key_state)
    grad_query_low = (grad_query * HEAD_DIM ** (-0.5)).astype(jnp.bfloat16)
    grad_key_low = grad_key.astype(jnp.bfloat16)
    grad_value_low = grad_value.astype(jnp.bfloat16)
    grad_offsets = grad_query_off + grad_key_off
    grad_off_all = lax.all_gather(grad_offsets, "seq", axis=0, tiled=True)
    later = (all_pos[None, :] >= local_pos[:, None]).astype(jnp.float32)
    grad_log = jnp.dot(later, grad_off_all, precision=HIGHEST)
    grad_logit = grad_log * jax.nn.sigmoid(-forget_logit)
    forget_table = w_forget.astype(jnp.float32)
    part_one = (
        contract_cols(grad_query_low, w_query)
        + contract_cols(grad_key_low, w_key)
        + contract_cols(grad_value_low, w_value)
        + lax.dot_general(grad_logit, forget_table, (((1,), (1,)), ((), ())), precision=HIGHEST)
    )
    grad_one = lax.psum(part_one.astype(jnp.bfloat16), "head").astype(jnp.float32)
    back_one, gain_one = norm_back(grad_one, normed_one, inverse_one, attn_gain)
    tokens_grad = (grad_middle + back_one).astype(jnp.bfloat16)
    forget_term = lax.dot_general(
        h_one.astype(jnp.float32), grad_logit, (((0,), (0,)), ((), ())), precision=HIGHEST
    )
    scatter_cols = [
        contract_rows(grad_attn, mixed),
        contract_rows(h_two, grad_gate),
        contract_rows(h_two, grad_up),
        contract_rows(out_grad, activation),
        contract_rows(h_one, grad_query_low),
        contract_rows(h_one, grad_key_low),
        contract_rows(h_one, grad_value_low),
        jnp.pad(forget_term, ((0, 0), (0, 128 - local_heads))),
    ]
    first_sum = lax.psum_scatter(
        jnp.concatenate([t.astype(jnp.bfloat16) for t in scatter_cols[:4]], axis=1),
        "seq",
        scatter_dimension=0,
        tiled=True,
    ).astype(jnp.float32)
    second_sum = lax.psum_scatter(
        jnp.concatenate([t.astype(jnp.bfloat16) for t in scatter_cols[4:]], axis=1),
        "seq",
        scatter_dimension=0,
        tiled=True,
    ).astype(jnp.float32)
    out_weight_grad = first_sum[:, :head_cols].T
    gate_weight_grad = first_sum[:, head_cols : head_cols + hidden]
    up_weight_grad = first_sum[:, head_cols + hidden : head_cols + 2 * hidden]
    down_weight_grad = first_sum[:, head_cols + 2 * hidden :].T
    query_weight_grad = second_sum[:, :head_cols]
    key_weight_grad = second_sum[:, head_cols : 2 * head_cols]
    value_weight_grad = second_sum[:, 2 * head_cols : 3 * head_cols]
    forget_weight_grad = second_sum[:, 3 * head_cols : 3 * head_cols + local_heads]
    attn_gain_grad, ffn_gain_grad, forget_bias_grad = lax.psum(
        (gain_one, gain_two, jnp.sum(grad_logit, axis=0)), "seq"
    )
    return (
        layer_out,
        tokens_grad,
        attn_gain_grad,
        query_weight_grad,
        key_weight_grad,
        value_weight_grad,
        forget_weight_grad,
        forget_bias_grad,
        out_weight_grad,
        ffn_gain_grad,
        gate_weight_grad,
        up_weight_grad,
        down_weight_grad,
    )


def body(*args):
    fits = kernels_fit(args[0], args[6], args[9])
    return (kernel_body if fits else plain_body)(*args)


def solution(mesh):
    return jax.shard_map(
        body,
        mesh=mesh,
        in_specs=(
            P("seq", None),
            P(),
            P("seq", "head"),
            P("seq", "head"),
            P("seq", "head"),
            P("seq", "head"),
            P("head"),
            P("head", "seq"),
            P(),
            P("seq", "head"),
            P("seq", "head"),
            P("head", "seq"),
            P(),
            P("seq", None),
        ),
        out_specs=(
            P("seq", None),
            P("seq", None),
            P(),
            P("seq", "head"),
            P("seq", "head"),
            P("seq", "head"),
            P("seq", "head"),
            P("head"),
            P("head", "seq"),
            P(),
            P("seq", "head"),
            P("seq", "head"),
            P("head", "seq"),
        ),
        check_vma=False,
    )
```
